32 devices in a mesh: section: 2 (over core), shard: 4 (over z), rep: 4 (over y, x).
Axes of the slice: x: 2, y: 2, z: 4, core: 2. Of those that a mesh axis runs over, the one named last changes fastest.
Arguments:
- boundary_in: bfloat16 [2, 2, 4, 1024, 1536], P('section', None, 'rep', 'shard'), may hold values from -6 to 6
- lengths: int32 [2, 4, 4], P(None, 'rep'), may hold values from 0 to 1024, as said below
- seq_order: int32 [2, 4, 4], P(None, 'rep'), may hold values from 0 to 3, each once within a row
- norm_gain: bfloat16 [2, 1536], P('section', 'shard'), may hold values from 0.5 to 1.5
- in_weight: bfloat16 [2, 1536, 6448], P('section', 'shard'), may hold values from -0.15625 to 0.15625
- conv_weight: bfloat16 [2, 4, 3328], P('section', None, 'shard'), may hold values from -3 to 3
- conv_bias: bfloat16 [2, 3328], P('section', 'shard'), may hold values from -1.5 to 1.5
- dt_bias: bfloat16 [2, 48], P('section', 'shard'), may hold values from -12 to -3
- a_log: bfloat16 [2, 48], P('section', 'shard'), may hold values from -0.5 to 0.5
- d_skip: bfloat16 [2, 48], P('section', 'shard'), may hold values from 0.5 to 1.5
- out_gain: bfloat16 [2, 3072], P('section', 'shard'), may hold values from 0.5 to 1.5
- out_weight: bfloat16 [2, 3072, 1536], P('section', 'shard'), may hold values from -0.109375 to 0.109375
Outputs:
- boundary: float32 [2, 2, 4, 1024, 1536], P('section', None, 'rep', 'shard')
- norm_gain_grad: float32 [2, 1536], P('section', 'shard')
- in_weight_grad: float32 [2, 1536, 6448], P('section', 'shard')
- conv_weight_grad: float32 [2, 4, 3328], P('section', None, 'shard')
- conv_bias_grad: float32 [2, 3328], P('section', 'shard')
- dt_bias_grad: float32 [2, 48], P('section', 'shard')
- a_log_grad: float32 [2, 48], P('section', 'shard')
- d_skip_grad: float32 [2, 48], P('section', 'shard')
- out_gain_grad: float32 [2, 3072], P('section', 'shard')
- out_weight_grad: float32 [2, 3072, 1536], P('section', 'shard')
The draws below stay inside these ranges and needn't reach their ends.
Inputs may be any that keep to these rules, and one draw needn't show every extreme that they name: Each row of 4 lengths sums to 1024; in each replica one micro-batch, chosen by the seed, is one sequence of all 1024 tokens with zeros in its other slots; other rows may hold zeros. `seq_order`: each row is a permutation of the 4 slots.
All inputs are finite; a program needn't handle non-finite values.
Results may differ from the reference program's by a relative error of at most 0.025.
Values may be sent and summed in bfloat16 or wider, within the bound.
A program may use at most 384 MiB of HBM per device.

```python
import jax
import jax.numpy as jnp
from jax import lax

D = 1536
P_SIZE = 64
N = 128
KW = 4
BLOCK = 256
MICRO = 2
NSEQ = 4
DI = 3072
H = 48
CONV = 3328
PIN = 6448
SEQTOK = 1024
N_REP = 4


def draw_lengths(key, part):
    key = jax.random.fold_in(key, 11)
    cut_key, pick_key = jax.random.split(key)
    cut_points = jax.random.randint(cut_key, (MICRO, N_REP, NSEQ - 1), 0, SEQTOK + 1)
    cut_points = jnp.sort(cut_points, axis=-1).astype(jnp.int32)
    low_border = jnp.zeros((MICRO, N_REP, 1), jnp.int32)
    high_border = jnp.full((MICRO, N_REP, 1), SEQTOK, jnp.int32)
    borders = jnp.concatenate([low_border, cut_points, high_border], axis=-1)
    ragged = borders[:, :, 1:] - borders[:, :, :-1]
    complete = jnp.zeros((NSEQ,), jnp.int32).at[0].set(SEQTOK)
    chosen = jax.random.randint(pick_key, (N_REP,), 0, MICRO)
    single = jnp.arange(MICRO)[:, None] == chosen[None, :]
    return jnp.where(single[:, :, None], complete[None, None, :], ragged).astype(jnp.int32)


def shard_levels(own_key, extent, shards, smallest, top_value):
    def one(dim, parts):
        steps = jax.random.uniform(jax.random.fold_in(jax.random.fold_in(own_key, 6), dim), (parts,), jnp.float32, smallest / len(shards), top_value / len(shards))
        return jnp.repeat(jnp.exp(steps), extent[dim] // parts).reshape((-1,) + (1,) * (len(extent) - dim - 1))

    gain = one(*shards[0])
    for cut in shards[1:]:
        gain = gain * one(*cut)
    return gain


def noise(key, extent, scale, bound, shards=(), held_as=jnp.bfloat16):
    gain = shard_levels(key, extent, shards, -0.22, 0.18) if shards else 1.0
    values = jax.random.normal(key, extent, jnp.float32) * scale * gain
    return jnp.minimum(jnp.maximum(values, -bound), bound).astype(held_as)


def setup_inputs(seed: int = 0) -> dict:
    seeds = jax.random.split(jax.random.key(seed), 13)
    boundary_in = noise(seeds[0], (2, MICRO, N_REP, SEQTOK, D), 1.0, 6.0, ((0, 2), (2, 4), (3, 4)))
    lengths = draw_lengths(jax.random.fold_in(seeds[12], 71), 0)
    seq_order = jax.vmap(lambda own: jax.random.permutation(own, NSEQ))(jax.random.split(seeds[2], MICRO * N_REP)).reshape((MICRO, N_REP, NSEQ)).astype(jnp.int32)
    norm_gain = jnp.clip(1.0 + 0.1 * jax.random.normal(seeds[3], (2, D), jnp.float32), 0.5, 1.5).astype(jnp.bfloat16)
    in_weight = noise(seeds[4], (2, D, PIN), D ** -0.5, 0.15625, ((0, 2), (1, 4)))
    conv_weight = noise(seeds[5], (2, KW, CONV), KW ** -0.5, 3.0, ((0, 2), (2, 4)))
    conv_bias = noise(seeds[6], (2, CONV), 0.3, 1.5, ((0, 2), (1, 4)))
    dt_bias = jnp.clip(-12.0 + 9.0 * jax.random.uniform(seeds[7], (2, H), jnp.float32) ** shard_levels(seeds[7], (2, H), ((0, 2), (1, 4)), -0.2, 0.2), -12.0, -3.0).astype(jnp.bfloat16)
    a_log = jnp.clip(jax.random.uniform(seeds[8], (2, H), jnp.float32, -0.5, 0.5) * shard_levels(seeds[8], (2, H), ((0, 2), (1, 4)), -0.4, 0.0), -0.5, 0.5).astype(jnp.bfloat16)
    d_skip = jnp.clip(0.5 + 1.0 * jax.random.uniform(seeds[9], (2, H), jnp.float32) ** shard_levels(seeds[9], (2, H), ((0, 2), (1, 4)), -0.2, 0.2), 0.5, 1.5).astype(jnp.bfloat16)
    out_gain = jnp.clip(1.0 + 0.1 * jax.random.normal(seeds[10], (2, DI), jnp.float32), 0.5, 1.5).astype(jnp.bfloat16)
    out_weight = noise(seeds[11], (2, DI, D), DI ** -0.5, 0.109375, ((0, 2), (1, 4)))
    return {"boundary_in": boundary_in, "lengths": lengths, "seq_order": seq_order, "norm_gain": norm_gain, "in_weight": in_weight, "conv_weight": conv_weight, "conv_bias": conv_bias, "dt_bias": dt_bias, "a_log": a_log, "d_skip": d_skip, "out_gain": out_gain, "out_weight": out_weight}


EPSILON = 1e-05
PRECISE = lax.Precision.HIGHEST

@jax.custom_vjp
def low(v):
    return lax.optimization_barrier(v.astype(jnp.bfloat16)).astype(jnp.float32)

@jax.custom_vjp
def low_back(v):
    return v

def low_keep(v):
    return (low(v), None)

def low_pass(kept, grad):
    return (grad,)

def back_keep(v):
    return (v, None)

def back_low(kept, grad):
    return (low(grad),)
low.defvjp(low_keep, low_pass)
low_back.defvjp(back_keep, back_low)

def place_segments(positions, seq_lengths, row_order):
    placed = jnp.take(seq_lengths, row_order).astype(jnp.int32)
    finish = jnp.cumsum(placed, dtype=jnp.int32)
    segment = lax.optimization_barrier(jnp.sum((positions[:, None] >= finish[None, :]).astype(jnp.int32), axis=1))
    return jnp.where(positions < 0, -1, segment).astype(jnp.int32)

def block_step(carry_state, pieces):
    x_heads, b_rows, c_rows, log_decay, step_size, segment, before = pieces
    running = jnp.cumsum(log_decay, axis=0)
    places = jnp.arange(x_heads.shape[0])
    linked = (places[:, None] >= places[None, :]) & (segment[:, None] == segment[None, :])
    linked3 = linked[:, :, None]
    gap_sums = jnp.where(linked3, running[:, None, :] - running[None, :, :], 0.0)
    decays = jnp.where(linked3, jnp.exp(gap_sums), 0.0)
    scores = jnp.dot(c_rows, b_rows.T, precision=PRECISE)
    mixing = scores[:, :, None] * decays * step_size[None, :, :]
    inside_part = jnp.einsum('tsh,shp->thp', mixing, x_heads, precision=PRECISE)
    carried = (segment == before).astype(jnp.float32)
    reach = jnp.exp(running) * carried[:, None]
    carried_part = jnp.einsum('tn,hpn->thp', c_rows, carry_state, precision=PRECISE) * reach[:, :, None]
    closing = segment[-1]
    tail_weight = jnp.exp(running[-1][None, :] - running) * step_size * (segment == closing).astype(jnp.float32)[:, None]
    fresh_state = jnp.einsum('sh,shp,sn->hpn', tail_weight, x_heads, b_rows, precision=PRECISE)
    retained = jnp.exp(running[-1]) * (closing == before).astype(jnp.float32)
    return (retained[:, None, None] * carry_state + fresh_state, inside_part + carried_part)

def mamba_layer(source, params, segment, befores):
    norm_gain, in_weight, conv_weight, conv_bias, dt_bias, a_log, d_skip, out_gain, out_weight = params
    rows_here = source.shape[0]
    inv_rms = lax.rsqrt(lax.optimization_barrier(jnp.mean(source * source, axis=-1, keepdims=True)) + EPSILON)
    normed = low(source * inv_rms * norm_gain)
    projected = low_back(low(jnp.dot(normed, in_weight, precision=PRECISE)))
    gate_part = projected[:, :DI]
    mixed_part = projected[:, DI:DI + CONV]
    raw_step = projected[:, DI + CONV:]
    conv_sum = conv_bias + conv_weight[KW - 1] * mixed_part
    for lag in range(1, KW):
        shifted = jnp.concatenate([jnp.zeros((lag, CONV), jnp.float32), mixed_part[:-lag]], axis=0)
        same_seq = jnp.concatenate([jnp.zeros((lag,), jnp.float32), (segment[lag:] == segment[:-lag]).astype(jnp.float32)])
        conv_sum = conv_sum + conv_weight[KW - 1 - lag] * shifted * same_seq[:, None]
    active = jax.nn.silu(conv_sum)
    x_heads = active[:, :DI].reshape(rows_here, H, P_SIZE)
    b_rows = active[:, DI:DI + N]
    c_rows = active[:, DI + N:]
    step_size = jax.nn.softplus(raw_step + dt_bias)
    log_decay = -step_size * jnp.exp(a_log)

    def blocks(member):
        return member.reshape((rows_here // BLOCK, BLOCK) + member.shape[1:])
    start_state = jnp.zeros((H, P_SIZE, N), jnp.float32)
    pieces = (blocks(x_heads), blocks(b_rows), blocks(c_rows), blocks(log_decay), blocks(step_size), blocks(segment), befores)
    final_state, mixer_out = lax.scan(jax.checkpoint(block_step), start_state, pieces)
    mixer_out = mixer_out.reshape(rows_here, H, P_SIZE) + d_skip[:, None] * x_heads
    gated = mixer_out.reshape(rows_here, DI) * jax.nn.silu(gate_part)
    inv_gated = lax.rsqrt(lax.optimization_barrier(jnp.mean(gated * gated, axis=-1, keepdims=True)) + EPSILON)
    outgoing = low(gated * inv_gated * out_gain)
    return source + jnp.dot(outgoing, out_weight, precision=PRECISE)

def reference(boundary_in, lengths, seq_order, norm_gain, in_weight, conv_weight, conv_bias, dt_bias, a_log, d_skip, out_gain, out_weight):
    weights = tuple((member.astype(jnp.float32) for member in (norm_gain, in_weight, conv_weight, conv_bias, dt_bias, a_log, d_skip, out_gain, out_weight)))
    positions = jnp.arange(SEQTOK, dtype=jnp.int32)

    def one_group(grad_sums, group_index):
        micro_slot = group_index // N_REP
        replica = group_index % N_REP
        segment = place_segments(positions, lengths[micro_slot, replica], seq_order[micro_slot, replica])
        shifted = jnp.concatenate([jnp.full((1,), -1, jnp.int32), segment[:-1].astype(jnp.int32)])
        befores = shifted[::BLOCK]
        source = boundary_in[0, micro_slot, replica].astype(jnp.float32)
        cotangent = boundary_in[1, micro_slot, replica].astype(jnp.float32)

        def two_layers(layer_in, params):
            lower = tuple((member[0] for member in params))
            upper = tuple((member[1] for member in params))
            middle = low_back(low(mamba_layer(layer_in, lower, segment, befores)))
            return mamba_layer(middle, upper, segment, befores)
        result, pullback = jax.vjp(two_layers, source, weights)
        source_grad, weight_grads = pullback(cotangent)
        grad_sums = tuple((running_sum + piece_grad for running_sum, piece_grad in zip(grad_sums, weight_grads)))
        return (grad_sums, (source_grad, result))
    zero_sums = tuple((jnp.zeros_like(member) for member in weights))
    grad_sums, outputs = lax.scan(one_group, zero_sums, jnp.arange(MICRO * N_REP, dtype=jnp.int32))
    boundary = jnp.stack([outputs[0], outputs[1]]).reshape(2, MICRO, N_REP, SEQTOK, D)
    return (boundary, grad_sums[0], grad_sums[1], grad_sums[2], grad_sums[3], grad_sums[4], grad_sums[5], grad_sums[6], grad_sums[7], grad_sums[8])
```

```python
import functools

import jax
import jax.numpy as jnp
from jax import lax
from jax.experimental import pallas as pl
from jax.experimental.pallas import tpu as pltpu
from jax.sharding import PartitionSpec as P

D = 1536
P_SIZE = 64
N = 128
KW = 4
BLOCK = 256
MICRO = 2
NSEQ = 4
DI = 3072
H = 48
CONV = 3328


EPSILON = 1e-05
PRECISE = lax.Precision.HIGHEST


def from_behind(shard, axis, by):
    devices = lax.axis_size(axis)
    pairs = [(i, i + by) for i in range(devices) if 0 <= i + by < devices]
    return lax.ppermute(shard, axis, pairs)


def entering(value, axis, join, neutral):
    count, mine = (lax.axis_size(axis), lax.axis_index(axis))
    pieces = jax.tree.map(lambda part: lax.all_gather(part, axis), value)
    subtotal = jax.tree.map(
        lambda part, zero: jnp.full_like(part, 0) + jnp.asarray(zero, part.dtype), value, neutral
    )

    def turn(position, subtotal):
        longer = join(subtotal, jax.tree.map(lambda part: part[position], pieces))
        return jax.tree.map(lambda new, old: jnp.where(position < mine, new, old), longer, subtotal)

    return lax.fori_loop(0, count - 1, turn, subtotal)


def entering_2(shard, axis, join, neutral):
    count = lax.axis_size(axis)
    place = lax.axis_index(axis)
    ahead = count - 1 - place
    gathered = jax.tree.map(
        lambda a, kind: lax.all_gather(a.astype(kind), axis),
        shard,
        jax.tree.map(lambda a: jnp.bfloat16 if a.dtype == jnp.float32 else a.dtype, shard),
    )
    state = jax.tree.map(lambda a, e: jnp.zeros_like(a) + jnp.asarray(e, a.dtype), shard, neutral)

    def one(turn, state):
        source = count - 1 - turn
        return join(
            state,
            jax.tree.map(
                lambda a, own: lax.dynamic_index_in_dim(a, source, 0, False).astype(own.dtype),
                gathered,
                shard,
            ),
        )

    return lax.fori_loop(0, ahead, one, state)


def contract(left, right, left_dim, right_dim):
    return lax.dot_general(
        left, right, (((left_dim,), (right_dim,)), ((), ())), preferred_element_type=jnp.float32
    )


def input_norm(source, gain):
    inv_rms = lax.rsqrt(jnp.mean(source * source, axis=-1, keepdims=True) + EPSILON)
    return source * inv_rms * gain


def block_step(carry_state, pieces):
    x_heads, b_rows, c_rows, log_decay, step_size, segment, before = pieces
    running = jnp.cumsum(log_decay, axis=0)
    places = jnp.arange(x_heads.shape[0])
    linked = (places[:, None] >= places[None, :]) & (segment[:, None] == segment[None, :])
    linked3 = linked[:, :, None]
    gap_sums = jnp.where(linked3, running[:, None, :] - running[None, :, :], 0.0)
    decays = jnp.where(linked3, jnp.exp(gap_sums), 0.0)
    scores = jnp.dot(c_rows, b_rows.T, precision=PRECISE)
    mixing = scores[:, :, None] * decays * step_size[None, :, :]
    inside_part = jnp.einsum("tsh,shp->thp", mixing, x_heads, precision=PRECISE)
    carried = (segment == before).astype(jnp.float32)
    reach = jnp.exp(running) * carried[:, None]
    carried_part = (
        jnp.einsum("tn,hpn->thp", c_rows, carry_state, precision=PRECISE) * reach[:, :, None]
    )
    closing = segment[-1]
    tail_weight = (
        jnp.exp(running[-1][None, :] - running)
        * step_size
        * (segment == closing).astype(jnp.float32)[:, None]
    )
    fresh_state = jnp.einsum("sh,shp,sn->hpn", tail_weight, x_heads, b_rows, precision=PRECISE)
    retained = jnp.exp(running[-1]) * (closing == before).astype(jnp.float32)
    return (retained[:, None, None] * carry_state + fresh_state, inside_part + carried_part)


def conv_inputs(wide_rows, raw_step, conv_weight, conv_bias, dt_bias, a_log, lag_masks):
    rows_here = raw_step.shape[0]
    conv_sum = conv_bias + conv_weight[KW - 1] * wide_rows[KW - 1 :]
    for lag in range(1, KW):
        conv_sum = (
            conv_sum
            + conv_weight[KW - 1 - lag]
            * wide_rows[KW - 1 - lag : KW - 1 - lag + rows_here]
            * lag_masks[lag - 1][:, None]
        )
    active = jax.nn.silu(conv_sum)
    x_heads = active[:, :DI].reshape(rows_here, H, P_SIZE)
    b_rows = active[:, DI : DI + N]
    c_rows = active[:, DI + N :]
    step_size = jax.nn.softplus(raw_step + dt_bias)
    log_decay = -step_size * jnp.exp(a_log)
    return (x_heads, b_rows, c_rows, log_decay, step_size)


def local_scan(x_heads, b_rows, c_rows, log_decay, step_size, segment, befores, seg_before):
    rows_here = x_heads.shape[0]

    def blocks(member):
        return member.reshape((rows_here // BLOCK, BLOCK) + member.shape[1:])

    start_state = jnp.zeros((H, P_SIZE, N), jnp.float32)
    pieces = (
        blocks(x_heads),
        blocks(b_rows),
        blocks(c_rows),
        blocks(log_decay),
        blocks(step_size),
        blocks(segment),
        befores,
    )
    end_state, mixer_out = lax.scan(jax.checkpoint(block_step), start_state, pieces)
    retained = jnp.exp(jnp.sum(log_decay, axis=0)) * (segment[-1] == seg_before).astype(jnp.float32)
    return (mixer_out.reshape(rows_here, H, P_SIZE), end_state, retained)


def state_entry(c_rows, log_decay, state_in, carried):
    reach = jnp.exp(jnp.cumsum(log_decay, axis=0)) * carried[:, None]
    return jnp.einsum("tn,hpn->thp", c_rows, state_in, precision=PRECISE) * reach[:, :, None]


def gate_norm(mixer_out, x_heads, d_skip, gate_part, out_gain):
    rows_here = x_heads.shape[0]
    total_out = mixer_out + d_skip[:, None] * x_heads
    gated = total_out.reshape(rows_here, DI) * jax.nn.silu(gate_part)
    inv_gated = lax.rsqrt(jnp.mean(gated * gated, axis=-1, keepdims=True) + EPSILON)
    return gated * inv_gated * out_gain


def carry_forward(earlier, later):
    return (earlier[0] * later[0], later[0][:, None, None] * earlier[1] + later[1])


def carry_backward(earlier, later):
    return (later[0] * earlier[0], later[1] + later[0][:, None, None] * earlier[1])


def segment_marks(lengths, seq_order, micro_slot, row_start, rows_here):
    micro_slot = jnp.clip(micro_slot, 0, MICRO - 1)
    seq_lengths = lax.dynamic_index_in_dim(lengths[:, 0], micro_slot, 0, keepdims=False)
    row_order = lax.dynamic_index_in_dim(seq_order[:, 0], micro_slot, 0, keepdims=False)
    picks = (row_order[:, None] == jnp.arange(NSEQ, dtype=jnp.int32)[None, :]).astype(jnp.int32)
    placed = jnp.sum(picks * seq_lengths[None, :], axis=1)
    finish = jnp.cumsum(placed, dtype=jnp.int32)
    positions = row_start + jnp.arange(-(KW - 1), rows_here, dtype=jnp.int32)
    extended = jnp.sum((positions[:, None] >= finish[None, :]).astype(jnp.int32), axis=1)
    extended = jnp.where(positions < 0, -1, extended)
    segment = extended[KW - 1 :]
    seg_before = extended[KW - 2]
    lag_masks = jnp.stack(
        [
            (extended[KW - 1 - lag : KW - 1 - lag + rows_here] == segment).astype(jnp.float32)
            for lag in range(1, KW)
        ]
    )
    befores = jnp.concatenate([seg_before[None], segment[:-1]])[::BLOCK]
    carried = (segment == seg_before).astype(jnp.float32)
    return (segment, lag_masks, befores, seg_before, carried)


def mixer_pass(projected, weights, marks):
    norm_gain, in_weight, conv_weight, conv_bias, dt_bias, a_log, d_skip, out_gain, out_weight = (
        weights
    )
    segment, lag_masks, befores, seg_before, carried = marks
    rows_here = projected.shape[0]
    gate_part = projected[:, :DI].astype(jnp.float32)
    mixed_part = projected[:, DI : DI + CONV]
    raw_step = projected[:, DI + CONV :].astype(jnp.float32)
    rim_rows = from_behind(mixed_part[rows_here - (KW - 1) :], "shard", 1)
    wide_rows = jnp.concatenate([rim_rows, mixed_part], axis=0).astype(jnp.float32)

    def conv_section(wide_rows, raw_step, conv_weight, conv_bias, dt_bias, a_log):
        return conv_inputs(wide_rows, raw_step, conv_weight, conv_bias, dt_bias, a_log, lag_masks)

    conv_outs, conv_pull = jax.vjp(
        conv_section, wide_rows, raw_step, conv_weight, conv_bias, dt_bias, a_log
    )
    x_heads, b_rows, c_rows, log_decay, step_size = conv_outs

    def scan_section(x_heads, b_rows, c_rows, log_decay, step_size):
        return local_scan(
            x_heads, b_rows, c_rows, log_decay, step_size, segment, befores, seg_before
        )

    scan_outs, scan_pull = jax.vjp(scan_section, x_heads, b_rows, c_rows, log_decay, step_size)
    local_out, end_state, retained = scan_outs
    identity = (jnp.ones((H,), jnp.float32), jnp.zeros((H, P_SIZE, N), jnp.float32))
    prefix = entering((retained, end_state), "shard", carry_forward, identity)
    state_in = prefix[1]

    def entry_section(c_rows, log_decay, state_in):
        return state_entry(c_rows, log_decay, state_in, carried)

    entered, entry_pull = jax.vjp(entry_section, c_rows, log_decay, state_in)
    mixer_out = local_out + entered
    outgoing, norm_pull = jax.vjp(gate_norm, mixer_out, x_heads, d_skip, gate_part, out_gain)
    return (
        outgoing.astype(jnp.bfloat16),
        (conv_pull, scan_pull, entry_pull, norm_pull, retained, state_in),
    )


def mamba_forward(source, weights, marks):
    normed = input_norm(source, weights[0]).astype(jnp.bfloat16)
    projected = jnp.dot(normed, weights[1], preferred_element_type=jnp.float32).astype(jnp.bfloat16)
    outgoing, unused_pulls = mixer_pass(projected, weights, marks)
    return source + jnp.dot(outgoing, weights[8], preferred_element_type=jnp.float32)


def mamba_backward(source, incoming, weights, marks):
    norm_gain, in_weight, conv_weight, conv_bias, dt_bias, a_log, d_skip, out_gain, out_weight = (
        weights
    )
    rows_here = source.shape[0]
    normed, front_pull = jax.vjp(input_norm, source, norm_gain)
    normed_low = normed.astype(jnp.bfloat16)
    projected = jnp.dot(normed_low, in_weight, preferred_element_type=jnp.float32).astype(
        jnp.bfloat16
    )
    outgoing, pulls = mixer_pass(projected, weights, marks)
    conv_pull, scan_pull, entry_pull, norm_pull, retained, state_in = pulls
    incoming_low = incoming.astype(jnp.bfloat16)
    out_weight_grad = contract(outgoing, incoming_low, 0, 0)
    outgoing_grad = contract(incoming_low, out_weight, 1, 1)
    mixer_grad, x_grad_a, d_skip_grad, gate_grad, out_gain_grad = norm_pull(outgoing_grad)
    c_grad_a, decay_grad_a, direct = entry_pull(mixer_grad)
    identity = (jnp.ones((H,), jnp.float32), jnp.zeros((H, P_SIZE, N), jnp.float32))
    suffix = entering_2((retained, direct), "shard", carry_backward, identity)
    later_grad = suffix[1]
    retained_grad = jnp.sum(later_grad * state_in, axis=(1, 2))
    x_grad_b, b_grad, c_grad_b, decay_grad_b, step_grad = scan_pull(
        (mixer_grad, later_grad, retained_grad)
    )
    conv_grads = conv_pull(
        (x_grad_a + x_grad_b, b_grad, c_grad_a + c_grad_b, decay_grad_a + decay_grad_b, step_grad)
    )
    wide_grad, raw_grad, conv_weight_grad, conv_bias_grad, dt_bias_grad, a_log_grad = conv_grads
    back_rows = from_behind(wide_grad[: KW - 1].astype(jnp.bfloat16), "shard", -1).astype(
        jnp.float32
    )
    filler = jnp.zeros((rows_here - (KW - 1), CONV), jnp.float32)
    mixed_grad = wide_grad[KW - 1 :] + jnp.concatenate([filler, back_rows], axis=0)
    projected_grad = jnp.concatenate([gate_grad, mixed_grad, raw_grad], axis=1).astype(jnp.bfloat16)
    in_weight_grad = contract(normed_low, projected_grad, 0, 0)
    normed_grad = contract(projected_grad, in_weight, 1, 1)
    source_grad, norm_gain_grad = front_pull(normed_grad)
    weight_grads = (
        norm_gain_grad,
        in_weight_grad,
        conv_weight_grad,
        conv_bias_grad,
        dt_bias_grad,
        a_log_grad,
        d_skip_grad,
        out_gain_grad,
        out_weight_grad,
    )
    return (incoming + source_grad, weight_grads)


def per_device(
    boundary_in,
    lengths,
    seq_order,
    norm_gain,
    in_weight,
    conv_weight,
    conv_bias,
    dt_bias,
    a_log,
    d_skip,
    out_gain,
    out_weight,
):
    section_index = lax.axis_index("section")
    is_first = section_index == 0
    rows_here = boundary_in.shape[3]
    row_start = lax.axis_index("shard") * rows_here

    def current():
        whole = (
            lax.all_gather(norm_gain, "shard", axis=1, tiled=True),
            lax.all_gather(in_weight, "shard", axis=1, tiled=True),
            lax.all_gather(conv_weight, "shard", axis=2, tiled=True),
            lax.all_gather(conv_bias, "shard", axis=1, tiled=True),
            lax.all_gather(dt_bias, "shard", axis=1, tiled=True),
            lax.all_gather(a_log, "shard", axis=1, tiled=True),
            lax.all_gather(d_skip, "shard", axis=1, tiled=True),
            lax.all_gather(out_gain, "shard", axis=1, tiled=True),
            lax.all_gather(out_weight, "shard", axis=1, tiled=True),
        )
        return tuple(
            (
                member[0] if slot_index in (1, 8) else member[0].astype(jnp.float32)
                for slot_index, member in enumerate(whole)
            )
        )

    source_rows = boundary_in[0, :, 0]
    arrived = jnp.zeros((rows_here, D), jnp.bfloat16)
    inputs = []
    results = []
    for step_index in range(MICRO + 1):
        own_rows = source_rows[min(step_index, MICRO - 1)]
        layer_in = jnp.where(is_first, own_rows, arrived)
        inputs.append(layer_in)
        marks = segment_marks(lengths, seq_order, step_index - section_index, row_start, rows_here)
        layer_out = mamba_forward(layer_in.astype(jnp.float32), current(), marks)
        results.append(layer_out)
        if step_index < MICRO:
            arrived = from_behind(layer_out.astype(jnp.bfloat16), "section", 1)
    returned = jnp.zeros((rows_here, D), jnp.bfloat16)
    totals = None
    source_grads = []
    for step_index in range(MICRO + 1):
        micro_slot = step_index - 1 + section_index
        is_valid = (micro_slot >= 0) & (micro_slot < MICRO)
        own_rows = source_rows[min(step_index, MICRO - 1)]
        incoming = jnp.where(is_first, returned, own_rows).astype(jnp.float32)
        incoming = jnp.where(is_valid, incoming, 0.0)
        layer_in = jnp.where(
            is_first, inputs[max(step_index - 1, 0)], inputs[min(step_index + 1, MICRO)]
        )
        marks = segment_marks(lengths, seq_order, micro_slot, row_start, rows_here)
        source_grad, weight_grads = mamba_backward(
            layer_in.astype(jnp.float32), incoming, current(), marks
        )
        if totals is None:
            totals = tuple(weight_grads)
        else:
            totals = tuple((earlier + added for earlier, added in zip(totals, weight_grads)))
        source_grads.append(source_grad)
        if step_index < MICRO:
            returned = from_behind(source_grad.astype(jnp.bfloat16), "section", -1)
    boundary = jnp.stack(
        [
            jnp.where(is_first, source_grads[micro_pos + 1], results[micro_pos + 1])
            for micro_pos in range(MICRO)
        ]
    )[None, :, None]
    shares = (
        lax.psum_scatter(
            totals[0][None].astype(jnp.bfloat16), "shard", scatter_dimension=1, tiled=True
        ).astype(jnp.float32),
        lax.psum_scatter(
            totals[1][None].astype(jnp.bfloat16), "shard", scatter_dimension=1, tiled=True
        ).astype(jnp.float32),
        lax.psum_scatter(
            totals[2][None].astype(jnp.bfloat16), "shard", scatter_dimension=2, tiled=True
        ).astype(jnp.float32),
        lax.psum_scatter(
            totals[3][None].astype(jnp.bfloat16), "shard", scatter_dimension=1, tiled=True
        ).astype(jnp.float32),
        lax.psum_scatter(
            totals[4][None].astype(jnp.bfloat16), "shard", scatter_dimension=1, tiled=True
        ).astype(jnp.float32),
        lax.psum_scatter(
            totals[5][None].astype(jnp.bfloat16), "shard", scatter_dimension=1, tiled=True
        ).astype(jnp.float32),
        lax.psum_scatter(
            totals[6][None].astype(jnp.bfloat16), "shard", scatter_dimension=1, tiled=True
        ).astype(jnp.float32),
        lax.psum_scatter(
            totals[7][None].astype(jnp.bfloat16), "shard", scatter_dimension=1, tiled=True
        ).astype(jnp.float32),
        lax.psum_scatter(
            totals[8][None].astype(jnp.bfloat16), "shard", scatter_dimension=1, tiled=True
        ).astype(jnp.float32),
    )
    reduced = (
        lax.psum(shares[0].astype(jnp.bfloat16), "rep").astype(jnp.float32),
        lax.psum(shares[1].astype(jnp.bfloat16), "rep").astype(jnp.float32),
        lax.psum(shares[2].astype(jnp.bfloat16), "rep").astype(jnp.float32),
        lax.psum(shares[3].astype(jnp.bfloat16), "rep").astype(jnp.float32),
        lax.psum(shares[4].astype(jnp.bfloat16), "rep").astype(jnp.float32),
        lax.psum(shares[5].astype(jnp.bfloat16), "rep").astype(jnp.float32),
        lax.psum(shares[6].astype(jnp.bfloat16), "rep").astype(jnp.float32),
        lax.psum(shares[7].astype(jnp.bfloat16), "rep").astype(jnp.float32),
        lax.psum(shares[8].astype(jnp.bfloat16), "rep").astype(jnp.float32),
    )
    return (boundary,) + tuple(reduced)


Q = 128
LANES = 128
VMEM_BYTES = 56 * 1024 * 1024
EXACT = lax.Precision.HIGHEST


def mm(a, b, da=1, db=0):
    return lax.dot_general(
        a, b, (((da,), (db,)), ((), ())), preferred_element_type=jnp.float32
    )


def exact(a, b):
    return jnp.dot(a, b, precision=EXACT, preferred_element_type=jnp.float32)


def low(v):
    return v.astype(jnp.bfloat16)


def iota(shape, dim):
    return lax.broadcasted_iota(jnp.int32, shape, dim)


def pair_cols(v, p):
    rows = v.shape[0]
    left = jnp.broadcast_to(v[:, 2 * p : 2 * p + 1], (rows, LANES))
    right = jnp.broadcast_to(v[:, 2 * p + 1 : 2 * p + 2], (rows, LANES))
    return jnp.where(iota((rows, LANES), 1) < LANES // 2, left, right)


def widen(v, pairs):
    return jnp.concatenate([pair_cols(v, p) for p in range(pairs)], axis=1)


def stack_pair(v, p):
    block = v[:, p * LANES : (p + 1) * LANES]
    left = iota(block.shape, 1) < LANES // 2
    zero = jnp.zeros_like(block)
    return jnp.concatenate([jnp.where(left, block, zero), jnp.where(left, zero, block)], axis=0)


def softplus(v):
    small = jnp.exp(-jnp.abs(v))
    series = small * (1 + small * (-1 / 2 + small * (1 / 3 + small * (-1 / 4 + small / 5))))
    return jnp.maximum(v, 0.0) + jnp.where(small < 0.01, series, jnp.log(1 + small))


def sigmoid(v):
    return 1.0 / (1.0 + jnp.exp(-v))


def chunk_parts(width, proj, before8, marks, seg_row, conv_w, conv_b, dt_bias, rate, pick):
    span = width + 2 * LANES
    gate = proj[:, :width].astype(jnp.float32)
    mixed = proj[:, width : width + span].astype(jnp.float32)
    raw = mm(proj[:, width + span :], pick)
    shifts = [mixed]
    top = iota((8, span), 0)
    for lag in range(1, KW):
        rolled = pltpu.roll(mixed, lag, 0)
        head = jnp.where(top < lag, pltpu.roll(before8, lag, 0), rolled[:8])
        moved = jnp.concatenate([head, rolled[8:]], axis=0)
        shifts.append(moved * marks[:, lag - 1 : lag])
    conv = conv_b
    for lag in range(KW):
        conv = conv + conv_w[KW - 1 - lag : KW - lag] * shifts[lag]
    sig = sigmoid(conv)
    active = conv * sig
    stepped = raw + dt_bias
    step = softplus(stepped)
    decay = -step * rate
    lower = iota((Q, Q), 0) >= iota((Q, Q), 1)
    total = exact(lower.astype(jnp.float32), decay)
    linked = lower & (marks[:, 5:6] == seg_row)
    shut = jnp.where(linked, 0.0, -1e30)
    reach = jnp.exp(total) * marks[:, 3:4]
    tail = jnp.exp(total[Q - 1 : Q] - total) * marks[:, 4:5]
    return gate, mixed, shifts, conv, sig, active, stepped, step, decay, total, shut, reach, tail


def forward_kernel(
    width, proj_ref, marks_ref, seg_ref, conv_w_ref, conv_b_ref, dt_bias_ref, rate_ref, pick_ref,
    skip_ref, gain_ref, gg_ref, squares_ref, mixer_ref, starts_ref, state, before,
):
    pairs = width // LANES

    @pl.when(pl.program_id(0) == 0)
    def _():
        state[...] = jnp.zeros_like(state)
        before[...] = jnp.zeros_like(before)

    gate, mixed, _, _, _, active, _, step, _, total, shut, reach, tail = chunk_parts(
        width, proj_ref[...], before[...], marks_ref[...], seg_ref[...], conv_w_ref[...],
        conv_b_ref[...], dt_bias_ref[...], rate_ref[...], pick_ref[...],
    )
    before[...] = mixed[Q - 8 :]
    heads = active[:, :width]
    b_low = low(active[:, width : width + LANES])
    c_low = low(active[:, width + LANES :])
    entry = state[...]
    starts_ref[0] = entry
    scores = mm(c_low, b_low, 1, 1)
    total_t = total.T
    scaled = heads * widen(step, pairs)
    scaled_low = low(scaled)
    inside = []
    for p in range(pairs):
        both = []
        for h in (2 * p, 2 * p + 1):
            both.append(low(jnp.exp(total[:, h : h + 1] - total_t[h : h + 1] + shut) * scores))
        inside.append(mm(jnp.concatenate(both, axis=1), stack_pair(scaled_low, p)))
    mixer = jnp.concatenate(inside, axis=1) + widen(reach, pairs) * mm(c_low, low(entry))
    b_turned = low(active[:, width : width + LANES].T)
    state[...] = entry * widen(reach[Q - 1 : Q], pairs) + mm(
        b_turned, low(scaled * widen(tail, pairs))
    )
    mixer_ref[...] = mixer
    gated = (mixer + skip_ref[...] * heads) * (gate * sigmoid(gate))
    squares_ref[...] = jnp.sum(gated * gated, axis=1, keepdims=True)
    gg_ref[...] = low(gated * gain_ref[...])


def backward_kernel(
    width, whole_width, proj_ref, rim_ref, marks_ref, seg_ref, conv_w_ref, conv_b_ref, dt_bias_ref,
    rate_ref, pick_ref, skip_ref, gain_ref, mixer_ref, starts_ref, og_ref, rows_ref,
    pg_ref, outgoing_ref, wide_ref, conv_ref, head_ref, later, after,
):
    pairs = width // LANES
    turn = pl.program_id(0)
    chunk = pl.num_programs(0) - 1 - turn

    @pl.when(turn == 0)
    def _():
        later[...] = jnp.zeros_like(later)
        after[...] = jnp.zeros_like(after)
        wide_ref[...] = jnp.zeros_like(wide_ref)
        conv_ref[...] = jnp.zeros_like(conv_ref)
        head_ref[...] = jnp.zeros_like(head_ref)

    span = width + 2 * LANES
    marks = marks_ref[...]
    rim = rim_ref[...][8:, width : width + span].astype(jnp.float32)
    rim = jnp.where(chunk > 0, rim, 0.0)
    gate, mixed, shifts, conv, sig, active, stepped, step, decay, total, shut, reach, tail = (
        chunk_parts(
            width, proj_ref[...], rim, marks, seg_ref[...], conv_w_ref[...], conv_b_ref[...],
            dt_bias_ref[...], rate_ref[...], pick_ref[...],
        )
    )
    heads = active[:, :width]
    b_low = low(active[:, width : width + LANES])
    c_low = low(active[:, width + LANES :])

    inv = rows_ref[:, 0:1]
    dots = rows_ref[:, 1:2]
    og = og_ref[...]
    mixer = mixer_ref[...]
    out = mixer + skip_ref[...] * heads
    gate_sig = sigmoid(gate)
    gate_on = gate * gate_sig
    hat = out * gate_on * inv
    outgoing_ref[...] = low(hat * gain_ref[...])
    gated_grad = inv * (gain_ref[...] * og - hat * (dots * (1.0 / whole_width)))
    out_grad = gated_grad * gate_on
    gate_grad = gated_grad * out * (gate_sig * (1.0 + gate * (1.0 - gate_sig)))

    entry = starts_ref[0]
    entry_low = low(entry)
    late = later[...]
    late_low = low(late)
    scores = mm(c_low, b_low, 1, 1)
    total_t = total.T
    step_wide = widen(step, pairs)
    scaled = heads * step_wide
    scaled_low = low(scaled)
    grad_low = low(out_grad)
    from_late = widen(tail, pairs) * mm(b_low, late_low)
    inside = []
    score_grad = jnp.zeros((Q, Q), jnp.float32)
    for p in range(pairs):
        gains = []
        both = []
        for h in (2 * p, 2 * p + 1):
            gain = jnp.exp(total[:, h : h + 1] - total_t[h : h + 1] + shut)
            gains.append(gain)
            both.append(low(gain * scores))
        stacked = stack_pair(grad_low, p)
        inside.append(mm(jnp.concatenate(both, axis=0), stacked, 0, 0))
        mix_grad = mm(stacked, scaled_low[:, p * LANES : (p + 1) * LANES], 1, 1)
        score_grad = score_grad + gains[0] * mix_grad[:Q] + gains[1] * mix_grad[Q:]
    scaled_grad = jnp.concatenate(inside, axis=1) + from_late
    reached = low(widen(reach, pairs) * out_grad)
    score_low = low(score_grad)
    c_grad = mm(score_low, b_low) + mm(reached, entry_low, 1, 1)
    b_grad = mm(score_low, c_low, 0, 0) + mm(low(scaled * widen(tail, pairs)), late_low, 1, 1)
    kept = widen(reach[Q - 1 : Q], pairs)
    later[...] = late * kept + mm(c_low, reached, 0, 0)

    scaled_seen = scaled_low.astype(jnp.float32)
    balance = grad_low.astype(jnp.float32) * mixer - scaled_seen * scaled_grad
    closing = jnp.sum(scaled_seen * from_late, axis=0, keepdims=True) + kept * jnp.sum(
        late * entry, axis=0, keepdims=True
    )
    picks = (iota((width, LANES), 0) // (LANES // 2) == iota((width, LANES), 1)).astype(jnp.float32)
    sums = exact(
        jnp.concatenate([balance, heads * scaled_grad, jnp.broadcast_to(closing, (8, width))], 0),
        picks,
    )
    upper = (iota((Q, Q), 0) <= iota((Q, Q), 1)).astype(jnp.float32)
    decay_grad = exact(upper, sums[:Q]) + sums[2 * Q : 2 * Q + 1]
    step_grad = sums[Q : 2 * Q] - decay_grad * rate_ref[...]
    raw_grad = step_grad * sigmoid(stepped)

    head_grad = step_wide * scaled_grad + skip_ref[...] * out_grad
    conv_grad = jnp.concatenate([head_grad, b_grad, c_grad], axis=1) * (
        sig * (1.0 + conv * (1.0 - sig))
    )
    mixed_grad = conv_w_ref[KW - 1 : KW] * conv_grad
    bottom = iota((8, span), 0)
    for lag in range(1, KW):
        sent = conv_grad * marks[:, lag - 1 : lag]
        rolled = pltpu.roll(sent, Q - lag, 0)
        ending = jnp.where(
            bottom >= 8 - lag, pltpu.roll(after[lag - 1], 8 - lag, 0), rolled[Q - 8 :]
        )
        mixed_grad = mixed_grad + conv_w_ref[KW - 1 - lag : KW - lag] * jnp.concatenate(
            [rolled[: Q - 8], ending], axis=0
        )
        after[lag - 1] = sent[:8]
    pg_ref[...] = low(
        jnp.concatenate([gate_grad, mixed_grad, mm(low(raw_grad), pick_ref[...], 1, 1)], axis=1)
    )

    wide_ref[0:1] += jnp.sum(hat * og, axis=0, keepdims=True)
    wide_ref[1:2] += jnp.sum(out_grad * heads, axis=0, keepdims=True)
    for lag in range(KW):
        conv_ref[KW - 1 - lag : KW - lag] += jnp.sum(
            conv_grad * shifts[lag], axis=0, keepdims=True
        )
    conv_ref[KW : KW + 1] += jnp.sum(conv_grad, axis=0, keepdims=True)
    head_ref[0:1] += jnp.sum(raw_grad, axis=0, keepdims=True)
    head_ref[1:2] += jnp.sum(decay_grad * decay, axis=0, keepdims=True)


def full_spec(shape):
    return pl.BlockSpec(shape, lambda i: (0,) * len(shape))


def mixer_forward(projected, marks, seg_row, small):
    rows, columns = projected.shape
    width = small["gain"].shape[1]
    chunks = rows // Q
    span = width + 2 * LANES

    def by_row(count):
        return pl.BlockSpec((Q, count), lambda i: (i, 0))

    weights = [small[k] for k in ("conv_w", "conv_b", "dt_bias", "rate", "pick", "skip", "gain")]
    return pl.pallas_call(
        functools.partial(forward_kernel, width),
        grid=(chunks,),
        in_specs=[by_row(columns), by_row(8), pl.BlockSpec((1, Q), lambda i: (0, i))]
        + [full_spec(w.shape) for w in weights],
        out_specs=[
            by_row(width),
            by_row(1),
            by_row(width),
            pl.BlockSpec((1, LANES, width), lambda i: (i, 0, 0)),
        ],
        out_shape=[
            jax.ShapeDtypeStruct((rows, width), jnp.bfloat16),
            jax.ShapeDtypeStruct((rows, 1), jnp.float32),
            jax.ShapeDtypeStruct((rows, width), jnp.float32),
            jax.ShapeDtypeStruct((chunks, LANES, width), jnp.float32),
        ],
        scratch_shapes=[
            pltpu.VMEM((LANES, width), jnp.float32),
            pltpu.VMEM((8, span), jnp.float32),
        ],
        compiler_params=pltpu.CompilerParams(vmem_limit_bytes=VMEM_BYTES),
        name="mixer_forward",
    )(projected, marks, seg_row, *weights)


def mixer_backward(projected, marks, seg_row, small, mixer, starts, og, per_row, whole_width):
    rows, columns = projected.shape
    width = small["gain"].shape[1]
    chunks = rows // Q
    span = width + 2 * LANES

    def by_row(count):
        return pl.BlockSpec((Q, count), lambda i: (chunks - 1 - i, 0))

    weights = [small[k] for k in ("conv_w", "conv_b", "dt_bias", "rate", "pick", "skip", "gain")]
    rim = pl.BlockSpec(
        (16, columns), lambda i: (jnp.maximum((chunks - 1 - i) * (Q // 16) - 1, 0), 0)
    )
    return pl.pallas_call(
        functools.partial(backward_kernel, width, whole_width),
        grid=(chunks,),
        in_specs=[by_row(columns), rim, by_row(8), pl.BlockSpec((1, Q), lambda i: (0, chunks - 1 - i))]
        + [full_spec(w.shape) for w in weights]
        + [
            by_row(width),
            pl.BlockSpec((1, LANES, width), lambda i: (chunks - 1 - i, 0, 0)),
            by_row(width),
            by_row(2),
        ],
        out_specs=[
            by_row(columns),
            by_row(width),
            full_spec((8, width)),
            full_spec((8, span)),
            full_spec((8, LANES)),
        ],
        out_shape=[
            jax.ShapeDtypeStruct((rows, columns), jnp.bfloat16),
            jax.ShapeDtypeStruct((rows, width), jnp.bfloat16),
            jax.ShapeDtypeStruct((8, width), jnp.float32),
            jax.ShapeDtypeStruct((8, span), jnp.float32),
            jax.ShapeDtypeStruct((8, LANES), jnp.float32),
        ],
        scratch_shapes=[
            pltpu.VMEM((LANES, width), jnp.float32),
            pltpu.VMEM((KW - 1, 8, span), jnp.float32),
        ],
        compiler_params=pltpu.CompilerParams(vmem_limit_bytes=VMEM_BYTES),
        name="mixer_backward",
    )(projected, projected, marks, seg_row, *weights, mixer, starts, og, per_row)


CORES = 2
GROUP = 4
SHARED = CONV - DI + H
LOCAL = 2 * DI // GROUP + SHARED + 16
HALF = LOCAL // 2
CHUNKS = 2
LANE_PART = D // 4
OUT_PART = DI // 16
UNITS = CHUNKS + 1


def place():
    c, z, r = (lax.axis_index(name) for name in ("section", "shard", "rep"))
    return c, z, lax.div(r, 2), lax.rem(r, 2)


def weight_pieces(quarter):
    part = DI // 16
    found = []
    for side in range(2):
        for zz in range(4):
            found.append(
                (side * 4 * part + zz * part, side * DI + zz * 4 * part + quarter * part, part)
            )
    found.append((8 * part, 2 * DI, SHARED))
    return found


def gather_kernel(
    layer, in_ref, out_ref, w_ref, wo_ref,
    local_sem, core_send, core_recv, right_send, left_send, z_recv, y_send, y_recv,
):
    c, z, y, x = place()
    core, y_other = {"section": 1 - c}, {"rep": (1 - y) * 2 + x}
    barrier = pltpu.get_barrier_semaphore()
    pl.semaphore_signal(barrier, inc=1, device_id=core, device_id_type=pl.DeviceIdType.MESH)
    pl.semaphore_signal(barrier, inc=1, device_id=y_other, device_id_type=pl.DeviceIdType.MESH)

    @pl.when(z < 3)
    def _():
        pl.semaphore_signal(
            barrier, inc=1, device_id={"shard": z + 1}, device_id_type=pl.DeviceIdType.MESH
        )

    @pl.when(z > 0)
    def _():
        pl.semaphore_signal(
            barrier, inc=1, device_id={"shard": z - 1}, device_id_type=pl.DeviceIdType.MESH
        )

    ends = jnp.where(z == 0, 1, 0) + jnp.where(z == 3, 1, 0)
    pl.semaphore_wait(barrier, 4 - ends)

    lanes = pl.ds(pl.multiple_of(z * LANE_PART, LANES), LANE_PART)
    out_rows = pl.ds(pl.multiple_of(z * OUT_PART, 16), OUT_PART)

    def own_pieces(quarter):
        found = []
        for at, start, count in weight_pieces(quarter):
            source = in_ref.at[pl.ds(pl.multiple_of(start, 16), count)]
            found.append((source, w_ref.at[pl.ds(at, count), lanes]))
        start = pl.multiple_of(quarter * OUT_PART, 16)
        found.append((out_ref.at[pl.ds(start, OUT_PART)], wo_ref.at[out_rows]))
        return found

    def local_copies():
        return [
            pltpu.make_async_copy(source, target, local_sem.at[i])
            for i, (source, target) in enumerate(own_pieces(2 * x + c))
        ]

    def core_copies():
        return [
            pltpu.make_async_remote_copy(
                src_ref=source, dst_ref=target, send_sem=core_send.at[i],
                recv_sem=core_recv.at[i], device_id=core, device_id_type=pl.DeviceIdType.MESH,
            )
            for i, (source, target) in enumerate(own_pieces(2 * x + 1 - c))
        ]

    w_ref[LOCAL - 16 :, lanes] = jnp.zeros((16, LANE_PART), w_ref.dtype)

    @pl.when(c == layer)
    def _():
        for copy in core_copies():
            copy.start()
        for copy in local_copies():
            copy.start()
        for copy in local_copies():
            copy.wait()

    @pl.when(c != layer)
    def _():
        for copy in core_copies():
            copy.wait_recv()

    def slab(unit, shard, side):
        if unit == CHUNKS:
            start = shard * OUT_PART + side * (OUT_PART // 2)
            return wo_ref.at[pl.ds(pl.multiple_of(start, 16), OUT_PART // 2)]
        start = pl.multiple_of(side * HALF + unit * (HALF // CHUNKS), 16)
        return w_ref.at[
            pl.ds(start, HALF // CHUNKS),
            pl.ds(pl.multiple_of(shard * LANE_PART, LANES), LANE_PART),
        ]

    def z_copy(unit, shard, step, k):
        there = z + 1 if step > 0 else z - 1
        return pltpu.make_async_remote_copy(
            src_ref=slab(unit, shard, y), dst_ref=slab(unit, shard, y),
            send_sem=(right_send if step > 0 else left_send).at[unit, k],
            recv_sem=z_recv.at[unit, shard],
            device_id={"shard": there}, device_id_type=pl.DeviceIdType.MESH,
        )

    def y_copy(unit, shard, side):
        return pltpu.make_async_remote_copy(
            src_ref=slab(unit, shard, side), dst_ref=slab(unit, shard, side),
            send_sem=y_send.at[unit, shard], recv_sem=y_recv.at[unit, shard],
            device_id=y_other, device_id_type=pl.DeviceIdType.MESH,
        )

    def first(unit):
        @pl.when(z < 3)
        def _():
            z_copy(unit, z, 1, 0).start()

        @pl.when(z > 0)
        def _():
            z_copy(unit, z, -1, 0).start()

    def arrive(unit, k):
        for step in (1, -1):
            shard = z - k * step
            there = (shard >= 0) if step > 0 else (shard <= 3)
            more = (z < 3) if step > 0 else (z > 0)

            @pl.when(there)
            def _():
                z_copy(unit, shard, step, 0).wait_recv()

                @pl.when(more)
                def _():
                    z_copy(unit, shard, step, k).start()

                y_copy(unit, shard, y).start()

    for unit in range(CHUNKS):
        first(unit)
    for k in (1, 2):
        for unit in range(CHUNKS):
            arrive(unit, k)
    first(CHUNKS)
    for unit in range(CHUNKS):
        arrive(unit, 3)
    for k in (1, 2, 3):
        arrive(CHUNKS, k)

    for unit in range(UNITS):
        for away in (1, 2, 3):
            shard = lax.rem(z + away, 4)
            y_copy(unit, shard, 1 - y).wait_recv()
            y_copy(unit, shard, y).wait_send()
        for step in (1, -1):
            for k in range(3):
                shard = z - k * step
                there = (shard >= 0) if step > 0 else (shard <= 3)
                more = (z < 3) if step > 0 else (z > 0)

                @pl.when(there & more)
                def _():
                    z_copy(unit, shard, step, k).wait_send()

    @pl.when(c == layer)
    def _():
        for copy in core_copies():
            copy.wait_send()


def gather_weights(layer, in_rows, out_rows):
    dma = pltpu.SemaphoreType.DMA
    return pl.pallas_call(
        functools.partial(gather_kernel, layer),
        in_specs=[pl.BlockSpec(memory_space=pl.ANY)] * 2,
        out_specs=[pl.BlockSpec(memory_space=pltpu.VMEM)] * 2,
        out_shape=[
            jax.ShapeDtypeStruct((LOCAL, D), jnp.bfloat16),
            jax.ShapeDtypeStruct((DI // GROUP, D), jnp.bfloat16),
        ],
        scratch_shapes=[
            dma((10,)), dma((10,)), dma((10,)),
            dma((UNITS, 3)), dma((UNITS, 3)), dma((UNITS, 4)), dma((UNITS, 4)), dma((UNITS, 4)),
        ],
        compiler_params=pltpu.CompilerParams(
            collective_id=layer, has_side_effects=True, vmem_limit_bytes=VMEM_BYTES
        ),
        name="gather_weights",
    )(in_rows, out_rows)


def swap_core(v):
    return lax.ppermute(v, "section", [(0, 1), (1, 0)])


def swap_x(v):
    return lax.ppermute(v, "rep", [(i, i ^ 1) for i in range(4)])


def swap_y(v):
    return lax.ppermute(v, "rep", [(i, i ^ 2) for i in range(4)])


def swap_z(v, bit):
    return lax.ppermute(v, "shard", [(i, i ^ bit) for i in range(4)])


def ordered(first, mine, other, axis=0):
    return jnp.where(first, jnp.stack([mine, other], axis), jnp.stack([other, mine], axis))


def joined(first, mine, other, axis=0):
    return jnp.where(
        first, jnp.concatenate([mine, other], axis), jnp.concatenate([other, mine], axis)
    )


def after(value, *earlier):
    return lax.optimization_barrier((value,) + earlier)[0]


def pick_last(v, quarter):
    parts = v.reshape(v.shape[:-1] + (4, GROUP, v.shape[-1] // (4 * GROUP)))
    return lax.dynamic_index_in_dim(parts, quarter, v.ndim, False).reshape(v.shape[:-1] + (-1,))


def place_last(v, quarter):
    parts = v.reshape(v.shape[:-1] + (4, 1, v.shape[-1] // 4))
    empty = jnp.zeros(v.shape[:-1] + (4, GROUP, v.shape[-1] // 4), v.dtype)
    return lax.dynamic_update_slice_in_dim(empty, parts, quarter, v.ndim).reshape(
        v.shape[:-1] + (-1,)
    )


def rows_at(start, count):
    return pl.ds(pl.multiple_of(start, 16), count)


def finish_kernel(
    grad_ref, out_grad_ref, late_ref, late_out_ref, tiny_ref,
    all_ref, out_all_ref, tiny_out_ref,
    y_buf, z_buf, s_buf, zo_buf, so_buf, yo_buf, yo_mine, t1_buf, t1_sum, t2_buf, t2_sum, t3_buf,
    y_send, y_recv, z_send, z_recv, zo_send, zo_recv, yo_sem,
    core_send, core_recv, x_send, x_recv, ya_send, ya_recv, relay_send, relay_recv,
    xo_send, xo_recv, t_send, t_recv, local_sem,
):
    c, z, y, x = place()
    quarter = 2 * x + c
    core, x_other, y_other = {"section": 1 - c}, {"rep": 2 * y + 1 - x}, {"rep": 2 * (1 - y) + x}
    diagonal = {"rep": 2 * (1 - y) + 1 - x}
    part = HALF // CHUNKS

    def copy(source, target, send, recv, device):
        return pltpu.make_async_remote_copy(
            src_ref=source, dst_ref=target, send_sem=send, recv_sem=recv,
            device_id=device, device_id_type=pl.DeviceIdType.MESH,
        )

    barrier = pltpu.get_barrier_semaphore()
    reps = (x_other, y_other, diagonal)
    shards = tuple({"shard": lax.rem(z + away, 4)} for away in (1, 2, 3))
    for device in (core,) + reps + shards:
        pl.semaphore_signal(barrier, inc=1, device_id=device, device_id_type=pl.DeviceIdType.MESH)
    pl.semaphore_wait(barrier, 7)

    orders = ((3, 2, 1, 0), (3, 0, 2, 1), (0, 3, 1, 2), (0, 1, 2, 3))

    def shard_at(i):
        found = jnp.int32(orders[3][i])
        for zz in range(3):
            found = jnp.where(z == zz, orders[zz][i], found)
        return found

    def grad_part(shard, side, ch):
        return grad_ref.at[
            rows_at(side * HALF + ch * part, part),
            pl.ds(pl.multiple_of(shard * LANE_PART, LANES), LANE_PART),
        ]

    def y_copy(shard, ch):
        return copy(
            grad_part(shard, 1 - y, ch), y_buf.at[shard, pl.ds(ch * part, part)],
            y_send.at[shard, ch], y_recv.at[shard, ch], y_other,
        )

    def z_target(shard):
        right = shard > z
        there = {"shard": jnp.clip(z + jnp.where(right, 1, -1), 0, 3)}
        slot = jnp.where(right, shard, jnp.where(shard == z - 1, 4, shard))
        return there, slot

    def z_copy(shard, ch):
        there, slot = z_target(shard)
        return copy(
            s_buf.at[shard, pl.ds(ch * part, part)], z_buf.at[slot, pl.ds(ch * part, part)],
            z_send.at[shard, ch], z_recv.at[slot, ch], there,
        )

    def z_wait(slot, ch):
        there, _ = z_target(shard_at(0))
        copy(
            s_buf.at[0, pl.ds(ch * part, part)], z_buf.at[slot, pl.ds(ch * part, part)],
            z_send.at[0, ch], z_recv.at[slot, ch], there,
        ).wait_recv()

    def zo_copy(shard):
        there, slot = z_target(shard)
        return copy(
            so_buf.at[shard], zo_buf.at[slot], zo_send.at[shard], zo_recv.at[slot], there
        )

    def zo_wait(slot):
        there, _ = z_target(shard_at(0))
        copy(so_buf.at[0], zo_buf.at[slot], zo_send.at[0], zo_recv.at[slot], there).wait_recv()

    def all_part(which, side, ch):
        return all_ref.at[which, rows_at(side * HALF + ch * part, part)]

    def out_part(which):
        return out_all_ref.at[rows_at(which * OUT_PART, OUT_PART)]

    def x_copy(who, ch):
        piece = all_part(2 * x + who, y, ch)
        return copy(piece, piece, x_send.at[who, ch], x_recv.at[who, ch], x_other)

    def ya_copy(who, ch):
        piece = all_part(2 * x + who, y, ch)
        return copy(piece, piece, ya_send.at[who, ch], ya_recv.at[who, ch], y_other)

    def relay_copy(who, ch):
        piece = all_part(2 * x + who, 1 - y, ch)
        return copy(piece, piece, relay_send.at[who, ch], relay_recv.at[who, ch], x_other)

    def xo_copy(who):
        piece = out_part(2 * x + who)
        return copy(piece, piece, xo_send.at[who], xo_recv.at[who], x_other)

    def spread(who, ch):
        x_copy(who, ch).start()
        ya_copy(who, ch).start()

    def late_copy(ch):
        return copy(
            late_ref.at[pl.ds(ch * part, part)], all_part(quarter, y, ch),
            core_send.at[ch], core_recv.at[ch], core,
        )

    def late_out_copy():
        return copy(
            late_out_ref, out_part(quarter), core_send.at[CHUNKS], core_recv.at[CHUNKS], core
        )

    def first_copy(ch):
        piece = all_part(quarter, y, ch)
        return copy(z_buf.at[4, pl.ds(ch * part, part)], piece, core_send.at[ch], core_recv.at[ch], core)

    def first_out_copy():
        return copy(
            yo_mine, out_part(quarter), core_send.at[CHUNKS], core_recv.at[CHUNKS], core
        )

    def t1_copy():
        return copy(tiny_ref.at[1 - c], t1_buf, t_send.at[0], t_recv.at[0], core)

    def t2_copy(away):
        return copy(
            t1_sum.at[lax.rem(z + away, 4)], t2_buf.at[away - 1],
            t_send.at[away], t_recv.at[away], shards[away - 1],
        )

    def t3_copy(i):
        return copy(t2_sum, t3_buf.at[i], t_send.at[4 + i], t_recv.at[4 + i], reps[i])

    def yo_copy():
        return copy(yo_mine, yo_buf, yo_sem.at[0], yo_sem.at[1], y_other)

    t1_copy().start()
    for i in range(4):
        shard = shard_at(i)
        for ch in range(CHUNKS):
            y_copy(shard, ch).start()

    @pl.when(c == 0)
    def _():
        for ch in range(CHUNKS):
            late_copy(ch).start()
        late_out_copy().start()

    @pl.when(c == 1)
    def _():
        for ch in range(CHUNKS):
            all_part(quarter, y, ch)[...] = late_ref[pl.ds(ch * part, part)]
        out_part(quarter)[...] = late_out_ref[...]

    def own_out(shard):
        return out_grad_ref[rows_at(shard * OUT_PART, OUT_PART)].astype(jnp.float32)

    def more(shard):
        return ((shard > z) & (z > 0)) | ((shard < z) & (z < 3))

    def send_out(i):
        shard = shard_at(i)

        @pl.when(more(shard))
        def _():
            zo_wait(shard)
            so_buf[shard] = low(own_out(shard) + zo_buf[shard].astype(jnp.float32))

        @pl.when(jnp.logical_not(more(shard)))
        def _():
            so_buf[shard] = out_grad_ref[rows_at(shard * OUT_PART, OUT_PART)]

        zo_copy(shard).start()

    def send_in(i, ch):
        shard = shard_at(i)
        span = pl.ds(ch * part, part)
        y_copy(shard, ch).wait_recv()
        both = grad_part(shard, y, ch)[...].astype(jnp.float32) + y_buf[shard, span].astype(
            jnp.float32
        )

        @pl.when(more(shard))
        def _():
            z_wait(shard, ch)
            s_buf[shard, span] = low(both + z_buf[shard, span].astype(jnp.float32))

        @pl.when(jnp.logical_not(more(shard)))
        def _():
            s_buf[shard, span] = low(both)

        z_copy(shard, ch).start()

    send_out(0)
    send_out(1)

    t1_copy().wait_recv()
    t1_sum[...] = tiny_ref[c] + t1_buf[...]
    for away in (1, 2, 3):
        t2_copy(away).start()

    @pl.when(c == 1)
    def _():
        for ch in range(CHUNKS):
            late_copy(ch).wait_recv()
            for who in range(CORES):
                spread(who, ch)
        late_out_copy().wait_recv()
        for who in range(CORES):
            xo_copy(who).start()

    for ch in range(CHUNKS):
        send_in(0, ch)
    send_out(2)
    for away in (1, 2, 3):
        t2_copy(away).wait_recv()
    t2_sum[...] = (t1_sum[z] + t2_buf[0]) + (t2_buf[1] + t2_buf[2])
    for i in range(3):
        t3_copy(i).start()
    for ch in range(CHUNKS):
        send_in(1, ch)

    yo_mine[...] = low(own_out(z))

    @pl.when(z > 0)
    def _():
        zo_wait(z)
        yo_mine[...] = low(own_out(z) + zo_buf[z].astype(jnp.float32))

    @pl.when(z < 3)
    def _():
        zo_wait(4)
        yo_mine[...] = low(yo_mine[...].astype(jnp.float32) + zo_buf[4].astype(jnp.float32))

    yo_copy().start()
    for ch in range(CHUNKS):
        send_in(2, ch)
    for i in range(3):
        t3_copy(i).wait_recv()
    tiny_out_ref[...] = (t2_sum[...] + t3_buf[0]) + (t3_buf[1] + t3_buf[2])

    yo_copy().wait()
    total = low(yo_mine[...].astype(jnp.float32) + yo_buf[...].astype(jnp.float32))

    @pl.when(c == 0)
    def _():
        out_part(quarter)[...] = total

    @pl.when(c == 1)
    def _():
        yo_mine[...] = total
        first_out_copy().start()

    @pl.when(c == 0)
    def _():
        first_out_copy().wait_recv()
        for who in range(CORES):
            xo_copy(who).start()

    for ch in range(CHUNKS):
        span = pl.ds(ch * part, part)
        y_copy(z, ch).wait_recv()
        s_buf[z, span] = low(
            grad_part(z, y, ch)[...].astype(jnp.float32) + y_buf[z, span].astype(jnp.float32)
        )

        @pl.when(z > 0)
        def _():
            z_wait(z, ch)
            s_buf[z, span] = low(
                s_buf[z, span].astype(jnp.float32) + z_buf[z, span].astype(jnp.float32)
            )

        @pl.when(z < 3)
        def _():
            z_wait(4, ch)
            s_buf[z, span] = low(
                s_buf[z, span].astype(jnp.float32) + z_buf[4, span].astype(jnp.float32)
            )

        @pl.when(c == 1)
        def _():
            z_buf[4, span] = s_buf[z, span]
            first_copy(ch).start()

        @pl.when(c == 0)
        def _():
            all_part(quarter, y, ch)[...] = s_buf[z, span]
            spread(0, ch)
            first_copy(ch).wait_recv()
            spread(1, ch)

    for ch in range(CHUNKS):
        for who in range(CORES):
            ya_copy(who, ch).wait_recv()
            relay_copy(who, ch).start()
    for ch in range(CHUNKS):
        for who in range(CORES):
            x_copy(who, ch).wait()
            ya_copy(who, ch).wait_send()
            relay_copy(who, ch).wait()
    for who in range(CORES):
        xo_copy(who).wait()
    t1_copy().wait_send()
    for away in (1, 2, 3):
        t2_copy(away).wait_send()
    for i in range(3):
        t3_copy(i).wait_send()
        zo_copy(shard_at(i)).wait_send()
        for ch in range(CHUNKS):
            z_copy(shard_at(i), ch).wait_send()
    for i in range(4):
        for ch in range(CHUNKS):
            y_copy(shard_at(i), ch).wait_send()

    @pl.when(c == 0)
    def _():
        for ch in range(CHUNKS):
            late_copy(ch).wait_send()
        late_out_copy().wait_send()

    @pl.when(c == 1)
    def _():
        for ch in range(CHUNKS):
            first_copy(ch).wait_send()
        first_out_copy().wait_send()


def finish_sums(grad, out_grad, late, late_out, tiny):
    dma = pltpu.SemaphoreType.DMA
    span = (HALF, LANE_PART)
    out = (OUT_PART, D)
    small = tiny.shape[2:]
    two = (CORES, CHUNKS)
    return pl.pallas_call(
        finish_kernel,
        in_specs=[pl.BlockSpec(memory_space=pltpu.VMEM)] * 5,
        out_specs=[pl.BlockSpec(memory_space=pltpu.VMEM)] * 3,
        out_shape=[
            jax.ShapeDtypeStruct((GROUP, LOCAL, LANE_PART), jnp.bfloat16),
            jax.ShapeDtypeStruct((DI // GROUP, D), jnp.bfloat16),
            jax.ShapeDtypeStruct(small, jnp.float32),
        ],
        scratch_shapes=[
            pltpu.VMEM((4,) + span, jnp.bfloat16),
            pltpu.VMEM((5,) + span, jnp.bfloat16),
            pltpu.VMEM((4,) + span, jnp.bfloat16),
            pltpu.VMEM((5,) + out, jnp.bfloat16),
            pltpu.VMEM((4,) + out, jnp.bfloat16),
            pltpu.VMEM(out, jnp.bfloat16),
            pltpu.VMEM(out, jnp.bfloat16),
            pltpu.VMEM((4,) + small, jnp.float32),
            pltpu.VMEM((4,) + small, jnp.float32),
            pltpu.VMEM((3,) + small, jnp.float32),
            pltpu.VMEM(small, jnp.float32),
            pltpu.VMEM((3,) + small, jnp.float32),
            dma((4, CHUNKS)), dma((4, CHUNKS)), dma((4, CHUNKS)), dma((5, CHUNKS)),
            dma((4,)), dma((5,)), dma((2,)),
            dma((CHUNKS + 1,)), dma((CHUNKS + 1,)),
            dma(two), dma(two), dma(two), dma(two), dma(two), dma(two),
            dma((CORES,)), dma((CORES,)), dma((7,)), dma((7,)), dma((1,)),
        ],
        compiler_params=pltpu.CompilerParams(
            collective_id=2, has_side_effects=True, vmem_limit_bytes=VMEM_BYTES
        ),
        name="finish_sums",
    )(grad, out_grad, late, late_out, tiny)


def assemble_kernel(part_ref, shared_ref, total_ref):
    last = pl.program_id(0) == 8
    step = DI // 16

    @pl.when(last)
    def _():
        shared = [shared_ref[i, :SHARED].astype(jnp.float32) for i in range(GROUP)]
        total_ref[:SHARED] = (shared[0] + shared[1]) + (shared[2] + shared[3])

    @pl.when(jnp.logical_not(last))
    def _():
        for i in range(GROUP):
            total_ref[i * step : (i + 1) * step] = part_ref[i].astype(jnp.float32)


def assemble_rows(parts):
    lanes = parts.shape[-1]
    step = DI // 16
    return pl.pallas_call(
        assemble_kernel,
        grid=(9,),
        in_specs=[
            pl.BlockSpec((GROUP, step, lanes), lambda i: (0, jnp.minimum(i, 7), 0)),
            pl.BlockSpec((GROUP, 2 * step, lanes), lambda i: (0, 4, 0)),
        ],
        out_specs=pl.BlockSpec((GROUP * step, lanes), lambda i: (i, 0)),
        out_shape=jax.ShapeDtypeStruct((DI + CONV + H, lanes), jnp.float32),
        compiler_params=pltpu.CompilerParams(vmem_limit_bytes=VMEM_BYTES),
        name="assemble_rows",
    )(parts, parts)


def per_device_split(
    boundary_in,
    lengths,
    seq_order,
    norm_gain,
    in_weight,
    conv_weight,
    conv_bias,
    dt_bias,
    a_log,
    d_skip,
    out_gain,
    out_weight,
):
    c = lax.axis_index("section")
    z = lax.axis_index("shard")
    r = lax.axis_index("rep")
    y, x = r // 2, r % 2
    block = boundary_in.shape[3]
    rows = GROUP * block
    width = DI // GROUP
    heads = H // GROUP
    span = width + 2 * N
    quarter = 2 * x + c

    def spot(cc, zz, rr):
        return (cc * 4 + zz) * 4 + rr

    def home(m, zz, rr):
        return spot(zz % 2, 2 * m + rr % 2, (rr // 2) * 2 + zz // 2)

    places = [(cc, zz, rr) for cc in range(2) for zz in range(4) for rr in range(4)]
    axes = ("section", "shard", "rep")
    straight = [(spot(*p), home(p[0], p[1], p[2])) for p in places]
    crossed = [(spot(*p), home(1 - p[0], p[1], p[2])) for p in places]

    def go_back(value, cc):
        ways = []
        for m in range(MICRO):
            pairs = [(home(m, zz, rr), spot(cc, zz, rr)) for zz in range(4) for rr in range(4)]
            ways.append(lax.ppermute(value, axes, pairs))
        return ways

    in_rows = jnp.swapaxes(in_weight[0], 0, 1)
    w_in0, w_out0 = gather_weights(0, in_rows, out_weight[0])

    arrive_a = lax.ppermute(
        lax.dynamic_index_in_dim(boundary_in[0, :, 0], c, 0, False), axes, straight
    )
    arrive_b = lax.ppermute(
        lax.dynamic_index_in_dim(boundary_in[0, :, 0], 1 - c, 0, False), axes, crossed
    )
    source = jnp.where(z < 2, arrive_a, arrive_b)
    cotangent = jnp.where(z < 2, arrive_b, arrive_a)

    order = jnp.stack([lengths[:, 0], seq_order[:, 0]])
    order = jnp.where(x == z % 2, order, swap_x(order))
    order = lax.dynamic_index_in_dim(order, z // 2, 1, False)
    chosen = (order[1][:, None] == jnp.arange(NSEQ, dtype=jnp.int32)[None, :]).astype(jnp.int32)
    finish = jnp.cumsum(jnp.sum(chosen * order[0][None, :], axis=1), dtype=jnp.int32)

    def segment_of(positions):
        found = jnp.sum((positions[:, None] >= finish[None, :]).astype(jnp.int32), axis=1)
        return jnp.where(positions < 0, -1, found)

    token = jnp.arange(rows, dtype=jnp.int32)
    segment = segment_of(token)
    opening = token // Q * Q
    columns = [segment_of(token - lag) == segment for lag in range(1, KW)]
    columns.append(segment_of(opening - 1) == segment)
    columns.append(segment_of(opening + (Q - 1)) == segment)
    columns = [column.astype(jnp.float32) for column in columns] + [segment.astype(jnp.float32)]
    marks = jnp.stack(columns + [jnp.zeros((rows,), jnp.float32)] * 2, axis=1)
    seg_row = segment.astype(jnp.float32)[None]

    params = (norm_gain, conv_weight, conv_bias, dt_bias, a_log, d_skip, out_gain)
    count = sum(p.size for p in params)
    filler = -count % LANES
    flat = jnp.concatenate([p.reshape(-1) for p in params] + [jnp.zeros((filler,), jnp.bfloat16)])
    flat = ordered(c == 0, flat, swap_core(flat))
    flat = ordered(z % 2 == 0, flat, swap_z(flat, 1))
    flat = ordered(z // 2 == 0, flat, swap_z(flat, 2))
    flat = flat.reshape((4, CORES, count + filler)).astype(jnp.float32)

    given = jnp.arange(SHARED - 2 * N + 16)[:, None]
    local = jnp.arange(LANES)[None, :]
    picked = (given % 12 // 3 == quarter) & (local == given // 12 * 3 + given % 3) & (given < H)
    picked = low(picked.astype(jnp.float32))

    def layer_params(layer):
        found = []
        at = 0
        for p in params:
            part = flat[:, layer, at : at + p.size].reshape((4,) + p.shape[1:])
            at += p.size
            found.append(jnp.moveaxis(part, 0, -2).reshape(p.shape[1:-1] + (-1,)))
        gain, conv_w, conv_b, dt_b, log_a, skip, gain_out = found

        def spread(v):
            return jnp.pad(pick_last(v, quarter), (0, LANES - heads))[None]

        def taps(v):
            return jnp.concatenate([pick_last(v[:, :DI], quarter), v[:, DI:]], axis=1)

        return {
            "norm": gain,
            "conv_w": taps(conv_w),
            "conv_b": taps(conv_b[None]),
            "dt_bias": spread(dt_b),
            "rate": spread(jnp.exp(log_a)),
            "pick": picked,
            "skip": jnp.repeat(pick_last(skip, quarter), P_SIZE)[None],
            "gain": pick_last(gain_out, quarter)[None],
        }

    small = [layer_params(0), layer_params(1)]

    def group_rows(v):
        count = v.shape[0]
        near = swap_x(v)
        other = swap_core(v)
        far = swap_core(near)
        whole = jnp.zeros((GROUP * count,) + v.shape[1:], v.dtype)
        for part, at in (
            (v, 2 * x + c),
            (other, 2 * x + 1 - c),
            (near, 2 * (1 - x) + c),
            (far, 2 * (1 - x) + 1 - c),
        ):
            whole = lax.dynamic_update_slice_in_dim(whole, part, at * count, 0)
        return whole

    def group_product(left, product):
        blocks = left.reshape((2, 2, block) + left.shape[1:])
        theirs = lax.dynamic_index_in_dim(blocks, 1 - c, 1, False)
        theirs = product(theirs.reshape((2 * block,) + left.shape[1:]))
        received = swap_core(low(theirs)).reshape((2, block, -1))
        mine = lax.dynamic_index_in_dim(blocks, c, 1, False)

        def summed(at):
            part = product(lax.dynamic_index_in_dim(mine, at, 0, False))
            return part + lax.dynamic_index_in_dim(received, at, 0, False).astype(jnp.float32)

        across = swap_x(low(summed(1 - x)))
        return summed(x) + across.astype(jnp.float32)

    def own(v):
        return lax.dynamic_slice_in_dim(v, (2 * x + c) * block, block, 0)

    def forward(layer, entering, w_in, w_out):
        gain = small[layer]["norm"]
        inv = lax.rsqrt(jnp.mean(entering * entering, axis=-1, keepdims=True) + EPSILON)
        normed = group_rows(low(entering * inv * gain))
        projected = low(mm(normed, w_in, 1, 1))
        gg, squares, mixer, starts = mixer_forward(projected, marks, seg_row, small[layer])
        half = squares.reshape((rows // LANES, LANES))
        half = half + swap_core(half)
        half = half + swap_x(half)
        out_inv = lax.rsqrt(half / DI + EPSILON).reshape((rows, 1))
        product = group_product(gg, lambda v: mm(v, w_out))
        added = own(out_inv) * product
        return entering + added, (entering, inv, normed, projected, mixer, starts, out_inv, added)

    def backward(layer, kept, incoming, w_in, w_out):
        entering, inv, normed, projected, mixer, starts, out_inv, added = kept
        gain = small[layer]["norm"]
        incoming32 = incoming.astype(jnp.float32)
        dots = jnp.sum(incoming32 * added, axis=1).reshape((-1, LANES))
        dots = group_rows(dots).reshape((rows, 1))
        g = group_rows(incoming)
        og = mm(g, w_out, 1, 1)
        per_row = jnp.concatenate([out_inv, dots], axis=1)
        pg, outgoing, wide, conv, head = mixer_backward(
            projected, marks, seg_row, small[layer], mixer, starts, og, per_row, DI
        )
        out_grad = low(mm(outgoing, g, 0, 0))
        normed_grad = group_product(pg, lambda v: mm(v, w_in))
        in_grad = low(mm(pg, normed, 0, 0))
        hat = entering * inv
        hat_grad = normed_grad * gain
        mean = jnp.mean(hat_grad * hat, axis=-1, keepdims=True)
        source_grad = incoming32 + inv * (hat_grad - hat * mean)
        norm_grad = jnp.sum(normed_grad * hat, axis=0)
        taps = jnp.concatenate([place_last(conv[:5, :width], quarter), conv[:5, width:]], axis=1)
        tiny = [
            norm_grad[None],
            taps[:KW],
            taps[KW:],
            place_last(head[0:1, :heads], quarter),
            place_last(head[1:2, :heads], quarter),
            place_last(wide[1].reshape((1, heads, P_SIZE)).sum(axis=2), quarter),
            place_last(wide[0:1], quarter),
        ]
        tiny = [jnp.moveaxis(t.reshape((t.shape[0], 4, -1)), 1, 0).reshape((4, -1)) for t in tiny]
        tiny = jnp.concatenate(tiny + [jnp.zeros((4, filler), jnp.float32)], axis=1)
        return source_grad, in_grad, out_grad, tiny

    def scatter_in(grad):
        parts = grad.reshape((2, HALF, D))
        sent = swap_y(lax.dynamic_index_in_dim(parts, 1 - y, 0, False))
        kept = lax.dynamic_index_in_dim(parts, y, 0, False)
        both = low(kept.astype(jnp.float32) + sent.astype(jnp.float32))
        both = jnp.stack([both[:, zz * LANE_PART : (zz + 1) * LANE_PART] for zz in range(4)])
        return lax.psum_scatter(both, "shard", scatter_dimension=0, tiled=False)

    def scatter_out(grad):
        part = lax.psum_scatter(
            grad.reshape((4, OUT_PART, D)), "shard", scatter_dimension=0, tiled=False
        )
        return low(part.astype(jnp.float32) + swap_y(part).astype(jnp.float32))

    middle, kept0 = forward(0, source.astype(jnp.float32), w_in0, w_out0)
    in_rows_late = after(in_rows, kept0[4])
    w_in1, w_out1 = gather_weights(1, in_rows_late, out_weight[0])
    result, kept1 = forward(1, low(middle).astype(jnp.float32), w_in1, w_out1)
    result_ways = go_back(low(result), 1)
    middle_grad, in_grad1, out_grad1, tiny1 = backward(1, kept1, cotangent, w_in1, w_out1)
    out_part1 = scatter_out(out_grad1)
    in_part1 = scatter_in(in_grad1)
    entry_grad, in_grad0, out_grad0, tiny0 = backward(0, kept0, low(middle_grad), w_in0, w_out0)
    grad_ways = go_back(low(entry_grad), 0)

    boundary = jnp.stack(
        [jnp.where(c == 0, grad_ways[m], result_ways[m]) for m in range(MICRO)]
    ).astype(jnp.float32)[None, :, None]

    tiny = jnp.stack([tiny0, tiny1]).reshape((CORES, 4, -1, LANES))
    in_grad0 = after(in_grad0, entry_grad)
    in_all, out_all, tiny = finish_sums(in_grad0, out_grad0, in_part1, out_part1, tiny)
    in_total = jnp.swapaxes(assemble_rows(in_all), 0, 1)[None]
    out_total = out_all.astype(jnp.float32)[None]
    tiny = tiny.reshape(-1)
    totals = []
    at = 0
    for p in params:
        totals.append(tiny[at : at + p.size].reshape(p.shape))
        at += p.size
    norm_total, conv_total, bias_total, dt_total, log_total, skip_total, gain_total = totals
    return (
        boundary,
        norm_total,
        in_total,
        conv_total,
        bias_total,
        dt_total,
        log_total,
        skip_total,
        gain_total,
        out_total,
    )


def solution(mesh):
    fits = mesh.shape["shard"] == GROUP and mesh.shape["rep"] == 4
    return jax.shard_map(
        per_device_split if fits else per_device,
        mesh=mesh,
        in_specs=(
            P("section", None, "rep", "shard", None),
            P(None, "rep", None),
            P(None, "rep", None),
            P("section", "shard"),
            P("section", "shard", None),
            P("section", None, "shard"),
            P("section", "shard"),
            P("section", "shard"),
            P("section", "shard"),
            P("section", "shard"),
            P("section", "shard"),
            P("section", "shard", None),
        ),
        out_specs=(
            P("section", None, "rep", "shard", None),
            P("section", "shard"),
            P("section", "shard", None),
            P("section", None, "shard"),
            P("section", "shard"),
            P("section", "shard"),
            P("section", "shard"),
            P("section", "shard"),
            P("section", "shard"),
            P("section", "shard", None),
        ),
        check_vma=False,
    )
```

```python
import functools

import jax
import jax.numpy as jnp
from jax import lax
from jax.experimental import pallas as pl
from jax.experimental.pallas import tpu as pltpu
from jax.sharding import PartitionSpec as P

D = 1536
P_SIZE = 64
N = 128
KW = 4
BLOCK = 256
MICRO = 2
NSEQ = 4
DI = 3072
H = 48
CONV = 3328


EPSILON = 1e-05
PRECISE = lax.Precision.HIGHEST


def from_behind(shard, axis, by):
    devices = lax.axis_size(axis)
    pairs = [(i, i + by) for i in range(devices) if 0 <= i + by < devices]
    return lax.ppermute(shard, axis, pairs)


def entering(value, axis, join, neutral):
    count, mine = (lax.axis_size(axis), lax.axis_index(axis))
    pieces = jax.tree.map(lambda part: lax.all_gather(part, axis), value)
    subtotal = jax.tree.map(
        lambda part, zero: jnp.full_like(part, 0) + jnp.asarray(zero, part.dtype), value, neutral
    )

    def turn(position, subtotal):
        longer = join(subtotal, jax.tree.map(lambda part: part[position], pieces))
        return jax.tree.map(lambda new, old: jnp.where(position < mine, new, old), longer, subtotal)

    return lax.fori_loop(0, count - 1, turn, subtotal)


def entering_2(shard, axis, join, neutral):
    count = lax.axis_size(axis)
    place = lax.axis_index(axis)
    ahead = count - 1 - place
    gathered = jax.tree.map(
        lambda a, kind: lax.all_gather(a.astype(kind), axis),
        shard,
        jax.tree.map(lambda a: jnp.bfloat16 if a.dtype == jnp.float32 else a.dtype, shard),
    )
    state = jax.tree.map(lambda a, e: jnp.zeros_like(a) + jnp.asarray(e, a.dtype), shard, neutral)

    def one(turn, state):
        source = count - 1 - turn
        return join(
            state,
            jax.tree.map(
                lambda a, own: lax.dynamic_index_in_dim(a, source, 0, False).astype(own.dtype),
                gathered,
                shard,
            ),
        )

    return lax.fori_loop(0, ahead, one, state)


def contract(left, right, left_dim, right_dim):
    return lax.dot_general(
        left, right, (((left_dim,), (right_dim,)), ((), ())), preferred_element_type=jnp.float32
    )


def input_norm(source, gain):
    inv_rms = lax.rsqrt(jnp.mean(source * source, axis=-1, keepdims=True) + EPSILON)
    return source * inv_rms * gain


def block_step(carry_state, pieces):
    x_heads, b_rows, c_rows, log_decay, step_size, segment, before = pieces
    running = jnp.cumsum(log_decay, axis=0)
    places = jnp.arange(x_heads.shape[0])
    linked = (places[:, None] >= places[None, :]) & (segment[:, None] == segment[None, :])
    linked3 = linked[:, :, None]
    gap_sums = jnp.where(linked3, running[:, None, :] - running[None, :, :], 0.0)
    decays = jnp.where(linked3, jnp.exp(gap_sums), 0.0)
    scores = jnp.dot(c_rows, b_rows.T, precision=PRECISE)
    mixing = scores[:, :, None] * decays * step_size[None, :, :]
    inside_part = jnp.einsum("tsh,shp->thp", mixing, x_heads, precision=PRECISE)
    carried = (segment == before).astype(jnp.float32)
    reach = jnp.exp(running) * carried[:, None]
    carried_part = (
        jnp.einsum("tn,hpn->thp", c_rows, carry_state, precision=PRECISE) * reach[:, :, None]
    )
    closing = segment[-1]
    tail_weight = (
        jnp.exp(running[-1][None, :] - running)
        * step_size
        * (segment == closing).astype(jnp.float32)[:, None]
    )
    fresh_state = jnp.einsum("sh,shp,sn->hpn", tail_weight, x_heads, b_rows, precision=PRECISE)
    retained = jnp.exp(running[-1]) * (closing == before).astype(jnp.float32)
    return (retained[:, None, None] * carry_state + fresh_state, inside_part + carried_part)


def conv_inputs(wide_rows, raw_step, conv_weight, conv_bias, dt_bias, a_log, lag_masks):
    rows_here = raw_step.shape[0]
    conv_sum = conv_bias + conv_weight[KW - 1] * wide_rows[KW - 1 :]
    for lag in range(1, KW):
        conv_sum = (
            conv_sum
            + conv_weight[KW - 1 - lag]
            * wide_rows[KW - 1 - lag : KW - 1 - lag + rows_here]
            * lag_masks[lag - 1][:, None]
        )
    active = jax.nn.silu(conv_sum)
    x_heads = active[:, :DI].reshape(rows_here, H, P_SIZE)
    b_rows = active[:, DI : DI + N]
    c_rows = active[:, DI + N :]
    step_size = jax.nn.softplus(raw_step + dt_bias)
    log_decay = -step_size * jnp.exp(a_log)
    return (x_heads, b_rows, c_rows, log_decay, step_size)


def local_scan(x_heads, b_rows, c_rows, log_decay, step_size, segment, befores, seg_before):
    rows_here = x_heads.shape[0]

    def blocks(member):
        return member.reshape((rows_here // BLOCK, BLOCK) + member.shape[1:])

    start_state = jnp.zeros((H, P_SIZE, N), jnp.float32)
    pieces = (
        blocks(x_heads),
        blocks(b_rows),
        blocks(c_rows),
        blocks(log_decay),
        blocks(step_size),
        blocks(segment),
        befores,
    )
    end_state, mixer_out = lax.scan(jax.checkpoint(block_step), start_state, pieces)
    retained = jnp.exp(jnp.sum(log_decay, axis=0)) * (segment[-1] == seg_before).astype(jnp.float32)
    return (mixer_out.reshape(rows_here, H, P_SIZE), end_state, retained)


def state_entry(c_rows, log_decay, state_in, carried):
    reach = jnp.exp(jnp.cumsum(log_decay, axis=0)) * carried[:, None]
    return jnp.einsum("tn,hpn->thp", c_rows, state_in, precision=PRECISE) * reach[:, :, None]


def gate_norm(mixer_out, x_heads, d_skip, gate_part, out_gain):
    rows_here = x_heads.shape[0]
    total_out = mixer_out + d_skip[:, None] * x_heads
    gated = total_out.reshape(rows_here, DI) * jax.nn.silu(gate_part)
    inv_gated = lax.rsqrt(jnp.mean(gated * gated, axis=-1, keepdims=True) + EPSILON)
    return gated * inv_gated * out_gain


def carry_forward(earlier, later):
    return (earlier[0] * later[0], later[0][:, None, None] * earlier[1] + later[1])


def carry_backward(earlier, later):
    return (later[0] * earlier[0], later[1] + later[0][:, None, None] * earlier[1])


def segment_marks(lengths, seq_order, micro_slot, row_start, rows_here):
    micro_slot = jnp.clip(micro_slot, 0, MICRO - 1)
    seq_lengths = lax.dynamic_index_in_dim(lengths[:, 0], micro_slot, 0, keepdims=False)
    row_order = lax.dynamic_index_in_dim(seq_order[:, 0], micro_slot, 0, keepdims=False)
    picks = (row_order[:, None] == jnp.arange(NSEQ, dtype=jnp.int32)[None, :]).astype(jnp.int32)
    placed = jnp.sum(picks * seq_lengths[None, :], axis=1)
    finish = jnp.cumsum(placed, dtype=jnp.int32)
    positions = row_start + jnp.arange(-(KW - 1), rows_here, dtype=jnp.int32)
    extended = jnp.sum((positions[:, None] >= finish[None, :]).astype(jnp.int32), axis=1)
    extended = jnp.where(positions < 0, -1, extended)
    segment = extended[KW - 1 :]
    seg_before = extended[KW - 2]
    lag_masks = jnp.stack(
        [
            (extended[KW - 1 - lag : KW - 1 - lag + rows_here] == segment).astype(jnp.float32)
            for lag in range(1, KW)
        ]
    )
    befores = jnp.concatenate([seg_before[None], segment[:-1]])[::BLOCK]
    carried = (segment == seg_before).astype(jnp.float32)
    return (segment, lag_masks, befores, seg_before, carried)


def mixer_pass(projected, weights, marks):
    norm_gain, in_weight, conv_weight, conv_bias, dt_bias, a_log, d_skip, out_gain, out_weight = (
        weights
    )
    segment, lag_masks, befores, seg_before, carried = marks
    rows_here = projected.shape[0]
    gate_part = projected[:, :DI].astype(jnp.float32)
    mixed_part = projected[:, DI : DI + CONV]
    raw_step = projected[:, DI + CONV :].astype(jnp.float32)
    rim_rows = from_behind(mixed_part[rows_here - (KW - 1) :], "shard", 1)
    wide_rows = jnp.concatenate([rim_rows, mixed_part], axis=0).astype(jnp.float32)

    def conv_section(wide_rows, raw_step, conv_weight, conv_bias, dt_bias, a_log):
        return conv_inputs(wide_rows, raw_step, conv_weight, conv_bias, dt_bias, a_log, lag_masks)

    conv_outs, conv_pull = jax.vjp(
        conv_section, wide_rows, raw_step, conv_weight, conv_bias, dt_bias, a_log
    )
    x_heads, b_rows, c_rows, log_decay, step_size = conv_outs

    def scan_section(x_heads, b_rows, c_rows, log_decay, step_size):
        return local_scan(
            x_heads, b_rows, c_rows, log_decay, step_size, segment, befores, seg_before
        )

    scan_outs, scan_pull = jax.vjp(scan_section, x_heads, b_rows, c_rows, log_decay, step_size)
    local_out, end_state, retained = scan_outs
    identity = (jnp.ones((H,), jnp.float32), jnp.zeros((H, P_SIZE, N), jnp.float32))
    prefix = entering((retained, end_state), "shard", carry_forward, identity)
    state_in = prefix[1]

    def entry_section(c_rows, log_decay, state_in):
        return state_entry(c_rows, log_decay, state_in, carried)

    entered, entry_pull = jax.vjp(entry_section, c_rows, log_decay, state_in)
    mixer_out = local_out + entered
    outgoing, norm_pull = jax.vjp(gate_norm, mixer_out, x_heads, d_skip, gate_part, out_gain)
    return (
        outgoing.astype(jnp.bfloat16),
        (conv_pull, scan_pull, entry_pull, norm_pull, retained, state_in),
    )


def mamba_forward(source, weights, marks):
    normed = input_norm(source, weights[0]).astype(jnp.bfloat16)
    projected = jnp.dot(normed, weights[1], preferred_element_type=jnp.float32).astype(jnp.bfloat16)
    outgoing, unused_pulls = mixer_pass(projected, weights, marks)
    return source + jnp.dot(outgoing, weights[8], preferred_element_type=jnp.float32)


def mamba_backward(source, incoming, weights, marks):
    norm_gain, in_weight, conv_weight, conv_bias, dt_bias, a_log, d_skip, out_gain, out_weight = (
        weights
    )
    rows_here = source.shape[0]
    normed, front_pull = jax.vjp(input_norm, source, norm_gain)
    normed_low = normed.astype(jnp.bfloat16)
    projected = jnp.dot(normed_low, in_weight, preferred_element_type=jnp.float32).astype(
        jnp.bfloat16
    )
    outgoing, pulls = mixer_pass(projected, weights, marks)
    conv_pull, scan_pull, entry_pull, norm_pull, retained, state_in = pulls
    incoming_low = incoming.astype(jnp.bfloat16)
    out_weight_grad = contract(outgoing, incoming_low, 0, 0)
    outgoing_grad = contract(incoming_low, out_weight, 1, 1)
    mixer_grad, x_grad_a, d_skip_grad, gate_grad, out_gain_grad = norm_pull(outgoing_grad)
    c_grad_a, decay_grad_a, direct = entry_pull(mixer_grad)
    identity = (jnp.ones((H,), jnp.float32), jnp.zeros((H, P_SIZE, N), jnp.float32))
    suffix = entering_2((retained, direct), "shard", carry_backward, identity)
    later_grad = suffix[1]
    retained_grad = jnp.sum(later_grad * state_in, axis=(1, 2))
    x_grad_b, b_grad, c_grad_b, decay_grad_b, step_grad = scan_pull(
        (mixer_grad, later_grad, retained_grad)
    )
    conv_grads = conv_pull(
        (x_grad_a + x_grad_b, b_grad, c_grad_a + c_grad_b, decay_grad_a + decay_grad_b, step_grad)
    )
    wide_grad, raw_grad, conv_weight_grad, conv_bias_grad, dt_bias_grad, a_log_grad = conv_grads
    back_rows = from_behind(wide_grad[: KW - 1].astype(jnp.bfloat16), "shard", -1).astype(
        jnp.float32
    )
    filler = jnp.zeros((rows_here - (KW - 1), CONV), jnp.float32)
    mixed_grad = wide_grad[KW - 1 :] + jnp.concatenate([filler, back_rows], axis=0)
    projected_grad = jnp.concatenate([gate_grad, mixed_grad, raw_grad], axis=1).astype(jnp.bfloat16)
    in_weight_grad = contract(normed_low, projected_grad, 0, 0)
    normed_grad = contract(projected_grad, in_weight, 1, 1)
    source_grad, norm_gain_grad = front_pull(normed_grad)
    weight_grads = (
        norm_gain_grad,
        in_weight_grad,
        conv_weight_grad,
        conv_bias_grad,
        dt_bias_grad,
        a_log_grad,
        d_skip_grad,
        out_gain_grad,
        out_weight_grad,
    )
    return (incoming + source_grad, weight_grads)


def per_device(
    boundary_in,
    lengths,
    seq_order,
    norm_gain,
    in_weight,
    conv_weight,
    conv_bias,
    dt_bias,
    a_log,
    d_skip,
    out_gain,
    out_weight,
):
    section_index = lax.axis_index("section")
    is_first = section_index == 0
    rows_here = boundary_in.shape[3]
    row_start = lax.axis_index("shard") * rows_here

    def current():
        whole = (
            lax.all_gather(norm_gain, "shard", axis=1, tiled=True),
            lax.all_gather(in_weight, "shard", axis=1, tiled=True),
            lax.all_gather(conv_weight, "shard", axis=2, tiled=True),
            lax.all_gather(conv_bias, "shard", axis=1, tiled=True),
            lax.all_gather(dt_bias, "shard", axis=1, tiled=True),
            lax.all_gather(a_log, "shard", axis=1, tiled=True),
            lax.all_gather(d_skip, "shard", axis=1, tiled=True),
            lax.all_gather(out_gain, "shard", axis=1, tiled=True),
            lax.all_gather(out_weight, "shard", axis=1, tiled=True),
        )
        return tuple(
            (
                member[0] if slot_index in (1, 8) else member[0].astype(jnp.float32)
                for slot_index, member in enumerate(whole)
            )
        )

    source_rows = boundary_in[0, :, 0]
    arrived = jnp.zeros((rows_here, D), jnp.bfloat16)
    inputs = []
    results = []
    for step_index in range(MICRO + 1):
        own_rows = source_rows[min(step_index, MICRO - 1)]
        layer_in = jnp.where(is_first, own_rows, arrived)
        inputs.append(layer_in)
        marks = segment_marks(lengths, seq_order, step_index - section_index, row_start, rows_here)
        layer_out = mamba_forward(layer_in.astype(jnp.float32), current(), marks)
        results.append(layer_out)
        if step_index < MICRO:
            arrived = from_behind(layer_out.astype(jnp.bfloat16), "section", 1)
    returned = jnp.zeros((rows_here, D), jnp.bfloat16)
    totals = None
    source_grads = []
    for step_index in range(MICRO + 1):
        micro_slot = step_index - 1 + section_index
        is_valid = (micro_slot >= 0) & (micro_slot < MICRO)
        own_rows = source_rows[min(step_index, MICRO - 1)]
        incoming = jnp.where(is_first, returned, own_rows).astype(jnp.float32)
        incoming = jnp.where(is_valid, incoming, 0.0)
        layer_in = jnp.where(
            is_first, inputs[max(step_index - 1, 0)], inputs[min(step_index + 1, MICRO)]
        )
        marks = segment_marks(lengths, seq_order, micro_slot, row_start, rows_here)
        source_grad, weight_grads = mamba_backward(
            layer_in.astype(jnp.float32), incoming, current(), marks
        )
        if totals is None:
            totals = tuple(weight_grads)
        else:
            totals = tuple((earlier + added for earlier, added in zip(totals, weight_grads)))
        source_grads.append(source_grad)
        if step_index < MICRO:
            returned = from_behind(source_grad.astype(jnp.bfloat16), "section", -1)
    boundary = jnp.stack(
        [
            jnp.where(is_first, source_grads[micro_pos + 1], results[micro_pos + 1])
            for micro_pos in range(MICRO)
        ]
    )[None, :, None]
    shares = (
        lax.psum_scatter(
            totals[0][None].astype(jnp.bfloat16), "shard", scatter_dimension=1, tiled=True
        ).astype(jnp.float32),
        lax.psum_scatter(
            totals[1][None].astype(jnp.bfloat16), "shard", scatter_dimension=1, tiled=True
        ).astype(jnp.float32),
        lax.psum_scatter(
            totals[2][None].astype(jnp.bfloat16), "shard", scatter_dimension=2, tiled=True
        ).astype(jnp.float32),
        lax.psum_scatter(
            totals[3][None].astype(jnp.bfloat16), "shard", scatter_dimension=1, tiled=True
        ).astype(jnp.float32),
        lax.psum_scatter(
            totals[4][None].astype(jnp.bfloat16), "shard", scatter_dimension=1, tiled=True
        ).astype(jnp.float32),
        lax.psum_scatter(
            totals[5][None].astype(jnp.bfloat16), "shard", scatter_dimension=1, tiled=True
        ).astype(jnp.float32),
        lax.psum_scatter(
            totals[6][None].astype(jnp.bfloat16), "shard", scatter_dimension=1, tiled=True
        ).astype(jnp.float32),
        lax.psum_scatter(
            totals[7][None].astype(jnp.bfloat16), "shard", scatter_dimension=1, tiled=True
        ).astype(jnp.float32),
        lax.psum_scatter(
            totals[8][None].astype(jnp.bfloat16), "shard", scatter_dimension=1, tiled=True
        ).astype(jnp.float32),
    )
    reduced = (
        lax.psum(shares[0].astype(jnp.bfloat16), "rep").astype(jnp.float32),
        lax.psum(shares[1].astype(jnp.bfloat16), "rep").astype(jnp.float32),
        lax.psum(shares[2].astype(jnp.bfloat16), "rep").astype(jnp.float32),
        lax.psum(shares[3].astype(jnp.bfloat16), "rep").astype(jnp.float32),
        lax.psum(shares[4].astype(jnp.bfloat16), "rep").astype(jnp.float32),
        lax.psum(shares[5].astype(jnp.bfloat16), "rep").astype(jnp.float32),
        lax.psum(shares[6].astype(jnp.bfloat16), "rep").astype(jnp.float32),
        lax.psum(shares[7].astype(jnp.bfloat16), "rep").astype(jnp.float32),
        lax.psum(shares[8].astype(jnp.bfloat16), "rep").astype(jnp.float32),
    )
    return (boundary,) + tuple(reduced)


Q = 128
LANES = 128
VMEM_BYTES = 56 * 1024 * 1024
EXACT = lax.Precision.HIGHEST


def mm(a, b, da=1, db=0):
    return lax.dot_general(
        a, b, (((da,), (db,)), ((), ())), preferred_element_type=jnp.float32
    )


def exact(a, b):
    return jnp.dot(a, b, precision=EXACT, preferred_element_type=jnp.float32)


def low(v):
    return v.astype(jnp.bfloat16)


def iota(shape, dim):
    return lax.broadcasted_iota(jnp.int32, shape, dim)


def pair_cols(v, p):
    rows = v.shape[0]
    left = jnp.broadcast_to(v[:, 2 * p : 2 * p + 1], (rows, LANES))
    right = jnp.broadcast_to(v[:, 2 * p + 1 : 2 * p + 2], (rows, LANES))
    return jnp.where(iota((rows, LANES), 1) < LANES // 2, left, right)


def widen(v, pairs):
    return jnp.concatenate([pair_cols(v, p) for p in range(pairs)], axis=1)


def stack_pair(v, p):
    block = v[:, p * LANES : (p + 1) * LANES]
    left = iota(block.shape, 1) < LANES // 2
    zero = jnp.zeros_like(block)
    return jnp.concatenate([jnp.where(left, block, zero), jnp.where(left, zero, block)], axis=0)


def softplus(v):
    small = jnp.exp(-jnp.abs(v))
    series = small * (1 + small * (-1 / 2 + small * (1 / 3 + small * (-1 / 4 + small / 5))))
    return jnp.maximum(v, 0.0) + jnp.where(small < 0.01, series, jnp.log(1 + small))


def sigmoid(v):
    return 1.0 / (1.0 + jnp.exp(-v))


def chunk_parts(width, proj, before8, marks, seg_row, conv_w, conv_b, dt_bias, rate, pick):
    span = width + 2 * LANES
    gate = proj[:, :width].astype(jnp.float32)
    mixed = proj[:, width : width + span].astype(jnp.float32)
    raw = mm(proj[:, width + span :], pick)
    shifts = [mixed]
    top = iota((8, span), 0)
    for lag in range(1, KW):
        rolled = pltpu.roll(mixed, lag, 0)
        head = jnp.where(top < lag, pltpu.roll(before8, lag, 0), rolled[:8])
        moved = jnp.concatenate([head, rolled[8:]], axis=0)
        shifts.append(moved * marks[:, lag - 1 : lag])
    conv = conv_b
    for lag in range(KW):
        conv = conv + conv_w[KW - 1 - lag : KW - lag] * shifts[lag]
    sig = sigmoid(conv)
    active = conv * sig
    stepped = raw + dt_bias
    step = softplus(stepped)
    decay = -step * rate
    lower = iota((Q, Q), 0) >= iota((Q, Q), 1)
    total = exact(lower.astype(jnp.float32), decay)
    linked = lower & (marks[:, 5:6] == seg_row)
    shut = jnp.where(linked, 0.0, -1e30)
    reach = jnp.exp(total) * marks[:, 3:4]
    tail = jnp.exp(total[Q - 1 : Q] - total) * marks[:, 4:5]
    return gate, mixed, shifts, conv, sig, active, stepped, step, decay, total, shut, reach, tail


def forward_kernel(
    width, proj_ref, marks_ref, seg_ref, conv_w_ref, conv_b_ref, dt_bias_ref, rate_ref, pick_ref,
    skip_ref, gain_ref, gg_ref, squares_ref, mixer_ref, starts_ref, state, before,
):
    pairs = width // LANES

    @pl.when(pl.program_id(0) == 0)
    def _():
        state[...] = jnp.zeros_like(state)
        before[...] = jnp.zeros_like(before)

    gate, mixed, _, _, _, active, _, step, _, total, shut, reach, tail = chunk_parts(
        width, proj_ref[...], before[...], marks_ref[...], seg_ref[...], conv_w_ref[...],
        conv_b_ref[...], dt_bias_ref[...], rate_ref[...], pick_ref[...],
    )
    before[...] = mixed[Q - 8 :]
    heads = active[:, :width]
    b_low = low(active[:, width : width + LANES])
    c_low = low(active[:, width + LANES :])
    entry = state[...]
    starts_ref[0] = entry
    scores = mm(c_low, b_low, 1, 1)
    total_t = total.T
    scaled = heads * widen(step, pairs)
    scaled_low = low(scaled)
    inside = []
    for p in range(pairs):
        both = []
        for h in (2 * p, 2 * p + 1):
            both.append(low(jnp.exp(total[:, h : h + 1] - total_t[h : h + 1] + shut) * scores))
        inside.append(mm(jnp.concatenate(both, axis=1), stack_pair(scaled_low, p)))
    mixer = jnp.concatenate(inside, axis=1) + widen(reach, pairs) * mm(c_low, low(entry))
    b_turned = low(active[:, width : width + LANES].T)
    state[...] = entry * widen(reach[Q - 1 : Q], pairs) + mm(
        b_turned, low(scaled * widen(tail, pairs))
    )
    mixer_ref[...] = mixer
    gated = (mixer + skip_ref[...] * heads) * (gate * sigmoid(gate))
    squares_ref[...] = jnp.sum(gated * gated, axis=1, keepdims=True)
    gg_ref[...] = low(gated * gain_ref[...])


def backward_kernel(
    width, whole_width, proj_ref, rim_ref, marks_ref, seg_ref, conv_w_ref, conv_b_ref, dt_bias_ref,
    rate_ref, pick_ref, skip_ref, gain_ref, mixer_ref, starts_ref, og_ref, rows_ref,
    pg_ref, outgoing_ref, wide_ref, conv_ref, head_ref, later, after,
):
    pairs = width // LANES
    turn = pl.program_id(0)
    chunk = pl.num_programs(0) - 1 - turn

    @pl.when(turn == 0)
    def _():
        later[...] = jnp.zeros_like(later)
        after[...] = jnp.zeros_like(after)
        wide_ref[...] = jnp.zeros_like(wide_ref)
        conv_ref[...] = jnp.zeros_like(conv_ref)
        head_ref[...] = jnp.zeros_like(head_ref)

    span = width + 2 * LANES
    marks = marks_ref[...]
    rim = rim_ref[...][8:, width : width + span].astype(jnp.float32)
    rim = jnp.where(chunk > 0, rim, 0.0)
    gate, mixed, shifts, conv, sig, active, stepped, step, decay, total, shut, reach, tail = (
        chunk_parts(
            width, proj_ref[...], rim, marks, seg_ref[...], conv_w_ref[...], conv_b_ref[...],
            dt_bias_ref[...], rate_ref[...], pick_ref[...],
        )
    )
    heads = active[:, :width]
    b_low = low(active[:, width : width + LANES])
    c_low = low(active[:, width + LANES :])

    inv = rows_ref[:, 0:1]
    dots = rows_ref[:, 1:2]
    og = og_ref[...]
    mixer = mixer_ref[...]
    out = mixer + skip_ref[...] * heads
    gate_sig = sigmoid(gate)
    gate_on = gate * gate_sig
    hat = out * gate_on * inv
    outgoing_ref[...] = low(hat * gain_ref[...])
    gated_grad = inv * (gain_ref[...] * og - hat * (dots * (1.0 / whole_width)))
    out_grad = gated_grad * gate_on
    gate_grad = gated_grad * out * (gate_sig * (1.0 + gate * (1.0 - gate_sig)))

    entry = starts_ref[0]
    entry_low = low(entry)
    late = later[...]
    late_low = low(late)
    scores = mm(c_low, b_low, 1, 1)
    total_t = total.T
    step_wide = widen(step, pairs)
    scaled = heads * step_wide
    scaled_low = low(scaled)
    grad_low = low(out_grad)
    from_late = widen(tail, pairs) * mm(b_low, late_low)
    inside = []
    score_grad = jnp.zeros((Q, Q), jnp.float32)
    for p in range(pairs):
        gains = []
        both = []
        for h in (2 * p, 2 * p + 1):
            gain = jnp.exp(total[:, h : h + 1] - total_t[h : h + 1] + shut)
            gains.append(gain)
            both.append(low(gain * scores))
        stacked = stack_pair(grad_low, p)
        inside.append(mm(jnp.concatenate(both, axis=0), stacked, 0, 0))
        mix_grad = mm(stacked, scaled_low[:, p * LANES : (p + 1) * LANES], 1, 1)
        score_grad = score_grad + gains[0] * mix_grad[:Q] + gains[1] * mix_grad[Q:]
    scaled_grad = jnp.concatenate(inside, axis=1) + from_late
    reached = low(widen(reach, pairs) * out_grad)
    score_low = low(score_grad)
    c_grad = mm(score_low, b_low) + mm(reached, entry_low, 1, 1)
    b_grad = mm(score_low, c_low, 0, 0) + mm(low(scaled * widen(tail, pairs)), late_low, 1, 1)
    kept = widen(reach[Q - 1 : Q], pairs)
    later[...] = late * kept + mm(c_low, reached, 0, 0)

    scaled_seen = scaled_low.astype(jnp.float32)
    balance = grad_low.astype(jnp.float32) * mixer - scaled_seen * scaled_grad
    closing = jnp.sum(scaled_seen * from_late, axis=0, keepdims=True) + kept * jnp.sum(
        late * entry, axis=0, keepdims=True
    )
    picks = (iota((width, LANES), 0) // (LANES // 2) == iota((width, LANES), 1)).astype(jnp.float32)
    sums = exact(
        jnp.concatenate([balance, heads * scaled_grad, jnp.broadcast_to(closing, (8, width))], 0),
        picks,
    )
    upper = (iota((Q, Q), 0) <= iota((Q, Q), 1)).astype(jnp.float32)
    decay_grad = exact(upper, sums[:Q]) + sums[2 * Q : 2 * Q + 1]
    step_grad = sums[Q : 2 * Q] - decay_grad * rate_ref[...]
    raw_grad = step_grad * sigmoid(stepped)

    head_grad = step_wide * scaled_grad + skip_ref[...] * out_grad
    conv_grad = jnp.concatenate([head_grad, b_grad, c_grad], axis=1) * (
        sig * (1.0 + conv * (1.0 - sig))
    )
    mixed_grad = conv_w_ref[KW - 1 : KW] * conv_grad
    bottom = iota((8, span), 0)
    for lag in range(1, KW):
        sent = conv_grad * marks[:, lag - 1 : lag]
        rolled = pltpu.roll(sent, Q - lag, 0)
        ending = jnp.where(
            bottom >= 8 - lag, pltpu.roll(after[lag - 1], 8 - lag, 0), rolled[Q - 8 :]
        )
        mixed_grad = mixed_grad + conv_w_ref[KW - 1 - lag : KW - lag] * jnp.concatenate(
            [rolled[: Q - 8], ending], axis=0
        )
        after[lag - 1] = sent[:8]
    pg_ref[...] = low(
        jnp.concatenate([gate_grad, mixed_grad, mm(low(raw_grad), pick_ref[...], 1, 1)], axis=1)
    )

    wide_ref[0:1] += jnp.sum(hat * og, axis=0, keepdims=True)
    wide_ref[1:2] += jnp.sum(out_grad * heads, axis=0, keepdims=True)
    for lag in range(KW):
        conv_ref[KW - 1 - lag : KW - lag] += jnp.sum(
            conv_grad * shifts[lag], axis=0, keepdims=True
        )
    conv_ref[KW : KW + 1] += jnp.sum(conv_grad, axis=0, keepdims=True)
    head_ref[0:1] += jnp.sum(raw_grad, axis=0, keepdims=True)
    head_ref[1:2] += jnp.sum(decay_grad * decay, axis=0, keepdims=True)


def full_spec(shape):
    return pl.BlockSpec(shape, lambda i: (0,) * len(shape))


def mixer_forward(projected, marks, seg_row, small):
    rows, columns = projected.shape
    width = small["gain"].shape[1]
    chunks = rows // Q
    span = width + 2 * LANES

    def by_row(count):
        return pl.BlockSpec((Q, count), lambda i: (i, 0))

    weights = [small[k] for k in ("conv_w", "conv_b", "dt_bias", "rate", "pick", "skip", "gain")]
    return pl.pallas_call(
        functools.partial(forward_kernel, width),
        grid=(chunks,),
        in_specs=[by_row(columns), by_row(8), pl.BlockSpec((1, Q), lambda i: (0, i))]
        + [full_spec(w.shape) for w in weights],
        out_specs=[
            by_row(width),
            by_row(1),
            by_row(width),
            pl.BlockSpec((1, LANES, width), lambda i: (i, 0, 0)),
        ],
        out_shape=[
            jax.ShapeDtypeStruct((rows, width), jnp.bfloat16),
            jax.ShapeDtypeStruct((rows, 1), jnp.float32),
            jax.ShapeDtypeStruct((rows, width), jnp.float32),
            jax.ShapeDtypeStruct((chunks, LANES, width), jnp.float32),
        ],
        scratch_shapes=[
            pltpu.VMEM((LANES, width), jnp.float32),
            pltpu.VMEM((8, span), jnp.float32),
        ],
        compiler_params=pltpu.CompilerParams(vmem_limit_bytes=VMEM_BYTES),
        name="mixer_forward",
    )(projected, marks, seg_row, *weights)


def mixer_backward(projected, marks, seg_row, small, mixer, starts, og, per_row, whole_width):
    rows, columns = projected.shape
    width = small["gain"].shape[1]
    chunks = rows // Q
    span = width + 2 * LANES

    def by_row(count):
        return pl.BlockSpec((Q, count), lambda i: (chunks - 1 - i, 0))

    weights = [small[k] for k in ("conv_w", "conv_b", "dt_bias", "rate", "pick", "skip", "gain")]
    rim = pl.BlockSpec(
        (16, columns), lambda i: (jnp.maximum((chunks - 1 - i) * (Q // 16) - 1, 0), 0)
    )
    return pl.pallas_call(
        functools.partial(backward_kernel, width, whole_width),
        grid=(chunks,),
        in_specs=[by_row(columns), rim, by_row(8), pl.BlockSpec((1, Q), lambda i: (0, chunks - 1 - i))]
        + [full_spec(w.shape) for w in weights]
        + [
            by_row(width),
            pl.BlockSpec((1, LANES, width), lambda i: (chunks - 1 - i, 0, 0)),
            by_row(width),
            by_row(2),
        ],
        out_specs=[
            by_row(columns),
            by_row(width),
            full_spec((8, width)),
            full_spec((8, span)),
            full_spec((8, LANES)),
        ],
        out_shape=[
            jax.ShapeDtypeStruct((rows, columns), jnp.bfloat16),
            jax.ShapeDtypeStruct((rows, width), jnp.bfloat16),
            jax.ShapeDtypeStruct((8, width), jnp.float32),
            jax.ShapeDtypeStruct((8, span), jnp.float32),
            jax.ShapeDtypeStruct((8, LANES), jnp.float32),
        ],
        scratch_shapes=[
            pltpu.VMEM((LANES, width), jnp.float32),
            pltpu.VMEM((KW - 1, 8, span), jnp.float32),
        ],
        compiler_params=pltpu.CompilerParams(vmem_limit_bytes=VMEM_BYTES),
        name="mixer_backward",
    )(projected, projected, marks, seg_row, *weights, mixer, starts, og, per_row)


CORES = 2
GROUP = 4
SHARED = CONV - DI + H
LOCAL = 2 * DI // GROUP + SHARED + 16
HALF = LOCAL // 2
CHUNKS = 2
LANE_PART = D // 4
OUT_PART = DI // 16
UNITS = CHUNKS + 1


def place():
    c, z, r = (lax.axis_index(name) for name in ("section", "shard", "rep"))
    return c, z, lax.div(r, 2), lax.rem(r, 2)


def weight_pieces(quarter):
    part = DI // 16
    found = []
    for side in range(2):
        for zz in range(4):
            found.append(
                (side * 4 * part + zz * part, side * DI + zz * 4 * part + quarter * part, part)
            )
    found.append((8 * part, 2 * DI, SHARED))
    return found


def mesh_copy(source, target, send, recv, device):
    return pltpu.make_async_remote_copy(
        src_ref=source, dst_ref=target, send_sem=send, recv_sem=recv,
        device_id=device, device_id_type=pl.DeviceIdType.MESH,
    )


def greet(barrier, device):
    pl.semaphore_signal(barrier, inc=1, device_id=device, device_id_type=pl.DeviceIdType.MESH)


def rows_at(start, count):
    return pl.ds(pl.multiple_of(start, 16), count)


class WeightGather:
    def __init__(self, layer, in_ref, out_ref, w_ref, wo_ref, sems):
        self.layer, self.in_ref, self.out_ref = layer, in_ref, out_ref
        self.w_ref, self.wo_ref = w_ref, wo_ref
        (
            self.local_sem, self.core_send, self.core_recv, self.right_send, self.left_send,
            self.z_recv, self.y_send, self.y_recv,
        ) = sems
        self.c, self.z, self.y, self.x = place()
        self.core = {"section": 1 - self.c}
        self.y_other = {"rep": (1 - self.y) * 2 + self.x}

    def own_pieces(self, quarter):
        lanes = pl.ds(pl.multiple_of(self.z * LANE_PART, LANES), LANE_PART)
        found = []
        for at, start, count in weight_pieces(quarter):
            found.append((self.in_ref.at[rows_at(start, count)], self.w_ref.at[pl.ds(at, count), lanes]))
        found.append(
            (
                self.out_ref.at[rows_at(quarter * OUT_PART, OUT_PART)],
                self.wo_ref.at[rows_at(self.z * OUT_PART, OUT_PART)],
            )
        )
        return found

    def local_copies(self):
        return [
            pltpu.make_async_copy(source, target, self.local_sem.at[i])
            for i, (source, target) in enumerate(self.own_pieces(2 * self.x + self.c))
        ]

    def core_copies(self):
        return [
            mesh_copy(source, target, self.core_send.at[i], self.core_recv.at[i], self.core)
            for i, (source, target) in enumerate(self.own_pieces(2 * self.x + 1 - self.c))
        ]

    def begin(self):
        lanes = pl.ds(pl.multiple_of(self.z * LANE_PART, LANES), LANE_PART)
        self.w_ref[LOCAL - 16 :, lanes] = jnp.zeros((16, LANE_PART), self.w_ref.dtype)

        @pl.when(self.c == self.layer)
        def _():
            for copy in self.core_copies():
                copy.start()
            for copy in self.local_copies():
                copy.start()
            for copy in self.local_copies():
                copy.wait()

        @pl.when(self.c != self.layer)
        def _():
            for copy in self.core_copies():
                copy.wait_recv()

    def slab(self, unit, shard, side):
        if unit == CHUNKS:
            return self.wo_ref.at[rows_at(shard * OUT_PART + side * (OUT_PART // 2), OUT_PART // 2)]
        return self.w_ref.at[
            rows_at(side * HALF + unit * (HALF // CHUNKS), HALF // CHUNKS),
            pl.ds(pl.multiple_of(shard * LANE_PART, LANES), LANE_PART),
        ]

    def z_copy(self, unit, shard, step, k):
        piece = self.slab(unit, shard, self.y)
        send = (self.right_send if step > 0 else self.left_send).at[unit, k]
        return mesh_copy(piece, piece, send, self.z_recv.at[unit, shard], {"shard": self.z + step})

    def y_copy(self, unit, shard, side):
        piece = self.slab(unit, shard, side)
        return mesh_copy(
            piece, piece, self.y_send.at[unit, shard], self.y_recv.at[unit, shard], self.y_other
        )

    def cases(self, step, k):
        shard = self.z - k * step
        there = (shard >= 0) if step > 0 else (shard <= 3)
        more = (self.z < 3) if step > 0 else (self.z > 0)
        return shard, there, more

    def first(self, unit):
        for step in (1, -1):
            _, _, more = self.cases(step, 0)

            @pl.when(more)
            def _():
                self.z_copy(unit, self.z, step, 0).start()

    def arrive(self, unit, k):
        for step in (1, -1):
            shard, there, more = self.cases(step, k)

            @pl.when(there)
            def _():
                self.z_copy(unit, shard, step, 0).wait_recv()

                @pl.when(more)
                def _():
                    self.z_copy(unit, shard, step, k).start()

                self.y_copy(unit, shard, self.y).start()

    def end(self):
        for unit in range(UNITS):
            for away in (1, 2, 3):
                shard = lax.rem(self.z + away, 4)
                self.y_copy(unit, shard, 1 - self.y).wait_recv()
                self.y_copy(unit, shard, self.y).wait_send()
            for step in (1, -1):
                for k in range(3):
                    shard, there, more = self.cases(step, k)

                    @pl.when(there & more)
                    def _():
                        self.z_copy(unit, shard, step, k).wait_send()

        @pl.when(self.c == self.layer)
        def _():
            for copy in self.core_copies():
                copy.wait_send()


def weight_scratch():
    dma = pltpu.SemaphoreType.DMA
    return [
        dma((10,)), dma((10,)), dma((10,)),
        dma((UNITS, 3)), dma((UNITS, 3)), dma((UNITS, 4)), dma((UNITS, 4)), dma((UNITS, 4)),
    ]


class RowGather:
    def __init__(self, whole, count, sems):
        self.whole, self.count = whole, count
        self.send, self.recv = sems
        self.c, self.z, self.y, self.x = place()

    def copy(self, i, xx, cc, device):
        piece = self.whole.at[rows_at((2 * xx + cc) * self.count, self.count)]
        return mesh_copy(piece, piece, self.send.at[i], self.recv.at[i], device)

    def near(self):
        return self.copy(0, self.x, self.c, {"rep": 2 * self.y + 1 - self.x})

    def other(self):
        return self.copy(1, self.x, self.c, {"section": 1 - self.c})

    def far(self):
        return self.copy(2, 1 - self.x, self.c, {"section": 1 - self.c})

    def begin(self, value):
        self.whole[rows_at((2 * self.x + self.c) * self.count, self.count)] = value
        self.near().start()
        self.other().start()

    def middle(self):
        self.near().wait_recv()
        self.far().start()

    def end(self):
        self.near().wait_send()
        self.other().wait()
        self.far().wait()


def normal_rows(rows, gain):
    inv = lax.rsqrt(jnp.mean(rows * rows, axis=-1, keepdims=True) + EPSILON)
    return low(rows * inv * gain)


def enter_first_kernel(
    in_ref, out_ref, blocks_ref, flat_ref, w_ref, wo_ref, rows_ref, normed_ref, params_ref,
    row_send, row_recv, home_send, home_recv, p_send, p_recv, *sems,
):
    c, z, y, x = place()
    weights = WeightGather(0, in_ref, out_ref, w_ref, wo_ref, sems)
    gather = RowGather(normed_ref, rows_ref.shape[0], (row_send, row_recv))
    source = {"section": 0, "shard": 2 * x + c, "rep": 2 * y + lax.rem(z, 2)}
    from_self = (c == 0) & (z == 2 * x) & (x == lax.rem(z, 2))
    targets = tuple(
        {"section": lax.rem(z, 2), "shard": 2 * m + x, "rep": 2 * y + lax.div(z, 2)}
        for m in range(MICRO)
    )
    to_self = tuple(
        (lax.rem(z, 2) == 0) & (z == 2 * m + x) & (x == lax.div(z, 2)) for m in range(MICRO)
    )
    others = [{"section": 1 - c}]
    for away in (1, 2, 3):
        others.append({"shard": lax.rem(z + away, 4)})
        others.append({"section": 1 - c, "shard": lax.rem(z + away, 4)})

    barrier = pltpu.get_barrier_semaphore()
    for device in others + [{"rep": 2 * y + 1 - x}, {"rep": 2 * (1 - y) + x}]:
        greet(barrier, device)

    @pl.when(jnp.logical_not(from_self))
    def _():
        greet(barrier, source)

    guests = sum(jnp.logical_not(own).astype(jnp.int32) for own in to_self)
    pl.semaphore_wait(barrier, 9 + jnp.where(c == 0, guests, 0))

    def home_copy(m):
        return mesh_copy(
            blocks_ref.at[0, m, 0], rows_ref, home_send.at[m], home_recv.at[0], targets[m]
        )

    def own_copy(m):
        return pltpu.make_async_copy(blocks_ref.at[0, m, 0], rows_ref, home_send.at[m])

    def param_copy(i):
        return mesh_copy(
            flat_ref, params_ref.at[4 * c + z], p_send.at[i], p_recv.at[i], others[i]
        )

    def param_from(i):
        cc = c if i % 2 == 1 else 1 - c
        zz = z if i == 0 else lax.rem(z + 4 - (i + 1) // 2, 4)
        return mesh_copy(
            flat_ref, params_ref.at[4 * cc + zz], p_send.at[i], p_recv.at[i], others[i]
        )

    for m in range(MICRO):

        @pl.when((c == 0) & jnp.logical_not(to_self[m]))
        def _():
            home_copy(m).start()

        @pl.when((c == 0) & to_self[m])
        def _():
            own_copy(m).start()

    for i in range(7):
        param_copy(i).start()
    params_ref[4 * c + z] = flat_ref[...]
    weights.begin()
    for unit in range(CHUNKS):
        weights.first(unit)
    for unit in range(CHUNKS):
        weights.arrive(unit, 1)

    for i in range(7):
        param_from(i).wait_recv()

    @pl.when(jnp.logical_not(from_self))
    def _():
        home_copy(0).wait_recv()

    for m in range(MICRO):

        @pl.when((c == 0) & to_self[m])
        def _():
            own_copy(m).wait()

    gains = [params_ref[zz].astype(jnp.float32) for zz in range(4)]
    gain = jnp.concatenate([g[i : i + 1] for g in gains for i in range(3)], axis=1)
    gather.begin(normal_rows(rows_ref[...].astype(jnp.float32), gain))
    for unit in range(CHUNKS):
        weights.arrive(unit, 2)
    weights.first(CHUNKS)
    gather.middle()
    for unit in range(CHUNKS):
        weights.arrive(unit, 3)
    for k in (1, 2, 3):
        weights.arrive(CHUNKS, k)
    weights.end()
    gather.end()
    for i in range(7):
        param_copy(i).wait_send()
    for m in range(MICRO):

        @pl.when((c == 0) & jnp.logical_not(to_self[m]))
        def _():
            home_copy(m).wait_send()


def weight_shapes():
    return [
        jax.ShapeDtypeStruct((LOCAL, D), jnp.bfloat16),
        jax.ShapeDtypeStruct((DI // GROUP, D), jnp.bfloat16),
    ]


def enter_first(in_rows, out_rows, blocks, flat):
    dma = pltpu.SemaphoreType.DMA
    block = blocks.shape[-2]
    anywhere, inside = pl.BlockSpec(memory_space=pl.ANY), pl.BlockSpec(memory_space=pltpu.VMEM)
    return pl.pallas_call(
        enter_first_kernel,
        in_specs=[anywhere] * 3 + [inside],
        out_specs=[inside] * 5,
        out_shape=weight_shapes()
        + [
            jax.ShapeDtypeStruct((block, D), jnp.bfloat16),
            jax.ShapeDtypeStruct((GROUP * block, D), jnp.bfloat16),
            jax.ShapeDtypeStruct((2 * 4,) + flat.shape, jnp.bfloat16),
        ],
        scratch_shapes=[dma((3,)), dma((3,)), dma((MICRO,)), dma((1,)), dma((7,)), dma((7,))]
        + weight_scratch(),
        compiler_params=pltpu.CompilerParams(
            collective_id=0, has_side_effects=True, vmem_limit_bytes=VMEM_BYTES
        ),
        name="enter_first",
    )(in_rows, out_rows, blocks, flat)


def enter_second_kernel(
    in_ref, out_ref, theirs_ref, mine_ref, squares_ref, entering_ref, gain_ref, g_ref,
    w_ref, wo_ref, added_ref, middle_ref, normed_ref, g_all_ref, inv_ref,
    n_core, n_send, n_across, s_core, s_mine, s_across,
    row_send, row_recv, g_send, g_recv, n_sem, s_sem, *sems,
):
    c, z, y, x = place()
    weights = WeightGather(1, in_ref, out_ref, w_ref, wo_ref, sems)
    block = entering_ref.shape[0]
    gather = RowGather(normed_ref, block, (row_send, row_recv))
    g_gather = RowGather(g_all_ref, block, (g_send, g_recv))
    core, x_other = {"section": 1 - c}, {"rep": 2 * y + 1 - x}
    barrier = pltpu.get_barrier_semaphore()
    for device in (core, x_other, {"rep": 2 * (1 - y) + x}):
        greet(barrier, device)

    @pl.when(z < 3)
    def _():
        greet(barrier, {"shard": z + 1})

    @pl.when(z > 0)
    def _():
        greet(barrier, {"shard": z - 1})

    ends = jnp.where(z == 0, 1, 0) + jnp.where(z == 3, 1, 0)
    pl.semaphore_wait(barrier, 5 - ends)

    n_core_copy = mesh_copy(theirs_ref, n_core, n_sem.at[0], n_sem.at[1], core)
    n_x_copy = mesh_copy(n_send, n_across, n_sem.at[2], n_sem.at[3], x_other)
    s_core_copy = mesh_copy(squares_ref, s_core, s_sem.at[0], s_sem.at[1], core)
    s_x_copy = mesh_copy(s_mine, s_across, s_sem.at[2], s_sem.at[3], x_other)

    n_core_copy.start()
    s_core_copy.start()
    weights.begin()
    for unit in range(CHUNKS):
        weights.first(unit)

    def summed(which):
        rows = rows_at(which * block, block)
        return mine_ref[rows] + n_core[rows].astype(jnp.float32)

    s_core_copy.wait_recv()
    s_mine[...] = squares_ref[...] + s_core[...]
    s_x_copy.start()
    n_core_copy.wait_recv()
    n_send[...] = low(summed(1 - x))
    n_x_copy.start()
    for unit in range(CHUNKS):
        weights.arrive(unit, 1)

    s_x_copy.wait_recv()
    inv_ref[...] = lax.rsqrt((s_mine[...] + s_across[...]) * (1.0 / DI) + EPSILON)
    n_x_copy.wait_recv()
    product = summed(x) + n_across[...].astype(jnp.float32)
    per = block // LANES
    here = (2 * x + c) * per
    own_inv = jnp.concatenate(
        [
            jnp.broadcast_to(inv_ref[pl.ds(here + i, 1)], (LANES, LANES)).T[:, :1]
            for i in range(per)
        ],
        axis=0,
    )
    added = own_inv * product
    added_ref[...] = added
    middle = low(entering_ref[...].astype(jnp.float32) + added)
    middle_ref[...] = middle
    gather.begin(normal_rows(middle.astype(jnp.float32), gain_ref[...]))
    g_gather.begin(g_ref[...])
    for unit in range(CHUNKS):
        weights.arrive(unit, 2)
    weights.first(CHUNKS)
    for unit in range(CHUNKS):
        weights.arrive(unit, 3)
    gather.middle()
    for k in (1, 2, 3):
        weights.arrive(CHUNKS, k)
    g_gather.middle()
    weights.end()
    gather.end()
    g_gather.end()
    n_core_copy.wait_send()
    n_x_copy.wait_send()
    s_core_copy.wait_send()
    s_x_copy.wait_send()


def enter_second(in_rows, out_rows, theirs, mine, squares, entering, gain, g):
    dma = pltpu.SemaphoreType.DMA
    block = entering.shape[0]
    anywhere, inside = pl.BlockSpec(memory_space=pl.ANY), pl.BlockSpec(memory_space=pltpu.VMEM)
    whole = jax.ShapeDtypeStruct((GROUP * block, D), jnp.bfloat16)
    return pl.pallas_call(
        enter_second_kernel,
        in_specs=[anywhere] * 2 + [inside] * 6,
        out_specs=[inside] * 7,
        out_shape=weight_shapes()
        + [
            jax.ShapeDtypeStruct((block, D), jnp.float32),
            jax.ShapeDtypeStruct((block, D), jnp.bfloat16),
            whole,
            whole,
            jax.ShapeDtypeStruct(squares.shape, jnp.float32),
        ],
        scratch_shapes=[
            pltpu.VMEM(theirs.shape, jnp.bfloat16),
            pltpu.VMEM(entering.shape, jnp.bfloat16),
            pltpu.VMEM(entering.shape, jnp.bfloat16),
            pltpu.VMEM(squares.shape, jnp.float32),
            pltpu.VMEM(squares.shape, jnp.float32),
            pltpu.VMEM(squares.shape, jnp.float32),
            dma((3,)), dma((3,)), dma((3,)), dma((3,)), dma((4,)), dma((4,)),
        ]
        + weight_scratch(),
        compiler_params=pltpu.CompilerParams(
            collective_id=1, has_side_effects=True, vmem_limit_bytes=VMEM_BYTES
        ),
        name="enter_second",
    )(in_rows, out_rows, theirs, mine, squares, entering, gain, g)


def swap_core(v):
    return lax.ppermute(v, "section", [(0, 1), (1, 0)])


def swap_x(v):
    return lax.ppermute(v, "rep", [(i, i ^ 1) for i in range(4)])


def swap_y(v):
    return lax.ppermute(v, "rep", [(i, i ^ 2) for i in range(4)])


def swap_z(v, bit):
    return lax.ppermute(v, "shard", [(i, i ^ bit) for i in range(4)])


def ordered(first, mine, other, axis=0):
    return jnp.where(first, jnp.stack([mine, other], axis), jnp.stack([other, mine], axis))


def joined(first, mine, other, axis=0):
    return jnp.where(
        first, jnp.concatenate([mine, other], axis), jnp.concatenate([other, mine], axis)
    )


def after(value, *earlier):
    return lax.optimization_barrier((value,) + earlier)[0]


def pick_last(v, quarter):
    parts = v.reshape(v.shape[:-1] + (4, GROUP, v.shape[-1] // (4 * GROUP)))
    return lax.dynamic_index_in_dim(parts, quarter, v.ndim, False).reshape(v.shape[:-1] + (-1,))


def place_last(v, quarter):
    parts = v.reshape(v.shape[:-1] + (4, 1, v.shape[-1] // 4))
    empty = jnp.zeros(v.shape[:-1] + (4, GROUP, v.shape[-1] // 4), v.dtype)
    return lax.dynamic_update_slice_in_dim(empty, parts, quarter, v.ndim).reshape(
        v.shape[:-1] + (-1,)
    )


def finish_kernel(
    grad_ref, out_grad_ref, late_ref, late_out_ref, tiny_ref,
    theirs_ref, mine_ref, entering_ref, incoming_ref, gain_ref,
    all_ref, out_all_ref, tiny_out_ref, bound_ref,
    n_core, n_send, n_across, n_done, tiny_mine, y_buf, z_buf, s_buf, zo_buf, so_buf, yo_buf, yo_mine, t1_buf, t1_sum, t2_buf, t2_sum, t3_buf,
    y_send, y_recv, z_send, z_recv, zo_send, zo_recv, yo_sem,
    core_send, core_recv, x_send, x_recv, ya_send, ya_recv, relay_send, relay_recv,
    xo_send, xo_recv, t_send, t_recv, n_sem, home_send, home_recv,
):
    c, z, y, x = place()
    quarter = 2 * x + c
    core, x_other, y_other = {"section": 1 - c}, {"rep": 2 * y + 1 - x}, {"rep": 2 * (1 - y) + x}
    diagonal = {"rep": 2 * (1 - y) + 1 - x}
    part = HALF // CHUNKS

    copy = mesh_copy

    block = n_done.shape[0]
    home = {"section": 0, "shard": quarter, "rep": 2 * y + lax.rem(z, 2)}
    at_home = (c == 0) & (z == quarter) & (x == lax.rem(z, 2))
    guests = tuple(
        {"section": lax.rem(z, 2), "shard": 2 * m + x, "rep": 2 * y + lax.div(z, 2)}
        for m in range(MICRO)
    )

    barrier = pltpu.get_barrier_semaphore()
    reps = (x_other, y_other, diagonal)
    shards = tuple({"shard": lax.rem(z + away, 4)} for away in (1, 2, 3))

    for device in (core,) + reps + shards:
        greet(barrier, device)
    for m in range(MICRO):
        own = (lax.rem(z, 2) == 0) & (z == 2 * m + x) & (x == lax.div(z, 2))

        @pl.when((c == 0) & jnp.logical_not(own))
        def _():
            greet(barrier, guests[m])

    pl.semaphore_wait(barrier, 8 - at_home.astype(jnp.int32))

    orders = ((3, 2, 1, 0), (3, 0, 2, 1), (0, 3, 1, 2), (0, 1, 2, 3))

    def shard_at(i):
        found = jnp.int32(orders[3][i])
        for zz in range(3):
            found = jnp.where(z == zz, orders[zz][i], found)
        return found

    def grad_part(shard, side, ch):
        return grad_ref.at[
            rows_at(side * HALF + ch * part, part),
            pl.ds(pl.multiple_of(shard * LANE_PART, LANES), LANE_PART),
        ]

    def y_copy(shard, ch):
        return copy(
            grad_part(shard, 1 - y, ch), y_buf.at[shard, pl.ds(ch * part, part)],
            y_send.at[shard, ch], y_recv.at[shard, ch], y_other,
        )

    def z_target(shard):
        right = shard > z
        there = {"shard": jnp.clip(z + jnp.where(right, 1, -1), 0, 3)}
        slot = jnp.where(right, shard, jnp.where(shard == z - 1, 4, shard))
        return there, slot

    def z_copy(shard, ch):
        there, slot = z_target(shard)
        return copy(
            s_buf.at[shard, pl.ds(ch * part, part)], z_buf.at[slot, pl.ds(ch * part, part)],
            z_send.at[shard, ch], z_recv.at[slot, ch], there,
        )

    def z_wait(slot, ch):
        there, _ = z_target(shard_at(0))
        copy(
            s_buf.at[0, pl.ds(ch * part, part)], z_buf.at[slot, pl.ds(ch * part, part)],
            z_send.at[0, ch], z_recv.at[slot, ch], there,
        ).wait_recv()

    def zo_copy(shard):
        there, slot = z_target(shard)
        return copy(
            so_buf.at[shard], zo_buf.at[slot], zo_send.at[shard], zo_recv.at[slot], there
        )

    def zo_wait(slot):
        there, _ = z_target(shard_at(0))
        copy(so_buf.at[0], zo_buf.at[slot], zo_send.at[0], zo_recv.at[slot], there).wait_recv()

    def all_part(which, side, ch):
        return all_ref.at[which, rows_at(side * HALF + ch * part, part)]

    def out_part(which):
        return out_all_ref.at[rows_at(which * OUT_PART, OUT_PART)]

    def x_copy(who, ch):
        piece = all_part(2 * x + who, y, ch)
        return copy(piece, piece, x_send.at[who, ch], x_recv.at[who, ch], x_other)

    def ya_copy(who, ch):
        piece = all_part(2 * x + who, y, ch)
        return copy(piece, piece, ya_send.at[who, ch], ya_recv.at[who, ch], y_other)

    def relay_copy(who, ch):
        piece = all_part(2 * x + who, 1 - y, ch)
        return copy(piece, piece, relay_send.at[who, ch], relay_recv.at[who, ch], x_other)

    def xo_copy(who):
        piece = out_part(2 * x + who)
        return copy(piece, piece, xo_send.at[who], xo_recv.at[who], x_other)

    def spread(who, ch):
        x_copy(who, ch).start()
        ya_copy(who, ch).start()

    def late_copy(ch):
        return copy(
            late_ref.at[pl.ds(ch * part, part)], all_part(quarter, y, ch),
            core_send.at[ch], core_recv.at[ch], core,
        )

    def late_out_copy():
        return copy(
            late_out_ref, out_part(quarter), core_send.at[CHUNKS], core_recv.at[CHUNKS], core
        )

    def first_copy(ch):
        piece = all_part(quarter, y, ch)
        return copy(z_buf.at[4, pl.ds(ch * part, part)], piece, core_send.at[ch], core_recv.at[ch], core)

    def first_out_copy():
        return copy(
            yo_mine, out_part(quarter), core_send.at[CHUNKS], core_recv.at[CHUNKS], core
        )

    def t1_copy():
        return copy(tiny_mine.at[1 - c], t1_buf, t_send.at[0], t_recv.at[0], core)

    def t2_copy(away):
        return copy(
            t1_sum.at[lax.rem(z + away, 4)], t2_buf.at[away - 1],
            t_send.at[away], t_recv.at[away], shards[away - 1],
        )

    def t3_copy(i):
        return copy(t2_sum, t3_buf.at[i], t_send.at[4 + i], t_recv.at[4 + i], reps[i])

    def yo_copy():
        return copy(yo_mine, yo_buf, yo_sem.at[0], yo_sem.at[1], y_other)

    def n_core_copy():
        return copy(theirs_ref, n_core, n_sem.at[0], n_sem.at[1], core)

    def n_x_copy():
        return copy(n_send, n_across, n_sem.at[2], n_sem.at[3], x_other)

    def home_copy(m):
        return copy(n_done, bound_ref.at[m], home_send.at[0], home_recv.at[m], home)

    n_core_copy().start()
    for i in range(4):
        shard = shard_at(i)
        for ch in range(CHUNKS):
            y_copy(shard, ch).start()

    @pl.when(c == 0)
    def _():
        for ch in range(CHUNKS):
            late_copy(ch).start()
        late_out_copy().start()

    @pl.when(c == 1)
    def _():
        for ch in range(CHUNKS):
            all_part(quarter, y, ch)[...] = late_ref[pl.ds(ch * part, part)]
        out_part(quarter)[...] = late_out_ref[...]

    def own_out(shard):
        return out_grad_ref[rows_at(shard * OUT_PART, OUT_PART)].astype(jnp.float32)

    def more(shard):
        return ((shard > z) & (z > 0)) | ((shard < z) & (z < 3))

    def send_out(i):
        shard = shard_at(i)

        @pl.when(more(shard))
        def _():
            zo_wait(shard)
            so_buf[shard] = low(own_out(shard) + zo_buf[shard].astype(jnp.float32))

        @pl.when(jnp.logical_not(more(shard)))
        def _():
            so_buf[shard] = out_grad_ref[rows_at(shard * OUT_PART, OUT_PART)]

        zo_copy(shard).start()

    def send_in(i, ch):
        shard = shard_at(i)
        span = pl.ds(ch * part, part)
        y_copy(shard, ch).wait_recv()
        both = grad_part(shard, y, ch)[...].astype(jnp.float32) + y_buf[shard, span].astype(
            jnp.float32
        )

        @pl.when(more(shard))
        def _():
            z_wait(shard, ch)
            s_buf[shard, span] = low(both + z_buf[shard, span].astype(jnp.float32))

        @pl.when(jnp.logical_not(more(shard)))
        def _():
            s_buf[shard, span] = low(both)

        z_copy(shard, ch).start()

    send_out(0)

    def summed(which):
        rows = rows_at(which * block, block)
        return mine_ref[rows] + n_core[rows].astype(jnp.float32)

    n_core_copy().wait_recv()
    n_send[...] = low(summed(1 - x))
    n_x_copy().start()
    for ch in range(CHUNKS):
        send_in(0, ch)
    send_out(1)

    n_x_copy().wait_recv()
    normed_grad = summed(x) + n_across[...].astype(jnp.float32)
    entering = entering_ref[...].astype(jnp.float32)
    inv = lax.rsqrt(jnp.mean(entering * entering, axis=-1, keepdims=True) + EPSILON)
    hat = entering * inv
    hat_grad = normed_grad * gain_ref[...]
    mean = jnp.mean(hat_grad * hat, axis=-1, keepdims=True)
    n_done[...] = low(incoming_ref[...].astype(jnp.float32) + inv * (hat_grad - hat * mean))
    for m in range(MICRO):
        there = lax.div(z, 2) == m

        @pl.when(there & jnp.logical_not(at_home))
        def _():
            home_copy(m).start()

        @pl.when(there & at_home)
        def _():
            bound_ref[m] = n_done[...]

    norm_grad = jnp.sum(normed_grad * hat, axis=0, keepdims=True)
    tiny_mine[...] = tiny_ref[...]
    for zz in range(4):
        for row in range(3):
            at = (3 * zz + row) * LANES
            tiny_mine[0, zz, row : row + 1] += norm_grad[:, at : at + LANES]
    t1_copy().start()

    @pl.when(c == 1)
    def _():
        for ch in range(CHUNKS):
            late_copy(ch).wait_recv()
            for who in range(CORES):
                x_copy(who, ch).start()
        late_out_copy().wait_recv()
        for who in range(CORES):
            xo_copy(who).start()

    for ch in range(CHUNKS):
        send_in(1, ch)
    send_out(2)

    t1_copy().wait_recv()
    t1_sum[...] = tiny_mine[c] + t1_buf[...]
    for away in (1, 2, 3):
        t2_copy(away).start()
    for ch in range(CHUNKS):
        send_in(2, ch)

    @pl.when(c == 1)
    def _():
        for ch in range(CHUNKS):
            for who in range(CORES):
                ya_copy(who, ch).start()

    yo_mine[...] = low(own_out(z))

    @pl.when(z > 0)
    def _():
        zo_wait(z)
        yo_mine[...] = low(own_out(z) + zo_buf[z].astype(jnp.float32))

    @pl.when(z < 3)
    def _():
        zo_wait(4)
        yo_mine[...] = low(yo_mine[...].astype(jnp.float32) + zo_buf[4].astype(jnp.float32))

    yo_copy().start()
    for away in (1, 2, 3):
        t2_copy(away).wait_recv()
    t2_sum[...] = (t1_sum[z] + t2_buf[0]) + (t2_buf[1] + t2_buf[2])
    for i in range(3):
        t3_copy(i).start()

    for ch in range(CHUNKS):
        span = pl.ds(ch * part, part)
        y_copy(z, ch).wait_recv()
        s_buf[z, span] = low(
            grad_part(z, y, ch)[...].astype(jnp.float32) + y_buf[z, span].astype(jnp.float32)
        )

        @pl.when(z > 0)
        def _():
            z_wait(z, ch)
            s_buf[z, span] = low(
                s_buf[z, span].astype(jnp.float32) + z_buf[z, span].astype(jnp.float32)
            )

        @pl.when(z < 3)
        def _():
            z_wait(4, ch)
            s_buf[z, span] = low(
                s_buf[z, span].astype(jnp.float32) + z_buf[4, span].astype(jnp.float32)
            )

        @pl.when(c == 1)
        def _():
            z_buf[4, span] = s_buf[z, span]
            first_copy(ch).start()

        @pl.when(c == 0)
        def _():
            all_part(quarter, y, ch)[...] = s_buf[z, span]
            spread(0, ch)
            first_copy(ch).wait_recv()
            spread(1, ch)

    yo_copy().wait()
    total = low(yo_mine[...].astype(jnp.float32) + yo_buf[...].astype(jnp.float32))

    @pl.when(c == 0)
    def _():
        out_part(quarter)[...] = total

    @pl.when(c == 1)
    def _():
        yo_mine[...] = total
        first_out_copy().start()

    @pl.when(c == 0)
    def _():
        first_out_copy().wait_recv()
        for who in range(CORES):
            xo_copy(who).start()

    for i in range(3):
        t3_copy(i).wait_recv()
    tiny_out_ref[...] = (t2_sum[...] + t3_buf[0]) + (t3_buf[1] + t3_buf[2])

    for ch in range(CHUNKS):
        for who in range(CORES):
            ya_copy(who, ch).wait_recv()
            relay_copy(who, ch).start()
    for ch in range(CHUNKS):
        for who in range(CORES):
            x_copy(who, ch).wait()
            ya_copy(who, ch).wait_send()
            relay_copy(who, ch).wait()
    for who in range(CORES):
        xo_copy(who).wait()
    n_core_copy().wait_send()
    n_x_copy().wait_send()

    @pl.when(jnp.logical_not(at_home))
    def _():
        home_copy(0).wait_send()

    for m in range(MICRO):
        own = (lax.rem(z, 2) == 0) & (z == 2 * m + x) & (x == lax.div(z, 2))

        @pl.when((c == 0) & jnp.logical_not(own))
        def _():
            home_copy(m).wait_recv()

    t1_copy().wait_send()
    for away in (1, 2, 3):
        t2_copy(away).wait_send()
    for i in range(3):
        t3_copy(i).wait_send()
        zo_copy(shard_at(i)).wait_send()
        for ch in range(CHUNKS):
            z_copy(shard_at(i), ch).wait_send()
    for i in range(4):
        for ch in range(CHUNKS):
            y_copy(shard_at(i), ch).wait_send()

    @pl.when(c == 0)
    def _():
        for ch in range(CHUNKS):
            late_copy(ch).wait_send()
        late_out_copy().wait_send()

    @pl.when(c == 1)
    def _():
        for ch in range(CHUNKS):
            first_copy(ch).wait_send()
        first_out_copy().wait_send()


def finish_sums(grad, out_grad, late, late_out, tiny, theirs, mine, entering, incoming, gain):
    dma = pltpu.SemaphoreType.DMA
    span = (HALF, LANE_PART)
    out = (OUT_PART, D)
    small = tiny.shape[2:]
    two = (CORES, CHUNKS)
    return pl.pallas_call(
        finish_kernel,
        in_specs=[pl.BlockSpec(memory_space=pltpu.VMEM)] * 10,
        out_specs=[pl.BlockSpec(memory_space=pltpu.VMEM)] * 4,
        out_shape=[
            jax.ShapeDtypeStruct((GROUP, LOCAL, LANE_PART), jnp.bfloat16),
            jax.ShapeDtypeStruct((DI // GROUP, D), jnp.bfloat16),
            jax.ShapeDtypeStruct(small, jnp.float32),
            jax.ShapeDtypeStruct((MICRO,) + entering.shape, jnp.bfloat16),
        ],
        scratch_shapes=[
            pltpu.VMEM(theirs.shape, jnp.bfloat16),
            pltpu.VMEM(entering.shape, jnp.bfloat16),
            pltpu.VMEM(entering.shape, jnp.bfloat16),
            pltpu.VMEM(entering.shape, jnp.bfloat16),
            pltpu.VMEM(tiny.shape, jnp.float32),
            pltpu.VMEM((4,) + span, jnp.bfloat16),
            pltpu.VMEM((5,) + span, jnp.bfloat16),
            pltpu.VMEM((4,) + span, jnp.bfloat16),
            pltpu.VMEM((5,) + out, jnp.bfloat16),
            pltpu.VMEM((4,) + out, jnp.bfloat16),
            pltpu.VMEM(out, jnp.bfloat16),
            pltpu.VMEM(out, jnp.bfloat16),
            pltpu.VMEM((4,) + small, jnp.float32),
            pltpu.VMEM((4,) + small, jnp.float32),
            pltpu.VMEM((3,) + small, jnp.float32),
            pltpu.VMEM(small, jnp.float32),
            pltpu.VMEM((3,) + small, jnp.float32),
            dma((4, CHUNKS)), dma((4, CHUNKS)), dma((4, CHUNKS)), dma((5, CHUNKS)),
            dma((4,)), dma((5,)), dma((2,)),
            dma((CHUNKS + 1,)), dma((CHUNKS + 1,)),
            dma(two), dma(two), dma(two), dma(two), dma(two), dma(two),
            dma((CORES,)), dma((CORES,)), dma((7,)), dma((7,)), dma((4,)), dma((1,)), dma((MICRO,)),
        ],
        compiler_params=pltpu.CompilerParams(
            collective_id=2, has_side_effects=True, vmem_limit_bytes=VMEM_BYTES
        ),
        name="finish_sums",
    )(grad, out_grad, late, late_out, tiny, theirs, mine, entering, incoming, gain)


def assemble_kernel(part_ref, shared_ref, total_ref):
    last = pl.program_id(0) == 8
    step = DI // 16

    @pl.when(last)
    def _():
        shared = [shared_ref[i, :SHARED].astype(jnp.float32) for i in range(GROUP)]
        total_ref[:SHARED] = (shared[0] + shared[1]) + (shared[2] + shared[3])

    @pl.when(jnp.logical_not(last))
    def _():
        for i in range(GROUP):
            total_ref[i * step : (i + 1) * step] = part_ref[i].astype(jnp.float32)


def assemble_rows(parts):
    lanes = parts.shape[-1]
    step = DI // 16
    return pl.pallas_call(
        assemble_kernel,
        grid=(9,),
        in_specs=[
            pl.BlockSpec((GROUP, step, lanes), lambda i: (0, jnp.minimum(i, 7), 0)),
            pl.BlockSpec((GROUP, 2 * step, lanes), lambda i: (0, 4, 0)),
        ],
        out_specs=pl.BlockSpec((GROUP * step, lanes), lambda i: (i, 0)),
        out_shape=jax.ShapeDtypeStruct((DI + CONV + H, lanes), jnp.float32),
        compiler_params=pltpu.CompilerParams(vmem_limit_bytes=VMEM_BYTES),
        name="assemble_rows",
    )(parts, parts)


def per_device_split(
    boundary_in,
    lengths,
    seq_order,
    norm_gain,
    in_weight,
    conv_weight,
    conv_bias,
    dt_bias,
    a_log,
    d_skip,
    out_gain,
    out_weight,
):
    c = lax.axis_index("section")
    z = lax.axis_index("shard")
    r = lax.axis_index("rep")
    y, x = r // 2, r % 2
    block = boundary_in.shape[3]
    rows = GROUP * block
    width = DI // GROUP
    heads = H // GROUP
    span = width + 2 * N
    quarter = 2 * x + c

    def spot(cc, zz, rr):
        return (cc * 4 + zz) * 4 + rr

    def home(m, zz, rr):
        return spot(zz % 2, 2 * m + rr % 2, (rr // 2) * 2 + zz // 2)

    places = [(cc, zz, rr) for cc in range(2) for zz in range(4) for rr in range(4)]
    axes = ("section", "shard", "rep")
    straight = [(spot(*p), home(p[0], p[1], p[2])) for p in places]
    crossed = [(spot(*p), home(1 - p[0], p[1], p[2])) for p in places]

    def go_back(value, cc):
        ways = []
        for m in range(MICRO):
            pairs = [(home(m, zz, rr), spot(cc, zz, rr)) for zz in range(4) for rr in range(4)]
            ways.append(lax.ppermute(value, axes, pairs))
        return ways

    params = (norm_gain, conv_weight, conv_bias, dt_bias, a_log, d_skip, out_gain)
    count = sum(p.size for p in params)
    filler = -count % LANES
    flat = jnp.concatenate(
        [p.reshape(-1) for p in params] + [jnp.zeros((-count % (16 * LANES),), jnp.bfloat16)]
    )
    in_rows = jnp.swapaxes(in_weight[0], 0, 1)
    w_in0, w_out0, source, normed0, flat = enter_first(
        in_rows, out_weight[0], boundary_in, flat.reshape((-1, LANES))
    )
    late_in = after(boundary_in, source)[0, :, 0]
    arrive_a = lax.ppermute(lax.dynamic_index_in_dim(late_in, c, 0, False), axes, straight)
    arrive_b = lax.ppermute(lax.dynamic_index_in_dim(late_in, 1 - c, 0, False), axes, crossed)
    cotangent = jnp.where(z < 2, arrive_b, arrive_a)

    order = jnp.stack([lengths[:, 0], seq_order[:, 0]])
    order = jnp.where(x == z % 2, order, swap_x(order))
    order = lax.dynamic_index_in_dim(order, z // 2, 1, False)
    chosen = (order[1][:, None] == jnp.arange(NSEQ, dtype=jnp.int32)[None, :]).astype(jnp.int32)
    finish = jnp.cumsum(jnp.sum(chosen * order[0][None, :], axis=1), dtype=jnp.int32)

    def segment_of(positions):
        found = jnp.sum((positions[:, None] >= finish[None, :]).astype(jnp.int32), axis=1)
        return jnp.where(positions < 0, -1, found)

    token = jnp.arange(rows, dtype=jnp.int32)
    segment = segment_of(token)
    opening = token // Q * Q
    columns = [segment_of(token - lag) == segment for lag in range(1, KW)]
    columns.append(segment_of(opening - 1) == segment)
    columns.append(segment_of(opening + (Q - 1)) == segment)
    columns = [column.astype(jnp.float32) for column in columns] + [segment.astype(jnp.float32)]
    marks = jnp.stack(columns + [jnp.zeros((rows,), jnp.float32)] * 2, axis=1)
    seg_row = segment.astype(jnp.float32)[None]

    flat = flat.reshape((CORES, 4, -1)).astype(jnp.float32)

    given = jnp.arange(SHARED - 2 * N + 16)[:, None]
    local = jnp.arange(LANES)[None, :]
    picked = (given % 12 // 3 == quarter) & (local == given // 12 * 3 + given % 3) & (given < H)
    picked = low(picked.astype(jnp.float32))

    def layer_params(layer):
        found = []
        at = 0
        for p in params:
            part = flat[layer, :, at : at + p.size].reshape((4,) + p.shape[1:])
            at += p.size
            found.append(jnp.moveaxis(part, 0, -2).reshape(p.shape[1:-1] + (-1,)))
        gain, conv_w, conv_b, dt_b, log_a, skip, gain_out = found

        def spread(v):
            return jnp.pad(pick_last(v, quarter), (0, LANES - heads))[None]

        def taps(v):
            return jnp.concatenate([pick_last(v[:, :DI], quarter), v[:, DI:]], axis=1)

        return {
            "norm": gain,
            "conv_w": taps(conv_w),
            "conv_b": taps(conv_b[None]),
            "dt_bias": spread(dt_b),
            "rate": spread(jnp.exp(log_a)),
            "pick": picked,
            "skip": jnp.repeat(pick_last(skip, quarter), P_SIZE)[None],
            "gain": pick_last(gain_out, quarter)[None],
        }

    small = [layer_params(0), layer_params(1)]

    def group_rows(v):
        count = v.shape[0]
        near = swap_x(v)
        other = swap_core(v)
        far = swap_core(near)
        whole = jnp.zeros((GROUP * count,) + v.shape[1:], v.dtype)
        for part, at in (
            (v, 2 * x + c),
            (other, 2 * x + 1 - c),
            (near, 2 * (1 - x) + c),
            (far, 2 * (1 - x) + 1 - c),
        ):
            whole = lax.dynamic_update_slice_in_dim(whole, part, at * count, 0)
        return whole

    def group_parts(left, product):
        blocks = left.reshape((2, 2, block) + left.shape[1:])
        theirs = lax.dynamic_index_in_dim(blocks, 1 - c, 1, False)
        theirs = low(product(theirs.reshape((2 * block,) + left.shape[1:])))
        mine = lax.dynamic_index_in_dim(blocks, c, 1, False)
        return theirs, product(mine.reshape((2 * block,) + left.shape[1:]))

    def group_sum(parts):
        theirs, mine = parts
        both = (mine + swap_core(theirs).astype(jnp.float32)).reshape((2, block, -1))
        across = swap_x(low(lax.dynamic_index_in_dim(both, 1 - x, 0, False)))
        return lax.dynamic_index_in_dim(both, x, 0, False) + across.astype(jnp.float32)

    def own(v):
        return lax.dynamic_slice_in_dim(v, (2 * x + c) * block, block, 0)

    def row_sums(v):
        v = v + swap_core(v)
        return v + swap_x(v)

    def forward(layer, normed, w_in):
        projected = low(mm(normed, w_in, 1, 1))
        gg, squares, mixer, starts = mixer_forward(projected, marks, seg_row, small[layer])
        return gg, squares.reshape((rows // LANES, LANES)), (normed, projected, mixer, starts)

    def inverse(sums):
        return lax.rsqrt(sums / DI + EPSILON)

    def backward(layer, kept, g, og, per_row):
        normed, projected, mixer, starts = kept
        pg, outgoing, wide, conv, head = mixer_backward(
            projected, marks, seg_row, small[layer], mixer, starts, og, per_row, DI
        )
        out_grad = low(mm(outgoing, g, 0, 0))
        in_grad = low(mm(pg, normed, 0, 0))
        taps = jnp.concatenate([place_last(conv[:5, :width], quarter), conv[:5, width:]], axis=1)
        tiny = [
            jnp.zeros((1, D), jnp.float32),
            taps[:KW],
            taps[KW:],
            place_last(head[0:1, :heads], quarter),
            place_last(head[1:2, :heads], quarter),
            place_last(wide[1].reshape((1, heads, P_SIZE)).sum(axis=2), quarter),
            place_last(wide[0:1], quarter),
        ]
        tiny = [jnp.moveaxis(t.reshape((t.shape[0], 4, -1)), 1, 0).reshape((4, -1)) for t in tiny]
        tiny = jnp.concatenate(tiny + [jnp.zeros((4, filler), jnp.float32)], axis=1)
        return pg, in_grad, out_grad, tiny

    def scatter_in(grad):
        parts = grad.reshape((2, HALF, D))
        sent = swap_y(lax.dynamic_index_in_dim(parts, 1 - y, 0, False))
        kept = lax.dynamic_index_in_dim(parts, y, 0, False)
        both = low(kept.astype(jnp.float32) + sent.astype(jnp.float32))
        both = jnp.stack([both[:, zz * LANE_PART : (zz + 1) * LANE_PART] for zz in range(4)])
        return lax.psum_scatter(both, "shard", scatter_dimension=0, tiled=False)

    def scatter_out(grad):
        part = lax.psum_scatter(
            grad.reshape((4, OUT_PART, D)), "shard", scatter_dimension=0, tiled=False
        )
        return low(part.astype(jnp.float32) + swap_y(part).astype(jnp.float32))

    gg0, squares0, kept0 = forward(0, normed0, w_in0)
    theirs, mine = group_parts(gg0, lambda v: mm(v, w_out0))
    w_in1, w_out1, added0, middle, normed1, g1, out_inv0 = enter_second(
        in_rows, out_weight[0], theirs, mine, squares0, source, small[1]["norm"][None], cotangent
    )
    out_inv0 = out_inv0.reshape((rows, 1))
    og1 = mm(g1, w_out1, 1, 1)
    middle32 = middle.astype(jnp.float32)
    gg1, squares1, kept1 = forward(1, normed1, w_in1)
    dots1 = jnp.sum(gg1.astype(jnp.float32) * og1, axis=1).reshape((rows // LANES, LANES))
    sums1 = row_sums(jnp.stack([squares1, dots1]))
    out_inv1 = inverse(sums1[0]).reshape((rows, 1))
    per_row1 = jnp.concatenate([out_inv1, out_inv1 * sums1[1].reshape((rows, 1))], axis=1)
    parts1 = group_parts(gg1, lambda v: mm(v, w_out1))
    pg1, in_grad1, out_grad1, tiny1 = backward(1, kept1, g1, og1, per_row1)
    result_ways = go_back(low(middle32 + own(out_inv1) * group_sum(parts1)), 1)

    normed_grad = group_sum(group_parts(pg1, lambda v: mm(v, w_in1)))
    inv = lax.rsqrt(jnp.mean(middle32 * middle32, axis=-1, keepdims=True) + EPSILON)
    hat = middle32 * inv
    hat_grad = normed_grad * small[1]["norm"]
    mean = jnp.mean(hat_grad * hat, axis=-1, keepdims=True)
    middle_grad = low(cotangent.astype(jnp.float32) + inv * (hat_grad - hat * mean))
    norm_grad1 = jnp.sum(normed_grad * hat, axis=0).reshape((4, LANE_PART))
    tiny1 = tiny1.at[:, :LANE_PART].add(norm_grad1)
    out_part1 = scatter_out(out_grad1)
    in_part1 = scatter_in(in_grad1)

    dots0 = jnp.sum(middle_grad.astype(jnp.float32) * added0, axis=1).reshape((-1, LANES))
    dots0 = group_rows(dots0).reshape((rows, 1))
    g0 = group_rows(middle_grad)
    og0 = mm(g0, w_out0, 1, 1)
    per_row0 = jnp.concatenate([out_inv0, dots0], axis=1)
    pg0, in_grad0, out_grad0, tiny0 = backward(0, kept0, g0, og0, per_row0)
    theirs, mine = group_parts(pg0, lambda v: mm(v, w_in0))
    tiny = jnp.stack([tiny0, tiny1]).reshape((CORES, 4, -1, LANES))
    in_all, out_all, tiny, entry_grads = finish_sums(
        in_grad0, out_grad0, in_part1, out_part1, tiny,
        theirs, mine, source, middle_grad, small[0]["norm"][None],
    )
    in_total = jnp.swapaxes(assemble_rows(in_all), 0, 1)[None]
    out_total = out_all.astype(jnp.float32)[None]
    tiny = tiny.reshape(-1)

    boundary = jnp.stack(
        [jnp.where(c == 0, entry_grads[m], result_ways[m]) for m in range(MICRO)]
    ).astype(jnp.float32)[None, :, None]

    totals = []
    at = 0
    for p in params:
        totals.append(tiny[at : at + p.size].reshape(p.shape))
        at += p.size
    norm_total, conv_total, bias_total, dt_total, log_total, skip_total, gain_total = totals
    return (
        boundary,
        norm_total,
        in_total,
        conv_total,
        bias_total,
        dt_total,
        log_total,
        skip_total,
        gain_total,
        out_total,
    )


def solution(mesh):
    fits = mesh.shape["shard"] == GROUP and mesh.shape["rep"] == 4
    return jax.shard_map(
        per_device_split if fits else per_device,
        mesh=mesh,
        in_specs=(
            P("section", None, "rep", "shard", None),
            P(None, "rep", None),
            P(None, "rep", None),
            P("section", "shard"),
            P("section", "shard", None),
            P("section", None, "shard"),
            P("section", "shard"),
            P("section", "shard"),
            P("section", "shard"),
            P("section", "shard"),
            P("section", "shard"),
            P("section", "shard", None),
        ),
        out_specs=(
            P("section", None, "rep", "shard", None),
            P("section", "shard"),
            P("section", "shard", None),
            P("section", None, "shard"),
            P("section", "shard"),
            P("section", "shard"),
            P("section", "shard"),
            P("section", "shard"),
            P("section", "shard"),
            P("section", "shard", None),
        ),
        check_vma=False,
    )
```

```python
import functools

import jax
import jax.numpy as jnp
from jax import lax
from jax.experimental import pallas as pl
from jax.experimental.pallas import tpu as pltpu
from jax.sharding import PartitionSpec as P

D = 1536
P_SIZE = 64
N = 128
KW = 4
BLOCK = 256
MICRO = 2
NSEQ = 4
DI = 3072
H = 48
CONV = 3328


EPSILON = 1e-05
PRECISE = lax.Precision.HIGHEST


def from_behind(shard, axis, by):
    devices = lax.axis_size(axis)
    pairs = [(i, i + by) for i in range(devices) if 0 <= i + by < devices]
    return lax.ppermute(shard, axis, pairs)


def entering(value, axis, join, neutral):
    count, mine = (lax.axis_size(axis), lax.axis_index(axis))
    pieces = jax.tree.map(lambda part: lax.all_gather(part, axis), value)
    subtotal = jax.tree.map(
        lambda part, zero: jnp.full_like(part, 0) + jnp.asarray(zero, part.dtype), value, neutral
    )

    def turn(position, subtotal):
        longer = join(subtotal, jax.tree.map(lambda part: part[position], pieces))
        return jax.tree.map(lambda new, old: jnp.where(position < mine, new, old), longer, subtotal)

    return lax.fori_loop(0, count - 1, turn, subtotal)


def entering_2(shard, axis, join, neutral):
    count = lax.axis_size(axis)
    place = lax.axis_index(axis)
    ahead = count - 1 - place
    gathered = jax.tree.map(
        lambda a, kind: lax.all_gather(a.astype(kind), axis),
        shard,
        jax.tree.map(lambda a: jnp.bfloat16 if a.dtype == jnp.float32 else a.dtype, shard),
    )
    state = jax.tree.map(lambda a, e: jnp.zeros_like(a) + jnp.asarray(e, a.dtype), shard, neutral)

    def one(turn, state):
        source = count - 1 - turn
        return join(
            state,
            jax.tree.map(
                lambda a, own: lax.dynamic_index_in_dim(a, source, 0, False).astype(own.dtype),
                gathered,
                shard,
            ),
        )

    return lax.fori_loop(0, ahead, one, state)


def contract(left, right, left_dim, right_dim):
    return lax.dot_general(
        left, right, (((left_dim,), (right_dim,)), ((), ())), preferred_element_type=jnp.float32
    )


def input_norm(source, gain):
    inv_rms = lax.rsqrt(jnp.mean(source * source, axis=-1, keepdims=True) + EPSILON)
    return source * inv_rms * gain


def block_step(carry_state, pieces):
    x_heads, b_rows, c_rows, log_decay, step_size, segment, before = pieces
    running = jnp.cumsum(log_decay, axis=0)
    places = jnp.arange(x_heads.shape[0])
    linked = (places[:, None] >= places[None, :]) & (segment[:, None] == segment[None, :])
    linked3 = linked[:, :, None]
    gap_sums = jnp.where(linked3, running[:, None, :] - running[None, :, :], 0.0)
    decays = jnp.where(linked3, jnp.exp(gap_sums), 0.0)
    scores = jnp.dot(c_rows, b_rows.T, precision=PRECISE)
    mixing = scores[:, :, None] * decays * step_size[None, :, :]
    inside_part = jnp.einsum("tsh,shp->thp", mixing, x_heads, precision=PRECISE)
    carried = (segment == before).astype(jnp.float32)
    reach = jnp.exp(running) * carried[:, None]
    carried_part = (
        jnp.einsum("tn,hpn->thp", c_rows, carry_state, precision=PRECISE) * reach[:, :, None]
    )
    closing = segment[-1]
    tail_weight = (
        jnp.exp(running[-1][None, :] - running)
        * step_size
        * (segment == closing).astype(jnp.float32)[:, None]
    )
    fresh_state = jnp.einsum("sh,shp,sn->hpn", tail_weight, x_heads, b_rows, precision=PRECISE)
    retained = jnp.exp(running[-1]) * (closing == before).astype(jnp.float32)
    return (retained[:, None, None] * carry_state + fresh_state, inside_part + carried_part)


def conv_inputs(wide_rows, raw_step, conv_weight, conv_bias, dt_bias, a_log, lag_masks):
    rows_here = raw_step.shape[0]
    conv_sum = conv_bias + conv_weight[KW - 1] * wide_rows[KW - 1 :]
    for lag in range(1, KW):
        conv_sum = (
            conv_sum
            + conv_weight[KW - 1 - lag]
            * wide_rows[KW - 1 - lag : KW - 1 - lag + rows_here]
            * lag_masks[lag - 1][:, None]
        )
    active = jax.nn.silu(conv_sum)
    x_heads = active[:, :DI].reshape(rows_here, H, P_SIZE)
    b_rows = active[:, DI : DI + N]
    c_rows = active[:, DI + N :]
    step_size = jax.nn.softplus(raw_step + dt_bias)
    log_decay = -step_size * jnp.exp(a_log)
    return (x_heads, b_rows, c_rows, log_decay, step_size)


def local_scan(x_heads, b_rows, c_rows, log_decay, step_size, segment, befores, seg_before):
    rows_here = x_heads.shape[0]

    def blocks(member):
        return member.reshape((rows_here // BLOCK, BLOCK) + member.shape[1:])

    start_state = jnp.zeros((H, P_SIZE, N), jnp.float32)
    pieces = (
        blocks(x_heads),
        blocks(b_rows),
        blocks(c_rows),
        blocks(log_decay),
        blocks(step_size),
        blocks(segment),
        befores,
    )
    end_state, mixer_out = lax.scan(jax.checkpoint(block_step), start_state, pieces)
    retained = jnp.exp(jnp.sum(log_decay, axis=0)) * (segment[-1] == seg_before).astype(jnp.float32)
    return (mixer_out.reshape(rows_here, H, P_SIZE), end_state, retained)


def state_entry(c_rows, log_decay, state_in, carried):
    reach = jnp.exp(jnp.cumsum(log_decay, axis=0)) * carried[:, None]
    return jnp.einsum("tn,hpn->thp", c_rows, state_in, precision=PRECISE) * reach[:, :, None]


def gate_norm(mixer_out, x_heads, d_skip, gate_part, out_gain):
    rows_here = x_heads.shape[0]
    total_out = mixer_out + d_skip[:, None] * x_heads
    gated = total_out.reshape(rows_here, DI) * jax.nn.silu(gate_part)
    inv_gated = lax.rsqrt(jnp.mean(gated * gated, axis=-1, keepdims=True) + EPSILON)
    return gated * inv_gated * out_gain


def carry_forward(earlier, later):
    return (earlier[0] * later[0], later[0][:, None, None] * earlier[1] + later[1])


def carry_backward(earlier, later):
    return (later[0] * earlier[0], later[1] + later[0][:, None, None] * earlier[1])


def segment_marks(lengths, seq_order, micro_slot, row_start, rows_here):
    micro_slot = jnp.clip(micro_slot, 0, MICRO - 1)
    seq_lengths = lax.dynamic_index_in_dim(lengths[:, 0], micro_slot, 0, keepdims=False)
    row_order = lax.dynamic_index_in_dim(seq_order[:, 0], micro_slot, 0, keepdims=False)
    picks = (row_order[:, None] == jnp.arange(NSEQ, dtype=jnp.int32)[None, :]).astype(jnp.int32)
    placed = jnp.sum(picks * seq_lengths[None, :], axis=1)
    finish = jnp.cumsum(placed, dtype=jnp.int32)
    positions = row_start + jnp.arange(-(KW - 1), rows_here, dtype=jnp.int32)
    extended = jnp.sum((positions[:, None] >= finish[None, :]).astype(jnp.int32), axis=1)
    extended = jnp.where(positions < 0, -1, extended)
    segment = extended[KW - 1 :]
    seg_before = extended[KW - 2]
    lag_masks = jnp.stack(
        [
            (extended[KW - 1 - lag : KW - 1 - lag + rows_here] == segment).astype(jnp.float32)
            for lag in range(1, KW)
        ]
    )
    befores = jnp.concatenate([seg_before[None], segment[:-1]])[::BLOCK]
    carried = (segment == seg_before).astype(jnp.float32)
    return (segment, lag_masks, befores, seg_before, carried)


def mixer_pass(projected, weights, marks):
    norm_gain, in_weight, conv_weight, conv_bias, dt_bias, a_log, d_skip, out_gain, out_weight = (
        weights
    )
    segment, lag_masks, befores, seg_before, carried = marks
    rows_here = projected.shape[0]
    gate_part = projected[:, :DI].astype(jnp.float32)
    mixed_part = projected[:, DI : DI + CONV]
    raw_step = projected[:, DI + CONV :].astype(jnp.float32)
    rim_rows = from_behind(mixed_part[rows_here - (KW - 1) :], "shard", 1)
    wide_rows = jnp.concatenate([rim_rows, mixed_part], axis=0).astype(jnp.float32)

    def conv_section(wide_rows, raw_step, conv_weight, conv_bias, dt_bias, a_log):
        return conv_inputs(wide_rows, raw_step, conv_weight, conv_bias, dt_bias, a_log, lag_masks)

    conv_outs, conv_pull = jax.vjp(
        conv_section, wide_rows, raw_step, conv_weight, conv_bias, dt_bias, a_log
    )
    x_heads, b_rows, c_rows, log_decay, step_size = conv_outs

    def scan_section(x_heads, b_rows, c_rows, log_decay, step_size):
        return local_scan(
            x_heads, b_rows, c_rows, log_decay, step_size, segment, befores, seg_before
        )

    scan_outs, scan_pull = jax.vjp(scan_section, x_heads, b_rows, c_rows, log_decay, step_size)
    local_out, end_state, retained = scan_outs
    identity = (jnp.ones((H,), jnp.float32), jnp.zeros((H, P_SIZE, N), jnp.float32))
    prefix = entering((retained, end_state), "shard", carry_forward, identity)
    state_in = prefix[1]

    def entry_section(c_rows, log_decay, state_in):
        return state_entry(c_rows, log_decay, state_in, carried)

    entered, entry_pull = jax.vjp(entry_section, c_rows, log_decay, state_in)
    mixer_out = local_out + entered
    outgoing, norm_pull = jax.vjp(gate_norm, mixer_out, x_heads, d_skip, gate_part, out_gain)
    return (
        outgoing.astype(jnp.bfloat16),
        (conv_pull, scan_pull, entry_pull, norm_pull, retained, state_in),
    )


def mamba_forward(source, weights, marks):
    normed = input_norm(source, weights[0]).astype(jnp.bfloat16)
    projected = jnp.dot(normed, weights[1], preferred_element_type=jnp.float32).astype(jnp.bfloat16)
    outgoing, unused_pulls = mixer_pass(projected, weights, marks)
    return source + jnp.dot(outgoing, weights[8], preferred_element_type=jnp.float32)


def mamba_backward(source, incoming, weights, marks):
    norm_gain, in_weight, conv_weight, conv_bias, dt_bias, a_log, d_skip, out_gain, out_weight = (
        weights
    )
    rows_here = source.shape[0]
    normed, front_pull = jax.vjp(input_norm, source, norm_gain)
    normed_low = normed.astype(jnp.bfloat16)
    projected = jnp.dot(normed_low, in_weight, preferred_element_type=jnp.float32).astype(
        jnp.bfloat16
    )
    outgoing, pulls = mixer_pass(projected, weights, marks)
    conv_pull, scan_pull, entry_pull, norm_pull, retained, state_in = pulls
    incoming_low = incoming.astype(jnp.bfloat16)
    out_weight_grad = contract(outgoing, incoming_low, 0, 0)
    outgoing_grad = contract(incoming_low, out_weight, 1, 1)
    mixer_grad, x_grad_a, d_skip_grad, gate_grad, out_gain_grad = norm_pull(outgoing_grad)
    c_grad_a, decay_grad_a, direct = entry_pull(mixer_grad)
    identity = (jnp.ones((H,), jnp.float32), jnp.zeros((H, P_SIZE, N), jnp.float32))
    suffix = entering_2((retained, direct), "shard", carry_backward, identity)
    later_grad = suffix[1]
    retained_grad = jnp.sum(later_grad * state_in, axis=(1, 2))
    x_grad_b, b_grad, c_grad_b, decay_grad_b, step_grad = scan_pull(
        (mixer_grad, later_grad, retained_grad)
    )
    conv_grads = conv_pull(
        (x_grad_a + x_grad_b, b_grad, c_grad_a + c_grad_b, decay_grad_a + decay_grad_b, step_grad)
    )
    wide_grad, raw_grad, conv_weight_grad, conv_bias_grad, dt_bias_grad, a_log_grad = conv_grads
    back_rows = from_behind(wide_grad[: KW - 1].astype(jnp.bfloat16), "shard", -1).astype(
        jnp.float32
    )
    filler = jnp.zeros((rows_here - (KW - 1), CONV), jnp.float32)
    mixed_grad = wide_grad[KW - 1 :] + jnp.concatenate([filler, back_rows], axis=0)
    projected_grad = jnp.concatenate([gate_grad, mixed_grad, raw_grad], axis=1).astype(jnp.bfloat16)
    in_weight_grad = contract(normed_low, projected_grad, 0, 0)
    normed_grad = contract(projected_grad, in_weight, 1, 1)
    source_grad, norm_gain_grad = front_pull(normed_grad)
    weight_grads = (
        norm_gain_grad,
        in_weight_grad,
        conv_weight_grad,
        conv_bias_grad,
        dt_bias_grad,
        a_log_grad,
        d_skip_grad,
        out_gain_grad,
        out_weight_grad,
    )
    return (incoming + source_grad, weight_grads)


def per_device(
    boundary_in,
    lengths,
    seq_order,
    norm_gain,
    in_weight,
    conv_weight,
    conv_bias,
    dt_bias,
    a_log,
    d_skip,
    out_gain,
    out_weight,
):
    section_index = lax.axis_index("section")
    is_first = section_index == 0
    rows_here = boundary_in.shape[3]
    row_start = lax.axis_index("shard") * rows_here

    def current():
        whole = (
            lax.all_gather(norm_gain, "shard", axis=1, tiled=True),
            lax.all_gather(in_weight, "shard", axis=1, tiled=True),
            lax.all_gather(conv_weight, "shard", axis=2, tiled=True),
            lax.all_gather(conv_bias, "shard", axis=1, tiled=True),
            lax.all_gather(dt_bias, "shard", axis=1, tiled=True),
            lax.all_gather(a_log, "shard", axis=1, tiled=True),
            lax.all_gather(d_skip, "shard", axis=1, tiled=True),
            lax.all_gather(out_gain, "shard", axis=1, tiled=True),
            lax.all_gather(out_weight, "shard", axis=1, tiled=True),
        )
        return tuple(
            (
                member[0] if slot_index in (1, 8) else member[0].astype(jnp.float32)
                for slot_index, member in enumerate(whole)
            )
        )

    source_rows = boundary_in[0, :, 0]
    arrived = jnp.zeros((rows_here, D), jnp.bfloat16)
    inputs = []
    results = []
    for step_index in range(MICRO + 1):
        own_rows = source_rows[min(step_index, MICRO - 1)]
        layer_in = jnp.where(is_first, own_rows, arrived)
        inputs.append(layer_in)
        marks = segment_marks(lengths, seq_order, step_index - section_index, row_start, rows_here)
        layer_out = mamba_forward(layer_in.astype(jnp.float32), current(), marks)
        results.append(layer_out)
        if step_index < MICRO:
            arrived = from_behind(layer_out.astype(jnp.bfloat16), "section", 1)
    returned = jnp.zeros((rows_here, D), jnp.bfloat16)
    totals = None
    source_grads = []
    for step_index in range(MICRO + 1):
        micro_slot = step_index - 1 + section_index
        is_valid = (micro_slot >= 0) & (micro_slot < MICRO)
        own_rows = source_rows[min(step_index, MICRO - 1)]
        incoming = jnp.where(is_first, returned, own_rows).astype(jnp.float32)
        incoming = jnp.where(is_valid, incoming, 0.0)
        layer_in = jnp.where(
            is_first, inputs[max(step_index - 1, 0)], inputs[min(step_index + 1, MICRO)]
        )
        marks = segment_marks(lengths, seq_order, micro_slot, row_start, rows_here)
        source_grad, weight_grads = mamba_backward(
            layer_in.astype(jnp.float32), incoming, current(), marks
        )
        if totals is None:
            totals = tuple(weight_grads)
        else:
            totals = tuple((earlier + added for earlier, added in zip(totals, weight_grads)))
        source_grads.append(source_grad)
        if step_index < MICRO:
            returned = from_behind(source_grad.astype(jnp.bfloat16), "section", -1)
    boundary = jnp.stack(
        [
            jnp.where(is_first, source_grads[micro_pos + 1], results[micro_pos + 1])
            for micro_pos in range(MICRO)
        ]
    )[None, :, None]
    shares = (
        lax.psum_scatter(
            totals[0][None].astype(jnp.bfloat16), "shard", scatter_dimension=1, tiled=True
        ).astype(jnp.float32),
        lax.psum_scatter(
            totals[1][None].astype(jnp.bfloat16), "shard", scatter_dimension=1, tiled=True
        ).astype(jnp.float32),
        lax.psum_scatter(
            totals[2][None].astype(jnp.bfloat16), "shard", scatter_dimension=2, tiled=True
        ).astype(jnp.float32),
        lax.psum_scatter(
            totals[3][None].astype(jnp.bfloat16), "shard", scatter_dimension=1, tiled=True
        ).astype(jnp.float32),
        lax.psum_scatter(
            totals[4][None].astype(jnp.bfloat16), "shard", scatter_dimension=1, tiled=True
        ).astype(jnp.float32),
        lax.psum_scatter(
            totals[5][None].astype(jnp.bfloat16), "shard", scatter_dimension=1, tiled=True
        ).astype(jnp.float32),
        lax.psum_scatter(
            totals[6][None].astype(jnp.bfloat16), "shard", scatter_dimension=1, tiled=True
        ).astype(jnp.float32),
        lax.psum_scatter(
            totals[7][None].astype(jnp.bfloat16), "shard", scatter_dimension=1, tiled=True
        ).astype(jnp.float32),
        lax.psum_scatter(
            totals[8][None].astype(jnp.bfloat16), "shard", scatter_dimension=1, tiled=True
        ).astype(jnp.float32),
    )
    reduced = (
        lax.psum(shares[0].astype(jnp.bfloat16), "rep").astype(jnp.float32),
        lax.psum(shares[1].astype(jnp.bfloat16), "rep").astype(jnp.float32),
        lax.psum(shares[2].astype(jnp.bfloat16), "rep").astype(jnp.float32),
        lax.psum(shares[3].astype(jnp.bfloat16), "rep").astype(jnp.float32),
        lax.psum(shares[4].astype(jnp.bfloat16), "rep").astype(jnp.float32),
        lax.psum(shares[5].astype(jnp.bfloat16), "rep").astype(jnp.float32),
        lax.psum(shares[6].astype(jnp.bfloat16), "rep").astype(jnp.float32),
        lax.psum(shares[7].astype(jnp.bfloat16), "rep").astype(jnp.float32),
        lax.psum(shares[8].astype(jnp.bfloat16), "rep").astype(jnp.float32),
    )
    return (boundary,) + tuple(reduced)


Q = 128
LANES = 128
VMEM_BYTES = 56 * 1024 * 1024
EXACT = lax.Precision.HIGHEST


def mm(a, b, da=1, db=0):
    return lax.dot_general(
        a, b, (((da,), (db,)), ((), ())), preferred_element_type=jnp.float32
    )


def exact(a, b):
    return jnp.dot(a, b, precision=EXACT, preferred_element_type=jnp.float32)


def low(v):
    return v.astype(jnp.bfloat16)


def split(v, parts):
    found = []
    for _ in range(parts):
        found.append(low(v))
        v = v - found[-1].astype(jnp.float32)
    return found


def pick_sums(v, ones, parts=2):
    return sum(mm(part, ones) for part in split(v, parts))


def sums_of(ones, v, parts=3):
    return sum(mm(ones, part) for part in split(v, parts))


def iota(shape, dim):
    return lax.broadcasted_iota(jnp.int32, shape, dim)


def pair_cols(v, p):
    rows = v.shape[0]
    left = jnp.broadcast_to(v[:, 2 * p : 2 * p + 1], (rows, LANES))
    right = jnp.broadcast_to(v[:, 2 * p + 1 : 2 * p + 2], (rows, LANES))
    return jnp.where(iota((rows, LANES), 1) < LANES // 2, left, right)


def widen(v, pairs):
    return jnp.concatenate([pair_cols(v, p) for p in range(pairs)], axis=1)


def stack_pair(v, p):
    block = v[:, p * LANES : (p + 1) * LANES]
    left = iota(block.shape, 1) < LANES // 2
    zero = jnp.zeros_like(block)
    return jnp.concatenate([jnp.where(left, block, zero), jnp.where(left, zero, block)], axis=0)


def softplus(v):
    small = jnp.exp(-jnp.abs(v))
    series = small * (1 + small * (-1 / 2 + small * (1 / 3 + small * (-1 / 4 + small / 5))))
    return jnp.maximum(v, 0.0) + jnp.where(small < 0.01, series, jnp.log(1 + small))


def sigmoid(v):
    return 1.0 / (1.0 + jnp.exp(-v))


def head_picks():
    quarter = 2 * lax.rem(lax.axis_index("rep"), 2) + lax.axis_index("section")
    given, local = iota((64, LANES), 0), iota((64, LANES), 1)
    per = H // 16
    taken = (lax.rem(lax.div(given, per), 4) == quarter) & (given < H)
    taken = taken & (local == lax.div(given, 4 * per) * per + lax.rem(given, per))
    return jnp.where(taken, 1.0, 0.0).astype(jnp.bfloat16)


def chunk_parts(width, proj, before8, marks, seg_row, small_ref, pick):
    conv_w = small_ref[0, 0:KW]
    conv_b = small_ref[0, KW : KW + 1]
    dt_bias = small_ref[0, 7:8, :LANES]
    rate = small_ref[0, 8:9, :LANES]
    span = width + 2 * LANES
    gate = proj[:, :width].astype(jnp.float32)
    mixed = proj[:, width : width + span].astype(jnp.float32)
    raw = mm(proj[:, width + span :], pick)
    shifts = [mixed]
    top = iota((8, span), 0)
    for lag in range(1, KW):
        rolled = pltpu.roll(mixed, lag, 0)
        head = jnp.where(top < lag, pltpu.roll(before8, lag, 0), rolled[:8])
        moved = jnp.concatenate([head, rolled[8:]], axis=0)
        shifts.append(moved * marks[:, lag - 1 : lag])
    conv = conv_b
    for lag in range(KW):
        conv = conv + conv_w[KW - 1 - lag : KW - lag] * shifts[lag]
    sig = sigmoid(conv)
    active = conv * sig
    stepped = raw + dt_bias
    step = softplus(stepped)
    decay = -step * rate
    lower = iota((Q, Q), 0) >= iota((Q, Q), 1)
    total = sums_of(jnp.where(lower, 1.0, 0.0).astype(jnp.bfloat16), decay)
    linked = lower & (marks[:, 5:6] == seg_row)
    shut = jnp.where(linked, 0.0, -1e30)
    reach = jnp.exp(total) * marks[:, 3:4]
    tail = jnp.exp(total[Q - 1 : Q] - total) * marks[:, 4:5]
    return gate, mixed, shifts, conv, sig, active, stepped, step, decay, total, shut, reach, tail


def forward_kernel(
    width, proj_ref, marks_ref, seg_ref, small_ref, gg_ref, squares_ref, mixer_ref, starts_ref, state, before,
):
    pairs = width // LANES

    @pl.when(pl.program_id(0) == 0)
    def _():
        state[...] = jnp.zeros_like(state)
        before[...] = jnp.zeros_like(before)

    gate, mixed, _, _, _, active, _, step, _, total, shut, reach, tail = chunk_parts(
        width, proj_ref[...], before[...], marks_ref[...], seg_ref[...], small_ref, head_picks()
    )
    skip, gain = small_ref[0, 6:7, :width], small_ref[0, 5:6, :width]
    before[...] = mixed[Q - 8 :]
    heads = active[:, :width]
    b_low = low(active[:, width : width + LANES])
    c_low = low(active[:, width + LANES :])
    entry = state[...]
    starts_ref[0] = entry
    scores = mm(c_low, b_low, 1, 1)
    total_t = total.T
    scaled = heads * widen(step, pairs)
    scaled_low = low(scaled)
    inside = []
    for p in range(pairs):
        both = []
        for h in (2 * p, 2 * p + 1):
            both.append(low(jnp.exp(total[:, h : h + 1] - total_t[h : h + 1] + shut) * scores))
        inside.append(mm(jnp.concatenate(both, axis=1), stack_pair(scaled_low, p)))
    mixer = jnp.concatenate(inside, axis=1) + widen(reach, pairs) * mm(c_low, low(entry))
    b_turned = low(active[:, width : width + LANES].T)
    state[...] = entry * widen(reach[Q - 1 : Q], pairs) + mm(
        b_turned, low(scaled * widen(tail, pairs))
    )
    out = mixer + skip * heads
    mixer_ref[...] = out
    gated = out * (gate * sigmoid(gate))
    squares_ref[...] = jnp.sum(gated * gated, axis=1, keepdims=True)
    gg_ref[...] = low(gated * gain)


def gate_kernel(width, whole_width, proj_ref, small_ref, out_ref, og_ref, rows_ref, gate_grad_ref, out_grad_ref, sums_ref):
    @pl.when(pl.program_id(0) == 0)
    def _():
        sums_ref[...] = jnp.zeros_like(sums_ref)

    gate = proj_ref[...].astype(jnp.float32)
    inv = rows_ref[:, 0:1]
    dots = rows_ref[:, 1:2]
    og = og_ref[...]
    out = out_ref[...]
    gate_sig = sigmoid(gate)
    gate_on = gate * gate_sig
    hat = out * gate_on * inv
    gated_grad = inv * (small_ref[0, 5:6, :width] * og - hat * (dots * (1.0 / whole_width)))
    out_grad_ref[...] = low(gated_grad * gate_on)
    gate_grad_ref[...] = low(gated_grad * out * (gate_sig * (1.0 + gate * (1.0 - gate_sig))))
    sums_ref[0:1] += jnp.sum(hat * og, axis=0, keepdims=True)


def gate_backward(layer, projected, small, out, og, per_row, whole_width):
    rows, width = out.shape
    step = 2 * Q

    def by_row(count):
        return pl.BlockSpec((step, count), lambda i: (i, 0))

    half = jax.ShapeDtypeStruct((rows, width), jnp.bfloat16)
    return pl.pallas_call(
        functools.partial(gate_kernel, width, whole_width),
        grid=(rows // step,),
        in_specs=[by_row(width), small_spec(layer), by_row(width), by_row(width), by_row(2)],
        out_specs=[by_row(width), by_row(width), full_spec((8, width))],
        out_shape=[half, half, jax.ShapeDtypeStruct((8, width), jnp.float32)],
        compiler_params=pltpu.CompilerParams(vmem_limit_bytes=VMEM_BYTES),
        cost_estimate=cost(6),
        name="gate_backward",
    )(projected, small, out, og, per_row)


def backward_kernel(
    width, proj_ref, rim_ref, marks_ref, seg_ref, small_ref, out_ref, starts_ref, out_grad_ref,
    gate_grad_ref, pg_ref, conv_ref, head_ref, later, after, skips,
):
    pairs = width // LANES
    turn = pl.program_id(0)
    chunk = pl.num_programs(0) - 1 - turn

    @pl.when(turn == 0)
    def _():
        later[...] = jnp.zeros_like(later)
        after[...] = jnp.zeros_like(after)
        skips[...] = jnp.zeros_like(skips)
        conv_ref[...] = jnp.zeros_like(conv_ref)
        head_ref[...] = jnp.zeros_like(head_ref)

    span = width + 2 * LANES
    marks = marks_ref[...]
    rim = rim_ref[...][8:, width : width + span].astype(jnp.float32)
    rim = jnp.where(chunk > 0, rim, 0.0)
    pick = head_picks()
    skip, rate = small_ref[0, 6:7, :width], small_ref[0, 8:9, :LANES]
    _, mixed, shifts, conv, sig, active, stepped, step, decay, total, shut, reach, tail = (
        chunk_parts(
            width, proj_ref[...], rim, marks, seg_ref[...], small_ref, pick
        )
    )
    heads = active[:, :width]
    b_low = low(active[:, width : width + LANES])
    c_low = low(active[:, width + LANES :])

    grad_low = out_grad_ref[...]
    out_grad = grad_low.astype(jnp.float32)
    mixer = out_ref[...] - skip * heads

    entry = starts_ref[0]
    entry_low = low(entry)
    late = later[...]
    late_low = low(late)
    scores = mm(c_low, b_low, 1, 1)
    total_t = total.T
    step_wide = widen(step, pairs)
    scaled = heads * step_wide
    scaled_low = low(scaled)
    from_late = widen(tail, pairs) * mm(b_low, late_low)
    inside = []
    score_grad = jnp.zeros((Q, Q), jnp.float32)
    for p in range(pairs):
        gains = []
        both = []
        for h in (2 * p, 2 * p + 1):
            gain = jnp.exp(total[:, h : h + 1] - total_t[h : h + 1] + shut)
            gains.append(gain)
            both.append(low(gain * scores))
        stacked = stack_pair(grad_low, p)
        inside.append(mm(jnp.concatenate(both, axis=0), stacked, 0, 0))
        mix_grad = mm(stacked, scaled_low[:, p * LANES : (p + 1) * LANES], 1, 1)
        score_grad = score_grad + gains[0] * mix_grad[:Q] + gains[1] * mix_grad[Q:]
    scaled_grad = jnp.concatenate(inside, axis=1) + from_late
    reached = low(widen(reach, pairs) * out_grad)
    score_low = low(score_grad)
    c_grad = mm(score_low, b_low) + mm(reached, entry_low, 1, 1)
    b_grad = mm(score_low, c_low, 0, 0) + mm(low(scaled * widen(tail, pairs)), late_low, 1, 1)
    kept = widen(reach[Q - 1 : Q], pairs)
    later[...] = late * kept + mm(c_low, reached, 0, 0)

    scaled_seen = scaled_low.astype(jnp.float32)
    balance = out_grad * mixer - scaled_seen * scaled_grad
    closing = jnp.sum(scaled_seen * from_late, axis=0, keepdims=True) + kept * jnp.sum(
        late * entry, axis=0, keepdims=True
    )
    picks = iota((width, LANES), 0) // (LANES // 2) == iota((width, LANES), 1)
    picks = jnp.where(picks, 1.0, 0.0).astype(jnp.bfloat16)
    sums = pick_sums(
        jnp.concatenate([balance, heads * scaled_grad, jnp.broadcast_to(closing, (8, width))], 0),
        picks,
    )
    upper = jnp.where(iota((Q, Q), 0) <= iota((Q, Q), 1), 1.0, 0.0).astype(jnp.bfloat16)
    decay_grad = sums_of(upper, sums[:Q]) + sums[2 * Q : 2 * Q + 1]
    step_grad = sums[Q : 2 * Q] - decay_grad * rate
    raw_grad = step_grad * sigmoid(stepped)

    head_grad = step_wide * scaled_grad + skip * out_grad
    conv_grad = jnp.concatenate([head_grad, b_grad, c_grad], axis=1) * (
        sig * (1.0 + conv * (1.0 - sig))
    )
    mixed_grad = small_ref[0, KW - 1 : KW] * conv_grad
    bottom = iota((8, span), 0)
    for lag in range(1, KW):
        sent = conv_grad * marks[:, lag - 1 : lag]
        rolled = pltpu.roll(sent, Q - lag, 0)
        ending = jnp.where(
            bottom >= 8 - lag, pltpu.roll(after[lag - 1], 8 - lag, 0), rolled[Q - 8 :]
        )
        mixed_grad = mixed_grad + small_ref[0, KW - 1 - lag : KW - lag] * jnp.concatenate(
            [rolled[: Q - 8], ending], axis=0
        )
        after[lag - 1] = sent[:8]
    pg_ref[:, :width] = gate_grad_ref[...]
    pg_ref[:, width:] = low(
        jnp.concatenate([mixed_grad, mm(low(raw_grad), pick, 1, 1)], axis=1)
    )

    skips[0:1] += jnp.sum(out_grad * heads, axis=0, keepdims=True)
    for lag in range(KW):
        conv_ref[KW - 1 - lag : KW - lag] += jnp.sum(
            conv_grad * shifts[lag], axis=0, keepdims=True
        )
    conv_ref[KW : KW + 1] += jnp.sum(conv_grad, axis=0, keepdims=True)
    head_ref[0:1] += jnp.sum(raw_grad, axis=0, keepdims=True)
    head_ref[1:2] += jnp.sum(decay_grad * decay, axis=0, keepdims=True)

    @pl.when(chunk == 0)
    def _():
        head_ref[2:3] = pick_sums(skips[...], picks, 3)[0:1]


def cost(micros):
    return pl.CostEstimate(flops=micros * 1_100_000_000, bytes_accessed=0, transcendentals=0)


def small_spec(layer):
    return pl.BlockSpec((1, 16, 2 * D // 3), lambda i: (layer, 0, 0))


def full_spec(shape):
    return pl.BlockSpec(shape, lambda i: (0,) * len(shape))


def product_kernel(place_ref, left_ref, weight_ref, theirs_ref, mine_ref):
    turn = pl.program_id(0)
    found = mm(left_ref[...], weight_ref[...])

    @pl.when(turn < 2)
    def _():
        theirs_ref[...] = low(found)

    @pl.when(turn >= 2)
    def _():
        mine_ref[...] = found


def group_parts(c, left, weight):
    rows, depth = left.shape
    block, columns = rows // 4, weight.shape[1]

    def left_at(i, at):
        return (2 * lax.rem(i, 2) + jnp.where(i < 2, 1 - at[0], at[0]), 0)

    return pl.pallas_call(
        product_kernel,
        grid_spec=pltpu.PrefetchScalarGridSpec(
            num_scalar_prefetch=1,
            grid=(4,),
            in_specs=[
                pl.BlockSpec((block, depth), left_at),
                pl.BlockSpec((depth, columns), lambda i, at: (0, 0)),
            ],
            out_specs=[
                pl.BlockSpec((block, columns), lambda i, at: (jnp.minimum(i, 1), 0)),
                pl.BlockSpec((block, columns), lambda i, at: (jnp.maximum(i - 2, 0), 0)),
            ],
        ),
        out_shape=[
            jax.ShapeDtypeStruct((2 * block, columns), jnp.bfloat16),
            jax.ShapeDtypeStruct((2 * block, columns), jnp.float32),
        ],
        compiler_params=pltpu.CompilerParams(vmem_limit_bytes=VMEM_BYTES),
        cost_estimate=cost(6),
        name="group_parts",
    )(c.reshape((1,)), left, weight)


def projection_kernel(left_ref, weight_ref, out_ref):
    out_ref[...] = low(mm(left_ref[...], weight_ref[...], 1, 1))


def projection(left, weight):
    rows, depth = left.shape
    block, columns = rows // 4, weight.shape[0]
    return pl.pallas_call(
        projection_kernel,
        grid=(4,),
        in_specs=[
            pl.BlockSpec((block, depth), lambda i: (i, 0)),
            pl.BlockSpec((columns, depth), lambda i: (0, 0)),
        ],
        out_specs=pl.BlockSpec((block, columns), lambda i: (i, 0)),
        out_shape=jax.ShapeDtypeStruct((rows, columns), jnp.bfloat16),
        compiler_params=pltpu.CompilerParams(vmem_limit_bytes=VMEM_BYTES),
        cost_estimate=cost(6),
        name="projection",
    )(left, weight)


def mixer_forward(layer, projected, marks, seg_row, small):
    rows, columns = projected.shape
    width = DI // 4
    chunks = rows // Q
    span = width + 2 * LANES

    def by_row(count):
        return pl.BlockSpec((Q, count), lambda i: (i, 0))

    return pl.pallas_call(
        functools.partial(forward_kernel, width),
        grid=(chunks,),
        in_specs=[
            by_row(columns), by_row(8), pl.BlockSpec((1, Q), lambda i: (0, i)), small_spec(layer),
        ],
        out_specs=[
            by_row(width),
            by_row(1),
            by_row(width),
            pl.BlockSpec((1, LANES, width), lambda i: (i, 0, 0)),
        ],
        out_shape=[
            jax.ShapeDtypeStruct((rows, width), jnp.bfloat16),
            jax.ShapeDtypeStruct((rows, 1), jnp.float32),
            jax.ShapeDtypeStruct((rows, width), jnp.float32),
            jax.ShapeDtypeStruct((chunks, LANES, width), jnp.float32),
        ],
        scratch_shapes=[
            pltpu.VMEM((LANES, width), jnp.float32),
            pltpu.VMEM((8, span), jnp.float32),
        ],
        compiler_params=pltpu.CompilerParams(vmem_limit_bytes=VMEM_BYTES),
        cost_estimate=cost(16),
        name="mixer_forward",
    )(projected, marks, seg_row, small)


def mixer_backward(layer, projected, marks, seg_row, small, out, starts, out_grad, gate_grad):
    rows, columns = projected.shape
    width = out.shape[1]
    chunks = rows // Q
    span = width + 2 * LANES

    def by_row(count):
        return pl.BlockSpec((Q, count), lambda i: (chunks - 1 - i, 0))

    rim = pl.BlockSpec(
        (16, columns), lambda i: (jnp.maximum((chunks - 1 - i) * (Q // 16) - 1, 0), 0)
    )
    return pl.pallas_call(
        functools.partial(backward_kernel, width),
        grid=(chunks,),
        in_specs=[
            by_row(columns),
            rim,
            by_row(8),
            pl.BlockSpec((1, Q), lambda i: (0, chunks - 1 - i)),
            small_spec(layer),
            by_row(width),
            pl.BlockSpec((1, LANES, width), lambda i: (chunks - 1 - i, 0, 0)),
            by_row(width),
            by_row(width),
        ],
        out_specs=[
            by_row(columns),
            full_spec((8, span)),
            full_spec((8, LANES)),
        ],
        out_shape=[
            jax.ShapeDtypeStruct((rows, columns), jnp.bfloat16),
            jax.ShapeDtypeStruct((8, span), jnp.float32),
            jax.ShapeDtypeStruct((8, LANES), jnp.float32),
        ],
        scratch_shapes=[
            pltpu.VMEM((LANES, width), jnp.float32),
            pltpu.VMEM((KW - 1, 8, span), jnp.float32),
            pltpu.VMEM((8, width), jnp.float32),
        ],
        compiler_params=pltpu.CompilerParams(vmem_limit_bytes=VMEM_BYTES),
        cost_estimate=cost(33),
        name="mixer_backward",
    )(projected, projected, marks, seg_row, small, out, starts, out_grad, gate_grad)


CORES = 2
GROUP = 4
SHARED = CONV - DI + H
LOCAL = 2 * DI // GROUP + SHARED + 16
HALF = LOCAL // 2
CHUNKS = 2
LANE_PART = D // 4
OUT_PART = DI // 16
UNITS = CHUNKS + 1
GATE = DI // GROUP
GATE_HALF = GATE // 2
REST_HALF = HALF - GATE_HALF
STEPS = ((0, 192), (192, 192), (0, 272), (272, 272))


def place():
    c, z, r = (lax.axis_index(name) for name in ("section", "shard", "rep"))
    return c, z, lax.div(r, 2), lax.rem(r, 2)


def weight_pieces(quarter):
    part = DI // 16
    found = []
    for side in range(2):
        for zz in range(4):
            found.append(
                (side * 4 * part + zz * part, side * DI + zz * 4 * part + quarter * part, part)
            )
    found.append((8 * part, 2 * DI, SHARED))
    return found


def mesh_copy(source, target, send, recv, device):
    return pltpu.make_async_remote_copy(
        src_ref=source, dst_ref=target, send_sem=send, recv_sem=recv,
        device_id=device, device_id_type=pl.DeviceIdType.MESH,
    )


def greet(barrier, device):
    pl.semaphore_signal(barrier, inc=1, device_id=device, device_id_type=pl.DeviceIdType.MESH)


def rows_at(start, count):
    return pl.ds(pl.multiple_of(start, 16), count)


class WeightGather:
    def __init__(self, layer, in_ref, out_ref, w_ref, wo_ref, sems):
        self.layer, self.in_ref, self.out_ref = layer, in_ref, out_ref
        self.w_ref, self.wo_ref = w_ref, wo_ref
        (
            self.local_sem, self.core_send, self.core_recv, self.right_send, self.left_send,
            self.z_recv, self.y_send, self.y_recv,
        ) = sems
        self.c, self.z, self.y, self.x = place()
        self.core = {"section": 1 - self.c}
        self.y_other = {"rep": (1 - self.y) * 2 + self.x}

    def own_pieces(self, quarter):
        lanes = pl.ds(pl.multiple_of(self.z * LANE_PART, LANES), LANE_PART)
        found = []
        for at, start, count in weight_pieces(quarter):
            found.append((self.in_ref.at[rows_at(start, count)], self.w_ref.at[pl.ds(at, count), lanes]))
        found.append(
            (
                self.out_ref.at[rows_at(quarter * OUT_PART, OUT_PART)],
                self.wo_ref.at[rows_at(self.z * OUT_PART, OUT_PART)],
            )
        )
        return found

    def local_copies(self):
        return [
            pltpu.make_async_copy(source, target, self.local_sem.at[i])
            for i, (source, target) in enumerate(self.own_pieces(2 * self.x + self.c))
        ]

    def core_copies(self):
        return [
            mesh_copy(source, target, self.core_send.at[i], self.core_recv.at[i], self.core)
            for i, (source, target) in enumerate(self.own_pieces(2 * self.x + 1 - self.c))
        ]

    def begin(self):
        lanes = pl.ds(pl.multiple_of(self.z * LANE_PART, LANES), LANE_PART)
        self.w_ref[LOCAL - 16 :, lanes] = jnp.zeros((16, LANE_PART), self.w_ref.dtype)

        @pl.when(self.c == self.layer)
        def _():
            for copy in self.core_copies():
                copy.start()
            for copy in self.local_copies():
                copy.start()
            for copy in self.local_copies():
                copy.wait()

        @pl.when(self.c != self.layer)
        def _():
            for copy in self.core_copies():
                copy.wait_recv()

    def slab(self, unit, shard, side):
        if unit == CHUNKS:
            return self.wo_ref.at[rows_at(shard * OUT_PART + side * (OUT_PART // 2), OUT_PART // 2)]
        return self.w_ref.at[
            rows_at(side * HALF + unit * (HALF // CHUNKS), HALF // CHUNKS),
            pl.ds(pl.multiple_of(shard * LANE_PART, LANES), LANE_PART),
        ]

    def z_copy(self, unit, shard, step, k):
        piece = self.slab(unit, shard, self.y)
        send = (self.right_send if step > 0 else self.left_send).at[unit, k]
        return mesh_copy(piece, piece, send, self.z_recv.at[unit, shard], {"shard": self.z + step})

    def y_copy(self, unit, shard, side):
        piece = self.slab(unit, shard, side)
        return mesh_copy(
            piece, piece, self.y_send.at[unit, shard], self.y_recv.at[unit, shard], self.y_other
        )

    def cases(self, step, k):
        shard = self.z - k * step
        there = (shard >= 0) if step > 0 else (shard <= 3)
        more = (self.z < 3) if step > 0 else (self.z > 0)
        return shard, there, more

    def first(self, unit):
        for step in (1, -1):
            _, _, more = self.cases(step, 0)

            @pl.when(more)
            def _():
                self.z_copy(unit, self.z, step, 0).start()

    def arrive(self, unit, k):
        for step in (1, -1):
            shard, there, more = self.cases(step, k)

            @pl.when(there)
            def _():
                self.z_copy(unit, shard, step, 0).wait_recv()

                @pl.when(more)
                def _():
                    self.z_copy(unit, shard, step, k).start()

                self.y_copy(unit, shard, self.y).start()

    def end(self):
        for unit in range(UNITS):
            for away in (1, 2, 3):
                shard = lax.rem(self.z + away, 4)
                self.y_copy(unit, shard, 1 - self.y).wait_recv()
                self.y_copy(unit, shard, self.y).wait_send()
            for step in (1, -1):
                for k in range(3):
                    shard, there, more = self.cases(step, k)

                    @pl.when(there & more)
                    def _():
                        self.z_copy(unit, shard, step, k).wait_send()

        @pl.when(self.c == self.layer)
        def _():
            for copy in self.core_copies():
                copy.wait_send()


def weight_scratch():
    dma = pltpu.SemaphoreType.DMA
    return [
        dma((10,)), dma((10,)), dma((10,)),
        dma((UNITS, 3)), dma((UNITS, 3)), dma((UNITS, 4)), dma((UNITS, 4)), dma((UNITS, 4)),
    ]


class RowGather:
    def __init__(self, whole, count, sems):
        self.whole, self.count = whole, count
        self.send, self.recv = sems
        self.c, self.z, self.y, self.x = place()

    def copy(self, i, xx, cc, device):
        if self.count is None:
            piece = self.whole.at[2 * xx + cc]
        else:
            piece = self.whole.at[rows_at((2 * xx + cc) * self.count, self.count)]
        return mesh_copy(piece, piece, self.send.at[i], self.recv.at[i], device)

    def near(self):
        return self.copy(0, self.x, self.c, {"rep": 2 * self.y + 1 - self.x})

    def other(self):
        return self.copy(1, self.x, self.c, {"section": 1 - self.c})

    def far(self):
        return self.copy(2, 1 - self.x, self.c, {"section": 1 - self.c})

    def begin(self, value):
        if self.count is None:
            self.whole[2 * self.x + self.c] = value
        else:
            self.whole[rows_at((2 * self.x + self.c) * self.count, self.count)] = value
        self.near().start()
        self.other().start()

    def middle(self):
        self.near().wait_recv()
        self.far().start()

    def end(self):
        self.near().wait_send()
        self.other().wait()
        self.far().wait()


def normal_rows(rows, gain):
    inv = lax.rsqrt(jnp.mean(rows * rows, axis=-1, keepdims=True) + EPSILON)
    return low(rows * inv * gain)


def turn_by(value, step, counts, which):
    found = pltpu.roll(value, step * counts[0], 1) if counts[0] else value
    for k in range(1, len(counts)):
        other = pltpu.roll(value, step * counts[k], 1) if counts[k] else value
        found = jnp.where(which == k, other, found)
    return found


def small_parts(layer, quarter, params_ref, small_ref):
    width, group = DI // GROUP, DI // 16
    piece = CONV // 4
    lane = iota((16, width), 1)
    pieces = [params_ref[4 * layer + zz].astype(jnp.float32) for zz in range(4)]
    gap = jnp.zeros((16, CONV - pieces[0].shape[1]), jnp.float32)
    conv = jnp.zeros((16, CONV), jnp.float32)
    for zz in range(4):
        own = jnp.where(iota(pieces[zz].shape, 1) < piece, pieces[zz], 0.0)
        conv = conv + pltpu.roll(jnp.concatenate([own, gap], axis=1), zz * piece, 1)

    def turned(part, zz):
        moved = turn_by(part, group, [(zz - k) % GROUP for k in range(GROUP)], quarter)
        return jnp.where(lax.div(lane, group) == zz, moved, 0.0)

    taps = sum(turned(conv[:, zz * width : (zz + 1) * width], zz) for zz in range(4))
    gain = sum(turned(pieces[zz][:, :width], zz) for zz in range(4))
    per = H // 16
    head, given = iota((LANES, LANES), 1), iota((LANES, LANES), 0)
    heads = jnp.zeros((16, LANES), jnp.float32)
    for zz in range(4):
        taken = (lax.div(head, per) == zz) & (given == per * quarter + lax.rem(head, per))
        heads = heads + mm(low(pieces[zz][:, :LANES]), jnp.where(taken, 1.0, 0.0).astype(jnp.bfloat16))
    wide_head = iota((LANES, width), 1)
    wide = jnp.where(lax.div(wide_head, P_SIZE) == iota((LANES, width), 0), 1.0, 0.0)
    skip = mm(low(heads), wide.astype(jnp.bfloat16))
    small_ref[layer] = jnp.zeros(small_ref.shape[1:], jnp.float32)
    small_ref[layer, 0:5, :width] = taps[0:5]
    small_ref[layer, 0:5, width:] = conv[0:5, DI:]
    small_ref[layer, 5:6, :width] = gain[5:6]
    small_ref[layer, 6:7, :width] = skip[9:10]
    small_ref[layer, 7:8, :LANES] = heads[7:8]
    rate = jnp.exp(heads[8:9])
    small_ref[layer, 8:9, :LANES] = jnp.where(iota((1, LANES), 1) < H // GROUP, rate, 0.0)


def enter_first_kernel(
    in_ref, out_ref, blocks_ref, flat_ref, w_ref, wo_ref, rows_ref, normed_ref, small_ref, norms_ref,
    params_ref, row_send, row_recv, home_send, home_recv, p_send, p_recv, *sems,
):
    c, z, y, x = place()
    weights = WeightGather(0, in_ref, out_ref, w_ref, wo_ref, sems)
    gather = RowGather(normed_ref, rows_ref.shape[0], (row_send, row_recv))
    source = {"section": 0, "shard": 2 * x + c, "rep": 2 * y + lax.rem(z, 2)}
    from_self = (c == 0) & (z == 2 * x) & (x == lax.rem(z, 2))
    targets = tuple(
        {"section": lax.rem(z, 2), "shard": 2 * m + x, "rep": 2 * y + lax.div(z, 2)}
        for m in range(MICRO)
    )
    to_self = tuple(
        (lax.rem(z, 2) == 0) & (z == 2 * m + x) & (x == lax.div(z, 2)) for m in range(MICRO)
    )
    others = [{"section": 1 - c}]
    for away in (1, 2, 3):
        others.append({"shard": lax.rem(z + away, 4)})
        others.append({"section": 1 - c, "shard": lax.rem(z + away, 4)})

    barrier = pltpu.get_barrier_semaphore()
    for device in others + [{"rep": 2 * y + 1 - x}, {"rep": 2 * (1 - y) + x}]:
        greet(barrier, device)

    @pl.when(jnp.logical_not(from_self))
    def _():
        greet(barrier, source)

    guests = sum(jnp.logical_not(own).astype(jnp.int32) for own in to_self)
    pl.semaphore_wait(barrier, 9 + jnp.where(c == 0, guests, 0))

    def home_copy(m):
        return mesh_copy(
            blocks_ref.at[0, m, 0], rows_ref, home_send.at[m], home_recv.at[0], targets[m]
        )

    def own_copy(m):
        return pltpu.make_async_copy(blocks_ref.at[0, m, 0], rows_ref, home_send.at[m])

    def param_copy(i):
        return mesh_copy(
            flat_ref, params_ref.at[4 * c + z], p_send.at[i], p_recv.at[i], others[i]
        )

    def param_from(i):
        cc = c if i % 2 == 1 else 1 - c
        zz = z if i == 0 else lax.rem(z + 4 - (i + 1) // 2, 4)
        return mesh_copy(
            flat_ref, params_ref.at[4 * cc + zz], p_send.at[i], p_recv.at[i], others[i]
        )

    for m in range(MICRO):

        @pl.when((c == 0) & jnp.logical_not(to_self[m]))
        def _():
            home_copy(m).start()

        @pl.when((c == 0) & to_self[m])
        def _():
            own_copy(m).start()

    for i in range(7):
        param_copy(i).start()
    params_ref[4 * c + z] = flat_ref[...]
    weights.begin()
    for i in range(7):
        param_from(i).wait_recv()

    @pl.when(jnp.logical_not(from_self))
    def _():
        home_copy(0).wait_recv()

    for m in range(MICRO):

        @pl.when((c == 0) & to_self[m])
        def _():
            own_copy(m).wait()

    for layer in range(2):
        for zz in range(4):
            part = params_ref[4 * layer + zz].astype(jnp.float32)[6:7, :LANE_PART]
            norms_ref[layer, :, zz * LANE_PART : (zz + 1) * LANE_PART] = jnp.broadcast_to(
                part, (8, LANE_PART)
            )
    gain = norms_ref[0, 0:1]
    for unit in range(CHUNKS):
        weights.first(unit)
    gather.begin(normal_rows(rows_ref[...].astype(jnp.float32), gain))
    for k in (1, 2):
        for unit in range(CHUNKS):
            weights.arrive(unit, k)
    weights.first(CHUNKS)
    gather.middle()
    for layer in range(2):
        small_parts(layer, 2 * x + c, params_ref, small_ref)
    for unit in range(CHUNKS):
        weights.arrive(unit, 3)
    for k in (1, 2, 3):
        weights.arrive(CHUNKS, k)
    weights.end()
    gather.end()
    for i in range(7):
        param_copy(i).wait_send()
    for m in range(MICRO):

        @pl.when((c == 0) & jnp.logical_not(to_self[m]))
        def _():
            home_copy(m).wait_send()


def weight_shapes():
    return [
        jax.ShapeDtypeStruct((LOCAL, D), jnp.bfloat16),
        jax.ShapeDtypeStruct((DI // GROUP, D), jnp.bfloat16),
    ]


def enter_first(in_rows, out_rows, blocks, flat):
    dma = pltpu.SemaphoreType.DMA
    block = blocks.shape[-2]
    anywhere, inside = pl.BlockSpec(memory_space=pl.ANY), pl.BlockSpec(memory_space=pltpu.VMEM)
    return pl.pallas_call(
        enter_first_kernel,
        in_specs=[anywhere] * 3 + [inside],
        out_specs=[inside] * 6,
        out_shape=weight_shapes()
        + [
            jax.ShapeDtypeStruct((block, D), jnp.bfloat16),
            jax.ShapeDtypeStruct((GROUP * block, D), jnp.bfloat16),
            jax.ShapeDtypeStruct((CORES, 16, DI // GROUP + 2 * N), jnp.float32),
            jax.ShapeDtypeStruct((CORES, 8, D), jnp.float32),
        ],
        scratch_shapes=[pltpu.VMEM((2 * 4,) + flat.shape, jnp.bfloat16), dma((3,)), dma((3,)), dma((MICRO,)), dma((1,)), dma((7,)), dma((7,))]
        + weight_scratch(),
        compiler_params=pltpu.CompilerParams(
            collective_id=0, has_side_effects=True, vmem_limit_bytes=VMEM_BYTES
        ),
        name="enter_first",
    )(in_rows, out_rows, blocks, flat)


def enter_second_kernel(
    in_ref, out_ref, theirs_ref, mine_ref, squares_ref, entering_ref, gain_ref, g_ref,
    w_ref, wo_ref, added_ref, middle_ref, normed_ref, g_all_ref, inv_ref,
    n_core, n_send, n_across, s_core, s_mine, s_across,
    row_send, row_recv, g_send, g_recv, n_sem, s_sem, *sems,
):
    c, z, y, x = place()
    weights = WeightGather(1, in_ref, out_ref, w_ref, wo_ref, sems)
    block = entering_ref.shape[0]
    gather = RowGather(normed_ref, block, (row_send, row_recv))
    g_gather = RowGather(g_all_ref, block, (g_send, g_recv))
    core, x_other = {"section": 1 - c}, {"rep": 2 * y + 1 - x}
    barrier = pltpu.get_barrier_semaphore()
    for device in (core, x_other, {"rep": 2 * (1 - y) + x}):
        greet(barrier, device)

    @pl.when(z < 3)
    def _():
        greet(barrier, {"shard": z + 1})

    @pl.when(z > 0)
    def _():
        greet(barrier, {"shard": z - 1})

    ends = jnp.where(z == 0, 1, 0) + jnp.where(z == 3, 1, 0)
    pl.semaphore_wait(barrier, 5 - ends)

    n_core_copy = mesh_copy(theirs_ref, n_core, n_sem.at[0], n_sem.at[1], core)
    n_x_copy = mesh_copy(n_send, n_across, n_sem.at[2], n_sem.at[3], x_other)
    s_core_copy = mesh_copy(squares_ref, s_core, s_sem.at[0], s_sem.at[1], core)
    s_x_copy = mesh_copy(s_mine, s_across, s_sem.at[2], s_sem.at[3], x_other)

    n_core_copy.start()
    s_core_copy.start()
    weights.begin()
    for unit in range(CHUNKS):
        weights.first(unit)

    def summed(which):
        rows = rows_at(which * block, block)
        return mine_ref[rows] + n_core[rows].astype(jnp.float32)

    s_core_copy.wait_recv()
    s_mine[...] = squares_ref[...] + s_core[...]
    s_x_copy.start()
    n_core_copy.wait_recv()
    n_send[...] = low(summed(1 - x))
    n_x_copy.start()
    for unit in range(CHUNKS):
        weights.arrive(unit, 1)

    s_x_copy.wait_recv()
    inv_ref[...] = lax.rsqrt((s_mine[...] + s_across[...]) * (1.0 / DI) + EPSILON)
    n_x_copy.wait_recv()
    product = summed(x) + n_across[...].astype(jnp.float32)
    per = block // LANES
    here = (2 * x + c) * per
    own_inv = jnp.concatenate(
        [
            jnp.broadcast_to(inv_ref[pl.ds(here + i, 1)], (LANES, LANES)).T[:, :1]
            for i in range(per)
        ],
        axis=0,
    )
    added = own_inv * product
    added_ref[...] = added
    middle = low(entering_ref[...].astype(jnp.float32) + added)
    middle_ref[...] = middle
    gather.begin(normal_rows(middle.astype(jnp.float32), gain_ref[...]))
    g_gather.begin(g_ref[...])
    for unit in range(CHUNKS):
        weights.arrive(unit, 2)
    weights.first(CHUNKS)
    for unit in range(CHUNKS):
        weights.arrive(unit, 3)
    gather.middle()
    for k in (1, 2, 3):
        weights.arrive(CHUNKS, k)
    g_gather.middle()
    weights.end()
    gather.end()
    g_gather.end()
    n_core_copy.wait_send()
    n_x_copy.wait_send()
    s_core_copy.wait_send()
    s_x_copy.wait_send()


def enter_second(in_rows, out_rows, theirs, mine, squares, entering, gain, g):
    dma = pltpu.SemaphoreType.DMA
    block = entering.shape[0]
    anywhere, inside = pl.BlockSpec(memory_space=pl.ANY), pl.BlockSpec(memory_space=pltpu.VMEM)
    whole = jax.ShapeDtypeStruct((GROUP * block, D), jnp.bfloat16)
    return pl.pallas_call(
        enter_second_kernel,
        in_specs=[anywhere] * 2 + [inside] * 6,
        out_specs=[inside] * 7,
        out_shape=weight_shapes()
        + [
            jax.ShapeDtypeStruct((block, D), jnp.float32),
            jax.ShapeDtypeStruct((block, D), jnp.bfloat16),
            whole,
            whole,
            jax.ShapeDtypeStruct(squares.shape, jnp.float32),
        ],
        scratch_shapes=[
            pltpu.VMEM(theirs.shape, jnp.bfloat16),
            pltpu.VMEM(entering.shape, jnp.bfloat16),
            pltpu.VMEM(entering.shape, jnp.bfloat16),
            pltpu.VMEM(squares.shape, jnp.float32),
            pltpu.VMEM(squares.shape, jnp.float32),
            pltpu.VMEM(squares.shape, jnp.float32),
            dma((3,)), dma((3,)), dma((3,)), dma((3,)), dma((4,)), dma((4,)),
        ]
        + weight_scratch(),
        compiler_params=pltpu.CompilerParams(
            collective_id=1, has_side_effects=True, vmem_limit_bytes=VMEM_BYTES
        ),
        name="enter_second",
    )(in_rows, out_rows, theirs, mine, squares, entering, gain, g)


def swap_core(v):
    return lax.ppermute(v, "section", [(0, 1), (1, 0)])


def swap_x(v):
    return lax.ppermute(v, "rep", [(i, i ^ 1) for i in range(4)])


def swap_y(v):
    return lax.ppermute(v, "rep", [(i, i ^ 2) for i in range(4)])


def swap_z(v, bit):
    return lax.ppermute(v, "shard", [(i, i ^ bit) for i in range(4)])


def ordered(first, mine, other, axis=0):
    return jnp.where(first, jnp.stack([mine, other], axis), jnp.stack([other, mine], axis))


def joined(first, mine, other, axis=0):
    return jnp.where(
        first, jnp.concatenate([mine, other], axis), jnp.concatenate([other, mine], axis)
    )


def after(value, *earlier):
    return lax.optimization_barrier((value,) + earlier)[0]


def sum_kernel(layer, *refs):
    last = layer == 0
    (
        gate_ref, grad_ref, out_grad_ref, theirs_ref, mine_ref, entering_ref, incoming_ref, gain_ref,
        extra_ref,
    ) = refs[:9]
    if last:
        small_refs = (refs[9:12], refs[12:15])
        late_refs, late_out_refs = refs[15:19], refs[19:21]
        refs = refs[:9] + refs[21:]
    else:
        r_theirs_ref, r_mine_ref, r_inv_ref = refs[9:12]
        refs = refs[:9] + refs[12:]
    all_ref, out_all_ref, bound_ref = refs[9:12]
    (
        n_core, n_send, n_across, n_done, y_buf, z_buf, s_buf, yo_buf, yo_mine,
        y_send, y_recv, z_send, z_recv, yo_sem, core_send, core_recv,
        x_send, x_recv, ya_send, ya_recv, relay_send, relay_recv, xo_send, xo_recv, n_sem,
    ) = refs[19:44]
    if last:
        total_refs = refs[12:19]
        tiny_mine, t1_buf, t1_sum, t2_buf, t2_sum, t3_buf = refs[44:50]
        t_send, t_recv, home_send, home_recv = refs[50:]
    else:
        g_ref, g_all_ref, dots_ref, norm_ref = refs[12:16]
        r_core, r_send, r_across = refs[44:47]
        row_send, row_recv, dot_send, dot_recv, r_sem, home_send, home_recv = refs[47:]
    c, z, y, x = place()
    quarter = 2 * x + c
    core, x_other, y_other = {"section": 1 - c}, {"rep": 2 * y + 1 - x}, {"rep": 2 * (1 - y) + x}
    chunks = range(len(STEPS))
    block = n_done.shape[0]
    copy = mesh_copy

    home = {"section": layer, "shard": quarter, "rep": 2 * y + lax.rem(z, 2)}
    at_home = (c == layer) & (z == quarter) & (x == lax.rem(z, 2))
    guests = tuple(
        {"section": lax.rem(z, 2), "shard": 2 * m + x, "rep": 2 * y + lax.div(z, 2)}
        for m in range(MICRO)
    )
    guest_self = tuple(
        (c == layer) & (lax.rem(z, 2) == layer) & (z == 2 * m + x) & (x == lax.div(z, 2))
        for m in range(MICRO)
    )
    reps = (x_other, y_other, {"rep": 2 * (1 - y) + 1 - x})
    shards = tuple({"shard": lax.rem(z + away, 4)} for away in (1, 2, 3))
    barrier = pltpu.get_barrier_semaphore()
    for device in (core,) + reps + shards:
        greet(barrier, device)
    for m in range(MICRO):

        @pl.when((c == layer) & jnp.logical_not(guest_self[m]))
        def _():
            greet(barrier, guests[m])

    pl.semaphore_wait(barrier, 8 - at_home.astype(jnp.int32))

    orders = ((3, 2, 1, 0), (3, 0, 2, 1), (0, 3, 1, 2), (0, 1, 2, 3))

    def shard_at(i):
        found = jnp.int32(orders[3][i])
        for zz in range(3):
            found = jnp.where(z == zz, orders[zz][i], found)
        return found

    def grad_part(shard, side, ch):
        lanes = pl.ds(pl.multiple_of(shard * LANE_PART, LANES), LANE_PART)
        if ch < 2:
            return gate_ref.at[pl.ds(*STEPS[ch]), lanes]
        return grad_ref.at[rows_at(side * REST_HALF + STEPS[ch][0], STEPS[ch][1]), lanes]

    def span_of(ch):
        return pl.ds(STEPS[ch][0] + (0 if ch < 2 else GATE_HALF), STEPS[ch][1])

    def y_copy(shard, ch):
        return copy(
            grad_part(shard, 1 - y, ch), y_buf.at[shard, span_of(ch)],
            y_send.at[shard, ch], y_recv.at[shard, ch], y_other,
        )

    def z_target(shard):
        right = shard > z
        there = {"shard": jnp.clip(z + jnp.where(right, 1, -1), 0, 3)}
        slot = jnp.where(right, shard, jnp.where(shard == z - 1, 4, shard))
        return there, slot

    def z_copy(shard, ch):
        there, slot = z_target(shard)
        return copy(
            s_buf.at[shard, span_of(ch)], z_buf.at[slot, span_of(ch)],
            z_send.at[shard, ch], z_recv.at[slot, ch], there,
        )

    def z_wait(slot, ch):
        there, _ = z_target(shard_at(0))
        copy(
            s_buf.at[0, span_of(ch)], z_buf.at[slot, span_of(ch)],
            z_send.at[0, ch], z_recv.at[slot, ch], there,
        ).wait_recv()

    def all_part(which, side, ch):
        start = side * GATE_HALF if ch < 2 else GATE + side * REST_HALF
        return all_ref.at[which, rows_at(start + STEPS[ch][0], STEPS[ch][1])]

    def out_part(which):
        return out_all_ref.at[rows_at(which * OUT_PART, OUT_PART)]

    def x_copy(who, ch):
        piece = all_part(2 * x + who, y, ch)
        return copy(piece, piece, x_send.at[who, ch], x_recv.at[who, ch], x_other)

    def ya_copy(who, ch):
        piece = all_part(2 * x + who, y, ch)
        return copy(piece, piece, ya_send.at[who, ch], ya_recv.at[who, ch], y_other)

    def relay_copy(who, ch):
        piece = all_part(2 * x + who, 1 - y, ch)
        return copy(piece, piece, relay_send.at[who, ch], relay_recv.at[who, ch], x_other)

    def xo_copy(who):
        piece = out_part(2 * x + who)
        return copy(piece, piece, xo_send.at[who], xo_recv.at[who], x_other)

    def spread(who, ch):
        x_copy(who, ch).start()
        ya_copy(who, ch).start()

    def owner_copy(ch):
        span = span_of(ch)
        piece = all_part(quarter, y, ch)
        return copy(s_buf.at[z, span], piece, core_send.at[ch], core_recv.at[ch], core)

    def owner_out_copy():
        return copy(
            yo_mine, out_part(quarter), core_send.at[len(STEPS)], core_recv.at[len(STEPS)], core
        )

    def yo_copy():
        return copy(out_grad_ref, yo_buf, yo_sem.at[0], yo_sem.at[1], y_other)

    def n_core_copy():
        return copy(theirs_ref, n_core, n_sem.at[0], n_sem.at[1], core)

    def n_x_copy():
        return copy(n_send, n_across, n_sem.at[2], n_sem.at[3], x_other)

    def home_copy(m):
        return copy(n_done, bound_ref.at[m], home_send.at[0], home_recv.at[m], home)

    def go_home():
        for m in range(MICRO):
            there = lax.div(z, 2) == m

            @pl.when(there & jnp.logical_not(at_home))
            def _():
                home_copy(m).start()

            @pl.when(there & at_home)
            def _():
                bound_ref[m] = n_done[...]

    if last:

        def t1_copy():
            return copy(tiny_mine.at[1 - c], t1_buf, t_send.at[0], t_recv.at[0], core)

        def t2_copy(away):
            return copy(
                t1_sum, t2_buf.at[away - 1], t_send.at[away], t_recv.at[away], shards[away - 1]
            )

        def t3_copy(i):
            return copy(t2_sum, t3_buf.at[i], t_send.at[4 + i], t_recv.at[4 + i], reps[i])

    else:

        def r_core_copy():
            return copy(r_theirs_ref, r_core, r_sem.at[0], r_sem.at[1], core)

        def r_x_copy():
            return copy(r_send, r_across, r_sem.at[2], r_sem.at[3], x_other)

        def r_summed(which):
            rows = rows_at(which * block, block)
            return r_mine_ref[rows] + r_core[rows].astype(jnp.float32)

        g_gather = RowGather(g_all_ref, block, (row_send, row_recv))
        dot_gather = RowGather(dots_ref, None, (dot_send, dot_recv))

    n_core_copy().start()
    if not last:
        r_core_copy().start()
    yo_copy().start()
    for ch in chunks[2:]:
        for i in range(4):
            y_copy(shard_at(i), ch).start()

    def more(shard):
        return ((shard > z) & (z > 0)) | ((shard < z) & (z < 3))

    def y_sum(shard, ch):
        own = grad_part(shard, y, ch)[...].astype(jnp.float32)
        if ch < 2:
            return own
        y_copy(shard, ch).wait_recv()
        return own + y_buf[shard, span_of(ch)].astype(jnp.float32)

    def send_in(i, ch):
        shard = shard_at(i)
        span = span_of(ch)
        both = y_sum(shard, ch)

        @pl.when(more(shard))
        def _():
            z_wait(shard, ch)
            s_buf[shard, span] = low(both + z_buf[shard, span].astype(jnp.float32))

        @pl.when(jnp.logical_not(more(shard)))
        def _():
            s_buf[shard, span] = low(both)

        z_copy(shard, ch).start()

    def finish(ch):
        span = span_of(ch)
        s_buf[z, span] = low(y_sum(z, ch))

        @pl.when(z > 0)
        def _():
            z_wait(z, ch)
            s_buf[z, span] = low(
                s_buf[z, span].astype(jnp.float32) + z_buf[z, span].astype(jnp.float32)
            )

        @pl.when(z < 3)
        def _():
            z_wait(4, ch)
            s_buf[z, span] = low(
                s_buf[z, span].astype(jnp.float32) + z_buf[4, span].astype(jnp.float32)
            )

        if not last:
            all_ref[span] = s_buf[z, span]
            return

        @pl.when(c != layer)
        def _():
            owner_copy(ch).start()

        @pl.when(c == layer)
        def _():
            all_part(quarter, y, ch)[...] = s_buf[z, span]
            spread(layer, ch)

    def pass_on(ch):
        if not last:
            return

        @pl.when(c == layer)
        def _():
            owner_copy(ch).wait_recv()
            spread(1 - layer, ch)

    def relay(ch):
        if not last:
            return

        @pl.when(c == layer)
        def _():
            for who in (layer, 1 - layer):
                ya_copy(who, ch).wait_recv()
                relay_copy(who, ch).start()

    def summed(which):
        rows = rows_at(which * block, block)
        return mine_ref[rows] + n_core[rows].astype(jnp.float32)

    n_core_copy().wait_recv()
    n_send[...] = low(summed(1 - x))
    n_x_copy().start()
    send_in(0, 0)
    send_in(0, 1)
    send_in(1, 0)
    send_in(1, 1)
    yo_copy().wait()
    yo_mine[...] = low(out_grad_ref[...].astype(jnp.float32) + yo_buf[...].astype(jnp.float32))

    if last:

        @pl.when(c != layer)
        def _():
            owner_out_copy().start()

        @pl.when(c == layer)
        def _():
            out_part(quarter)[...] = yo_mine[...]

    else:
        out_all_ref[...] = yo_mine[...]

    n_x_copy().wait_recv()
    normed_grad = summed(x) + n_across[...].astype(jnp.float32)
    entering = entering_ref[...].astype(jnp.float32)
    inv = lax.rsqrt(jnp.mean(entering * entering, axis=-1, keepdims=True) + EPSILON)
    hat = entering * inv
    hat_grad = normed_grad * gain_ref[...]
    mean = jnp.mean(hat_grad * hat, axis=-1, keepdims=True)
    source_grad = low(incoming_ref[...].astype(jnp.float32) + inv * (hat_grad - hat * mean))
    norm_grad = jnp.sum(normed_grad * hat, axis=0, keepdims=True)
    if last:
        n_done[...] = source_grad
        go_home()
        small_totals(0, quarter, small_refs[0], norm_grad, tiny_mine)
        small_totals(1, quarter, small_refs[1], extra_ref[...], tiny_mine)
        t1_copy().start()
    else:
        g_ref[...] = source_grad
        g_gather.begin(source_grad)
        norm_ref[...] = norm_grad
        dots = jnp.sum(source_grad.astype(jnp.float32) * extra_ref[...], axis=1, keepdims=True)
        flat = [
            jnp.broadcast_to(dots[i * LANES : (i + 1) * LANES], (LANES, LANES)).T[:1]
            for i in range(block // LANES)
        ]
        flat.append(jnp.zeros((8 - len(flat), LANES), jnp.float32))
        dot_gather.begin(jnp.concatenate(flat, axis=0))
        r_core_copy().wait_recv()
        r_send[...] = low(r_summed(1 - x))
        r_x_copy().start()

    send_in(2, 0)
    send_in(2, 1)
    send_in(0, 2)
    finish(0)
    if last:

        @pl.when(c == layer)
        def _():
            owner_out_copy().wait_recv()
            for who in range(CORES):
                xo_copy(who).start()

        t1_copy().wait_recv()
        t1_sum[...] = tiny_mine[c] + t1_buf[...]
        for away in (1, 2, 3):
            t2_copy(away).start()
    else:
        g_gather.middle()
        dot_gather.middle()
    send_in(1, 2)
    finish(1)
    pass_on(0)
    send_in(2, 2)
    send_in(0, 3)
    pass_on(1)
    if last:
        for away in (1, 2, 3):
            t2_copy(away).wait_recv()
        t2_sum[...] = (t1_sum[...] + t2_buf[0]) + (t2_buf[1] + t2_buf[2])
        for i in range(3):
            t3_copy(i).start()
    else:
        r_x_copy().wait_recv()
        product = r_summed(x) + r_across[...].astype(jnp.float32)
        n_done[...] = low(entering + r_inv_ref[...] * product)
        go_home()
    send_in(1, 3)
    finish(2)
    relay(0)
    send_in(2, 3)
    pass_on(2)
    relay(1)
    finish(3)
    pass_on(3)
    relay(2)
    relay(3)

    if last:

        @pl.when(c == layer)
        def _():
            for ch in chunks:
                for who in range(CORES):
                    x_copy(who, ch).wait()
                    ya_copy(who, ch).wait_send()
                    relay_copy(who, ch).wait()
            for who in range(CORES):
                xo_copy(who).wait()

        @pl.when(c != layer)
        def _():
            for i, (xx, yy) in enumerate(((x, y), (1 - x, y), (x, 1 - y), (1 - x, 1 - y))):
                for who in range(CORES):
                    for ch in chunks:
                        all_part(2 * xx + who, yy, ch)[...] = late_refs[i][who, span_of(ch)]
            for i, xx in enumerate((x, 1 - x)):
                for who in range(CORES):
                    out_part(2 * xx + who)[...] = late_out_refs[i][who]

    if last:
        for i in range(3):
            t3_copy(i).wait_recv()
        t1_buf[...] = (t2_sum[...] + t3_buf[0]) + (t3_buf[1] + t3_buf[2])
        own_totals(z, t1_buf, total_refs)

        t1_copy().wait_send()
        for away in (1, 2, 3):
            t2_copy(away).wait_send()
        for i in range(3):
            t3_copy(i).wait_send()
    else:
        g_gather.end()
        dot_gather.end()
        r_core_copy().wait_send()
        r_x_copy().wait_send()

    @pl.when(jnp.logical_not(at_home))
    def _():
        home_copy(0).wait_send()

    for m in range(MICRO):

        @pl.when((c == layer) & jnp.logical_not(guest_self[m]))
        def _():
            home_copy(m).wait_recv()

    n_core_copy().wait_send()
    n_x_copy().wait_send()
    for i in range(3):
        for ch in chunks:
            z_copy(shard_at(i), ch).wait_send()
    for i in range(4):
        for ch in chunks[2:]:
            y_copy(shard_at(i), ch).wait_send()

    if last:

        @pl.when(c != layer)
        def _():
            for ch in chunks:
                owner_copy(ch).wait_send()
            owner_out_copy().wait_send()


def small_totals(layer, quarter, refs, norm_grad, tiny):
    conv_ref, gain_ref, head_ref = refs
    width, group = DI // GROUP, DI // 16
    lane = iota((8, width), 1)
    wide = jnp.where(iota((8, width), 0) == 5, jnp.broadcast_to(gain_ref[0:1], (8, width)), conv_ref[:, :width])
    for zz in range(4):
        moved = turn_by(wide, group, [(k - zz) % GROUP for k in range(GROUP)], quarter)
        tiny[layer, :, zz * width : (zz + 1) * width] = jnp.where(
            lax.div(lane, group) == quarter, moved, 0.0
        )
    tiny[layer, :, DI:] = conv_ref[:, width:]
    tiny[layer, 6:7, :D] = norm_grad
    per = H // 16
    given, head = iota((LANES, LANES), 0), iota((LANES, LANES), 1)
    taken = (lax.rem(lax.div(head, per), 4) == quarter) & (head < H)
    taken = taken & (given == lax.div(head, 4 * per) * per + lax.rem(head, per))
    heads = exact(head_ref[...], jnp.where(taken, 1.0, 0.0))
    for row in range(3):
        tiny[layer, 6:7, D + row * LANES : D + (row + 1) * LANES] = heads[row : row + 1]


def own_totals(z, whole, refs):
    norm_ref, taps_ref, bias_ref, *head_refs, gain_ref = refs
    piece = CONV // 4
    taps = turn_by(whole[...], piece, [(4 - k) % 4 for k in range(4)], z)
    taps_ref[...] = taps[0:KW, :piece]
    bias_ref[...] = taps[KW : KW + 1, :piece]
    width = DI // 4
    gain_ref[...] = whole[:, pl.ds(pl.multiple_of(z * width, LANES), width)][5:6]
    norm_ref[...] = whole[:, pl.ds(pl.multiple_of(z * LANE_PART, LANES), LANE_PART)][6:7]
    per = H // 4
    for row, ref in enumerate(head_refs):
        heads = whole[:, D + row * LANES : D + (row + 1) * LANES]
        heads = turn_by(heads, 1, [(LANES - k * per) % LANES for k in range(4)], z)
        ref[...] = heads[6:7, :per]


def layer_sums(layer, gate, grad, out_grad, theirs, mine, entering, incoming, gain, extra, *more):
    dma = pltpu.SemaphoreType.DMA
    inside = pl.BlockSpec(memory_space=pltpu.VMEM)
    span = (HALF, LANE_PART)
    out = (OUT_PART, D)
    steps = len(STEPS)
    two = (CORES, steps)
    rows = entering.shape
    half, whole = jnp.bfloat16, jnp.float32
    last = layer == 0
    out_shape = [
        jax.ShapeDtypeStruct((GROUP, LOCAL, LANE_PART) if last else span, half),
        jax.ShapeDtypeStruct((DI // GROUP, D) if last else out, half),
        jax.ShapeDtypeStruct((MICRO,) + rows, half),
    ]
    scratch = [
        pltpu.VMEM(theirs.shape, half),
        pltpu.VMEM(rows, half),
        pltpu.VMEM(rows, half),
        pltpu.VMEM(rows, half),
        pltpu.VMEM((4,) + span, half),
        pltpu.VMEM((5,) + span, half),
        pltpu.VMEM((4,) + span, half),
        pltpu.VMEM(out, half),
        pltpu.VMEM(out, half),
        dma((4, steps)), dma((4, steps)), dma((4, steps)), dma((5, steps)), dma((2,)),
        dma((steps + 1,)), dma((steps + 1,)),
        dma(two), dma(two), dma(two), dma(two), dma(two), dma(two),
        dma((CORES,)), dma((CORES,)), dma((4,)),
    ]
    if layer == 0:
        small = (8, CONV)
        piece = CONV // 4
        shapes = ((1, LANE_PART), (KW, piece), (1, piece)) + ((1, H // 4),) * 3 + ((1, DI // 4),)
        out_shape += [jax.ShapeDtypeStruct(shape, whole) for shape in shapes]
        scratch += [
            pltpu.VMEM((CORES,) + small, whole),
            pltpu.VMEM(small, whole),
            pltpu.VMEM(small, whole),
            pltpu.VMEM((3,) + small, whole),
            pltpu.VMEM(small, whole),
            pltpu.VMEM((3,) + small, whole),
            dma((7,)), dma((7,)), dma((1,)), dma((MICRO,)),
        ]
    else:
        out_shape += [
            jax.ShapeDtypeStruct(rows, half),
            jax.ShapeDtypeStruct((GROUP * rows[0], D), half),
            jax.ShapeDtypeStruct((GROUP, 8, LANES), whole),
            jax.ShapeDtypeStruct((1, D), whole),
        ]
        out_shape += [jax.ShapeDtypeStruct((8, LANES), whole)] * 3
        scratch += [
            pltpu.VMEM(theirs.shape, half),
            pltpu.VMEM(rows, half),
            pltpu.VMEM(rows, half),
            dma((3,)), dma((3,)), dma((3,)), dma((3,)), dma((4,)), dma((1,)), dma((MICRO,)),
        ]
    return pl.pallas_call(
        functools.partial(sum_kernel, layer),
        in_specs=[inside] * (9 + len(more)),
        out_specs=[inside] * 10,
        out_shape=out_shape,
        scratch_shapes=scratch,
        compiler_params=pltpu.CompilerParams(
            collective_id=2 + layer, has_side_effects=True, vmem_limit_bytes=VMEM_BYTES
        ),
        name="layer_sums",
    )(gate, grad, out_grad, theirs, mine, entering, incoming, gain, extra, *more)


def assemble_kernel(part_ref, shared_ref, total_ref):
    last = pl.program_id(0) == 8
    step = DI // 16

    @pl.when(last)
    def _():
        shared = [shared_ref[i, :SHARED].astype(jnp.float32) for i in range(GROUP)]
        total_ref[:SHARED] = (shared[0] + shared[1]) + (shared[2] + shared[3])

    @pl.when(jnp.logical_not(last))
    def _():
        for i in range(GROUP):
            total_ref[i * step : (i + 1) * step] = part_ref[i].astype(jnp.float32)


def assemble_rows(parts):
    lanes = parts.shape[-1]
    step = DI // 16
    return pl.pallas_call(
        assemble_kernel,
        grid=(9,),
        in_specs=[
            pl.BlockSpec((GROUP, step, lanes), lambda i: (0, jnp.minimum(i, 7), 0)),
            pl.BlockSpec((GROUP, 2 * step, lanes), lambda i: (0, 4, 0)),
        ],
        out_specs=pl.BlockSpec((GROUP * step, lanes), lambda i: (i, 0)),
        out_shape=jax.ShapeDtypeStruct((DI + CONV + H, lanes), jnp.float32),
        compiler_params=pltpu.CompilerParams(vmem_limit_bytes=VMEM_BYTES),
        name="assemble_rows",
    )(parts, parts)


def per_device_split(
    boundary_in,
    lengths,
    seq_order,
    norm_gain,
    in_weight,
    conv_weight,
    conv_bias,
    dt_bias,
    a_log,
    d_skip,
    out_gain,
    out_weight,
):
    c = lax.axis_index("section")
    z = lax.axis_index("shard")
    r = lax.axis_index("rep")
    y, x = r // 2, r % 2
    block = boundary_in.shape[3]
    rows = GROUP * block
    width = DI // GROUP
    heads = H // GROUP
    span = width + 2 * N
    quarter = 2 * x + c

    def spot(cc, zz, rr):
        return (cc * 4 + zz) * 4 + rr

    def home(m, zz, rr):
        return spot(zz % 2, 2 * m + rr % 2, (rr // 2) * 2 + zz // 2)

    places = [(cc, zz, rr) for cc in range(2) for zz in range(4) for rr in range(4)]
    axes = ("section", "shard", "rep")
    straight = [(spot(*p), home(p[0], p[1], p[2])) for p in places]
    crossed = [(spot(*p), home(1 - p[0], p[1], p[2])) for p in places]

    params = (norm_gain, conv_weight, conv_bias, dt_bias, a_log, d_skip, out_gain)
    lanes = -(-conv_bias.shape[1] // LANES) * LANES
    given = (conv_weight[0], conv_bias, out_gain, norm_gain, dt_bias, a_log, d_skip)
    flat = [jnp.pad(p, ((0, 0), (0, lanes - p.shape[1]))) for p in given]
    flat = jnp.concatenate(flat + [jnp.zeros((6, lanes), jnp.bfloat16)], axis=0)
    in_rows = jnp.swapaxes(in_weight[0], 0, 1)
    w_in0, w_out0, source, normed0, small, norms = enter_first(
        in_rows, out_weight[0], boundary_in, flat
    )
    late_in = after(boundary_in, source)[0, :, 0]
    arrive_a = lax.ppermute(lax.dynamic_index_in_dim(late_in, c, 0, False), axes, straight)
    arrive_b = lax.ppermute(lax.dynamic_index_in_dim(late_in, 1 - c, 0, False), axes, crossed)
    cotangent = jnp.where(z < 2, arrive_b, arrive_a)

    order = jnp.stack([lengths[:, 0], seq_order[:, 0]])
    order = jnp.where(x == z % 2, order, swap_x(order))
    order = lax.dynamic_index_in_dim(order, z // 2, 1, False)
    chosen = (order[1][:, None] == jnp.arange(NSEQ, dtype=jnp.int32)[None, :]).astype(jnp.int32)
    finish = jnp.cumsum(jnp.sum(chosen * order[0][None, :], axis=1), dtype=jnp.int32)

    def segment_of(positions):
        found = jnp.sum((positions[:, None] >= finish[None, :]).astype(jnp.int32), axis=1)
        return jnp.where(positions < 0, -1, found)

    token = jnp.arange(rows, dtype=jnp.int32)
    segment = segment_of(token)
    opening = token // Q * Q
    columns = [segment_of(token - lag) == segment for lag in range(1, KW)]
    columns.append(segment_of(opening - 1) == segment)
    columns.append(segment_of(opening + (Q - 1)) == segment)
    columns = [column.astype(jnp.float32) for column in columns] + [segment.astype(jnp.float32)]
    marks = jnp.stack(columns + [jnp.zeros((rows,), jnp.float32)] * 2, axis=1)
    seg_row = segment.astype(jnp.float32)[None]

    def own(v):
        return lax.dynamic_slice_in_dim(v, (2 * x + c) * block, block, 0)

    def row_sums(v):
        v = v + swap_core(v)
        return v + swap_x(v)

    def forward(layer, normed, w_in):
        projected = projection(normed, w_in)
        gg, squares, mixer, starts = mixer_forward(layer, projected, marks, seg_row, small)
        return gg, squares.reshape((rows // LANES, LANES)), (normed, projected, mixer, starts)

    def inverse(sums):
        return lax.rsqrt(sums / DI + EPSILON)

    def out_sum(gg, out_inv, g):
        outgoing = low(gg.astype(jnp.float32) * out_inv)
        grad = low(mm(outgoing, g, 0, 0)).reshape((4, OUT_PART, D))
        return lax.psum_scatter(grad, "shard", scatter_dimension=0, tiled=False)

    def backward(layer, kept, og, per_row, ready=(), sent_on=()):
        normed, projected, out, starts = kept
        gate_grad, out_grad, gains = gate_backward(
            layer, projected, small, out, og, per_row, DI
        )
        gate = low(mm(gate_grad, normed, 0, 0)).reshape((2, GATE_HALF, D))
        sent = lax.dynamic_index_in_dim(gate, 1 - y, 0, False)
        received = swap_y(sent)
        gate = lax.dynamic_index_in_dim(gate, y, 0, False)
        pg, conv, head = mixer_backward(
            layer, projected, marks, seg_row, small, out, starts, out_grad, after(gate_grad, sent, *ready)
        )
        pg = after(pg, *sent_on)
        gate = low(gate.astype(jnp.float32) + received.astype(jnp.float32))
        rest = low(mm(pg[:, GATE:], normed, 0, 0))
        return pg, gate, rest, (conv, gains, head)

    gg0, squares0, kept0 = forward(0, normed0, w_in0)
    theirs, mine = group_parts(c, gg0, w_out0)
    w_in1, w_out1, added0, middle, normed1, g1, out_inv0 = enter_second(
        in_rows, out_weight[0], theirs, mine, squares0, source, norms[1, 0:1], cotangent
    )
    out_inv0 = out_inv0.reshape((rows, 1))
    og1 = mm(g1, w_out1, 1, 1)
    gg1, squares1, kept1 = forward(1, normed1, w_in1)
    dots1 = jnp.sum(gg1.astype(jnp.float32) * og1, axis=1).reshape((rows // LANES, LANES))
    sums1 = row_sums(jnp.stack([squares1, dots1]))
    out_inv1 = inverse(sums1[0]).reshape((rows, 1))
    per_row1 = jnp.concatenate([out_inv1, out_inv1 * sums1[1].reshape((rows, 1))], axis=1)
    out_theirs, out_mine = group_parts(c, gg1, w_out1)
    out_part1 = out_sum(gg1, out_inv1, g1)
    pg1, gate1, rest1, small_grads1 = backward(1, kept1, og1, per_row1)
    theirs, mine = group_parts(c, pg1, w_in1)
    in_sum1, out_sum1, results, middle_grad, g0, dots0, norm_grad1, *_ = layer_sums(
        1, gate1, rest1, out_part1, theirs, mine, middle, cotangent, norms[1, 0:1], added0,
        out_theirs, out_mine, own(out_inv1),
    )
    dots0 = dots0[:, : block // LANES].reshape((rows, 1))

    def on_second(v, flip):
        return lax.ppermute(v, ("section", "rep"), [(4 + i, 4 + (i ^ flip)) for i in range(4)])

    def to_second(v):
        return jnp.stack([lax.ppermute(v, "section", [(0, 1)]), v])

    in_own, out_own = to_second(in_sum1), to_second(out_sum1)
    in_near, in_across = on_second(in_own, 1), on_second(in_own, 2)
    out_near = on_second(out_own, 1)
    in_far = on_second(in_across, 1)

    og0 = mm(g0, w_out0, 1, 1)
    out_part0 = out_sum(gg0, out_inv0, g0)
    per_row0 = jnp.concatenate([out_inv0, dots0], axis=1)
    pg0, gate0, rest0, small_grads0 = backward(
        0, kept0, og0, per_row0, (in_own, out_own), (in_near, in_across, out_near)
    )
    theirs, mine = group_parts(c, pg0, w_in0)
    in_all, out_all, entry_grads, *totals = layer_sums(
        0, gate0, rest0, out_part0, theirs, mine, source, middle_grad, norms[0, 0:1], norm_grad1,
        *small_grads0, *small_grads1, in_own, in_near, in_across, in_far, out_own, out_near,
    )
    in_total = jnp.swapaxes(assemble_rows(in_all), 0, 1)[None]
    out_total = out_all.astype(jnp.float32)[None]

    boundary = jnp.stack(
        [jnp.where(c == 0, entry_grads[m], results[m]) for m in range(MICRO)]
    ).astype(jnp.float32)[None, :, None]

    norm_total, conv_total, bias_total, dt_total, log_total, skip_total, gain_total = totals
    return (
        boundary,
        norm_total,
        in_total,
        conv_total[None],
        bias_total,
        dt_total,
        log_total,
        skip_total,
        gain_total,
        out_total,
    )


def solution(mesh):
    fits = mesh.shape["shard"] == GROUP and mesh.shape["rep"] == 4
    return jax.shard_map(
        per_device_split if fits else per_device,
        mesh=mesh,
        in_specs=(
            P("section", None, "rep", "shard", None),
            P(None, "rep", None),
            P(None, "rep", None),
            P("section", "shard"),
            P("section", "shard", None),
            P("section", None, "shard"),
            P("section", "shard"),
            P("section", "shard"),
            P("section", "shard"),
            P("section", "shard"),
            P("section", "shard"),
            P("section", "shard", None),
        ),
        out_specs=(
            P("section", None, "rep", "shard", None),
            P("section", "shard"),
            P("section", "shard", None),
            P("section", None, "shard"),
            P("section", "shard"),
            P("section", "shard"),
            P("section", "shard"),
            P("section", "shard"),
            P("section", "shard"),
            P("section", "shard", None),
        ),
        check_vma=False,
    )
```

```python
import functools

import jax
import jax.numpy as jnp
from jax import lax
from jax.experimental import pallas as pl
from jax.experimental.pallas import tpu as pltpu
from jax.sharding import PartitionSpec as P

D = 1536
P_SIZE = 64
N = 128
KW = 4
BLOCK = 256
MICRO = 2
NSEQ = 4
DI = 3072
H = 48
CONV = 3328


EPSILON = 1e-05
PRECISE = lax.Precision.HIGHEST


def from_behind(shard, axis, by):
    devices = lax.axis_size(axis)
    pairs = [(i, i + by) for i in range(devices) if 0 <= i + by < devices]
    return lax.ppermute(shard, axis, pairs)


def entering(value, axis, join, neutral):
    count, mine = (lax.axis_size(axis), lax.axis_index(axis))
    pieces = jax.tree.map(lambda part: lax.all_gather(part, axis), value)
    subtotal = jax.tree.map(
        lambda part, zero: jnp.full_like(part, 0) + jnp.asarray(zero, part.dtype), value, neutral
    )

    def turn(position, subtotal):
        longer = join(subtotal, jax.tree.map(lambda part: part[position], pieces))
        return jax.tree.map(lambda new, old: jnp.where(position < mine, new, old), longer, subtotal)

    return lax.fori_loop(0, count - 1, turn, subtotal)


def entering_2(shard, axis, join, neutral):
    count = lax.axis_size(axis)
    place = lax.axis_index(axis)
    ahead = count - 1 - place
    gathered = jax.tree.map(
        lambda a, kind: lax.all_gather(a.astype(kind), axis),
        shard,
        jax.tree.map(lambda a: jnp.bfloat16 if a.dtype == jnp.float32 else a.dtype, shard),
    )
    state = jax.tree.map(lambda a, e: jnp.zeros_like(a) + jnp.asarray(e, a.dtype), shard, neutral)

    def one(turn, state):
        source = count - 1 - turn
        return join(
            state,
            jax.tree.map(
                lambda a, own: lax.dynamic_index_in_dim(a, source, 0, False).astype(own.dtype),
                gathered,
                shard,
            ),
        )

    return lax.fori_loop(0, ahead, one, state)


def contract(left, right, left_dim, right_dim):
    return lax.dot_general(
        left, right, (((left_dim,), (right_dim,)), ((), ())), preferred_element_type=jnp.float32
    )


def input_norm(source, gain):
    inv_rms = lax.rsqrt(jnp.mean(source * source, axis=-1, keepdims=True) + EPSILON)
    return source * inv_rms * gain


def block_step(carry_state, pieces):
    x_heads, b_rows, c_rows, log_decay, step_size, segment, before = pieces
    running = jnp.cumsum(log_decay, axis=0)
    places = jnp.arange(x_heads.shape[0])
    linked = (places[:, None] >= places[None, :]) & (segment[:, None] == segment[None, :])
    linked3 = linked[:, :, None]
    gap_sums = jnp.where(linked3, running[:, None, :] - running[None, :, :], 0.0)
    decays = jnp.where(linked3, jnp.exp(gap_sums), 0.0)
    scores = jnp.dot(c_rows, b_rows.T, precision=PRECISE)
    mixing = scores[:, :, None] * decays * step_size[None, :, :]
    inside_part = jnp.einsum("tsh,shp->thp", mixing, x_heads, precision=PRECISE)
    carried = (segment == before).astype(jnp.float32)
    reach = jnp.exp(running) * carried[:, None]
    carried_part = (
        jnp.einsum("tn,hpn->thp", c_rows, carry_state, precision=PRECISE) * reach[:, :, None]
    )
    closing = segment[-1]
    tail_weight = (
        jnp.exp(running[-1][None, :] - running)
        * step_size
        * (segment == closing).astype(jnp.float32)[:, None]
    )
    fresh_state = jnp.einsum("sh,shp,sn->hpn", tail_weight, x_heads, b_rows, precision=PRECISE)
    retained = jnp.exp(running[-1]) * (closing == before).astype(jnp.float32)
    return (retained[:, None, None] * carry_state + fresh_state, inside_part + carried_part)


def conv_inputs(wide_rows, raw_step, conv_weight, conv_bias, dt_bias, a_log, lag_masks):
    rows_here = raw_step.shape[0]
    conv_sum = conv_bias + conv_weight[KW - 1] * wide_rows[KW - 1 :]
    for lag in range(1, KW):
        conv_sum = (
            conv_sum
            + conv_weight[KW - 1 - lag]
            * wide_rows[KW - 1 - lag : KW - 1 - lag + rows_here]
            * lag_masks[lag - 1][:, None]
        )
    active = jax.nn.silu(conv_sum)
    x_heads = active[:, :DI].reshape(rows_here, H, P_SIZE)
    b_rows = active[:, DI : DI + N]
    c_rows = active[:, DI + N :]
    step_size = jax.nn.softplus(raw_step + dt_bias)
    log_decay = -step_size * jnp.exp(a_log)
    return (x_heads, b_rows, c_rows, log_decay, step_size)


def local_scan(x_heads, b_rows, c_rows, log_decay, step_size, segment, befores, seg_before):
    rows_here = x_heads.shape[0]

    def blocks(member):
        return member.reshape((rows_here // BLOCK, BLOCK) + member.shape[1:])

    start_state = jnp.zeros((H, P_SIZE, N), jnp.float32)
    pieces = (
        blocks(x_heads),
        blocks(b_rows),
        blocks(c_rows),
        blocks(log_decay),
        blocks(step_size),
        blocks(segment),
        befores,
    )
    end_state, mixer_out = lax.scan(jax.checkpoint(block_step), start_state, pieces)
    retained = jnp.exp(jnp.sum(log_decay, axis=0)) * (segment[-1] == seg_before).astype(jnp.float32)
    return (mixer_out.reshape(rows_here, H, P_SIZE), end_state, retained)


def state_entry(c_rows, log_decay, state_in, carried):
    reach = jnp.exp(jnp.cumsum(log_decay, axis=0)) * carried[:, None]
    return jnp.einsum("tn,hpn->thp", c_rows, state_in, precision=PRECISE) * reach[:, :, None]


def gate_norm(mixer_out, x_heads, d_skip, gate_part, out_gain):
    rows_here = x_heads.shape[0]
    total_out = mixer_out + d_skip[:, None] * x_heads
    gated = total_out.reshape(rows_here, DI) * jax.nn.silu(gate_part)
    inv_gated = lax.rsqrt(jnp.mean(gated * gated, axis=-1, keepdims=True) + EPSILON)
    return gated * inv_gated * out_gain


def carry_forward(earlier, later):
    return (earlier[0] * later[0], later[0][:, None, None] * earlier[1] + later[1])


def carry_backward(earlier, later):
    return (later[0] * earlier[0], later[1] + later[0][:, None, None] * earlier[1])


def segment_marks(lengths, seq_order, micro_slot, row_start, rows_here):
    micro_slot = jnp.clip(micro_slot, 0, MICRO - 1)
    seq_lengths = lax.dynamic_index_in_dim(lengths[:, 0], micro_slot, 0, keepdims=False)
    row_order = lax.dynamic_index_in_dim(seq_order[:, 0], micro_slot, 0, keepdims=False)
    picks = (row_order[:, None] == jnp.arange(NSEQ, dtype=jnp.int32)[None, :]).astype(jnp.int32)
    placed = jnp.sum(picks * seq_lengths[None, :], axis=1)
    finish = jnp.cumsum(placed, dtype=jnp.int32)
    positions = row_start + jnp.arange(-(KW - 1), rows_here, dtype=jnp.int32)
    extended = jnp.sum((positions[:, None] >= finish[None, :]).astype(jnp.int32), axis=1)
    extended = jnp.where(positions < 0, -1, extended)
    segment = extended[KW - 1 :]
    seg_before = extended[KW - 2]
    lag_masks = jnp.stack(
        [
            (extended[KW - 1 - lag : KW - 1 - lag + rows_here] == segment).astype(jnp.float32)
            for lag in range(1, KW)
        ]
    )
    befores = jnp.concatenate([seg_before[None], segment[:-1]])[::BLOCK]
    carried = (segment == seg_before).astype(jnp.float32)
    return (segment, lag_masks, befores, seg_before, carried)


def mixer_pass(projected, weights, marks):
    norm_gain, in_weight, conv_weight, conv_bias, dt_bias, a_log, d_skip, out_gain, out_weight = (
        weights
    )
    segment, lag_masks, befores, seg_before, carried = marks
    rows_here = projected.shape[0]
    gate_part = projected[:, :DI].astype(jnp.float32)
    mixed_part = projected[:, DI : DI + CONV]
    raw_step = projected[:, DI + CONV :].astype(jnp.float32)
    rim_rows = from_behind(mixed_part[rows_here - (KW - 1) :], "shard", 1)
    wide_rows = jnp.concatenate([rim_rows, mixed_part], axis=0).astype(jnp.float32)

    def conv_section(wide_rows, raw_step, conv_weight, conv_bias, dt_bias, a_log):
        return conv_inputs(wide_rows, raw_step, conv_weight, conv_bias, dt_bias, a_log, lag_masks)

    conv_outs, conv_pull = jax.vjp(
        conv_section, wide_rows, raw_step, conv_weight, conv_bias, dt_bias, a_log
    )
    x_heads, b_rows, c_rows, log_decay, step_size = conv_outs

    def scan_section(x_heads, b_rows, c_rows, log_decay, step_size):
        return local_scan(
            x_heads, b_rows, c_rows, log_decay, step_size, segment, befores, seg_before
        )

    scan_outs, scan_pull = jax.vjp(scan_section, x_heads, b_rows, c_rows, log_decay, step_size)
    local_out, end_state, retained = scan_outs
    identity = (jnp.ones((H,), jnp.float32), jnp.zeros((H, P_SIZE, N), jnp.float32))
    prefix = entering((retained, end_state), "shard", carry_forward, identity)
    state_in = prefix[1]

    def entry_section(c_rows, log_decay, state_in):
        return state_entry(c_rows, log_decay, state_in, carried)

    entered, entry_pull = jax.vjp(entry_section, c_rows, log_decay, state_in)
    mixer_out = local_out + entered
    outgoing, norm_pull = jax.vjp(gate_norm, mixer_out, x_heads, d_skip, gate_part, out_gain)
    return (
        outgoing.astype(jnp.bfloat16),
        (conv_pull, scan_pull, entry_pull, norm_pull, retained, state_in),
    )


def mamba_forward(source, weights, marks):
    normed = input_norm(source, weights[0]).astype(jnp.bfloat16)
    projected = jnp.dot(normed, weights[1], preferred_element_type=jnp.float32).astype(jnp.bfloat16)
    outgoing, unused_pulls = mixer_pass(projected, weights, marks)
    return source + jnp.dot(outgoing, weights[8], preferred_element_type=jnp.float32)


def mamba_backward(source, incoming, weights, marks):
    norm_gain, in_weight, conv_weight, conv_bias, dt_bias, a_log, d_skip, out_gain, out_weight = (
        weights
    )
    rows_here = source.shape[0]
    normed, front_pull = jax.vjp(input_norm, source, norm_gain)
    normed_low = normed.astype(jnp.bfloat16)
    projected = jnp.dot(normed_low, in_weight, preferred_element_type=jnp.float32).astype(
        jnp.bfloat16
    )
    outgoing, pulls = mixer_pass(projected, weights, marks)
    conv_pull, scan_pull, entry_pull, norm_pull, retained, state_in = pulls
    incoming_low = incoming.astype(jnp.bfloat16)
    out_weight_grad = contract(outgoing, incoming_low, 0, 0)
    outgoing_grad = contract(incoming_low, out_weight, 1, 1)
    mixer_grad, x_grad_a, d_skip_grad, gate_grad, out_gain_grad = norm_pull(outgoing_grad)
    c_grad_a, decay_grad_a, direct = entry_pull(mixer_grad)
    identity = (jnp.ones((H,), jnp.float32), jnp.zeros((H, P_SIZE, N), jnp.float32))
    suffix = entering_2((retained, direct), "shard", carry_backward, identity)
    later_grad = suffix[1]
    retained_grad = jnp.sum(later_grad * state_in, axis=(1, 2))
    x_grad_b, b_grad, c_grad_b, decay_grad_b, step_grad = scan_pull(
        (mixer_grad, later_grad, retained_grad)
    )
    conv_grads = conv_pull(
        (x_grad_a + x_grad_b, b_grad, c_grad_a + c_grad_b, decay_grad_a + decay_grad_b, step_grad)
    )
    wide_grad, raw_grad, conv_weight_grad, conv_bias_grad, dt_bias_grad, a_log_grad = conv_grads
    back_rows = from_behind(wide_grad[: KW - 1].astype(jnp.bfloat16), "shard", -1).astype(
        jnp.float32
    )
    filler = jnp.zeros((rows_here - (KW - 1), CONV), jnp.float32)
    mixed_grad = wide_grad[KW - 1 :] + jnp.concatenate([filler, back_rows], axis=0)
    projected_grad = jnp.concatenate([gate_grad, mixed_grad, raw_grad], axis=1).astype(jnp.bfloat16)
    in_weight_grad = contract(normed_low, projected_grad, 0, 0)
    normed_grad = contract(projected_grad, in_weight, 1, 1)
    source_grad, norm_gain_grad = front_pull(normed_grad)
    weight_grads = (
        norm_gain_grad,
        in_weight_grad,
        conv_weight_grad,
        conv_bias_grad,
        dt_bias_grad,
        a_log_grad,
        d_skip_grad,
        out_gain_grad,
        out_weight_grad,
    )
    return (incoming + source_grad, weight_grads)


def per_device(
    boundary_in,
    lengths,
    seq_order,
    norm_gain,
    in_weight,
    conv_weight,
    conv_bias,
    dt_bias,
    a_log,
    d_skip,
    out_gain,
    out_weight,
):
    section_index = lax.axis_index("section")
    is_first = section_index == 0
    rows_here = boundary_in.shape[3]
    row_start = lax.axis_index("shard") * rows_here

    def current():
        whole = (
            lax.all_gather(norm_gain, "shard", axis=1, tiled=True),
            lax.all_gather(in_weight, "shard", axis=1, tiled=True),
            lax.all_gather(conv_weight, "shard", axis=2, tiled=True),
            lax.all_gather(conv_bias, "shard", axis=1, tiled=True),
            lax.all_gather(dt_bias, "shard", axis=1, tiled=True),
            lax.all_gather(a_log, "shard", axis=1, tiled=True),
            lax.all_gather(d_skip, "shard", axis=1, tiled=True),
            lax.all_gather(out_gain, "shard", axis=1, tiled=True),
            lax.all_gather(out_weight, "shard", axis=1, tiled=True),
        )
        return tuple(
            (
                member[0] if slot_index in (1, 8) else member[0].astype(jnp.float32)
                for slot_index, member in enumerate(whole)
            )
        )

    source_rows = boundary_in[0, :, 0]
    arrived = jnp.zeros((rows_here, D), jnp.bfloat16)
    inputs = []
    results = []
    for step_index in range(MICRO + 1):
        own_rows = source_rows[min(step_index, MICRO - 1)]
        layer_in = jnp.where(is_first, own_rows, arrived)
        inputs.append(layer_in)
        marks = segment_marks(lengths, seq_order, step_index - section_index, row_start, rows_here)
        layer_out = mamba_forward(layer_in.astype(jnp.float32), current(), marks)
        results.append(layer_out)
        if step_index < MICRO:
            arrived = from_behind(layer_out.astype(jnp.bfloat16), "section", 1)
    returned = jnp.zeros((rows_here, D), jnp.bfloat16)
    totals = None
    source_grads = []
    for step_index in range(MICRO + 1):
        micro_slot = step_index - 1 + section_index
        is_valid = (micro_slot >= 0) & (micro_slot < MICRO)
        own_rows = source_rows[min(step_index, MICRO - 1)]
        incoming = jnp.where(is_first, returned, own_rows).astype(jnp.float32)
        incoming = jnp.where(is_valid, incoming, 0.0)
        layer_in = jnp.where(
            is_first, inputs[max(step_index - 1, 0)], inputs[min(step_index + 1, MICRO)]
        )
        marks = segment_marks(lengths, seq_order, micro_slot, row_start, rows_here)
        source_grad, weight_grads = mamba_backward(
            layer_in.astype(jnp.float32), incoming, current(), marks
        )
        if totals is None:
            totals = tuple(weight_grads)
        else:
            totals = tuple((earlier + added for earlier, added in zip(totals, weight_grads)))
        source_grads.append(source_grad)
        if step_index < MICRO:
            returned = from_behind(source_grad.astype(jnp.bfloat16), "section", -1)
    boundary = jnp.stack(
        [
            jnp.where(is_first, source_grads[micro_pos + 1], results[micro_pos + 1])
            for micro_pos in range(MICRO)
        ]
    )[None, :, None]
    shares = (
        lax.psum_scatter(
            totals[0][None].astype(jnp.bfloat16), "shard", scatter_dimension=1, tiled=True
        ).astype(jnp.float32),
        lax.psum_scatter(
            totals[1][None].astype(jnp.bfloat16), "shard", scatter_dimension=1, tiled=True
        ).astype(jnp.float32),
        lax.psum_scatter(
            totals[2][None].astype(jnp.bfloat16), "shard", scatter_dimension=2, tiled=True
        ).astype(jnp.float32),
        lax.psum_scatter(
            totals[3][None].astype(jnp.bfloat16), "shard", scatter_dimension=1, tiled=True
        ).astype(jnp.float32),
        lax.psum_scatter(
            totals[4][None].astype(jnp.bfloat16), "shard", scatter_dimension=1, tiled=True
        ).astype(jnp.float32),
        lax.psum_scatter(
            totals[5][None].astype(jnp.bfloat16), "shard", scatter_dimension=1, tiled=True
        ).astype(jnp.float32),
        lax.psum_scatter(
            totals[6][None].astype(jnp.bfloat16), "shard", scatter_dimension=1, tiled=True
        ).astype(jnp.float32),
        lax.psum_scatter(
            totals[7][None].astype(jnp.bfloat16), "shard", scatter_dimension=1, tiled=True
        ).astype(jnp.float32),
        lax.psum_scatter(
            totals[8][None].astype(jnp.bfloat16), "shard", scatter_dimension=1, tiled=True
        ).astype(jnp.float32),
    )
    reduced = (
        lax.psum(shares[0].astype(jnp.bfloat16), "rep").astype(jnp.float32),
        lax.psum(shares[1].astype(jnp.bfloat16), "rep").astype(jnp.float32),
        lax.psum(shares[2].astype(jnp.bfloat16), "rep").astype(jnp.float32),
        lax.psum(shares[3].astype(jnp.bfloat16), "rep").astype(jnp.float32),
        lax.psum(shares[4].astype(jnp.bfloat16), "rep").astype(jnp.float32),
        lax.psum(shares[5].astype(jnp.bfloat16), "rep").astype(jnp.float32),
        lax.psum(shares[6].astype(jnp.bfloat16), "rep").astype(jnp.float32),
        lax.psum(shares[7].astype(jnp.bfloat16), "rep").astype(jnp.float32),
        lax.psum(shares[8].astype(jnp.bfloat16), "rep").astype(jnp.float32),
    )
    return (boundary,) + tuple(reduced)


Q = 128
LANES = 128
VMEM_BYTES = 56 * 1024 * 1024
EXACT = lax.Precision.HIGHEST


def mm(a, b, da=1, db=0):
    return lax.dot_general(
        a, b, (((da,), (db,)), ((), ())), preferred_element_type=jnp.float32
    )


def exact(a, b):
    return jnp.dot(a, b, precision=EXACT, preferred_element_type=jnp.float32)


def low(v):
    return v.astype(jnp.bfloat16)


def split(v, parts):
    found = []
    for _ in range(parts):
        found.append(low(v))
        v = v - found[-1].astype(jnp.float32)
    return found


def pick_sums(v, ones, parts=2):
    return sum(mm(part, ones) for part in split(v, parts))


def sums_of(ones, v, parts=3):
    return sum(mm(ones, part) for part in split(v, parts))


def iota(shape, dim):
    return lax.broadcasted_iota(jnp.int32, shape, dim)


def pair_cols(v, p):
    rows = v.shape[0]
    left = jnp.broadcast_to(v[:, 2 * p : 2 * p + 1], (rows, LANES))
    right = jnp.broadcast_to(v[:, 2 * p + 1 : 2 * p + 2], (rows, LANES))
    return jnp.where(iota((rows, LANES), 1) < LANES // 2, left, right)


def widen(v, pairs):
    return jnp.concatenate([pair_cols(v, p) for p in range(pairs)], axis=1)


def stack_pair(v, p):
    block = v[:, p * LANES : (p + 1) * LANES]
    left = iota(block.shape, 1) < LANES // 2
    zero = jnp.zeros_like(block)
    return jnp.concatenate([jnp.where(left, block, zero), jnp.where(left, zero, block)], axis=0)


def softplus(v):
    small = jnp.exp(-jnp.abs(v))
    series = small * (1 + small * (-1 / 2 + small * (1 / 3 + small * (-1 / 4 + small / 5))))
    return jnp.maximum(v, 0.0) + jnp.where(small < 0.01, series, jnp.log(1 + small))


def sigmoid(v):
    return 1.0 / (1.0 + jnp.exp(-v))


def gate_of(v):
    return 0.5 * jnp.tanh(0.5 * v) + 0.5


def head_picks():
    quarter = 2 * lax.rem(lax.axis_index("rep"), 2) + lax.axis_index("section")
    given, local = iota((64, LANES), 0), iota((64, LANES), 1)
    per = H // 16
    taken = (lax.rem(lax.div(given, per), 4) == quarter) & (given < H)
    taken = taken & (local == lax.div(given, 4 * per) * per + lax.rem(given, per))
    return jnp.where(taken, 1.0, 0.0).astype(jnp.bfloat16)


def chunk_parts(width, proj, before8, marks, seg_row, small_ref, pick):
    conv_w = small_ref[0, 0:KW]
    conv_b = small_ref[0, KW : KW + 1]
    dt_bias = small_ref[0, 7:8, :LANES]
    rate = small_ref[0, 8:9, :LANES]
    span = width + 2 * LANES
    gate = proj[:, :width].astype(jnp.float32)
    mixed = proj[:, width : width + span].astype(jnp.float32)
    raw = mm(proj[:, width + span :], pick)
    shifts = [mixed]
    top = iota((8, span), 0)
    for lag in range(1, KW):
        rolled = pltpu.roll(mixed, lag, 0)
        head = jnp.where(top < lag, pltpu.roll(before8, lag, 0), rolled[:8])
        moved = jnp.concatenate([head, rolled[8:]], axis=0)
        shifts.append(moved * marks[:, lag - 1 : lag])
    conv = conv_b
    for lag in range(KW):
        conv = conv + conv_w[KW - 1 - lag : KW - lag] * shifts[lag]
    sig = gate_of(conv)
    active = conv * sig
    stepped = raw + dt_bias
    step = softplus(stepped)
    decay = -step * rate
    lower = iota((Q, Q), 0) >= iota((Q, Q), 1)
    total = sums_of(jnp.where(lower, 1.0, 0.0).astype(jnp.bfloat16), decay)
    linked = lower & (marks[:, 5:6] == seg_row)
    shut = jnp.where(linked, 0.0, -1e30)
    reach = jnp.exp(total) * marks[:, 3:4]
    tail = jnp.exp(total[Q - 1 : Q] - total) * marks[:, 4:5]
    return gate, mixed, shifts, conv, sig, active, stepped, step, decay, total, shut, reach, tail


def forward_kernel(
    width, proj_ref, marks_ref, seg_ref, small_ref, gg_ref, squares_ref, mixer_ref, starts_ref, state, before,
):
    pairs = width // LANES

    @pl.when(pl.program_id(0) == 0)
    def _():
        state[...] = jnp.zeros_like(state)
        before[...] = jnp.zeros_like(before)

    gate, mixed, _, _, _, active, _, step, _, total, shut, reach, tail = chunk_parts(
        width, proj_ref[...], before[...], marks_ref[...], seg_ref[...], small_ref, head_picks()
    )
    skip, gain = small_ref[0, 6:7, :width], small_ref[0, 5:6, :width]
    before[...] = mixed[Q - 8 :]
    heads = active[:, :width]
    b_low = low(active[:, width : width + LANES])
    c_low = low(active[:, width + LANES :])
    entry = state[...]
    starts_ref[0] = entry
    scores = mm(c_low, b_low, 1, 1)
    total_t = total.T
    scaled = heads * widen(step, pairs)
    scaled_low = low(scaled)
    inside = []
    for p in range(pairs):
        both = []
        for h in (2 * p, 2 * p + 1):
            both.append(low(jnp.exp(total[:, h : h + 1] - total_t[h : h + 1] + shut) * scores))
        inside.append(mm(jnp.concatenate(both, axis=1), stack_pair(scaled_low, p)))
    mixer = jnp.concatenate(inside, axis=1) + widen(reach, pairs) * mm(c_low, low(entry))
    b_turned = low(active[:, width : width + LANES].T)
    state[...] = entry * widen(reach[Q - 1 : Q], pairs) + mm(
        b_turned, low(scaled * widen(tail, pairs))
    )
    out = mixer + skip * heads
    mixer_ref[...] = out
    gated = out * (gate * gate_of(gate))
    squares_ref[...] = jnp.sum(gated * gated, axis=1, keepdims=True)
    gg_ref[...] = low(gated * gain)


def gate_kernel(width, whole_width, proj_ref, small_ref, out_ref, og_ref, rows_ref, gate_grad_ref, out_grad_ref, sums_ref):
    @pl.when(pl.program_id(0) == 0)
    def _():
        sums_ref[...] = jnp.zeros_like(sums_ref)

    gate = proj_ref[...].astype(jnp.float32)
    inv = rows_ref[:, 0:1]
    dots = rows_ref[:, 1:2]
    og = og_ref[...]
    out = out_ref[...]
    gate_sig = gate_of(gate)
    gate_on = gate * gate_sig
    hat = out * gate_on * inv
    gated_grad = inv * (small_ref[0, 5:6, :width] * og - hat * (dots * (1.0 / whole_width)))
    out_grad_ref[...] = low(gated_grad * gate_on)
    gate_grad_ref[...] = low(gated_grad * out * (gate_sig * (1.0 + gate * (1.0 - gate_sig))))
    sums_ref[0:1] += jnp.sum(hat * og, axis=0, keepdims=True)


def gate_backward(layer, projected, small, out, og, per_row, whole_width):
    rows, width = out.shape
    step = 2 * Q

    def by_row(count):
        return pl.BlockSpec((step, count), lambda i: (i, 0))

    half = jax.ShapeDtypeStruct((rows, width), jnp.bfloat16)
    return pl.pallas_call(
        functools.partial(gate_kernel, width, whole_width),
        grid=(rows // step,),
        in_specs=[by_row(width), small_spec(layer), by_row(width), by_row(width), by_row(2)],
        out_specs=[by_row(width), by_row(width), full_spec((8, width))],
        out_shape=[half, half, jax.ShapeDtypeStruct((8, width), jnp.float32)],
        compiler_params=pltpu.CompilerParams(vmem_limit_bytes=VMEM_BYTES),
        cost_estimate=cost(6),
        name="gate_backward",
    )(projected, small, out, og, per_row)


def backward_kernel(
    width, proj_ref, rim_ref, marks_ref, seg_ref, small_ref, out_ref, starts_ref, out_grad_ref,
    gate_grad_ref, pg_ref, conv_ref, head_ref, later, after, skips,
):
    pairs = width // LANES
    turn = pl.program_id(0)
    chunk = pl.num_programs(0) - 1 - turn

    @pl.when(turn == 0)
    def _():
        later[...] = jnp.zeros_like(later)
        after[...] = jnp.zeros_like(after)
        skips[...] = jnp.zeros_like(skips)
        conv_ref[...] = jnp.zeros_like(conv_ref)
        head_ref[...] = jnp.zeros_like(head_ref)

    span = width + 2 * LANES
    marks = marks_ref[...]
    rim = rim_ref[...][8:, width : width + span].astype(jnp.float32)
    rim = jnp.where(chunk > 0, rim, 0.0)
    pick = head_picks()
    skip, rate = small_ref[0, 6:7, :width], small_ref[0, 8:9, :LANES]
    _, mixed, shifts, conv, sig, active, stepped, step, decay, total, shut, reach, tail = (
        chunk_parts(
            width, proj_ref[...], rim, marks, seg_ref[...], small_ref, pick
        )
    )
    heads = active[:, :width]
    b_low = low(active[:, width : width + LANES])
    c_low = low(active[:, width + LANES :])

    grad_low = out_grad_ref[...]
    out_grad = grad_low.astype(jnp.float32)
    mixer = out_ref[...] - skip * heads

    entry = starts_ref[0]
    entry_low = low(entry)
    late = later[...]
    late_low = low(late)
    scores = mm(c_low, b_low, 1, 1)
    total_t = total.T
    step_wide = widen(step, pairs)
    scaled = heads * step_wide
    scaled_low = low(scaled)
    from_late = widen(tail, pairs) * mm(b_low, late_low)
    inside = []
    score_grad = jnp.zeros((Q, Q), jnp.float32)
    for p in range(pairs):
        gains = []
        both = []
        for h in (2 * p, 2 * p + 1):
            gain = jnp.exp(total[:, h : h + 1] - total_t[h : h + 1] + shut)
            gains.append(gain)
            both.append(low(gain * scores))
        stacked = stack_pair(grad_low, p)
        inside.append(mm(jnp.concatenate(both, axis=0), stacked, 0, 0))
        mix_grad = mm(stacked, scaled_low[:, p * LANES : (p + 1) * LANES], 1, 1)
        score_grad = score_grad + gains[0] * mix_grad[:Q] + gains[1] * mix_grad[Q:]
    scaled_grad = jnp.concatenate(inside, axis=1) + from_late
    reached = low(widen(reach, pairs) * out_grad)
    score_low = low(score_grad)
    c_grad = mm(score_low, b_low) + mm(reached, entry_low, 1, 1)
    b_grad = mm(score_low, c_low, 0, 0) + mm(low(scaled * widen(tail, pairs)), late_low, 1, 1)
    kept = widen(reach[Q - 1 : Q], pairs)
    later[...] = late * kept + mm(c_low, reached, 0, 0)

    scaled_seen = scaled_low.astype(jnp.float32)
    balance = out_grad * mixer - scaled_seen * scaled_grad
    closing = jnp.sum(scaled_seen * from_late, axis=0, keepdims=True) + kept * jnp.sum(
        late * entry, axis=0, keepdims=True
    )
    picks = iota((width, LANES), 0) // (LANES // 2) == iota((width, LANES), 1)
    picks = jnp.where(picks, 1.0, 0.0).astype(jnp.bfloat16)
    sums = pick_sums(
        jnp.concatenate([balance, heads * scaled_grad, jnp.broadcast_to(closing, (8, width))], 0),
        picks,
    )
    upper = jnp.where(iota((Q, Q), 0) <= iota((Q, Q), 1), 1.0, 0.0).astype(jnp.bfloat16)
    decay_grad = sums_of(upper, sums[:Q]) + sums[2 * Q : 2 * Q + 1]
    step_grad = sums[Q : 2 * Q] - decay_grad * rate
    raw_grad = step_grad * sigmoid(stepped)

    head_grad = step_wide * scaled_grad + skip * out_grad
    conv_grad = jnp.concatenate([head_grad, b_grad, c_grad], axis=1) * (
        sig * (1.0 + conv * (1.0 - sig))
    )
    mixed_grad = small_ref[0, KW - 1 : KW] * conv_grad
    bottom = iota((8, span), 0)
    for lag in range(1, KW):
        sent = conv_grad * marks[:, lag - 1 : lag]
        rolled = pltpu.roll(sent, Q - lag, 0)
        ending = jnp.where(
            bottom >= 8 - lag, pltpu.roll(after[lag - 1], 8 - lag, 0), rolled[Q - 8 :]
        )
        mixed_grad = mixed_grad + small_ref[0, KW - 1 - lag : KW - lag] * jnp.concatenate(
            [rolled[: Q - 8], ending], axis=0
        )
        after[lag - 1] = sent[:8]
    pg_ref[:, :width] = gate_grad_ref[...]
    pg_ref[:, width:] = low(
        jnp.concatenate([mixed_grad, mm(low(raw_grad), pick, 1, 1)], axis=1)
    )

    skips[0:1] += jnp.sum(out_grad * heads, axis=0, keepdims=True)
    for lag in range(KW):
        conv_ref[KW - 1 - lag : KW - lag] += jnp.sum(
            conv_grad * shifts[lag], axis=0, keepdims=True
        )
    conv_ref[KW : KW + 1] += jnp.sum(conv_grad, axis=0, keepdims=True)
    head_ref[0:1] += jnp.sum(raw_grad, axis=0, keepdims=True)
    head_ref[1:2] += jnp.sum(decay_grad * decay, axis=0, keepdims=True)

    @pl.when(chunk == 0)
    def _():
        head_ref[2:3] = pick_sums(skips[...], picks, 3)[0:1]


def cost(micros):
    return pl.CostEstimate(flops=micros * 1_100_000_000, bytes_accessed=0, transcendentals=0)


def small_spec(layer):
    return pl.BlockSpec((1, 16, 2 * D // 3), lambda i: (layer, 0, 0))


def full_spec(shape):
    return pl.BlockSpec(shape, lambda i: (0,) * len(shape))


def product_kernel(left_ref, weight_ref, theirs_ref, mine_ref, ordered_ref):
    c = lax.axis_index("section")
    block = left_ref.shape[0] // 4

    @pl.when(pl.program_id(0) == 0)
    def _():
        for i in range(4):
            at = 2 * (i % 2) + (1 - c if i < 2 else c)
            rows = pl.ds(pl.multiple_of(at * block, block), block)
            ordered_ref[i * block : (i + 1) * block] = left_ref[rows]

    found = mm(ordered_ref[...], weight_ref[...])
    theirs_ref[...] = low(found[: 2 * block])
    mine_ref[...] = found[2 * block :]


def group_parts(left, weight):
    rows, depth = left.shape
    columns = weight.shape[1]
    step = columns // 3
    half = rows // 2
    return pl.pallas_call(
        product_kernel,
        grid=(3,),
        in_specs=[
            pl.BlockSpec((rows, depth), lambda i: (0, 0)),
            pl.BlockSpec((depth, step), lambda i: (0, i)),
        ],
        out_specs=[pl.BlockSpec((half, step), lambda i: (0, i))] * 2,
        out_shape=[
            jax.ShapeDtypeStruct((half, columns), jnp.bfloat16),
            jax.ShapeDtypeStruct((half, columns), jnp.float32),
        ],
        scratch_shapes=[pltpu.VMEM((rows, depth), jnp.bfloat16)],
        compiler_params=pltpu.CompilerParams(vmem_limit_bytes=VMEM_BYTES),
        cost_estimate=cost(6),
        name="group_parts",
    )(left, weight)


def projection_kernel(left_ref, weight_ref, out_ref):
    out_ref[...] = low(mm(left_ref[...], weight_ref[...], 1, 1))


def projection(left, weight):
    rows, depth = left.shape
    columns = weight.shape[0]
    step = 640
    return pl.pallas_call(
        projection_kernel,
        grid=(pl.cdiv(columns, step),),
        in_specs=[
            pl.BlockSpec((rows, depth), lambda i: (0, 0)),
            pl.BlockSpec((step, depth), lambda i: (i, 0)),
        ],
        out_specs=pl.BlockSpec((rows, step), lambda i: (0, i)),
        out_shape=jax.ShapeDtypeStruct((rows, columns), jnp.bfloat16),
        compiler_params=pltpu.CompilerParams(vmem_limit_bytes=VMEM_BYTES),
        cost_estimate=cost(6),
        name="projection",
    )(left, weight)


def mixer_forward(layer, projected, marks, seg_row, small):
    rows, columns = projected.shape
    width = DI // 4
    chunks = rows // Q
    span = width + 2 * LANES

    def by_row(count):
        return pl.BlockSpec((Q, count), lambda i: (i, 0))

    return pl.pallas_call(
        functools.partial(forward_kernel, width),
        grid=(chunks,),
        in_specs=[
            by_row(columns), by_row(8), pl.BlockSpec((1, Q), lambda i: (0, i)), small_spec(layer),
        ],
        out_specs=[
            by_row(width),
            by_row(1),
            by_row(width),
            pl.BlockSpec((1, LANES, width), lambda i: (i, 0, 0)),
        ],
        out_shape=[
            jax.ShapeDtypeStruct((rows, width), jnp.bfloat16),
            jax.ShapeDtypeStruct((rows, 1), jnp.float32),
            jax.ShapeDtypeStruct((rows, width), jnp.float32),
            jax.ShapeDtypeStruct((chunks, LANES, width), jnp.float32),
        ],
        scratch_shapes=[
            pltpu.VMEM((LANES, width), jnp.float32),
            pltpu.VMEM((8, span), jnp.float32),
        ],
        compiler_params=pltpu.CompilerParams(vmem_limit_bytes=VMEM_BYTES),
        cost_estimate=cost(16),
        name="mixer_forward",
    )(projected, marks, seg_row, small)


def mixer_backward(layer, projected, marks, seg_row, small, out, starts, out_grad, gate_grad):
    rows, columns = projected.shape
    width = out.shape[1]
    chunks = rows // Q
    span = width + 2 * LANES

    def by_row(count):
        return pl.BlockSpec((Q, count), lambda i: (chunks - 1 - i, 0))

    rim = pl.BlockSpec(
        (16, columns), lambda i: (jnp.maximum((chunks - 1 - i) * (Q // 16) - 1, 0), 0)
    )
    return pl.pallas_call(
        functools.partial(backward_kernel, width),
        grid=(chunks,),
        in_specs=[
            by_row(columns),
            rim,
            by_row(8),
            pl.BlockSpec((1, Q), lambda i: (0, chunks - 1 - i)),
            small_spec(layer),
            by_row(width),
            pl.BlockSpec((1, LANES, width), lambda i: (chunks - 1 - i, 0, 0)),
            by_row(width),
            by_row(width),
        ],
        out_specs=[
            by_row(columns),
            full_spec((8, span)),
            full_spec((8, LANES)),
        ],
        out_shape=[
            jax.ShapeDtypeStruct((rows, columns), jnp.bfloat16),
            jax.ShapeDtypeStruct((8, span), jnp.float32),
            jax.ShapeDtypeStruct((8, LANES), jnp.float32),
        ],
        scratch_shapes=[
            pltpu.VMEM((LANES, width), jnp.float32),
            pltpu.VMEM((KW - 1, 8, span), jnp.float32),
            pltpu.VMEM((8, width), jnp.float32),
        ],
        compiler_params=pltpu.CompilerParams(vmem_limit_bytes=VMEM_BYTES),
        cost_estimate=cost(33),
        name="mixer_backward",
    )(projected, projected, marks, seg_row, small, out, starts, out_grad, gate_grad)


CORES = 2
GROUP = 4
SHARED = CONV - DI + H
LOCAL = 2 * DI // GROUP + SHARED + 16
HALF = LOCAL // 2
CHUNKS = 2
LANE_PART = D // 4
OUT_PART = DI // 16
UNITS = CHUNKS + 1
GATE = DI // GROUP
GATE_HALF = GATE // 2
REST_HALF = HALF - GATE_HALF
STEPS = ((0, 192), (192, 192), (0, 272), (272, 272))


def place():
    c, z, r = (lax.axis_index(name) for name in ("section", "shard", "rep"))
    return c, z, lax.div(r, 2), lax.rem(r, 2)


def weight_pieces(quarter):
    part = DI // 16
    found = []
    for side in range(2):
        for zz in range(4):
            found.append(
                (side * 4 * part + zz * part, side * DI + zz * 4 * part + quarter * part, part)
            )
    found.append((8 * part, 2 * DI, SHARED))
    return found


def mesh_copy(source, target, send, recv, device):
    return pltpu.make_async_remote_copy(
        src_ref=source, dst_ref=target, send_sem=send, recv_sem=recv,
        device_id=device, device_id_type=pl.DeviceIdType.MESH,
    )


def greet(barrier, device):
    pl.semaphore_signal(barrier, inc=1, device_id=device, device_id_type=pl.DeviceIdType.MESH)


def rows_at(start, count):
    return pl.ds(pl.multiple_of(start, 16), count)


class WeightGather:
    def __init__(self, layer, in_ref, out_ref, w_ref, wo_ref, sems):
        self.layer, self.in_ref, self.out_ref = layer, in_ref, out_ref
        self.w_ref, self.wo_ref = w_ref, wo_ref
        (
            self.local_sem, self.core_send, self.core_recv, self.right_send, self.left_send,
            self.z_recv, self.y_send, self.y_recv,
        ) = sems
        self.c, self.z, self.y, self.x = place()
        self.core = {"section": 1 - self.c}
        self.y_other = {"rep": (1 - self.y) * 2 + self.x}

    def own_pieces(self, quarter):
        lanes = pl.ds(pl.multiple_of(self.z * LANE_PART, LANES), LANE_PART)
        found = []
        for at, start, count in weight_pieces(quarter):
            found.append((self.in_ref.at[rows_at(start, count)], self.w_ref.at[pl.ds(at, count), lanes]))
        found.append(
            (
                self.out_ref.at[rows_at(quarter * OUT_PART, OUT_PART)],
                self.wo_ref.at[rows_at(self.z * OUT_PART, OUT_PART)],
            )
        )
        return found

    def local_copies(self):
        return [
            pltpu.make_async_copy(source, target, self.local_sem.at[i])
            for i, (source, target) in enumerate(self.own_pieces(2 * self.x + self.c))
        ]

    def core_copies(self):
        return [
            mesh_copy(source, target, self.core_send.at[i], self.core_recv.at[i], self.core)
            for i, (source, target) in enumerate(self.own_pieces(2 * self.x + 1 - self.c))
        ]

    def begin(self):
        lanes = pl.ds(pl.multiple_of(self.z * LANE_PART, LANES), LANE_PART)
        self.w_ref[LOCAL - 16 :, lanes] = jnp.zeros((16, LANE_PART), self.w_ref.dtype)

        @pl.when(self.c == self.layer)
        def _():
            for copy in self.core_copies():
                copy.start()
            for copy in self.local_copies():
                copy.start()
            for copy in self.local_copies():
                copy.wait()

        @pl.when(self.c != self.layer)
        def _():
            for copy in self.core_copies():
                copy.wait_recv()

    def slab(self, unit, shard, side):
        if unit == CHUNKS:
            return self.wo_ref.at[rows_at(shard * OUT_PART + side * (OUT_PART // 2), OUT_PART // 2)]
        return self.w_ref.at[
            rows_at(side * HALF + unit * (HALF // CHUNKS), HALF // CHUNKS),
            pl.ds(pl.multiple_of(shard * LANE_PART, LANES), LANE_PART),
        ]

    def z_copy(self, unit, shard, step, k):
        piece = self.slab(unit, shard, self.y)
        send = (self.right_send if step > 0 else self.left_send).at[unit, k]
        return mesh_copy(piece, piece, send, self.z_recv.at[unit, shard], {"shard": self.z + step})

    def y_copy(self, unit, shard, side):
        piece = self.slab(unit, shard, side)
        return mesh_copy(
            piece, piece, self.y_send.at[unit, shard], self.y_recv.at[unit, shard], self.y_other
        )

    def cases(self, step, k):
        shard = self.z - k * step
        there = (shard >= 0) if step > 0 else (shard <= 3)
        more = (self.z < 3) if step > 0 else (self.z > 0)
        return shard, there, more

    def first(self, unit):
        for step in (1, -1):
            _, _, more = self.cases(step, 0)

            @pl.when(more)
            def _():
                self.z_copy(unit, self.z, step, 0).start()

    def arrive(self, unit, k):
        for step in (1, -1):
            shard, there, more = self.cases(step, k)

            @pl.when(there)
            def _():
                self.z_copy(unit, shard, step, 0).wait_recv()

                @pl.when(more)
                def _():
                    self.z_copy(unit, shard, step, k).start()

                self.y_copy(unit, shard, self.y).start()

    def end(self):
        for unit in range(UNITS):
            for away in (1, 2, 3):
                shard = lax.rem(self.z + away, 4)
                self.y_copy(unit, shard, 1 - self.y).wait_recv()
                self.y_copy(unit, shard, self.y).wait_send()
            for step in (1, -1):
                for k in range(3):
                    shard, there, more = self.cases(step, k)

                    @pl.when(there & more)
                    def _():
                        self.z_copy(unit, shard, step, k).wait_send()

        @pl.when(self.c == self.layer)
        def _():
            for copy in self.core_copies():
                copy.wait_send()


def weight_scratch():
    dma = pltpu.SemaphoreType.DMA
    return [
        dma((10,)), dma((10,)), dma((10,)),
        dma((UNITS, 3)), dma((UNITS, 3)), dma((UNITS, 4)), dma((UNITS, 4)), dma((UNITS, 4)),
    ]


class RowGather:
    def __init__(self, whole, count, sems):
        self.whole, self.count = whole, count
        self.send, self.recv = sems
        self.c, self.z, self.y, self.x = place()

    def copy(self, i, xx, cc, device):
        if self.count is None:
            piece = self.whole.at[2 * xx + cc]
        else:
            piece = self.whole.at[rows_at((2 * xx + cc) * self.count, self.count)]
        return mesh_copy(piece, piece, self.send.at[i], self.recv.at[i], device)

    def near(self):
        return self.copy(0, self.x, self.c, {"rep": 2 * self.y + 1 - self.x})

    def other(self):
        return self.copy(1, self.x, self.c, {"section": 1 - self.c})

    def far(self):
        return self.copy(2, 1 - self.x, self.c, {"section": 1 - self.c})

    def begin(self, value):
        if self.count is None:
            self.whole[2 * self.x + self.c] = value
        else:
            self.whole[rows_at((2 * self.x + self.c) * self.count, self.count)] = value
        self.near().start()
        self.other().start()

    def middle(self):
        self.near().wait_recv()
        self.far().start()

    def end(self):
        self.near().wait_send()
        self.other().wait()
        self.far().wait()


def normal_rows(rows, gain):
    inv = lax.rsqrt(jnp.mean(rows * rows, axis=-1, keepdims=True) + EPSILON)
    return low(rows * inv * gain)


def turn_by(value, step, counts, which):
    found = pltpu.roll(value, step * counts[0], 1) if counts[0] else value
    for k in range(1, len(counts)):
        other = pltpu.roll(value, step * counts[k], 1) if counts[k] else value
        found = jnp.where(which == k, other, found)
    return found


def small_parts(layer, quarter, params_ref, small_ref):
    width, group = DI // GROUP, DI // 16
    piece = CONV // 4
    lane = iota((16, width), 1)
    pieces = [params_ref[4 * layer + zz].astype(jnp.float32) for zz in range(4)]
    gap = jnp.zeros((16, CONV - pieces[0].shape[1]), jnp.float32)
    conv = jnp.zeros((16, CONV), jnp.float32)
    for zz in range(4):
        own = jnp.where(iota(pieces[zz].shape, 1) < piece, pieces[zz], 0.0)
        conv = conv + pltpu.roll(jnp.concatenate([own, gap], axis=1), zz * piece, 1)

    def turned(part, zz):
        moved = turn_by(part, group, [(zz - k) % GROUP for k in range(GROUP)], quarter)
        return jnp.where(lax.div(lane, group) == zz, moved, 0.0)

    taps = sum(turned(conv[:, zz * width : (zz + 1) * width], zz) for zz in range(4))
    gain = sum(turned(pieces[zz][:, :width], zz) for zz in range(4))
    per = H // 16
    head, given = iota((LANES, LANES), 1), iota((LANES, LANES), 0)
    heads = jnp.zeros((16, LANES), jnp.float32)
    for zz in range(4):
        taken = (lax.div(head, per) == zz) & (given == per * quarter + lax.rem(head, per))
        heads = heads + mm(low(pieces[zz][:, :LANES]), jnp.where(taken, 1.0, 0.0).astype(jnp.bfloat16))
    wide_head = iota((LANES, width), 1)
    wide = jnp.where(lax.div(wide_head, P_SIZE) == iota((LANES, width), 0), 1.0, 0.0)
    skip = mm(low(heads), wide.astype(jnp.bfloat16))
    small_ref[layer] = jnp.zeros(small_ref.shape[1:], jnp.float32)
    small_ref[layer, 0:5, :width] = taps[0:5]
    small_ref[layer, 0:5, width:] = conv[0:5, DI:]
    small_ref[layer, 5:6, :width] = gain[5:6]
    small_ref[layer, 6:7, :width] = skip[9:10]
    small_ref[layer, 7:8, :LANES] = heads[7:8]
    rate = jnp.exp(heads[8:9])
    small_ref[layer, 8:9, :LANES] = jnp.where(iota((1, LANES), 1) < H // GROUP, rate, 0.0)


def enter_first_kernel(
    in_ref, out_ref, blocks_ref, flat_ref, w_ref, wo_ref, rows_ref, normed_ref, small_ref, norms_ref,
    params_ref, row_send, row_recv, home_send, home_recv, p_send, p_recv, *sems,
):
    c, z, y, x = place()
    weights = WeightGather(0, in_ref, out_ref, w_ref, wo_ref, sems)
    gather = RowGather(normed_ref, rows_ref.shape[0], (row_send, row_recv))
    source = {"section": 0, "shard": 2 * x + c, "rep": 2 * y + lax.rem(z, 2)}
    from_self = (c == 0) & (z == 2 * x) & (x == lax.rem(z, 2))
    targets = tuple(
        {"section": lax.rem(z, 2), "shard": 2 * m + x, "rep": 2 * y + lax.div(z, 2)}
        for m in range(MICRO)
    )
    to_self = tuple(
        (lax.rem(z, 2) == 0) & (z == 2 * m + x) & (x == lax.div(z, 2)) for m in range(MICRO)
    )
    others = [{"section": 1 - c}]
    for away in (1, 2, 3):
        others.append({"shard": lax.rem(z + away, 4)})
        others.append({"section": 1 - c, "shard": lax.rem(z + away, 4)})

    barrier = pltpu.get_barrier_semaphore()
    for device in others + [{"rep": 2 * y + 1 - x}, {"rep": 2 * (1 - y) + x}]:
        greet(barrier, device)

    @pl.when(jnp.logical_not(from_self))
    def _():
        greet(barrier, source)

    guests = sum(jnp.logical_not(own).astype(jnp.int32) for own in to_self)
    pl.semaphore_wait(barrier, 9 + jnp.where(c == 0, guests, 0))

    def home_copy(m):
        return mesh_copy(
            blocks_ref.at[0, m, 0], rows_ref, home_send.at[m], home_recv.at[0], targets[m]
        )

    def own_copy(m):
        return pltpu.make_async_copy(blocks_ref.at[0, m, 0], rows_ref, home_send.at[m])

    def param_copy(i):
        return mesh_copy(
            flat_ref, params_ref.at[4 * c + z], p_send.at[i], p_recv.at[i], others[i]
        )

    def param_from(i):
        cc = c if i % 2 == 1 else 1 - c
        zz = z if i == 0 else lax.rem(z + 4 - (i + 1) // 2, 4)
        return mesh_copy(
            flat_ref, params_ref.at[4 * cc + zz], p_send.at[i], p_recv.at[i], others[i]
        )

    for m in range(MICRO):

        @pl.when((c == 0) & jnp.logical_not(to_self[m]))
        def _():
            home_copy(m).start()

        @pl.when((c == 0) & to_self[m])
        def _():
            own_copy(m).start()

    for i in range(7):
        param_copy(i).start()
    params_ref[4 * c + z] = flat_ref[...]
    weights.begin()
    for i in range(7):
        param_from(i).wait_recv()

    @pl.when(jnp.logical_not(from_self))
    def _():
        home_copy(0).wait_recv()

    for m in range(MICRO):

        @pl.when((c == 0) & to_self[m])
        def _():
            own_copy(m).wait()

    for layer in range(2):
        for zz in range(4):
            part = params_ref[4 * layer + zz].astype(jnp.float32)[6:7, :LANE_PART]
            norms_ref[layer, :, zz * LANE_PART : (zz + 1) * LANE_PART] = jnp.broadcast_to(
                part, (8, LANE_PART)
            )
    gain = norms_ref[0, 0:1]
    for unit in range(CHUNKS):
        weights.first(unit)
    gather.begin(normal_rows(rows_ref[...].astype(jnp.float32), gain))
    for k in (1, 2):
        for unit in range(CHUNKS):
            weights.arrive(unit, k)
    weights.first(CHUNKS)
    gather.middle()
    for layer in range(2):
        small_parts(layer, 2 * x + c, params_ref, small_ref)
    for unit in range(CHUNKS):
        weights.arrive(unit, 3)
    for k in (1, 2, 3):
        weights.arrive(CHUNKS, k)
    weights.end()
    gather.end()
    for i in range(7):
        param_copy(i).wait_send()
    for m in range(MICRO):

        @pl.when((c == 0) & jnp.logical_not(to_self[m]))
        def _():
            home_copy(m).wait_send()


def weight_shapes():
    return [
        jax.ShapeDtypeStruct((LOCAL, D), jnp.bfloat16),
        jax.ShapeDtypeStruct((DI // GROUP, D), jnp.bfloat16),
    ]


def enter_first(in_rows, out_rows, blocks, flat):
    dma = pltpu.SemaphoreType.DMA
    block = blocks.shape[-2]
    anywhere, inside = pl.BlockSpec(memory_space=pl.ANY), pl.BlockSpec(memory_space=pltpu.VMEM)
    return pl.pallas_call(
        enter_first_kernel,
        in_specs=[anywhere] * 3 + [inside],
        out_specs=[inside] * 6,
        out_shape=weight_shapes()
        + [
            jax.ShapeDtypeStruct((block, D), jnp.bfloat16),
            jax.ShapeDtypeStruct((GROUP * block, D), jnp.bfloat16),
            jax.ShapeDtypeStruct((CORES, 16, DI // GROUP + 2 * N), jnp.float32),
            jax.ShapeDtypeStruct((CORES, 8, D), jnp.float32),
        ],
        scratch_shapes=[pltpu.VMEM((2 * 4,) + flat.shape, jnp.bfloat16), dma((3,)), dma((3,)), dma((MICRO,)), dma((1,)), dma((7,)), dma((7,))]
        + weight_scratch(),
        compiler_params=pltpu.CompilerParams(
            collective_id=0, has_side_effects=True, vmem_limit_bytes=VMEM_BYTES
        ),
        name="enter_first",
    )(in_rows, out_rows, blocks, flat)


def enter_second_kernel(
    in_ref, out_ref, theirs_ref, mine_ref, squares_ref, entering_ref, gain_ref, g_ref,
    w_ref, wo_ref, added_ref, middle_ref, normed_ref, g_all_ref, inv_ref,
    n_core, n_send, n_across, s_core, s_mine, s_across,
    row_send, row_recv, g_send, g_recv, n_sem, s_sem, *sems,
):
    c, z, y, x = place()
    weights = WeightGather(1, in_ref, out_ref, w_ref, wo_ref, sems)
    block = entering_ref.shape[0]
    gather = RowGather(normed_ref, block, (row_send, row_recv))
    g_gather = RowGather(g_all_ref, block, (g_send, g_recv))
    core, x_other = {"section": 1 - c}, {"rep": 2 * y + 1 - x}
    barrier = pltpu.get_barrier_semaphore()
    for device in (core, x_other, {"rep": 2 * (1 - y) + x}):
        greet(barrier, device)

    @pl.when(z < 3)
    def _():
        greet(barrier, {"shard": z + 1})

    @pl.when(z > 0)
    def _():
        greet(barrier, {"shard": z - 1})

    ends = jnp.where(z == 0, 1, 0) + jnp.where(z == 3, 1, 0)
    pl.semaphore_wait(barrier, 5 - ends)

    n_core_copy = mesh_copy(theirs_ref, n_core, n_sem.at[0], n_sem.at[1], core)
    n_x_copy = mesh_copy(n_send, n_across, n_sem.at[2], n_sem.at[3], x_other)
    s_core_copy = mesh_copy(squares_ref, s_core, s_sem.at[0], s_sem.at[1], core)
    s_x_copy = mesh_copy(s_mine, s_across, s_sem.at[2], s_sem.at[3], x_other)

    n_core_copy.start()
    s_core_copy.start()
    weights.begin()
    for unit in range(CHUNKS):
        weights.first(unit)

    def summed(which):
        rows = rows_at(which * block, block)
        return mine_ref[rows] + n_core[rows].astype(jnp.float32)

    s_core_copy.wait_recv()
    s_mine[...] = squares_ref[...] + s_core[...]
    s_x_copy.start()
    n_core_copy.wait_recv()
    n_send[...] = low(summed(1 - x))
    n_x_copy.start()
    for unit in range(CHUNKS):
        weights.arrive(unit, 1)

    s_x_copy.wait_recv()
    inv_ref[...] = lax.rsqrt((s_mine[...] + s_across[...]) * (1.0 / DI) + EPSILON)
    n_x_copy.wait_recv()
    product = summed(x) + n_across[...].astype(jnp.float32)
    per = block // LANES
    here = (2 * x + c) * per
    own_inv = jnp.concatenate(
        [
            jnp.broadcast_to(inv_ref[pl.ds(here + i, 1)], (LANES, LANES)).T[:, :1]
            for i in range(per)
        ],
        axis=0,
    )
    added = own_inv * product
    added_ref[...] = added
    middle = low(entering_ref[...].astype(jnp.float32) + added)
    middle_ref[...] = middle
    gather.begin(normal_rows(middle.astype(jnp.float32), gain_ref[...]))
    g_gather.begin(g_ref[...])
    for unit in range(CHUNKS):
        weights.arrive(unit, 2)
    weights.first(CHUNKS)
    for unit in range(CHUNKS):
        weights.arrive(unit, 3)
    gather.middle()
    for k in (1, 2, 3):
        weights.arrive(CHUNKS, k)
    g_gather.middle()
    weights.end()
    gather.end()
    g_gather.end()
    n_core_copy.wait_send()
    n_x_copy.wait_send()
    s_core_copy.wait_send()
    s_x_copy.wait_send()


def enter_second(in_rows, out_rows, theirs, mine, squares, entering, gain, g):
    dma = pltpu.SemaphoreType.DMA
    block = entering.shape[0]
    anywhere, inside = pl.BlockSpec(memory_space=pl.ANY), pl.BlockSpec(memory_space=pltpu.VMEM)
    whole = jax.ShapeDtypeStruct((GROUP * block, D), jnp.bfloat16)
    return pl.pallas_call(
        enter_second_kernel,
        in_specs=[anywhere] * 2 + [inside] * 6,
        out_specs=[inside] * 7,
        out_shape=weight_shapes()
        + [
            jax.ShapeDtypeStruct((block, D), jnp.float32),
            jax.ShapeDtypeStruct((block, D), jnp.bfloat16),
            whole,
            whole,
            jax.ShapeDtypeStruct(squares.shape, jnp.float32),
        ],
        scratch_shapes=[
            pltpu.VMEM(theirs.shape, jnp.bfloat16),
            pltpu.VMEM(entering.shape, jnp.bfloat16),
            pltpu.VMEM(entering.shape, jnp.bfloat16),
            pltpu.VMEM(squares.shape, jnp.float32),
            pltpu.VMEM(squares.shape, jnp.float32),
            pltpu.VMEM(squares.shape, jnp.float32),
            dma((3,)), dma((3,)), dma((3,)), dma((3,)), dma((4,)), dma((4,)),
        ]
        + weight_scratch(),
        compiler_params=pltpu.CompilerParams(
            collective_id=1, has_side_effects=True, vmem_limit_bytes=VMEM_BYTES
        ),
        name="enter_second",
    )(in_rows, out_rows, theirs, mine, squares, entering, gain, g)


def swap_core(v):
    return lax.ppermute(v, "section", [(0, 1), (1, 0)])


def swap_x(v):
    return lax.ppermute(v, "rep", [(i, i ^ 1) for i in range(4)])


def swap_y(v):
    return lax.ppermute(v, "rep", [(i, i ^ 2) for i in range(4)])


def swap_z(v, bit):
    return lax.ppermute(v, "shard", [(i, i ^ bit) for i in range(4)])


def ordered(first, mine, other, axis=0):
    return jnp.where(first, jnp.stack([mine, other], axis), jnp.stack([other, mine], axis))


def joined(first, mine, other, axis=0):
    return jnp.where(
        first, jnp.concatenate([mine, other], axis), jnp.concatenate([other, mine], axis)
    )


def after(value, *earlier):
    return lax.optimization_barrier((value,) + earlier)[0]


def sum_kernel(layer, *refs):
    last = layer == 0
    (
        gate_ref, grad_ref, out_grad_ref, theirs_ref, mine_ref, entering_ref, incoming_ref, gain_ref,
        extra_ref,
    ) = refs[:9]
    if last:
        small_refs = (refs[9:12], refs[12:15])
        late_refs, late_out_refs = refs[15:19], refs[19:21]
        refs = refs[:9] + refs[21:]
    else:
        r_theirs_ref, r_mine_ref, r_inv_ref = refs[9:12]
        refs = refs[:9] + refs[12:]
    all_ref, out_all_ref, bound_ref = refs[9:12]
    (
        n_core, n_send, n_across, y_buf, z_buf, s_buf, yo_buf, yo_mine,
        y_send, y_recv, z_send, z_recv, yo_sem, core_send, core_recv,
        x_send, x_recv, ya_send, ya_recv, relay_send, relay_recv, xo_send, xo_recv, n_sem,
    ) = refs[19:43]
    if last:
        total_refs = refs[12:19]
        tiny_mine, t1_buf, t1_sum, t2_buf, t2_sum, t3_buf, g_mine, g_buf, g_sum, g_all = refs[43:53]
        t_send, t_recv, g_send, g_recv = refs[53:]
    else:
        g_ref, g_all_ref, dots_ref, norm_ref = refs[12:16]
        r_core, r_send, r_across = refs[43:46]
        row_send, row_recv, dot_send, dot_recv, r_sem = refs[46:]
    c, z, y, x = place()
    quarter = 2 * x + c
    core, x_other, y_other = {"section": 1 - c}, {"rep": 2 * y + 1 - x}, {"rep": 2 * (1 - y) + x}
    chunks = range(len(STEPS))
    block = n_send.shape[0]
    copy = mesh_copy

    reps = (x_other, y_other, {"rep": 2 * (1 - y) + 1 - x})
    shards = tuple({"shard": lax.rem(z + away, 4)} for away in (1, 2, 3))
    barrier = pltpu.get_barrier_semaphore()
    for device in (core,) + reps + shards:
        greet(barrier, device)
    pl.semaphore_wait(barrier, 7)

    orders = ((3, 2, 1, 0), (3, 0, 2, 1), (0, 3, 1, 2), (0, 1, 2, 3))

    def shard_at(i):
        found = jnp.int32(orders[3][i])
        for zz in range(3):
            found = jnp.where(z == zz, orders[zz][i], found)
        return found

    def grad_part(shard, side, ch):
        lanes = pl.ds(pl.multiple_of(shard * LANE_PART, LANES), LANE_PART)
        if ch < 2:
            return gate_ref.at[pl.ds(*STEPS[ch]), lanes]
        return grad_ref.at[rows_at(side * REST_HALF + STEPS[ch][0], STEPS[ch][1]), lanes]

    def span_of(ch):
        return pl.ds(STEPS[ch][0] + (0 if ch < 2 else GATE_HALF), STEPS[ch][1])

    def y_copy(shard, ch):
        return copy(
            grad_part(shard, 1 - y, ch), y_buf.at[shard, span_of(ch)],
            y_send.at[shard, ch], y_recv.at[shard, ch], y_other,
        )

    def z_target(shard):
        right = shard > z
        there = {"shard": jnp.clip(z + jnp.where(right, 1, -1), 0, 3)}
        slot = jnp.where(right, shard, jnp.where(shard == z - 1, 4, shard))
        return there, slot

    def z_copy(shard, ch):
        there, slot = z_target(shard)
        return copy(
            s_buf.at[shard, span_of(ch)], z_buf.at[slot, span_of(ch)],
            z_send.at[shard, ch], z_recv.at[slot, ch], there,
        )

    def z_wait(slot, ch):
        there, _ = z_target(shard_at(0))
        copy(
            s_buf.at[0, span_of(ch)], z_buf.at[slot, span_of(ch)],
            z_send.at[0, ch], z_recv.at[slot, ch], there,
        ).wait_recv()

    def all_part(which, side, ch):
        start = side * GATE_HALF if ch < 2 else GATE + side * REST_HALF
        return all_ref.at[which, rows_at(start + STEPS[ch][0], STEPS[ch][1])]

    def out_part(which):
        return out_all_ref.at[rows_at(which * OUT_PART, OUT_PART)]

    def x_copy(who, ch):
        piece = all_part(2 * x + who, y, ch)
        return copy(piece, piece, x_send.at[who, ch], x_recv.at[who, ch], x_other)

    def ya_copy(who, ch):
        piece = all_part(2 * x + who, y, ch)
        return copy(piece, piece, ya_send.at[who, ch], ya_recv.at[who, ch], y_other)

    def relay_copy(who, ch):
        if who == 0:
            piece = all_part(2 * x, 1 - y, ch)
            return copy(piece, piece, relay_send.at[0, ch], relay_recv.at[0, ch], x_other)
        piece = all_part(2 * (1 - x) + 1, y, ch)
        return copy(piece, piece, relay_send.at[1, ch], relay_recv.at[1, ch], y_other)

    def xo_copy(who):
        piece = out_part(2 * x + who)
        return copy(piece, piece, xo_send.at[who], xo_recv.at[who], x_other)

    def spread(who, ch):
        x_copy(who, ch).start()
        ya_copy(who, ch).start()

    def owner_copy(ch):
        span = span_of(ch)
        piece = all_part(quarter, y, ch)
        return copy(s_buf.at[z, span], piece, core_send.at[ch], core_recv.at[ch], core)

    def owner_out_copy():
        return copy(
            yo_mine, out_part(quarter), core_send.at[len(STEPS)], core_recv.at[len(STEPS)], core
        )

    def yo_copy():
        return copy(out_grad_ref, yo_buf, yo_sem.at[0], yo_sem.at[1], y_other)

    def n_core_copy():
        return copy(theirs_ref, n_core, n_sem.at[0], n_sem.at[1], core)

    def n_x_copy():
        return copy(n_send, n_across, n_sem.at[2], n_sem.at[3], x_other)

    if last:

        def t1_copy():
            return copy(tiny_mine.at[1 - c], t1_buf, t_send.at[0], t_recv.at[0], core)

        def t2_copy(away):
            return copy(
                t1_sum, t2_buf.at[away - 1], t_send.at[away], t_recv.at[away], shards[away - 1]
            )

        def t3_copy(i):
            return copy(t2_sum, t3_buf.at[i], t_send.at[4 + i], t_recv.at[4 + i], reps[i])

        def g1_copy():
            return copy(g_mine, g_buf.at[0], g_send.at[0], g_recv.at[0], core)

        def g2_copy(away):
            return copy(g_sum, g_buf.at[away], g_send.at[away], g_recv.at[away], shards[away - 1])

        def g3_copy(i):
            return copy(g_all, g_buf.at[4 + i], g_send.at[4 + i], g_recv.at[4 + i], reps[i])

    else:

        def r_core_copy():
            return copy(r_theirs_ref, r_core, r_sem.at[0], r_sem.at[1], core)

        def r_x_copy():
            return copy(r_send, r_across, r_sem.at[2], r_sem.at[3], x_other)

        def r_summed(which):
            rows = rows_at(which * block, block)
            return r_mine_ref[rows] + r_core[rows].astype(jnp.float32)

        g_gather = RowGather(g_all_ref, block, (row_send, row_recv))
        dot_gather = RowGather(dots_ref, None, (dot_send, dot_recv))

    n_core_copy().start()
    if not last:
        r_core_copy().start()
    for ch in chunks[2:]:
        for i in range(4):
            y_copy(shard_at(i), ch).start()
        if ch == 2:
            yo_copy().start()

    def more(shard):
        return ((shard > z) & (z > 0)) | ((shard < z) & (z < 3))

    def y_sum(shard, ch):
        own = grad_part(shard, y, ch)[...].astype(jnp.float32)
        if ch < 2:
            return own
        y_copy(shard, ch).wait_recv()
        return own + y_buf[shard, span_of(ch)].astype(jnp.float32)

    def send_in(i, ch):
        shard = shard_at(i)
        span = span_of(ch)
        both = y_sum(shard, ch)

        @pl.when(more(shard))
        def _():
            z_wait(shard, ch)
            s_buf[shard, span] = low(both + z_buf[shard, span].astype(jnp.float32))

        @pl.when(jnp.logical_not(more(shard)))
        def _():
            s_buf[shard, span] = low(both)

        z_copy(shard, ch).start()

    def finish(ch):
        span = span_of(ch)
        s_buf[z, span] = low(y_sum(z, ch))

        @pl.when(z > 0)
        def _():
            z_wait(z, ch)
            s_buf[z, span] = low(
                s_buf[z, span].astype(jnp.float32) + z_buf[z, span].astype(jnp.float32)
            )

        @pl.when(z < 3)
        def _():
            z_wait(4, ch)
            s_buf[z, span] = low(
                s_buf[z, span].astype(jnp.float32) + z_buf[4, span].astype(jnp.float32)
            )

        if not last:
            all_ref[span] = s_buf[z, span]
            return

        @pl.when(c != layer)
        def _():
            owner_copy(ch).start()

        @pl.when(c == layer)
        def _():
            all_part(quarter, y, ch)[...] = s_buf[z, span]
            spread(layer, ch)

    def pass_on(ch):
        if not last:
            return

        @pl.when(c == layer)
        def _():
            owner_copy(ch).wait_recv()
            spread(1 - layer, ch)

    def relay(ch):
        if not last:
            return

        @pl.when(c == layer)
        def _():
            ya_copy(0, ch).wait_recv()
            relay_copy(0, ch).start()
            x_copy(1, ch).wait_recv()
            relay_copy(1, ch).start()

    def summed(which):
        rows = rows_at(which * block, block)
        return mine_ref[rows] + n_core[rows].astype(jnp.float32)

    def start_across():
        n_core_copy().wait_recv()
        n_send[...] = low(summed(1 - x))
        n_x_copy().start()

    def norm_step():
        n_x_copy().wait_recv()
        if not last:
            r_core_copy().wait_recv()
            r_send[...] = low(r_summed(1 - x))
            r_x_copy().start()
        normed_grad = summed(x) + n_across[...].astype(jnp.float32)
        entering = entering_ref[...].astype(jnp.float32)
        inv = lax.rsqrt(jnp.mean(entering * entering, axis=-1, keepdims=True) + EPSILON)
        hat = entering * inv
        hat_grad = normed_grad * gain_ref[...]
        mean = jnp.mean(hat_grad * hat, axis=-1, keepdims=True)
        source_grad = low(incoming_ref[...].astype(jnp.float32) + inv * (hat_grad - hat * mean))
        norm_grad = jnp.sum(normed_grad * hat, axis=0, keepdims=True)
        if last:
            bound_ref[...] = source_grad
            g_mine[...] = jnp.broadcast_to(norm_grad, g_mine.shape)

            @pl.when(c != layer)
            def _():
                g1_copy().start()

            return
        g_ref[...] = source_grad
        g_gather.begin(source_grad)
        norm_ref[...] = norm_grad
        dots = jnp.sum(source_grad.astype(jnp.float32) * extra_ref[...], axis=1, keepdims=True)
        flat = [
            jnp.broadcast_to(dots[i * LANES : (i + 1) * LANES], (LANES, LANES)).T[:1]
            for i in range(block // LANES)
        ]
        flat.append(jnp.zeros((8 - len(flat), LANES), jnp.float32))
        dot_gather.begin(jnp.concatenate(flat, axis=0))

    def result_step():
        r_x_copy().wait_recv()
        product = r_summed(x) + r_across[...].astype(jnp.float32)
        bound_ref[...] = low(entering_ref[...].astype(jnp.float32) + r_inv_ref[...] * product)

    def out_step():
        yo_copy().wait()
        total = low(out_grad_ref[...].astype(jnp.float32) + yo_buf[...].astype(jnp.float32))
        if not last:
            out_all_ref[...] = total
            return
        yo_mine[...] = total

        @pl.when(c != layer)
        def _():
            owner_out_copy().start()

        @pl.when(c == layer)
        def _():
            out_part(quarter)[...] = yo_mine[...]

    def out_across():
        @pl.when(c == layer)
        def _():
            owner_out_copy().wait_recv()
            for who in range(CORES):
                xo_copy(who).start()

    def early_small():
        if last:
            small_totals(0, quarter, small_refs[0], None, tiny_mine)
            small_totals(1, quarter, small_refs[1], extra_ref[...], tiny_mine)
            t1_copy().start()

    def small_along_z():
        if last:
            t1_copy().wait_recv()
            t1_sum[...] = tiny_mine[c] + t1_buf[...]
            for away in (1, 2, 3):
                t2_copy(away).start()

    def small_across():
        if last:
            for away in (1, 2, 3):
                t2_copy(away).wait_recv()
            t2_sum[...] = (t1_sum[...] + t2_buf[0]) + (t2_buf[1] + t2_buf[2])
            for i in range(3):
                t3_copy(i).start()

    def gain_along_z():
        @pl.when(c == layer)
        def _():
            g1_copy().wait_recv()
            g_sum[...] = g_mine[...] + g_buf[0]
            for away in (1, 2, 3):
                g2_copy(away).start()

    def gain_across():
        @pl.when(c == layer)
        def _():
            for away in (1, 2, 3):
                g2_copy(away).wait_recv()
            g_all[...] = (g_sum[...] + g_buf[1]) + (g_buf[2] + g_buf[3])
            for i in range(3):
                g3_copy(i).start()

    send_in(0, 0)
    send_in(0, 1)
    start_across()
    early_small()
    send_in(1, 0)
    send_in(0, 2)
    send_in(1, 1)
    small_along_z()
    send_in(2, 0)
    send_in(1, 2)
    send_in(2, 1)
    finish(0)
    small_across()
    norm_step()
    out_step()
    send_in(2, 2)
    finish(1)
    if last:
        out_across()
    pass_on(0)
    send_in(0, 3)
    pass_on(1)
    finish(2)
    if last:
        gain_along_z()
        send_in(1, 3)
        pass_on(2)
        relay(0)
        send_in(2, 3)
        relay(1)
        gain_across()
        finish(3)
        pass_on(3)
        relay(2)
        relay(3)
    else:
        send_in(1, 3)
        result_step()
        send_in(2, 3)
        g_gather.middle()
        dot_gather.middle()
        finish(3)

    if last:

        @pl.when(c == layer)
        def _():
            for ch in chunks:
                x_copy(0, ch).wait_recv()
                ya_copy(1, ch).wait_recv()
                for who in range(CORES):
                    x_copy(who, ch).wait_send()
                    ya_copy(who, ch).wait_send()
                    relay_copy(who, ch).wait()
            for who in range(CORES):
                xo_copy(who).wait()

        @pl.when(c != layer)
        def _():
            for i, (xx, yy) in enumerate(((x, y), (1 - x, y), (x, 1 - y), (1 - x, 1 - y))):
                for who in range(CORES):
                    for ch in chunks:
                        all_part(2 * xx + who, yy, ch)[...] = late_refs[i][who, span_of(ch)]
            for i, xx in enumerate((x, 1 - x)):
                for who in range(CORES):
                    out_part(2 * xx + who)[...] = late_out_refs[i][who]

    if last:
        for i in range(3):
            t3_copy(i).wait_recv()
        t1_buf[...] = (t2_sum[...] + t3_buf[0]) + (t3_buf[1] + t3_buf[2])

        @pl.when(c == layer)
        def _():
            for i in range(3):
                g3_copy(i).wait_recv()
            total = (g_all[...] + g_buf[4]) + (g_buf[5] + g_buf[6])
            t1_buf[6:7, :D] = total[0:1]
            for away in (1, 2, 3):
                g2_copy(away).wait_send()
            for i in range(3):
                g3_copy(i).wait_send()

        @pl.when(c != layer)
        def _():
            g1_copy().wait_send()

        own_totals(z, t1_buf, total_refs)

        t1_copy().wait_send()
        for away in (1, 2, 3):
            t2_copy(away).wait_send()
        for i in range(3):
            t3_copy(i).wait_send()
    else:
        g_gather.end()
        dot_gather.end()
        r_core_copy().wait_send()
        r_x_copy().wait_send()

    n_core_copy().wait_send()
    n_x_copy().wait_send()
    for i in range(3):
        for ch in chunks:
            z_copy(shard_at(i), ch).wait_send()
    for i in range(4):
        for ch in chunks[2:]:
            y_copy(shard_at(i), ch).wait_send()

    if last:

        @pl.when(c != layer)
        def _():
            for ch in chunks:
                owner_copy(ch).wait_send()
            owner_out_copy().wait_send()


def small_totals(layer, quarter, refs, norm_grad, tiny):
    conv_ref, gain_ref, head_ref = refs
    width, group = DI // GROUP, DI // 16
    lane = iota((8, width), 1)
    wide = jnp.where(iota((8, width), 0) == 5, jnp.broadcast_to(gain_ref[0:1], (8, width)), conv_ref[:, :width])
    for zz in range(4):
        moved = turn_by(wide, group, [(k - zz) % GROUP for k in range(GROUP)], quarter)
        tiny[layer, :, zz * width : (zz + 1) * width] = jnp.where(
            lax.div(lane, group) == quarter, moved, 0.0
        )
    tiny[layer, :, DI:] = conv_ref[:, width:]
    tiny[layer, 6:7, :D] = jnp.zeros((1, D), jnp.float32) if norm_grad is None else norm_grad
    per = H // 16
    given, head = iota((LANES, LANES), 0), iota((LANES, LANES), 1)
    taken = (lax.rem(lax.div(head, per), 4) == quarter) & (head < H)
    taken = taken & (given == lax.div(head, 4 * per) * per + lax.rem(head, per))
    heads = exact(head_ref[...], jnp.where(taken, 1.0, 0.0))
    for row in range(3):
        tiny[layer, 6:7, D + row * LANES : D + (row + 1) * LANES] = heads[row : row + 1]


def own_totals(z, whole, refs):
    norm_ref, taps_ref, bias_ref, *head_refs, gain_ref = refs
    piece = CONV // 4
    taps = turn_by(whole[...], piece, [(4 - k) % 4 for k in range(4)], z)
    taps_ref[...] = taps[0:KW, :piece]
    bias_ref[...] = taps[KW : KW + 1, :piece]
    width = DI // 4
    gain_ref[...] = whole[:, pl.ds(pl.multiple_of(z * width, LANES), width)][5:6]
    norm_ref[...] = whole[:, pl.ds(pl.multiple_of(z * LANE_PART, LANES), LANE_PART)][6:7]
    per = H // 4
    for row, ref in enumerate(head_refs):
        heads = whole[:, D + row * LANES : D + (row + 1) * LANES]
        heads = turn_by(heads, 1, [(LANES - k * per) % LANES for k in range(4)], z)
        ref[...] = heads[6:7, :per]


def layer_sums(layer, gate, grad, out_grad, theirs, mine, entering, incoming, gain, extra, *more):
    dma = pltpu.SemaphoreType.DMA
    inside = pl.BlockSpec(memory_space=pltpu.VMEM)
    span = (HALF, LANE_PART)
    out = (OUT_PART, D)
    steps = len(STEPS)
    two = (CORES, steps)
    rows = entering.shape
    half, whole = jnp.bfloat16, jnp.float32
    last = layer == 0
    out_shape = [
        jax.ShapeDtypeStruct((GROUP, LOCAL, LANE_PART) if last else span, half),
        jax.ShapeDtypeStruct((DI // GROUP, D) if last else out, half),
        jax.ShapeDtypeStruct(rows, half),
    ]
    scratch = [
        pltpu.VMEM(theirs.shape, half),
        pltpu.VMEM(rows, half),
        pltpu.VMEM(rows, half),
        pltpu.VMEM((4,) + span, half),
        pltpu.VMEM((5,) + span, half),
        pltpu.VMEM((4,) + span, half),
        pltpu.VMEM(out, half),
        pltpu.VMEM(out, half),
        dma((4, steps)), dma((4, steps)), dma((4, steps)), dma((5, steps)), dma((2,)),
        dma((steps + 1,)), dma((steps + 1,)),
        dma(two), dma(two), dma(two), dma(two), dma(two), dma(two),
        dma((CORES,)), dma((CORES,)), dma((4,)),
    ]
    if layer == 0:
        small = (8, CONV)
        piece = CONV // 4
        shapes = ((1, LANE_PART), (KW, piece), (1, piece)) + ((1, H // 4),) * 3 + ((1, DI // 4),)
        out_shape += [jax.ShapeDtypeStruct(shape, whole) for shape in shapes]
        scratch += [
            pltpu.VMEM((CORES,) + small, whole),
            pltpu.VMEM(small, whole),
            pltpu.VMEM(small, whole),
            pltpu.VMEM((3,) + small, whole),
            pltpu.VMEM(small, whole),
            pltpu.VMEM((3,) + small, whole),
            pltpu.VMEM((8, D), whole),
            pltpu.VMEM((7, 8, D), whole),
            pltpu.VMEM((8, D), whole),
            pltpu.VMEM((8, D), whole),
            dma((7,)), dma((7,)), dma((7,)), dma((7,)),
        ]
    else:
        out_shape += [
            jax.ShapeDtypeStruct(rows, half),
            jax.ShapeDtypeStruct((GROUP * rows[0], D), half),
            jax.ShapeDtypeStruct((GROUP, 8, LANES), whole),
            jax.ShapeDtypeStruct((1, D), whole),
        ]
        out_shape += [jax.ShapeDtypeStruct((8, LANES), whole)] * 3
        scratch += [
            pltpu.VMEM(theirs.shape, half),
            pltpu.VMEM(rows, half),
            pltpu.VMEM(rows, half),
            dma((3,)), dma((3,)), dma((3,)), dma((3,)), dma((4,)),
        ]
    return pl.pallas_call(
        functools.partial(sum_kernel, layer),
        in_specs=[inside] * (9 + len(more)),
        out_specs=[inside] * 10,
        out_shape=out_shape,
        scratch_shapes=scratch,
        compiler_params=pltpu.CompilerParams(
            collective_id=2 + layer, has_side_effects=True, vmem_limit_bytes=VMEM_BYTES
        ),
        name="layer_sums",
    )(gate, grad, out_grad, theirs, mine, entering, incoming, gain, extra, *more)


def assemble_kernel(part_ref, shared_ref, out_ref, total_ref, out_total_ref):
    turn = pl.program_id(0)
    step = DI // 16

    @pl.when(turn == 8)
    def _():
        shared = [shared_ref[i, :SHARED].astype(jnp.float32) for i in range(GROUP)]
        total_ref[:SHARED] = (shared[0] + shared[1]) + (shared[2] + shared[3])

    @pl.when(turn < 8)
    def _():
        for i in range(GROUP):
            total_ref[i * step : (i + 1) * step] = part_ref[i].astype(jnp.float32)
        out_total_ref[0] = out_ref[...].astype(jnp.float32)


def assemble_rows(parts, out):
    lanes = parts.shape[-1]
    step = DI // 16
    some = out.shape[0] // 8

    def near(i):
        return jnp.minimum(i, 7)

    return pl.pallas_call(
        assemble_kernel,
        grid=(9,),
        in_specs=[
            pl.BlockSpec((GROUP, step, lanes), lambda i: (0, near(i), 0)),
            pl.BlockSpec((GROUP, 2 * step, lanes), lambda i: (0, 4, 0)),
            pl.BlockSpec((some, out.shape[1]), lambda i: (near(i), 0)),
        ],
        out_specs=[
            pl.BlockSpec((GROUP * step, lanes), lambda i: (i, 0)),
            pl.BlockSpec((1, some, out.shape[1]), lambda i: (0, near(i), 0)),
        ],
        out_shape=[
            jax.ShapeDtypeStruct((DI + CONV + H, lanes), jnp.float32),
            jax.ShapeDtypeStruct((1,) + out.shape, jnp.float32),
        ],
        compiler_params=pltpu.CompilerParams(vmem_limit_bytes=VMEM_BYTES),
        name="assemble_rows",
    )(parts, parts, out)


def per_device_split(
    boundary_in,
    lengths,
    seq_order,
    norm_gain,
    in_weight,
    conv_weight,
    conv_bias,
    dt_bias,
    a_log,
    d_skip,
    out_gain,
    out_weight,
):
    c = lax.axis_index("section")
    z = lax.axis_index("shard")
    r = lax.axis_index("rep")
    y, x = r // 2, r % 2
    block = boundary_in.shape[3]
    rows = GROUP * block
    width = DI // GROUP
    heads = H // GROUP
    span = width + 2 * N
    quarter = 2 * x + c

    def spot(cc, zz, rr):
        return (cc * 4 + zz) * 4 + rr

    def home(m, zz, rr):
        return spot(zz % 2, 2 * m + rr % 2, (rr // 2) * 2 + zz // 2)

    axes = ("section", "shard", "rep")

    params = (norm_gain, conv_weight, conv_bias, dt_bias, a_log, d_skip, out_gain)
    lanes = -(-conv_bias.shape[1] // LANES) * LANES
    given = (conv_weight[0], conv_bias, out_gain, norm_gain, dt_bias, a_log, d_skip)
    flat = [jnp.pad(p, ((0, 0), (0, lanes - p.shape[1]))) for p in given]
    flat = jnp.concatenate(flat + [jnp.zeros((6, lanes), jnp.bfloat16)], axis=0)
    in_rows = jnp.swapaxes(in_weight[0], 0, 1)
    w_in0, w_out0, source, normed0, small, norms = enter_first(
        in_rows, out_weight[0], boundary_in, flat
    )
    late_in = after(boundary_in, source)[0, :, 0]
    arrivals = [
        lax.ppermute(
            late_in[m], axes, [(spot(1, zz, rr), home(m, zz, rr)) for zz in range(4) for rr in range(4)]
        )
        for m in range(MICRO)
    ]
    cotangent = jnp.where(z < 2, *arrivals)

    order = jnp.stack([lengths[:, 0], seq_order[:, 0]])
    order = jnp.where(x == z % 2, order, swap_x(order))
    order = lax.dynamic_index_in_dim(order, z // 2, 1, False)
    chosen = (order[1][:, None] == jnp.arange(NSEQ, dtype=jnp.int32)[None, :]).astype(jnp.int32)
    finish = jnp.cumsum(jnp.sum(chosen * order[0][None, :], axis=1), dtype=jnp.int32)

    def segment_of(positions):
        found = jnp.sum((positions[:, None] >= finish[None, :]).astype(jnp.int32), axis=1)
        return jnp.where(positions < 0, -1, found)

    token = jnp.arange(rows, dtype=jnp.int32)
    segment = segment_of(token)
    opening = token // Q * Q
    columns = [segment_of(token - lag) == segment for lag in range(1, KW)]
    columns.append(segment_of(opening - 1) == segment)
    columns.append(segment_of(opening + (Q - 1)) == segment)
    columns = [column.astype(jnp.float32) for column in columns] + [segment.astype(jnp.float32)]
    marks = jnp.stack(columns + [jnp.zeros((rows,), jnp.float32)] * 2, axis=1)
    seg_row = segment.astype(jnp.float32)[None]

    def own(v):
        return lax.dynamic_slice_in_dim(v, (2 * x + c) * block, block, 0)

    def row_sums(v):
        v = v + swap_core(v)
        return v + swap_x(v)

    def forward(layer, normed, w_in):
        projected = projection(normed, w_in)
        gg, squares, mixer, starts = mixer_forward(layer, projected, marks, seg_row, small)
        return gg, squares.reshape((rows // LANES, LANES)), (normed, projected, mixer, starts)

    def inverse(sums):
        return lax.rsqrt(sums / DI + EPSILON)

    def out_sum(gg, out_inv, g):
        outgoing = low(gg.astype(jnp.float32) * out_inv)
        grad = low(mm(outgoing, g, 0, 0)).reshape((4, OUT_PART, D))
        return lax.psum_scatter(grad, "shard", scatter_dimension=0, tiled=False)

    def backward(layer, kept, og, per_row, ready=(), sent_on=()):
        normed, projected, out, starts = kept
        gate_grad, out_grad, gains = gate_backward(
            layer, projected, small, out, og, per_row, DI
        )
        gate = low(mm(gate_grad, normed, 0, 0)).reshape((2, GATE_HALF, D))
        sent = lax.dynamic_index_in_dim(gate, 1 - y, 0, False)
        received = swap_y(sent)
        gate = lax.dynamic_index_in_dim(gate, y, 0, False)
        pg, conv, head = mixer_backward(
            layer, projected, marks, seg_row, small, out, starts, out_grad, after(gate_grad, sent, *ready)
        )
        pg = after(pg, *sent_on)
        gate = low(gate.astype(jnp.float32) + received.astype(jnp.float32))
        rest = low(mm(pg[:, GATE:], normed, 0, 0))
        return pg, gate, rest, (conv, gains, head)

    gg0, squares0, kept0 = forward(0, normed0, w_in0)
    theirs, mine = group_parts(gg0, w_out0)
    w_in1, w_out1, added0, middle, normed1, g1, out_inv0 = enter_second(
        in_rows, out_weight[0], theirs, mine, squares0, source, norms[1, 0:1], cotangent
    )
    out_inv0 = out_inv0.reshape((rows, 1))
    og1 = mm(g1, w_out1, 1, 1)
    gg1, squares1, kept1 = forward(1, normed1, w_in1)
    dots1 = jnp.sum(gg1.astype(jnp.float32) * og1, axis=1).reshape((rows // LANES, LANES))
    sums1 = row_sums(jnp.stack([squares1, dots1]))
    out_inv1 = inverse(sums1[0]).reshape((rows, 1))
    per_row1 = jnp.concatenate([out_inv1, out_inv1 * sums1[1].reshape((rows, 1))], axis=1)
    out_theirs, out_mine = group_parts(gg1, w_out1)
    out_part1 = out_sum(gg1, out_inv1, g1)
    pg1, gate1, rest1, small_grads1 = backward(1, kept1, og1, per_row1)
    theirs, mine = group_parts(pg1, w_in1)
    in_sum1, out_sum1, result, middle_grad, g0, dots0, norm_grad1, *_ = layer_sums(
        1, gate1, rest1, out_part1, theirs, mine, middle, cotangent, norms[1, 0:1], added0,
        out_theirs, out_mine, own(out_inv1),
    )
    dots0 = dots0[:, : block // LANES].reshape((rows, 1))

    def on_second(v, flip):
        return lax.ppermute(v, ("section", "rep"), [(4 + i, 4 + (i ^ flip)) for i in range(4)])

    def to_second(v):
        return jnp.stack([lax.ppermute(v, "section", [(0, 1)]), v])

    in_own, out_own = to_second(in_sum1), to_second(out_sum1)
    in_near, in_across = on_second(in_own, 1), on_second(in_own, 2)
    out_near = on_second(out_own, 1)
    in_far = on_second(in_across, 1)

    def go_home(value, cc):
        return [
            lax.ppermute(
                value, axes, [(home(m, zz, rr), spot(cc, zz, rr)) for zz in range(4) for rr in range(4)]
            )
            for m in range(MICRO)
        ]

    results = go_home(result, 1)

    og0 = mm(g0, w_out0, 1, 1)
    out_part0 = out_sum(gg0, out_inv0, after(g0, *results))
    per_row0 = jnp.concatenate([out_inv0, dots0], axis=1)
    pg0, gate0, rest0, small_grads0 = backward(
        0, kept0, og0, per_row0, (in_own, out_own), (in_near, in_across, out_near)
    )
    theirs, mine = group_parts(pg0, w_in0)
    in_all, out_all, entry_grad, *totals = layer_sums(
        0, gate0, rest0, out_part0, theirs, mine, source, middle_grad, norms[0, 0:1], norm_grad1,
        *small_grads0, *small_grads1, in_own, in_near, in_across, in_far, out_own, out_near,
    )
    entry_grads = go_home(entry_grad, 0)
    in_total, out_total = assemble_rows(in_all, out_all)
    in_total = jnp.swapaxes(in_total, 0, 1)[None]

    boundary = jnp.stack(
        [jnp.where(c == 0, entry_grads[m], results[m]) for m in range(MICRO)]
    ).astype(jnp.float32)[None, :, None]

    norm_total, conv_total, bias_total, dt_total, log_total, skip_total, gain_total = totals
    return (
        boundary,
        norm_total,
        in_total,
        conv_total[None],
        bias_total,
        dt_total,
        log_total,
        skip_total,
        gain_total,
        out_total,
    )


def solution(mesh):
    fits = mesh.shape["shard"] == GROUP and mesh.shape["rep"] == 4
    return jax.shard_map(
        per_device_split if fits else per_device,
        mesh=mesh,
        in_specs=(
            P("section", None, "rep", "shard", None),
            P(None, "rep", None),
            P(None, "rep", None),
            P("section", "shard"),
            P("section", "shard", None),
            P("section", None, "shard"),
            P("section", "shard"),
            P("section", "shard"),
            P("section", "shard"),
            P("section", "shard"),
            P("section", "shard"),
            P("section", "shard", None),
        ),
        out_specs=(
            P("section", None, "rep", "shard", None),
            P("section", "shard"),
            P("section", "shard", None),
            P("section", None, "shard"),
            P("section", "shard"),
            P("section", "shard"),
            P("section", "shard"),
            P("section", "shard"),
            P("section", "shard"),
            P("section", "shard", None),
        ),
        check_vma=False,
    )
```

```python
import functools

import jax
import jax.numpy as jnp
from jax import lax
from jax.experimental import pallas as pl
from jax.experimental.pallas import tpu as pltpu
from jax.sharding import PartitionSpec as P

D = 1536
P_SIZE = 64
N = 128
KW = 4
BLOCK = 256
MICRO = 2
NSEQ = 4
DI = 3072
H = 48
CONV = 3328


EPSILON = 1e-05
PRECISE = lax.Precision.HIGHEST


def from_behind(shard, axis, by):
    devices = lax.axis_size(axis)
    pairs = [(i, i + by) for i in range(devices) if 0 <= i + by < devices]
    return lax.ppermute(shard, axis, pairs)


def entering(value, axis, join, neutral):
    count, mine = (lax.axis_size(axis), lax.axis_index(axis))
    pieces = jax.tree.map(lambda part: lax.all_gather(part, axis), value)
    subtotal = jax.tree.map(
        lambda part, zero: jnp.full_like(part, 0) + jnp.asarray(zero, part.dtype), value, neutral
    )

    def turn(position, subtotal):
        longer = join(subtotal, jax.tree.map(lambda part: part[position], pieces))
        return jax.tree.map(lambda new, old: jnp.where(position < mine, new, old), longer, subtotal)

    return lax.fori_loop(0, count - 1, turn, subtotal)


def entering_2(shard, axis, join, neutral):
    count = lax.axis_size(axis)
    place = lax.axis_index(axis)
    ahead = count - 1 - place
    gathered = jax.tree.map(
        lambda a, kind: lax.all_gather(a.astype(kind), axis),
        shard,
        jax.tree.map(lambda a: jnp.bfloat16 if a.dtype == jnp.float32 else a.dtype, shard),
    )
    state = jax.tree.map(lambda a, e: jnp.zeros_like(a) + jnp.asarray(e, a.dtype), shard, neutral)

    def one(turn, state):
        source = count - 1 - turn
        return join(
            state,
            jax.tree.map(
                lambda a, own: lax.dynamic_index_in_dim(a, source, 0, False).astype(own.dtype),
                gathered,
                shard,
            ),
        )

    return lax.fori_loop(0, ahead, one, state)


def contract(left, right, left_dim, right_dim):
    return lax.dot_general(
        left, right, (((left_dim,), (right_dim,)), ((), ())), preferred_element_type=jnp.float32
    )


def input_norm(source, gain):
    inv_rms = lax.rsqrt(jnp.mean(source * source, axis=-1, keepdims=True) + EPSILON)
    return source * inv_rms * gain


def block_step(carry_state, pieces):
    x_heads, b_rows, c_rows, log_decay, step_size, segment, before = pieces
    running = jnp.cumsum(log_decay, axis=0)
    places = jnp.arange(x_heads.shape[0])
    linked = (places[:, None] >= places[None, :]) & (segment[:, None] == segment[None, :])
    linked3 = linked[:, :, None]
    gap_sums = jnp.where(linked3, running[:, None, :] - running[None, :, :], 0.0)
    decays = jnp.where(linked3, jnp.exp(gap_sums), 0.0)
    scores = jnp.dot(c_rows, b_rows.T, precision=PRECISE)
    mixing = scores[:, :, None] * decays * step_size[None, :, :]
    inside_part = jnp.einsum("tsh,shp->thp", mixing, x_heads, precision=PRECISE)
    carried = (segment == before).astype(jnp.float32)
    reach = jnp.exp(running) * carried[:, None]
    carried_part = (
        jnp.einsum("tn,hpn->thp", c_rows, carry_state, precision=PRECISE) * reach[:, :, None]
    )
    closing = segment[-1]
    tail_weight = (
        jnp.exp(running[-1][None, :] - running)
        * step_size
        * (segment == closing).astype(jnp.float32)[:, None]
    )
    fresh_state = jnp.einsum("sh,shp,sn->hpn", tail_weight, x_heads, b_rows, precision=PRECISE)
    retained = jnp.exp(running[-1]) * (closing == before).astype(jnp.float32)
    return (retained[:, None, None] * carry_state + fresh_state, inside_part + carried_part)


def conv_inputs(wide_rows, raw_step, conv_weight, conv_bias, dt_bias, a_log, lag_masks):
    rows_here = raw_step.shape[0]
    conv_sum = conv_bias + conv_weight[KW - 1] * wide_rows[KW - 1 :]
    for lag in range(1, KW):
        conv_sum = (
            conv_sum
            + conv_weight[KW - 1 - lag]
            * wide_rows[KW - 1 - lag : KW - 1 - lag + rows_here]
            * lag_masks[lag - 1][:, None]
        )
    active = jax.nn.silu(conv_sum)
    x_heads = active[:, :DI].reshape(rows_here, H, P_SIZE)
    b_rows = active[:, DI : DI + N]
    c_rows = active[:, DI + N :]
    step_size = jax.nn.softplus(raw_step + dt_bias)
    log_decay = -step_size * jnp.exp(a_log)
    return (x_heads, b_rows, c_rows, log_decay, step_size)


def local_scan(x_heads, b_rows, c_rows, log_decay, step_size, segment, befores, seg_before):
    rows_here = x_heads.shape[0]

    def blocks(member):
        return member.reshape((rows_here // BLOCK, BLOCK) + member.shape[1:])

    start_state = jnp.zeros((H, P_SIZE, N), jnp.float32)
    pieces = (
        blocks(x_heads),
        blocks(b_rows),
        blocks(c_rows),
        blocks(log_decay),
        blocks(step_size),
        blocks(segment),
        befores,
    )
    end_state, mixer_out = lax.scan(jax.checkpoint(block_step), start_state, pieces)
    retained = jnp.exp(jnp.sum(log_decay, axis=0)) * (segment[-1] == seg_before).astype(jnp.float32)
    return (mixer_out.reshape(rows_here, H, P_SIZE), end_state, retained)


def state_entry(c_rows, log_decay, state_in, carried):
    reach = jnp.exp(jnp.cumsum(log_decay, axis=0)) * carried[:, None]
    return jnp.einsum("tn,hpn->thp", c_rows, state_in, precision=PRECISE) * reach[:, :, None]


def gate_norm(mixer_out, x_heads, d_skip, gate_part, out_gain):
    rows_here = x_heads.shape[0]
    total_out = mixer_out + d_skip[:, None] * x_heads
    gated = total_out.reshape(rows_here, DI) * jax.nn.silu(gate_part)
    inv_gated = lax.rsqrt(jnp.mean(gated * gated, axis=-1, keepdims=True) + EPSILON)
    return gated * inv_gated * out_gain


def carry_forward(earlier, later):
    return (earlier[0] * later[0], later[0][:, None, None] * earlier[1] + later[1])


def carry_backward(earlier, later):
    return (later[0] * earlier[0], later[1] + later[0][:, None, None] * earlier[1])


def segment_marks(lengths, seq_order, micro_slot, row_start, rows_here):
    micro_slot = jnp.clip(micro_slot, 0, MICRO - 1)
    seq_lengths = lax.dynamic_index_in_dim(lengths[:, 0], micro_slot, 0, keepdims=False)
    row_order = lax.dynamic_index_in_dim(seq_order[:, 0], micro_slot, 0, keepdims=False)
    picks = (row_order[:, None] == jnp.arange(NSEQ, dtype=jnp.int32)[None, :]).astype(jnp.int32)
    placed = jnp.sum(picks * seq_lengths[None, :], axis=1)
    finish = jnp.cumsum(placed, dtype=jnp.int32)
    positions = row_start + jnp.arange(-(KW - 1), rows_here, dtype=jnp.int32)
    extended = jnp.sum((positions[:, None] >= finish[None, :]).astype(jnp.int32), axis=1)
    extended = jnp.where(positions < 0, -1, extended)
    segment = extended[KW - 1 :]
    seg_before = extended[KW - 2]
    lag_masks = jnp.stack(
        [
            (extended[KW - 1 - lag : KW - 1 - lag + rows_here] == segment).astype(jnp.float32)
            for lag in range(1, KW)
        ]
    )
    befores = jnp.concatenate([seg_before[None], segment[:-1]])[::BLOCK]
    carried = (segment == seg_before).astype(jnp.float32)
    return (segment, lag_masks, befores, seg_before, carried)


def mixer_pass(projected, weights, marks):
    norm_gain, in_weight, conv_weight, conv_bias, dt_bias, a_log, d_skip, out_gain, out_weight = (
        weights
    )
    segment, lag_masks, befores, seg_before, carried = marks
    rows_here = projected.shape[0]
    gate_part = projected[:, :DI].astype(jnp.float32)
    mixed_part = projected[:, DI : DI + CONV]
    raw_step = projected[:, DI + CONV :].astype(jnp.float32)
    rim_rows = from_behind(mixed_part[rows_here - (KW - 1) :], "shard", 1)
    wide_rows = jnp.concatenate([rim_rows, mixed_part], axis=0).astype(jnp.float32)

    def conv_section(wide_rows, raw_step, conv_weight, conv_bias, dt_bias, a_log):
        return conv_inputs(wide_rows, raw_step, conv_weight, conv_bias, dt_bias, a_log, lag_masks)

    conv_outs, conv_pull = jax.vjp(
        conv_section, wide_rows, raw_step, conv_weight, conv_bias, dt_bias, a_log
    )
    x_heads, b_rows, c_rows, log_decay, step_size = conv_outs

    def scan_section(x_heads, b_rows, c_rows, log_decay, step_size):
        return local_scan(
            x_heads, b_rows, c_rows, log_decay, step_size, segment, befores, seg_before
        )

    scan_outs, scan_pull = jax.vjp(scan_section, x_heads, b_rows, c_rows, log_decay, step_size)
    local_out, end_state, retained = scan_outs
    identity = (jnp.ones((H,), jnp.float32), jnp.zeros((H, P_SIZE, N), jnp.float32))
    prefix = entering((retained, end_state), "shard", carry_forward, identity)
    state_in = prefix[1]

    def entry_section(c_rows, log_decay, state_in):
        return state_entry(c_rows, log_decay, state_in, carried)

    entered, entry_pull = jax.vjp(entry_section, c_rows, log_decay, state_in)
    mixer_out = local_out + entered
    outgoing, norm_pull = jax.vjp(gate_norm, mixer_out, x_heads, d_skip, gate_part, out_gain)
    return (
        outgoing.astype(jnp.bfloat16),
        (conv_pull, scan_pull, entry_pull, norm_pull, retained, state_in),
    )


def mamba_forward(source, weights, marks):
    normed = input_norm(source, weights[0]).astype(jnp.bfloat16)
    projected = jnp.dot(normed, weights[1], preferred_element_type=jnp.float32).astype(jnp.bfloat16)
    outgoing, unused_pulls = mixer_pass(projected, weights, marks)
    return source + jnp.dot(outgoing, weights[8], preferred_element_type=jnp.float32)


def mamba_backward(source, incoming, weights, marks):
    norm_gain, in_weight, conv_weight, conv_bias, dt_bias, a_log, d_skip, out_gain, out_weight = (
        weights
    )
    rows_here = source.shape[0]
    normed, front_pull = jax.vjp(input_norm, source, norm_gain)
    normed_low = normed.astype(jnp.bfloat16)
    projected = jnp.dot(normed_low, in_weight, preferred_element_type=jnp.float32).astype(
        jnp.bfloat16
    )
    outgoing, pulls = mixer_pass(projected, weights, marks)
    conv_pull, scan_pull, entry_pull, norm_pull, retained, state_in = pulls
    incoming_low = incoming.astype(jnp.bfloat16)
    out_weight_grad = contract(outgoing, incoming_low, 0, 0)
    outgoing_grad = contract(incoming_low, out_weight, 1, 1)
    mixer_grad, x_grad_a, d_skip_grad, gate_grad, out_gain_grad = norm_pull(outgoing_grad)
    c_grad_a, decay_grad_a, direct = entry_pull(mixer_grad)
    identity = (jnp.ones((H,), jnp.float32), jnp.zeros((H, P_SIZE, N), jnp.float32))
    suffix = entering_2((retained, direct), "shard", carry_backward, identity)
    later_grad = suffix[1]
    retained_grad = jnp.sum(later_grad * state_in, axis=(1, 2))
    x_grad_b, b_grad, c_grad_b, decay_grad_b, step_grad = scan_pull(
        (mixer_grad, later_grad, retained_grad)
    )
    conv_grads = conv_pull(
        (x_grad_a + x_grad_b, b_grad, c_grad_a + c_grad_b, decay_grad_a + decay_grad_b, step_grad)
    )
    wide_grad, raw_grad, conv_weight_grad, conv_bias_grad, dt_bias_grad, a_log_grad = conv_grads
    back_rows = from_behind(wide_grad[: KW - 1].astype(jnp.bfloat16), "shard", -1).astype(
        jnp.float32
    )
    filler = jnp.zeros((rows_here - (KW - 1), CONV), jnp.float32)
    mixed_grad = wide_grad[KW - 1 :] + jnp.concatenate([filler, back_rows], axis=0)
    projected_grad = jnp.concatenate([gate_grad, mixed_grad, raw_grad], axis=1).astype(jnp.bfloat16)
    in_weight_grad = contract(normed_low, projected_grad, 0, 0)
    normed_grad = contract(projected_grad, in_weight, 1, 1)
    source_grad, norm_gain_grad = front_pull(normed_grad)
    weight_grads = (
        norm_gain_grad,
        in_weight_grad,
        conv_weight_grad,
        conv_bias_grad,
        dt_bias_grad,
        a_log_grad,
        d_skip_grad,
        out_gain_grad,
        out_weight_grad,
    )
    return (incoming + source_grad, weight_grads)


def per_device(
    boundary_in,
    lengths,
    seq_order,
    norm_gain,
    in_weight,
    conv_weight,
    conv_bias,
    dt_bias,
    a_log,
    d_skip,
    out_gain,
    out_weight,
):
    section_index = lax.axis_index("section")
    is_first = section_index == 0
    rows_here = boundary_in.shape[3]
    row_start = lax.axis_index("shard") * rows_here

    def current():
        whole = (
            lax.all_gather(norm_gain, "shard", axis=1, tiled=True),
            lax.all_gather(in_weight, "shard", axis=1, tiled=True),
            lax.all_gather(conv_weight, "shard", axis=2, tiled=True),
            lax.all_gather(conv_bias, "shard", axis=1, tiled=True),
            lax.all_gather(dt_bias, "shard", axis=1, tiled=True),
            lax.all_gather(a_log, "shard", axis=1, tiled=True),
            lax.all_gather(d_skip, "shard", axis=1, tiled=True),
            lax.all_gather(out_gain, "shard", axis=1, tiled=True),
            lax.all_gather(out_weight, "shard", axis=1, tiled=True),
        )
        return tuple(
            (
                member[0] if slot_index in (1, 8) else member[0].astype(jnp.float32)
                for slot_index, member in enumerate(whole)
            )
        )

    source_rows = boundary_in[0, :, 0]
    arrived = jnp.zeros((rows_here, D), jnp.bfloat16)
    inputs = []
    results = []
    for step_index in range(MICRO + 1):
        own_rows = source_rows[min(step_index, MICRO - 1)]
        layer_in = jnp.where(is_first, own_rows, arrived)
        inputs.append(layer_in)
        marks = segment_marks(lengths, seq_order, step_index - section_index, row_start, rows_here)
        layer_out = mamba_forward(layer_in.astype(jnp.float32), current(), marks)
        results.append(layer_out)
        if step_index < MICRO:
            arrived = from_behind(layer_out.astype(jnp.bfloat16), "section", 1)
    returned = jnp.zeros((rows_here, D), jnp.bfloat16)
    totals = None
    source_grads = []
    for step_index in range(MICRO + 1):
        micro_slot = step_index - 1 + section_index
        is_valid = (micro_slot >= 0) & (micro_slot < MICRO)
        own_rows = source_rows[min(step_index, MICRO - 1)]
        incoming = jnp.where(is_first, returned, own_rows).astype(jnp.float32)
        incoming = jnp.where(is_valid, incoming, 0.0)
        layer_in = jnp.where(
            is_first, inputs[max(step_index - 1, 0)], inputs[min(step_index + 1, MICRO)]
        )
        marks = segment_marks(lengths, seq_order, micro_slot, row_start, rows_here)
        source_grad, weight_grads = mamba_backward(
            layer_in.astype(jnp.float32), incoming, current(), marks
        )
        if totals is None:
            totals = tuple(weight_grads)
        else:
            totals = tuple((earlier + added for earlier, added in zip(totals, weight_grads)))
        source_grads.append(source_grad)
        if step_index < MICRO:
            returned = from_behind(source_grad.astype(jnp.bfloat16), "section", -1)
    boundary = jnp.stack(
        [
            jnp.where(is_first, source_grads[micro_pos + 1], results[micro_pos + 1])
            for micro_pos in range(MICRO)
        ]
    )[None, :, None]
    shares = (
        lax.psum_scatter(
            totals[0][None].astype(jnp.bfloat16), "shard", scatter_dimension=1, tiled=True
        ).astype(jnp.float32),
        lax.psum_scatter(
            totals[1][None].astype(jnp.bfloat16), "shard", scatter_dimension=1, tiled=True
        ).astype(jnp.float32),
        lax.psum_scatter(
            totals[2][None].astype(jnp.bfloat16), "shard", scatter_dimension=2, tiled=True
        ).astype(jnp.float32),
        lax.psum_scatter(
            totals[3][None].astype(jnp.bfloat16), "shard", scatter_dimension=1, tiled=True
        ).astype(jnp.float32),
        lax.psum_scatter(
            totals[4][None].astype(jnp.bfloat16), "shard", scatter_dimension=1, tiled=True
        ).astype(jnp.float32),
        lax.psum_scatter(
            totals[5][None].astype(jnp.bfloat16), "shard", scatter_dimension=1, tiled=True
        ).astype(jnp.float32),
        lax.psum_scatter(
            totals[6][None].astype(jnp.bfloat16), "shard", scatter_dimension=1, tiled=True
        ).astype(jnp.float32),
        lax.psum_scatter(
            totals[7][None].astype(jnp.bfloat16), "shard", scatter_dimension=1, tiled=True
        ).astype(jnp.float32),
        lax.psum_scatter(
            totals[8][None].astype(jnp.bfloat16), "shard", scatter_dimension=1, tiled=True
        ).astype(jnp.float32),
    )
    reduced = (
        lax.psum(shares[0].astype(jnp.bfloat16), "rep").astype(jnp.float32),
        lax.psum(shares[1].astype(jnp.bfloat16), "rep").astype(jnp.float32),
        lax.psum(shares[2].astype(jnp.bfloat16), "rep").astype(jnp.float32),
        lax.psum(shares[3].astype(jnp.bfloat16), "rep").astype(jnp.float32),
        lax.psum(shares[4].astype(jnp.bfloat16), "rep").astype(jnp.float32),
        lax.psum(shares[5].astype(jnp.bfloat16), "rep").astype(jnp.float32),
        lax.psum(shares[6].astype(jnp.bfloat16), "rep").astype(jnp.float32),
        lax.psum(shares[7].astype(jnp.bfloat16), "rep").astype(jnp.float32),
        lax.psum(shares[8].astype(jnp.bfloat16), "rep").astype(jnp.float32),
    )
    return (boundary,) + tuple(reduced)


Q = 128
LANES = 128
VMEM_BYTES = 56 * 1024 * 1024
EXACT = lax.Precision.HIGHEST


def mm(a, b, da=1, db=0):
    return lax.dot_general(
        a, b, (((da,), (db,)), ((), ())), preferred_element_type=jnp.float32
    )


def exact(a, b):
    return jnp.dot(a, b, precision=EXACT, preferred_element_type=jnp.float32)


def low(v):
    return v.astype(jnp.bfloat16)


def split(v, parts):
    found = []
    for _ in range(parts):
        found.append(low(v))
        v = v - found[-1].astype(jnp.float32)
    return found


def pick_sums(v, ones, parts=2):
    return sum(mm(part, ones) for part in split(v, parts))


def sums_of(ones, v, parts=3):
    return sum(mm(ones, part) for part in split(v, parts))


def iota(shape, dim):
    return lax.broadcasted_iota(jnp.int32, shape, dim)


def pair_cols(v, p):
    rows = v.shape[0]
    left = jnp.broadcast_to(v[:, 2 * p : 2 * p + 1], (rows, LANES))
    right = jnp.broadcast_to(v[:, 2 * p + 1 : 2 * p + 2], (rows, LANES))
    return jnp.where(iota((rows, LANES), 1) < LANES // 2, left, right)


def widen(v, pairs):
    return jnp.concatenate([pair_cols(v, p) for p in range(pairs)], axis=1)


def stack_pair(v, p):
    block = v[:, p * LANES : (p + 1) * LANES]
    left = iota(block.shape, 1) < LANES // 2
    zero = jnp.zeros_like(block)
    return jnp.concatenate([jnp.where(left, block, zero), jnp.where(left, zero, block)], axis=0)


def softplus(v):
    small = jnp.exp(-jnp.abs(v))
    series = small * (1 + small * (-1 / 2 + small * (1 / 3 + small * (-1 / 4 + small / 5))))
    return jnp.maximum(v, 0.0) + jnp.where(small < 0.01, series, jnp.log(1 + small))


def sigmoid(v):
    return 1.0 / (1.0 + jnp.exp(-v))


def gate_of(v):
    return 0.5 * jnp.tanh(0.5 * v) + 0.5


def head_picks():
    quarter = 2 * lax.rem(lax.axis_index("rep"), 2) + lax.axis_index("section")
    given, local = iota((64, LANES), 0), iota((64, LANES), 1)
    per = H // 16
    taken = (lax.rem(lax.div(given, per), 4) == quarter) & (given < H)
    taken = taken & (local == lax.div(given, 4 * per) * per + lax.rem(given, per))
    return jnp.where(taken, 1.0, 0.0).astype(jnp.bfloat16)


def chunk_parts(width, proj, before8, marks, seg_row, small_ref, pick):
    conv_w = small_ref[0, 0:KW]
    conv_b = small_ref[0, KW : KW + 1]
    dt_bias = small_ref[0, 7:8, :LANES]
    rate = small_ref[0, 8:9, :LANES]
    span = width + 2 * LANES
    gate = proj[:, :width].astype(jnp.float32)
    mixed = proj[:, width : width + span].astype(jnp.float32)
    raw = mm(proj[:, width + span :], pick)
    shifts = [mixed]
    top = iota((8, span), 0)
    for lag in range(1, KW):
        rolled = pltpu.roll(mixed, lag, 0)
        head = jnp.where(top < lag, pltpu.roll(before8, lag, 0), rolled[:8])
        moved = jnp.concatenate([head, rolled[8:]], axis=0)
        shifts.append(moved * marks[:, lag - 1 : lag])
    conv = conv_b
    for lag in range(KW):
        conv = conv + conv_w[KW - 1 - lag : KW - lag] * shifts[lag]
    sig = gate_of(conv)
    active = conv * sig
    stepped = raw + dt_bias
    step = softplus(stepped)
    decay = -step * rate
    lower = iota((Q, Q), 0) >= iota((Q, Q), 1)
    total = sums_of(jnp.where(lower, 1.0, 0.0).astype(jnp.bfloat16), decay)
    linked = lower & (marks[:, 5:6] == seg_row)
    shut = jnp.where(linked, 0.0, -1e30)
    reach = jnp.exp(total) * marks[:, 3:4]
    tail = jnp.exp(total[Q - 1 : Q] - total) * marks[:, 4:5]
    return gate, mixed, shifts, conv, sig, active, stepped, step, decay, total, shut, reach, tail


def forward_kernel(
    width, proj_ref, marks_ref, seg_ref, small_ref, gg_ref, squares_ref, mixer_ref, starts_ref, state, before,
):
    pairs = width // LANES

    @pl.when(pl.program_id(0) == 0)
    def _():
        state[...] = jnp.zeros_like(state)
        before[...] = jnp.zeros_like(before)

    gate, mixed, _, _, _, active, _, step, _, total, shut, reach, tail = chunk_parts(
        width, proj_ref[...], before[...], marks_ref[...], seg_ref[...], small_ref, head_picks()
    )
    skip, gain = small_ref[0, 6:7, :width], small_ref[0, 5:6, :width]
    before[...] = mixed[Q - 8 :]
    heads = active[:, :width]
    b_low = low(active[:, width : width + LANES])
    c_low = low(active[:, width + LANES :])
    entry = state[...]
    starts_ref[0] = entry
    scores = mm(c_low, b_low, 1, 1)
    total_t = total.T
    scaled = heads * widen(step, pairs)
    scaled_low = low(scaled)
    inside = []
    for p in range(pairs):
        both = []
        for h in (2 * p, 2 * p + 1):
            both.append(low(jnp.exp(total[:, h : h + 1] - total_t[h : h + 1] + shut) * scores))
        inside.append(mm(jnp.concatenate(both, axis=1), stack_pair(scaled_low, p)))
    mixer = jnp.concatenate(inside, axis=1) + widen(reach, pairs) * mm(c_low, low(entry))
    b_turned = low(active[:, width : width + LANES].T)
    state[...] = entry * widen(reach[Q - 1 : Q], pairs) + mm(
        b_turned, low(scaled * widen(tail, pairs))
    )
    out = mixer + skip * heads
    mixer_ref[...] = out
    gated = out * (gate * gate_of(gate))
    squares = jnp.sum(gated * gated, axis=1, keepdims=True)
    squares_ref[0] = jnp.broadcast_to(squares, (Q, LANES)).T[:1]
    gg_ref[...] = low(gated * gain)


def gate_kernel(width, whole_width, proj_ref, small_ref, out_ref, og_ref, rows_ref, gate_grad_ref, out_grad_ref, sums_ref):
    @pl.when(pl.program_id(0) == 0)
    def _():
        sums_ref[...] = jnp.zeros_like(sums_ref)

    gate = proj_ref[...].astype(jnp.float32)
    inv = rows_ref[:, 0:1]
    dots = rows_ref[:, 1:2]
    og = og_ref[...]
    out = out_ref[...]
    gate_sig = gate_of(gate)
    gate_on = gate * gate_sig
    hat = out * gate_on * inv
    gated_grad = inv * (small_ref[0, 5:6, :width] * og - hat * (dots * (1.0 / whole_width)))
    out_grad_ref[...] = low(gated_grad * gate_on)
    gate_grad_ref[...] = low(gated_grad * out * (gate_sig * (1.0 + gate * (1.0 - gate_sig))))
    sums_ref[0:1] += jnp.sum(hat * og, axis=0, keepdims=True)


def gate_backward(layer, projected, small, out, og, per_row, whole_width):
    rows, width = out.shape
    step = 2 * Q

    def by_row(count):
        return pl.BlockSpec((step, count), lambda i: (i, 0))

    half = jax.ShapeDtypeStruct((rows, width), jnp.bfloat16)
    return pl.pallas_call(
        functools.partial(gate_kernel, width, whole_width),
        grid=(rows // step,),
        in_specs=[by_row(width), small_spec(layer), by_row(width), by_row(width), by_row(2)],
        out_specs=[by_row(width), by_row(width), full_spec((8, width))],
        out_shape=[half, half, jax.ShapeDtypeStruct((8, width), jnp.float32)],
        compiler_params=pltpu.CompilerParams(vmem_limit_bytes=VMEM_BYTES),
        cost_estimate=cost(6),
        name="gate_backward",
    )(projected, small, out, og, per_row)


def backward_kernel(
    width, proj_ref, rim_ref, marks_ref, seg_ref, small_ref, out_ref, starts_ref, out_grad_ref,
    gate_grad_ref, pg_ref, conv_ref, head_ref, later, after, skips,
):
    pairs = width // LANES
    turn = pl.program_id(0)
    chunk = pl.num_programs(0) - 1 - turn

    @pl.when(turn == 0)
    def _():
        later[...] = jnp.zeros_like(later)
        after[...] = jnp.zeros_like(after)
        skips[...] = jnp.zeros_like(skips)
        conv_ref[...] = jnp.zeros_like(conv_ref)
        head_ref[...] = jnp.zeros_like(head_ref)

    span = width + 2 * LANES
    marks = marks_ref[...]
    rim = rim_ref[...][8:, width : width + span].astype(jnp.float32)
    rim = jnp.where(chunk > 0, rim, 0.0)
    pick = head_picks()
    skip, rate = small_ref[0, 6:7, :width], small_ref[0, 8:9, :LANES]
    _, mixed, shifts, conv, sig, active, stepped, step, decay, total, shut, reach, tail = (
        chunk_parts(
            width, proj_ref[...], rim, marks, seg_ref[...], small_ref, pick
        )
    )
    heads = active[:, :width]
    b_low = low(active[:, width : width + LANES])
    c_low = low(active[:, width + LANES :])

    grad_low = out_grad_ref[...]
    out_grad = grad_low.astype(jnp.float32)
    mixer = out_ref[...] - skip * heads

    entry = starts_ref[0]
    entry_low = low(entry)
    late = later[...]
    late_low = low(late)
    scores = mm(c_low, b_low, 1, 1)
    total_t = total.T
    step_wide = widen(step, pairs)
    scaled = heads * step_wide
    scaled_low = low(scaled)
    from_late = widen(tail, pairs) * mm(b_low, late_low)
    inside = []
    score_grad = jnp.zeros((Q, Q), jnp.float32)
    for p in range(pairs):
        gains = []
        both = []
        for h in (2 * p, 2 * p + 1):
            gain = jnp.exp(total[:, h : h + 1] - total_t[h : h + 1] + shut)
            gains.append(gain)
            both.append(low(gain * scores))
        stacked = stack_pair(grad_low, p)
        inside.append(mm(jnp.concatenate(both, axis=0), stacked, 0, 0))
        mix_grad = mm(stacked, scaled_low[:, p * LANES : (p + 1) * LANES], 1, 1)
        score_grad = score_grad + gains[0] * mix_grad[:Q] + gains[1] * mix_grad[Q:]
    scaled_grad = jnp.concatenate(inside, axis=1) + from_late
    reached = low(widen(reach, pairs) * out_grad)
    score_low = low(score_grad)
    c_grad = mm(score_low, b_low) + mm(reached, entry_low, 1, 1)
    b_grad = mm(score_low, c_low, 0, 0) + mm(low(scaled * widen(tail, pairs)), late_low, 1, 1)
    kept = widen(reach[Q - 1 : Q], pairs)
    later[...] = late * kept + mm(c_low, reached, 0, 0)

    scaled_seen = scaled_low.astype(jnp.float32)
    balance = out_grad * mixer - scaled_seen * scaled_grad
    closing = jnp.sum(scaled_seen * from_late, axis=0, keepdims=True) + kept * jnp.sum(
        late * entry, axis=0, keepdims=True
    )
    picks = iota((width, LANES), 0) // (LANES // 2) == iota((width, LANES), 1)
    picks = jnp.where(picks, 1.0, 0.0).astype(jnp.bfloat16)
    sums = pick_sums(
        jnp.concatenate([balance, heads * scaled_grad, jnp.broadcast_to(closing, (8, width))], 0),
        picks,
    )
    upper = jnp.where(iota((Q, Q), 0) <= iota((Q, Q), 1), 1.0, 0.0).astype(jnp.bfloat16)
    decay_grad = sums_of(upper, sums[:Q]) + sums[2 * Q : 2 * Q + 1]
    step_grad = sums[Q : 2 * Q] - decay_grad * rate
    raw_grad = step_grad * sigmoid(stepped)

    head_grad = step_wide * scaled_grad + skip * out_grad
    conv_grad = jnp.concatenate([head_grad, b_grad, c_grad], axis=1) * (
        sig * (1.0 + conv * (1.0 - sig))
    )
    mixed_grad = small_ref[0, KW - 1 : KW] * conv_grad
    bottom = iota((8, span), 0)
    for lag in range(1, KW):
        sent = conv_grad * marks[:, lag - 1 : lag]
        rolled = pltpu.roll(sent, Q - lag, 0)
        ending = jnp.where(
            bottom >= 8 - lag, pltpu.roll(after[lag - 1], 8 - lag, 0), rolled[Q - 8 :]
        )
        mixed_grad = mixed_grad + small_ref[0, KW - 1 - lag : KW - lag] * jnp.concatenate(
            [rolled[: Q - 8], ending], axis=0
        )
        after[lag - 1] = sent[:8]
    pg_ref[:, :width] = gate_grad_ref[...]
    pg_ref[:, width:] = low(
        jnp.concatenate([mixed_grad, mm(low(raw_grad), pick, 1, 1)], axis=1)
    )

    skips[0:1] += jnp.sum(out_grad * heads, axis=0, keepdims=True)
    for lag in range(KW):
        conv_ref[KW - 1 - lag : KW - lag] += jnp.sum(
            conv_grad * shifts[lag], axis=0, keepdims=True
        )
    conv_ref[KW : KW + 1] += jnp.sum(conv_grad, axis=0, keepdims=True)
    head_ref[0:1] += jnp.sum(raw_grad, axis=0, keepdims=True)
    head_ref[1:2] += jnp.sum(decay_grad * decay, axis=0, keepdims=True)

    @pl.when(chunk == 0)
    def _():
        head_ref[2:3] = pick_sums(skips[...], picks, 3)[0:1]


def cost(micros):
    return pl.CostEstimate(flops=micros * 1_100_000_000, bytes_accessed=0, transcendentals=0)


def small_spec(layer):
    return pl.BlockSpec((1, 16, 2 * D // 3), lambda i: (layer, 0, 0))


def full_spec(shape):
    return pl.BlockSpec(shape, lambda i: (0,) * len(shape))


def product_kernel(left_ref, weight_ref, theirs_ref, mine_ref, ordered_ref):
    c = lax.axis_index("section")
    block = left_ref.shape[0] // 4

    @pl.when(pl.program_id(0) == 0)
    def _():
        for i in range(4):
            at = 2 * (i % 2) + (1 - c if i < 2 else c)
            rows = pl.ds(pl.multiple_of(at * block, block), block)
            ordered_ref[i * block : (i + 1) * block] = left_ref[rows]

    found = mm(ordered_ref[...], weight_ref[...])
    theirs_ref[...] = low(found[: 2 * block])
    mine_ref[...] = found[2 * block :]


def group_parts(left, weight):
    rows, depth = left.shape
    columns = weight.shape[1]
    step = columns // 3
    half = rows // 2
    return pl.pallas_call(
        product_kernel,
        grid=(3,),
        in_specs=[
            pl.BlockSpec((rows, depth), lambda i: (0, 0)),
            pl.BlockSpec((depth, step), lambda i: (0, i)),
        ],
        out_specs=[pl.BlockSpec((half, step), lambda i: (0, i))] * 2,
        out_shape=[
            jax.ShapeDtypeStruct((half, columns), jnp.bfloat16),
            jax.ShapeDtypeStruct((half, columns), jnp.float32),
        ],
        scratch_shapes=[pltpu.VMEM((rows, depth), jnp.bfloat16)],
        compiler_params=pltpu.CompilerParams(vmem_limit_bytes=VMEM_BYTES),
        cost_estimate=cost(6),
        name="group_parts",
    )(left, weight)


def projection_kernel(left_ref, weight_ref, out_ref):
    out_ref[...] = low(mm(left_ref[...], weight_ref[...], 1, 1))


def projection(left, weight):
    rows, depth = left.shape
    columns = weight.shape[0]
    step = 640
    return pl.pallas_call(
        projection_kernel,
        grid=(pl.cdiv(columns, step),),
        in_specs=[
            pl.BlockSpec((rows, depth), lambda i: (0, 0)),
            pl.BlockSpec((step, depth), lambda i: (i, 0)),
        ],
        out_specs=pl.BlockSpec((rows, step), lambda i: (0, i)),
        out_shape=jax.ShapeDtypeStruct((rows, columns), jnp.bfloat16),
        compiler_params=pltpu.CompilerParams(vmem_limit_bytes=VMEM_BYTES),
        cost_estimate=cost(6),
        name="projection",
    )(left, weight)


def mixer_forward(layer, projected, marks, seg_row, small):
    rows, columns = projected.shape
    width = DI // 4
    chunks = rows // Q
    span = width + 2 * LANES

    def by_row(count):
        return pl.BlockSpec((Q, count), lambda i: (i, 0))

    return pl.pallas_call(
        functools.partial(forward_kernel, width),
        grid=(chunks,),
        in_specs=[
            by_row(columns), by_row(8), pl.BlockSpec((1, Q), lambda i: (0, i)), small_spec(layer),
        ],
        out_specs=[
            by_row(width),
            pl.BlockSpec((1, 1, Q), lambda i: (i, 0, 0)),
            by_row(width),
            pl.BlockSpec((1, LANES, width), lambda i: (i, 0, 0)),
        ],
        out_shape=[
            jax.ShapeDtypeStruct((rows, width), jnp.bfloat16),
            jax.ShapeDtypeStruct((chunks, 1, Q), jnp.float32),
            jax.ShapeDtypeStruct((rows, width), jnp.float32),
            jax.ShapeDtypeStruct((chunks, LANES, width), jnp.float32),
        ],
        scratch_shapes=[
            pltpu.VMEM((LANES, width), jnp.float32),
            pltpu.VMEM((8, span), jnp.float32),
        ],
        compiler_params=pltpu.CompilerParams(vmem_limit_bytes=VMEM_BYTES),
        cost_estimate=cost(16),
        name="mixer_forward",
    )(projected, marks, seg_row, small)


def mixer_backward(layer, projected, marks, seg_row, small, out, starts, out_grad, gate_grad):
    rows, columns = projected.shape
    width = out.shape[1]
    chunks = rows // Q
    span = width + 2 * LANES

    def by_row(count):
        return pl.BlockSpec((Q, count), lambda i: (chunks - 1 - i, 0))

    rim = pl.BlockSpec(
        (16, columns), lambda i: (jnp.maximum((chunks - 1 - i) * (Q // 16) - 1, 0), 0)
    )
    return pl.pallas_call(
        functools.partial(backward_kernel, width),
        grid=(chunks,),
        in_specs=[
            by_row(columns),
            rim,
            by_row(8),
            pl.BlockSpec((1, Q), lambda i: (0, chunks - 1 - i)),
            small_spec(layer),
            by_row(width),
            pl.BlockSpec((1, LANES, width), lambda i: (chunks - 1 - i, 0, 0)),
            by_row(width),
            by_row(width),
        ],
        out_specs=[
            by_row(columns),
            full_spec((8, span)),
            full_spec((8, LANES)),
        ],
        out_shape=[
            jax.ShapeDtypeStruct((rows, columns), jnp.bfloat16),
            jax.ShapeDtypeStruct((8, span), jnp.float32),
            jax.ShapeDtypeStruct((8, LANES), jnp.float32),
        ],
        scratch_shapes=[
            pltpu.VMEM((LANES, width), jnp.float32),
            pltpu.VMEM((KW - 1, 8, span), jnp.float32),
            pltpu.VMEM((8, width), jnp.float32),
        ],
        compiler_params=pltpu.CompilerParams(vmem_limit_bytes=VMEM_BYTES),
        cost_estimate=cost(33),
        name="mixer_backward",
    )(projected, projected, marks, seg_row, small, out, starts, out_grad, gate_grad)


CORES = 2
GROUP = 4
SHARED = CONV - DI + H
LOCAL = 2 * DI // GROUP + SHARED + 16
HALF = LOCAL // 2
CHUNKS = 2
LANE_PART = D // 4
OUT_PART = DI // 16
UNITS = CHUNKS + 1
GATE = DI // GROUP
GATE_HALF = GATE // 2
REST_HALF = HALF - GATE_HALF
STEPS = ((0, 192), (192, 192), (0, 272), (272, 272))


def place():
    c, z, r = (lax.axis_index(name) for name in ("section", "shard", "rep"))
    return c, z, lax.div(r, 2), lax.rem(r, 2)


def weight_pieces(quarter):
    part = DI // 16
    found = []
    for side in range(2):
        for zz in range(4):
            found.append(
                (side * 4 * part + zz * part, side * DI + zz * 4 * part + quarter * part, part)
            )
    found.append((8 * part, 2 * DI, SHARED))
    return found


def mesh_copy(source, target, send, recv, device):
    return pltpu.make_async_remote_copy(
        src_ref=source, dst_ref=target, send_sem=send, recv_sem=recv,
        device_id=device, device_id_type=pl.DeviceIdType.MESH,
    )


def greet(barrier, device):
    pl.semaphore_signal(barrier, inc=1, device_id=device, device_id_type=pl.DeviceIdType.MESH)


def rows_at(start, count):
    return pl.ds(pl.multiple_of(start, 16), count)


class WeightGather:
    def __init__(self, layer, in_ref, out_ref, w_ref, wo_ref, sems):
        self.layer, self.in_ref, self.out_ref = layer, in_ref, out_ref
        self.w_ref, self.wo_ref = w_ref, wo_ref
        (
            self.local_sem, self.core_send, self.core_recv, self.right_send, self.left_send,
            self.z_recv, self.y_send, self.y_recv,
        ) = sems
        self.c, self.z, self.y, self.x = place()
        self.core = {"section": 1 - self.c}
        self.y_other = {"rep": (1 - self.y) * 2 + self.x}

    def own_pieces(self, quarter):
        lanes = pl.ds(pl.multiple_of(self.z * LANE_PART, LANES), LANE_PART)
        found = []
        for at, start, count in weight_pieces(quarter):
            found.append((self.in_ref.at[rows_at(start, count)], self.w_ref.at[pl.ds(at, count), lanes]))
        found.append(
            (
                self.out_ref.at[rows_at(quarter * OUT_PART, OUT_PART)],
                self.wo_ref.at[rows_at(self.z * OUT_PART, OUT_PART)],
            )
        )
        return found

    def local_copies(self):
        return [
            pltpu.make_async_copy(source, target, self.local_sem.at[i])
            for i, (source, target) in enumerate(self.own_pieces(2 * self.x + self.c))
        ]

    def core_copies(self):
        return [
            mesh_copy(source, target, self.core_send.at[i], self.core_recv.at[i], self.core)
            for i, (source, target) in enumerate(self.own_pieces(2 * self.x + 1 - self.c))
        ]

    def begin(self):
        lanes = pl.ds(pl.multiple_of(self.z * LANE_PART, LANES), LANE_PART)
        self.w_ref[LOCAL - 16 :, lanes] = jnp.zeros((16, LANE_PART), self.w_ref.dtype)

        @pl.when(self.c == self.layer)
        def _():
            for copy in self.core_copies():
                copy.start()
            for copy in self.local_copies():
                copy.start()
            for copy in self.local_copies():
                copy.wait()

        @pl.when(self.c != self.layer)
        def _():
            for copy in self.core_copies():
                copy.wait_recv()

    def slab(self, unit, shard, side):
        if unit == CHUNKS:
            return self.wo_ref.at[rows_at(shard * OUT_PART + side * (OUT_PART // 2), OUT_PART // 2)]
        return self.w_ref.at[
            rows_at(side * HALF + unit * (HALF // CHUNKS), HALF // CHUNKS),
            pl.ds(pl.multiple_of(shard * LANE_PART, LANES), LANE_PART),
        ]

    def z_copy(self, unit, shard, step, k):
        piece = self.slab(unit, shard, self.y)
        send = (self.right_send if step > 0 else self.left_send).at[unit, k]
        return mesh_copy(piece, piece, send, self.z_recv.at[unit, shard], {"shard": self.z + step})

    def y_copy(self, unit, shard, side):
        piece = self.slab(unit, shard, side)
        return mesh_copy(
            piece, piece, self.y_send.at[unit, shard], self.y_recv.at[unit, shard], self.y_other
        )

    def cases(self, step, k):
        shard = self.z - k * step
        there = (shard >= 0) if step > 0 else (shard <= 3)
        more = (self.z < 3) if step > 0 else (self.z > 0)
        return shard, there, more

    def first(self, unit):
        for step in (1, -1):
            _, _, more = self.cases(step, 0)

            @pl.when(more)
            def _():
                self.z_copy(unit, self.z, step, 0).start()

    def arrive(self, unit, k):
        for step in (1, -1):
            shard, there, more = self.cases(step, k)

            @pl.when(there)
            def _():
                self.z_copy(unit, shard, step, 0).wait_recv()

                @pl.when(more)
                def _():
                    self.z_copy(unit, shard, step, k).start()

                self.y_copy(unit, shard, self.y).start()

    def end(self):
        for unit in range(UNITS):
            for away in (1, 2, 3):
                shard = lax.rem(self.z + away, 4)
                self.y_copy(unit, shard, 1 - self.y).wait_recv()
                self.y_copy(unit, shard, self.y).wait_send()
            for step in (1, -1):
                for k in range(3):
                    shard, there, more = self.cases(step, k)

                    @pl.when(there & more)
                    def _():
                        self.z_copy(unit, shard, step, k).wait_send()

        @pl.when(self.c == self.layer)
        def _():
            for copy in self.core_copies():
                copy.wait_send()


def weight_scratch():
    dma = pltpu.SemaphoreType.DMA
    return [
        dma((10,)), dma((10,)), dma((10,)),
        dma((UNITS, 3)), dma((UNITS, 3)), dma((UNITS, 4)), dma((UNITS, 4)), dma((UNITS, 4)),
    ]


class RowGather:
    def __init__(self, whole, count, sems):
        self.whole, self.count = whole, count
        self.send, self.recv = sems
        self.c, self.z, self.y, self.x = place()

    def copy(self, i, xx, cc, device):
        if self.count is None:
            piece = self.whole.at[2 * xx + cc]
        else:
            piece = self.whole.at[rows_at((2 * xx + cc) * self.count, self.count)]
        return mesh_copy(piece, piece, self.send.at[i], self.recv.at[i], device)

    def near(self):
        return self.copy(0, self.x, self.c, {"rep": 2 * self.y + 1 - self.x})

    def other(self):
        return self.copy(1, self.x, self.c, {"section": 1 - self.c})

    def far(self):
        return self.copy(2, 1 - self.x, self.c, {"section": 1 - self.c})

    def begin(self, value):
        if self.count is None:
            self.whole[2 * self.x + self.c] = value
        else:
            self.whole[rows_at((2 * self.x + self.c) * self.count, self.count)] = value
        self.near().start()
        self.other().start()

    def middle(self):
        self.near().wait_recv()
        self.far().start()

    def end(self):
        self.near().wait_send()
        self.other().wait()
        self.far().wait()


def normal_rows(rows, gain):
    inv = lax.rsqrt(jnp.mean(rows * rows, axis=-1, keepdims=True) + EPSILON)
    return low(rows * inv * gain)


def turn_by(value, step, counts, which):
    found = pltpu.roll(value, step * counts[0], 1) if counts[0] else value
    for k in range(1, len(counts)):
        other = pltpu.roll(value, step * counts[k], 1) if counts[k] else value
        found = jnp.where(which == k, other, found)
    return found


def small_parts(layer, quarter, params_ref, small_ref):
    width, group = DI // GROUP, DI // 16
    piece = CONV // 4
    lane = iota((16, width), 1)
    pieces = [params_ref[4 * layer + zz].astype(jnp.float32) for zz in range(4)]
    gap = jnp.zeros((16, CONV - pieces[0].shape[1]), jnp.float32)
    conv = jnp.zeros((16, CONV), jnp.float32)
    for zz in range(4):
        own = jnp.where(iota(pieces[zz].shape, 1) < piece, pieces[zz], 0.0)
        conv = conv + pltpu.roll(jnp.concatenate([own, gap], axis=1), zz * piece, 1)

    def turned(part, zz):
        moved = turn_by(part, group, [(zz - k) % GROUP for k in range(GROUP)], quarter)
        return jnp.where(lax.div(lane, group) == zz, moved, 0.0)

    taps = sum(turned(conv[:, zz * width : (zz + 1) * width], zz) for zz in range(4))
    gain = sum(turned(pieces[zz][:, :width], zz) for zz in range(4))
    per = H // 16
    head, given = iota((LANES, LANES), 1), iota((LANES, LANES), 0)
    heads = jnp.zeros((16, LANES), jnp.float32)
    for zz in range(4):
        taken = (lax.div(head, per) == zz) & (given == per * quarter + lax.rem(head, per))
        heads = heads + mm(low(pieces[zz][:, :LANES]), jnp.where(taken, 1.0, 0.0).astype(jnp.bfloat16))
    wide_head = iota((LANES, width), 1)
    wide = jnp.where(lax.div(wide_head, P_SIZE) == iota((LANES, width), 0), 1.0, 0.0)
    skip = mm(low(heads), wide.astype(jnp.bfloat16))
    small_ref[layer] = jnp.zeros(small_ref.shape[1:], jnp.float32)
    small_ref[layer, 0:5, :width] = taps[0:5]
    small_ref[layer, 0:5, width:] = conv[0:5, DI:]
    small_ref[layer, 5:6, :width] = gain[5:6]
    small_ref[layer, 6:7, :width] = skip[9:10]
    small_ref[layer, 7:8, :LANES] = heads[7:8]
    rate = jnp.exp(heads[8:9])
    small_ref[layer, 8:9, :LANES] = jnp.where(iota((1, LANES), 1) < H // GROUP, rate, 0.0)


def enter_first_kernel(
    in_ref, out_ref, blocks_ref, flat_ref, w_ref, wo_ref, rows_ref, normed_ref, small_ref, norms_ref,
    params_ref, row_send, row_recv, home_send, home_recv, p_send, p_recv, *sems,
):
    c, z, y, x = place()
    weights = WeightGather(0, in_ref, out_ref, w_ref, wo_ref, sems)
    gather = RowGather(normed_ref, rows_ref.shape[0], (row_send, row_recv))
    source = {"section": 0, "shard": 2 * x + c, "rep": 2 * y + lax.rem(z, 2)}
    from_self = (c == 0) & (z == 2 * x) & (x == lax.rem(z, 2))
    targets = tuple(
        {"section": lax.rem(z, 2), "shard": 2 * m + x, "rep": 2 * y + lax.div(z, 2)}
        for m in range(MICRO)
    )
    to_self = tuple(
        (lax.rem(z, 2) == 0) & (z == 2 * m + x) & (x == lax.div(z, 2)) for m in range(MICRO)
    )
    others = [{"section": 1 - c}]
    for away in (1, 2, 3):
        others.append({"shard": lax.rem(z + away, 4)})
        others.append({"section": 1 - c, "shard": lax.rem(z + away, 4)})

    barrier = pltpu.get_barrier_semaphore()
    for device in others + [{"rep": 2 * y + 1 - x}, {"rep": 2 * (1 - y) + x}]:
        greet(barrier, device)

    @pl.when(jnp.logical_not(from_self))
    def _():
        greet(barrier, source)

    guests = sum(jnp.logical_not(own).astype(jnp.int32) for own in to_self)
    pl.semaphore_wait(barrier, 9 + jnp.where(c == 0, guests, 0))

    def home_copy(m):
        return mesh_copy(
            blocks_ref.at[0, m, 0], rows_ref, home_send.at[m], home_recv.at[0], targets[m]
        )

    def own_copy(m):
        return pltpu.make_async_copy(blocks_ref.at[0, m, 0], rows_ref, home_send.at[m])

    def param_copy(i):
        return mesh_copy(
            flat_ref, params_ref.at[4 * c + z], p_send.at[i], p_recv.at[i], others[i]
        )

    def param_from(i):
        cc = c if i % 2 == 1 else 1 - c
        zz = z if i == 0 else lax.rem(z + 4 - (i + 1) // 2, 4)
        return mesh_copy(
            flat_ref, params_ref.at[4 * cc + zz], p_send.at[i], p_recv.at[i], others[i]
        )

    for m in range(MICRO):

        @pl.when((c == 0) & jnp.logical_not(to_self[m]))
        def _():
            home_copy(m).start()

        @pl.when((c == 0) & to_self[m])
        def _():
            own_copy(m).start()

    for i in range(7):
        param_copy(i).start()
    params_ref[4 * c + z] = flat_ref[...]
    weights.begin()
    for i in range(7):
        param_from(i).wait_recv()

    @pl.when(jnp.logical_not(from_self))
    def _():
        home_copy(0).wait_recv()

    for m in range(MICRO):

        @pl.when((c == 0) & to_self[m])
        def _():
            own_copy(m).wait()

    for layer in range(2):
        for zz in range(4):
            part = params_ref[4 * layer + zz].astype(jnp.float32)[6:7, :LANE_PART]
            norms_ref[layer, :, zz * LANE_PART : (zz + 1) * LANE_PART] = jnp.broadcast_to(
                part, (8, LANE_PART)
            )
    gain = norms_ref[0, 0:1]
    for unit in range(CHUNKS):
        weights.first(unit)
    gather.begin(normal_rows(rows_ref[...].astype(jnp.float32), gain))
    for k in (1, 2):
        for unit in range(CHUNKS):
            weights.arrive(unit, k)
    weights.first(CHUNKS)
    gather.middle()
    for layer in range(2):
        small_parts(layer, 2 * x + c, params_ref, small_ref)
    for unit in range(CHUNKS):
        weights.arrive(unit, 3)
    for k in (1, 2, 3):
        weights.arrive(CHUNKS, k)
    weights.end()
    gather.end()
    for i in range(7):
        param_copy(i).wait_send()
    for m in range(MICRO):

        @pl.when((c == 0) & jnp.logical_not(to_self[m]))
        def _():
            home_copy(m).wait_send()


def weight_shapes():
    return [
        jax.ShapeDtypeStruct((LOCAL, D), jnp.bfloat16),
        jax.ShapeDtypeStruct((DI // GROUP, D), jnp.bfloat16),
    ]


def enter_first(in_rows, out_rows, blocks, flat):
    dma = pltpu.SemaphoreType.DMA
    block = blocks.shape[-2]
    anywhere, inside = pl.BlockSpec(memory_space=pl.ANY), pl.BlockSpec(memory_space=pltpu.VMEM)
    return pl.pallas_call(
        enter_first_kernel,
        in_specs=[anywhere] * 3 + [inside],
        out_specs=[inside] * 6,
        out_shape=weight_shapes()
        + [
            jax.ShapeDtypeStruct((block, D), jnp.bfloat16),
            jax.ShapeDtypeStruct((GROUP * block, D), jnp.bfloat16),
            jax.ShapeDtypeStruct((CORES, 16, DI // GROUP + 2 * N), jnp.float32),
            jax.ShapeDtypeStruct((CORES, 8, D), jnp.float32),
        ],
        scratch_shapes=[pltpu.VMEM((2 * 4,) + flat.shape, jnp.bfloat16), dma((3,)), dma((3,)), dma((MICRO,)), dma((1,)), dma((7,)), dma((7,))]
        + weight_scratch(),
        compiler_params=pltpu.CompilerParams(
            collective_id=0, has_side_effects=True, vmem_limit_bytes=VMEM_BYTES
        ),
        name="enter_first",
    )(in_rows, out_rows, blocks, flat)


def enter_second_kernel(
    in_ref, out_ref, theirs_ref, mine_ref, squares_ref, entering_ref, gain_ref, g_ref,
    w_ref, wo_ref, added_ref, middle_ref, normed_ref, g_all_ref, inv_ref,
    n_core, n_send, n_across, s_core, s_mine, s_across,
    row_send, row_recv, g_send, g_recv, n_sem, s_sem, *sems,
):
    c, z, y, x = place()
    weights = WeightGather(1, in_ref, out_ref, w_ref, wo_ref, sems)
    block = entering_ref.shape[0]
    gather = RowGather(normed_ref, block, (row_send, row_recv))
    g_gather = RowGather(g_all_ref, block, (g_send, g_recv))
    core, x_other = {"section": 1 - c}, {"rep": 2 * y + 1 - x}
    barrier = pltpu.get_barrier_semaphore()
    for device in (core, x_other, {"rep": 2 * (1 - y) + x}):
        greet(barrier, device)

    @pl.when(z < 3)
    def _():
        greet(barrier, {"shard": z + 1})

    @pl.when(z > 0)
    def _():
        greet(barrier, {"shard": z - 1})

    ends = jnp.where(z == 0, 1, 0) + jnp.where(z == 3, 1, 0)
    pl.semaphore_wait(barrier, 5 - ends)

    n_core_copy = mesh_copy(theirs_ref, n_core, n_sem.at[0], n_sem.at[1], core)
    n_x_copy = mesh_copy(n_send, n_across, n_sem.at[2], n_sem.at[3], x_other)
    s_core_copy = mesh_copy(squares_ref, s_core, s_sem.at[0], s_sem.at[1], core)
    s_x_copy = mesh_copy(s_mine, s_across, s_sem.at[2], s_sem.at[3], x_other)

    n_core_copy.start()
    s_core_copy.start()
    weights.begin()
    for unit in range(CHUNKS):
        weights.first(unit)

    def summed(which):
        rows = rows_at(which * block, block)
        return mine_ref[rows] + n_core[rows].astype(jnp.float32)

    s_core_copy.wait_recv()
    s_mine[...] = squares_ref[...] + s_core[...]
    s_x_copy.start()
    n_core_copy.wait_recv()
    n_send[...] = low(summed(1 - x))
    n_x_copy.start()
    for unit in range(CHUNKS):
        weights.arrive(unit, 1)

    s_x_copy.wait_recv()
    inv_ref[...] = lax.rsqrt((s_mine[...] + s_across[...]) * (1.0 / DI) + EPSILON)
    n_x_copy.wait_recv()
    product = summed(x) + n_across[...].astype(jnp.float32)
    per = block // LANES
    here = (2 * x + c) * per
    own_inv = jnp.concatenate(
        [
            jnp.broadcast_to(inv_ref[pl.ds(here + i, 1)], (LANES, LANES)).T[:, :1]
            for i in range(per)
        ],
        axis=0,
    )
    added = own_inv * product
    added_ref[...] = added
    middle = low(entering_ref[...].astype(jnp.float32) + added)
    middle_ref[...] = middle
    gather.begin(normal_rows(middle.astype(jnp.float32), gain_ref[...]))
    g_gather.begin(g_ref[...])
    for unit in range(CHUNKS):
        weights.arrive(unit, 2)
    weights.first(CHUNKS)
    for unit in range(CHUNKS):
        weights.arrive(unit, 3)
    gather.middle()
    for k in (1, 2, 3):
        weights.arrive(CHUNKS, k)
    g_gather.middle()
    weights.end()
    gather.end()
    g_gather.end()
    n_core_copy.wait_send()
    n_x_copy.wait_send()
    s_core_copy.wait_send()
    s_x_copy.wait_send()


def enter_second(in_rows, out_rows, theirs, mine, squares, entering, gain, g):
    dma = pltpu.SemaphoreType.DMA
    block = entering.shape[0]
    anywhere, inside = pl.BlockSpec(memory_space=pl.ANY), pl.BlockSpec(memory_space=pltpu.VMEM)
    whole = jax.ShapeDtypeStruct((GROUP * block, D), jnp.bfloat16)
    return pl.pallas_call(
        enter_second_kernel,
        in_specs=[anywhere] * 2 + [inside] * 6,
        out_specs=[inside] * 7,
        out_shape=weight_shapes()
        + [
            jax.ShapeDtypeStruct((block, D), jnp.float32),
            jax.ShapeDtypeStruct((block, D), jnp.bfloat16),
            whole,
            whole,
            jax.ShapeDtypeStruct(squares.shape, jnp.float32),
        ],
        scratch_shapes=[
            pltpu.VMEM(theirs.shape, jnp.bfloat16),
            pltpu.VMEM(entering.shape, jnp.bfloat16),
            pltpu.VMEM(entering.shape, jnp.bfloat16),
            pltpu.VMEM(squares.shape, jnp.float32),
            pltpu.VMEM(squares.shape, jnp.float32),
            pltpu.VMEM(squares.shape, jnp.float32),
            dma((3,)), dma((3,)), dma((3,)), dma((3,)), dma((4,)), dma((4,)),
        ]
        + weight_scratch(),
        compiler_params=pltpu.CompilerParams(
            collective_id=1, has_side_effects=True, vmem_limit_bytes=VMEM_BYTES
        ),
        name="enter_second",
    )(in_rows, out_rows, theirs, mine, squares, entering, gain, g)


def swap_core(v):
    return lax.ppermute(v, "section", [(0, 1), (1, 0)])


def swap_x(v):
    return lax.ppermute(v, "rep", [(i, i ^ 1) for i in range(4)])


def swap_y(v):
    return lax.ppermute(v, "rep", [(i, i ^ 2) for i in range(4)])


def swap_z(v, bit):
    return lax.ppermute(v, "shard", [(i, i ^ bit) for i in range(4)])


def ordered(first, mine, other, axis=0):
    return jnp.where(first, jnp.stack([mine, other], axis), jnp.stack([other, mine], axis))


def joined(first, mine, other, axis=0):
    return jnp.where(
        first, jnp.concatenate([mine, other], axis), jnp.concatenate([other, mine], axis)
    )


def after(value, *earlier):
    return lax.optimization_barrier((value,) + earlier)[0]


def sum_kernel(layer, *refs):
    last = layer == 0
    (
        gate_ref, grad_ref, out_grad_ref, theirs_ref, mine_ref, entering_ref, incoming_ref, gain_ref,
        extra_ref,
    ) = refs[:9]
    if last:
        small_refs = (refs[9:12], refs[12:15])
        late_refs, late_out_refs = refs[15:19], refs[19:21]
        refs = refs[:9] + refs[21:]
    else:
        r_theirs_ref, r_mine_ref, r_inv_ref = refs[9:12]
        refs = refs[:9] + refs[12:]
    all_ref, out_all_ref, bound_ref = refs[9:12]
    (
        n_core, n_send, n_across, n_done, y_buf, z_buf, s_buf, yo_buf, yo_mine,
        y_send, y_recv, z_send, z_recv, yo_sem, core_send, core_recv,
        x_send, x_recv, ya_send, ya_recv, relay_send, relay_recv, xo_send, xo_recv, n_sem,
    ) = refs[19:44]
    if last:
        total_refs = refs[12:19]
        tiny_mine, t1_buf, t1_sum, t2_buf, t2_sum, t3_buf, g_mine, g_buf, g_sum, g_all = refs[44:54]
        t_send, t_recv, home_send, home_recv, g_send, g_recv = refs[54:]
    else:
        g_ref, g_all_ref, dots_ref, norm_ref = refs[12:16]
        r_core, r_send, r_across = refs[44:47]
        row_send, row_recv, dot_send, dot_recv, r_sem = refs[47:]
    c, z, y, x = place()
    quarter = 2 * x + c
    core, x_other, y_other = {"section": 1 - c}, {"rep": 2 * y + 1 - x}, {"rep": 2 * (1 - y) + x}
    chunks = range(len(STEPS))
    block = n_done.shape[0]
    copy = mesh_copy

    home = {"section": layer, "shard": quarter, "rep": 2 * y + lax.rem(z, 2)}
    at_home = (c == layer) & (z == quarter) & (x == lax.rem(z, 2))
    guests = tuple(
        {"section": lax.rem(z, 2), "shard": 2 * m + x, "rep": 2 * y + lax.div(z, 2)}
        for m in range(MICRO)
    )
    guest_self = tuple(
        (c == layer) & (lax.rem(z, 2) == layer) & (z == 2 * m + x) & (x == lax.div(z, 2))
        for m in range(MICRO)
    )
    reps = (x_other, y_other, {"rep": 2 * (1 - y) + 1 - x})
    shards = tuple({"shard": lax.rem(z + away, 4)} for away in (1, 2, 3))
    barrier = pltpu.get_barrier_semaphore()
    for device in (core,) + reps + shards:
        greet(barrier, device)
    if last:
        for m in range(MICRO):

            @pl.when((c == layer) & jnp.logical_not(guest_self[m]))
            def _():
                greet(barrier, guests[m])

        pl.semaphore_wait(barrier, 8 - at_home.astype(jnp.int32))
    else:
        pl.semaphore_wait(barrier, 7)

    orders = ((3, 2, 1, 0), (3, 0, 2, 1), (0, 3, 1, 2), (0, 1, 2, 3))

    def shard_at(i):
        found = jnp.int32(orders[3][i])
        for zz in range(3):
            found = jnp.where(z == zz, orders[zz][i], found)
        return found

    def grad_part(shard, side, ch):
        lanes = pl.ds(pl.multiple_of(shard * LANE_PART, LANES), LANE_PART)
        if ch < 2:
            return gate_ref.at[pl.ds(*STEPS[ch]), lanes]
        return grad_ref.at[rows_at(side * REST_HALF + STEPS[ch][0], STEPS[ch][1]), lanes]

    def span_of(ch):
        return pl.ds(STEPS[ch][0] + (0 if ch < 2 else GATE_HALF), STEPS[ch][1])

    def y_copy(shard, ch):
        return copy(
            grad_part(shard, 1 - y, ch), y_buf.at[shard, span_of(ch)],
            y_send.at[shard, ch], y_recv.at[shard, ch], y_other,
        )

    def z_target(shard):
        right = shard > z
        there = {"shard": jnp.clip(z + jnp.where(right, 1, -1), 0, 3)}
        slot = jnp.where(right, shard, jnp.where(shard == z - 1, 4, shard))
        return there, slot

    def z_copy(shard, ch):
        there, slot = z_target(shard)
        return copy(
            s_buf.at[shard, span_of(ch)], z_buf.at[slot, span_of(ch)],
            z_send.at[shard, ch], z_recv.at[slot, ch], there,
        )

    def z_wait(slot, ch):
        there, _ = z_target(shard_at(0))
        copy(
            s_buf.at[0, span_of(ch)], z_buf.at[slot, span_of(ch)],
            z_send.at[0, ch], z_recv.at[slot, ch], there,
        ).wait_recv()

    def all_part(which, side, ch):
        start = side * GATE_HALF if ch < 2 else GATE + side * REST_HALF
        return all_ref.at[which, rows_at(start + STEPS[ch][0], STEPS[ch][1])]

    def out_part(which):
        return out_all_ref.at[rows_at(which * OUT_PART, OUT_PART)]

    def x_copy(who, ch):
        piece = all_part(2 * x + who, y, ch)
        return copy(piece, piece, x_send.at[who, ch], x_recv.at[who, ch], x_other)

    def ya_copy(who, ch):
        piece = all_part(2 * x + who, y, ch)
        return copy(piece, piece, ya_send.at[who, ch], ya_recv.at[who, ch], y_other)

    def relay_copy(who, ch):
        if who == 0:
            piece = all_part(2 * x, 1 - y, ch)
            return copy(piece, piece, relay_send.at[0, ch], relay_recv.at[0, ch], x_other)
        piece = all_part(2 * (1 - x) + 1, y, ch)
        return copy(piece, piece, relay_send.at[1, ch], relay_recv.at[1, ch], y_other)

    def xo_copy(who):
        piece = out_part(2 * x + who)
        return copy(piece, piece, xo_send.at[who], xo_recv.at[who], x_other)

    def spread(who, ch):
        x_copy(who, ch).start()
        ya_copy(who, ch).start()

    def owner_copy(ch):
        span = span_of(ch)
        piece = all_part(quarter, y, ch) if last else all_ref.at[1 - layer, span]
        return copy(s_buf.at[z, span], piece, core_send.at[ch], core_recv.at[ch], core)

    def owner_out_copy():
        piece = out_part(quarter) if last else out_all_ref.at[1 - layer]
        return copy(
            yo_mine, piece, core_send.at[len(STEPS)], core_recv.at[len(STEPS)], core
        )

    def yo_copy():
        return copy(out_grad_ref, yo_buf, yo_sem.at[0], yo_sem.at[1], y_other)

    def n_core_copy():
        return copy(theirs_ref, n_core, n_sem.at[0], n_sem.at[1], core)

    def n_x_copy():
        return copy(n_send, n_across, n_sem.at[2], n_sem.at[3], x_other)

    def home_copy(m):
        return copy(n_done, bound_ref.at[m], home_send.at[0], home_recv.at[m], home)

    def go_home():
        for m in range(MICRO):
            there = lax.div(z, 2) == m

            @pl.when(there & jnp.logical_not(at_home))
            def _():
                home_copy(m).start()

            @pl.when(there & at_home)
            def _():
                bound_ref[m] = n_done[...]

    if last:

        def t1_copy():
            return copy(tiny_mine.at[1 - c], t1_buf, t_send.at[0], t_recv.at[0], core)

        def t2_copy(away):
            return copy(
                t1_sum, t2_buf.at[away - 1], t_send.at[away], t_recv.at[away], shards[away - 1]
            )

        def t3_copy(i):
            return copy(t2_sum, t3_buf.at[i], t_send.at[4 + i], t_recv.at[4 + i], reps[i])

        def g1_copy():
            return copy(g_mine, g_buf.at[0], g_send.at[0], g_recv.at[0], core)

        def g2_copy(away):
            return copy(g_sum, g_buf.at[away], g_send.at[away], g_recv.at[away], shards[away - 1])

        def g3_copy(i):
            return copy(g_all, g_buf.at[4 + i], g_send.at[4 + i], g_recv.at[4 + i], reps[i])

    else:

        def r_core_copy():
            return copy(r_theirs_ref, r_core, r_sem.at[0], r_sem.at[1], core)

        def r_x_copy():
            return copy(r_send, r_across, r_sem.at[2], r_sem.at[3], x_other)

        def r_summed(which):
            rows = rows_at(which * block, block)
            return r_mine_ref[rows] + r_core[rows].astype(jnp.float32)

        g_gather = RowGather(g_all_ref, block, (row_send, row_recv))
        dot_gather = RowGather(dots_ref, None, (dot_send, dot_recv))

    n_core_copy().start()
    if not last:
        r_core_copy().start()
    for ch in chunks[2:]:
        for i in range(4):
            y_copy(shard_at(i), ch).start()
        if ch == 2:
            yo_copy().start()

    def more(shard):
        return ((shard > z) & (z > 0)) | ((shard < z) & (z < 3))

    def y_sum(shard, ch):
        own = grad_part(shard, y, ch)[...].astype(jnp.float32)
        if ch < 2:
            return own
        y_copy(shard, ch).wait_recv()
        return own + y_buf[shard, span_of(ch)].astype(jnp.float32)

    def send_in(i, ch):
        shard = shard_at(i)
        span = span_of(ch)
        both = y_sum(shard, ch)

        @pl.when(more(shard))
        def _():
            z_wait(shard, ch)
            s_buf[shard, span] = low(both + z_buf[shard, span].astype(jnp.float32))

        @pl.when(jnp.logical_not(more(shard)))
        def _():
            s_buf[shard, span] = low(both)

        z_copy(shard, ch).start()

    def finish(ch):
        span = span_of(ch)
        s_buf[z, span] = low(y_sum(z, ch))

        @pl.when(z > 0)
        def _():
            z_wait(z, ch)
            s_buf[z, span] = low(
                s_buf[z, span].astype(jnp.float32) + z_buf[z, span].astype(jnp.float32)
            )

        @pl.when(z < 3)
        def _():
            z_wait(4, ch)
            s_buf[z, span] = low(
                s_buf[z, span].astype(jnp.float32) + z_buf[4, span].astype(jnp.float32)
            )

        @pl.when(c != layer)
        def _():
            owner_copy(ch).start()

        @pl.when(c == layer)
        def _():
            if last:
                all_part(quarter, y, ch)[...] = s_buf[z, span]
                spread(layer, ch)
            else:
                all_ref[layer, span] = s_buf[z, span]

    def pass_on(ch):
        if not last:
            return

        @pl.when(c == layer)
        def _():
            owner_copy(ch).wait_recv()
            spread(1 - layer, ch)

    def relay(ch):
        if not last:
            return

        @pl.when(c == layer)
        def _():
            ya_copy(0, ch).wait_recv()
            relay_copy(0, ch).start()
            x_copy(1, ch).wait_recv()
            relay_copy(1, ch).start()

    def summed(which):
        rows = rows_at(which * block, block)
        return mine_ref[rows] + n_core[rows].astype(jnp.float32)

    def start_across():
        n_core_copy().wait_recv()
        n_send[...] = low(summed(1 - x))
        n_x_copy().start()

    def norm_step():
        n_x_copy().wait_recv()
        if not last:
            r_core_copy().wait_recv()
            r_send[...] = low(r_summed(1 - x))
            r_x_copy().start()
        normed_grad = summed(x) + n_across[...].astype(jnp.float32)
        entering = entering_ref[...].astype(jnp.float32)
        inv = lax.rsqrt(jnp.mean(entering * entering, axis=-1, keepdims=True) + EPSILON)
        hat = entering * inv
        hat_grad = normed_grad * gain_ref[...]
        mean = jnp.mean(hat_grad * hat, axis=-1, keepdims=True)
        source_grad = low(incoming_ref[...].astype(jnp.float32) + inv * (hat_grad - hat * mean))
        norm_grad = jnp.sum(normed_grad * hat, axis=0, keepdims=True)
        if last:
            n_done[...] = source_grad
            g_mine[...] = jnp.broadcast_to(norm_grad, g_mine.shape)

            @pl.when(c != layer)
            def _():
                g1_copy().start()

            return
        g_ref[...] = source_grad
        g_gather.begin(source_grad)
        norm_ref[...] = norm_grad
        dots = jnp.sum(source_grad.astype(jnp.float32) * extra_ref[...], axis=1, keepdims=True)
        flat = [
            jnp.broadcast_to(dots[i * LANES : (i + 1) * LANES], (LANES, LANES)).T[:1]
            for i in range(block // LANES)
        ]
        flat.append(jnp.zeros((8 - len(flat), LANES), jnp.float32))
        dot_gather.begin(jnp.concatenate(flat, axis=0))

    def result_step():
        r_x_copy().wait_recv()
        product = r_summed(x) + r_across[...].astype(jnp.float32)
        bound_ref[...] = low(entering_ref[...].astype(jnp.float32) + r_inv_ref[...] * product)

    def out_step():
        yo_copy().wait()
        total = low(out_grad_ref[...].astype(jnp.float32) + yo_buf[...].astype(jnp.float32))
        yo_mine[...] = total

        @pl.when(c != layer)
        def _():
            owner_out_copy().start()

        @pl.when(c == layer)
        def _():
            if last:
                out_part(quarter)[...] = yo_mine[...]
            else:
                out_all_ref[layer] = yo_mine[...]

    def out_across():
        @pl.when(c == layer)
        def _():
            owner_out_copy().wait_recv()
            for who in range(CORES):
                xo_copy(who).start()

    def early_small():
        if last:
            small_totals(0, quarter, small_refs[0], None, tiny_mine)
            small_totals(1, quarter, small_refs[1], extra_ref[...], tiny_mine)
            t1_copy().start()

    def small_along_z():
        if last:
            t1_copy().wait_recv()
            t1_sum[...] = tiny_mine[c] + t1_buf[...]
            for away in (1, 2, 3):
                t2_copy(away).start()

    def small_across():
        if last:
            for away in (1, 2, 3):
                t2_copy(away).wait_recv()
            t2_sum[...] = (t1_sum[...] + t2_buf[0]) + (t2_buf[1] + t2_buf[2])
            for i in range(3):
                t3_copy(i).start()

    def gain_along_z():
        @pl.when(c == layer)
        def _():
            g1_copy().wait_recv()
            g_sum[...] = g_mine[...] + g_buf[0]
            for away in (1, 2, 3):
                g2_copy(away).start()

    def gain_across():
        @pl.when(c == layer)
        def _():
            for away in (1, 2, 3):
                g2_copy(away).wait_recv()
            g_all[...] = (g_sum[...] + g_buf[1]) + (g_buf[2] + g_buf[3])
            for i in range(3):
                g3_copy(i).start()

    send_in(0, 0)
    send_in(0, 1)
    start_across()
    early_small()
    send_in(1, 0)
    send_in(0, 2)
    send_in(1, 1)
    small_along_z()
    send_in(2, 0)
    send_in(1, 2)
    send_in(2, 1)
    finish(0)
    small_across()
    norm_step()
    out_step()
    send_in(2, 2)
    finish(1)
    if last:
        out_across()
    pass_on(0)
    send_in(0, 3)
    pass_on(1)
    finish(2)
    if last:
        gain_along_z()
        send_in(1, 3)
        pass_on(2)
        relay(0)
        send_in(2, 3)
        go_home()
        relay(1)
        gain_across()
        finish(3)
        pass_on(3)
        relay(2)
        relay(3)
    else:
        send_in(1, 3)
        result_step()
        send_in(2, 3)
        g_gather.middle()
        dot_gather.middle()
        finish(3)

    if last:

        @pl.when(c == layer)
        def _():
            for ch in chunks:
                x_copy(0, ch).wait_recv()
                ya_copy(1, ch).wait_recv()
                for who in range(CORES):
                    x_copy(who, ch).wait_send()
                    ya_copy(who, ch).wait_send()
                    relay_copy(who, ch).wait()
            for who in range(CORES):
                xo_copy(who).wait()

        @pl.when(c != layer)
        def _():
            for i, (xx, yy) in enumerate(((x, y), (1 - x, y), (x, 1 - y), (1 - x, 1 - y))):
                for who in range(CORES):
                    for ch in chunks:
                        all_part(2 * xx + who, yy, ch)[...] = late_refs[i][who, span_of(ch)]
            for i, xx in enumerate((x, 1 - x)):
                for who in range(CORES):
                    out_part(2 * xx + who)[...] = late_out_refs[i][who]

    if last:
        for i in range(3):
            t3_copy(i).wait_recv()
        t1_buf[...] = (t2_sum[...] + t3_buf[0]) + (t3_buf[1] + t3_buf[2])

        @pl.when(c == layer)
        def _():
            for i in range(3):
                g3_copy(i).wait_recv()
            total = (g_all[...] + g_buf[4]) + (g_buf[5] + g_buf[6])
            t1_buf[6:7, :D] = total[0:1]
            for away in (1, 2, 3):
                g2_copy(away).wait_send()
            for i in range(3):
                g3_copy(i).wait_send()

        @pl.when(c != layer)
        def _():
            g1_copy().wait_send()

        own_totals(z, t1_buf, total_refs)

        t1_copy().wait_send()
        for away in (1, 2, 3):
            t2_copy(away).wait_send()
        for i in range(3):
            t3_copy(i).wait_send()
    else:
        g_gather.end()
        dot_gather.end()
        r_core_copy().wait_send()
        r_x_copy().wait_send()

    if last:

        @pl.when(jnp.logical_not(at_home))
        def _():
            home_copy(0).wait_send()

        for m in range(MICRO):

            @pl.when((c == layer) & jnp.logical_not(guest_self[m]))
            def _():
                home_copy(m).wait_recv()

    n_core_copy().wait_send()
    n_x_copy().wait_send()
    for i in range(3):
        for ch in chunks:
            z_copy(shard_at(i), ch).wait_send()
    for i in range(4):
        for ch in chunks[2:]:
            y_copy(shard_at(i), ch).wait_send()


    @pl.when(c != layer)
    def _():
        for ch in chunks:
            owner_copy(ch).wait_send()
        owner_out_copy().wait_send()

    if not last:

        @pl.when(c == layer)
        def _():
            for ch in chunks:
                owner_copy(ch).wait_recv()
            owner_out_copy().wait_recv()


def small_totals(layer, quarter, refs, norm_grad, tiny):
    conv_ref, gain_ref, head_ref = refs
    width, group = DI // GROUP, DI // 16
    lane = iota((8, width), 1)
    wide = jnp.where(iota((8, width), 0) == 5, jnp.broadcast_to(gain_ref[0:1], (8, width)), conv_ref[:, :width])
    for zz in range(4):
        moved = turn_by(wide, group, [(k - zz) % GROUP for k in range(GROUP)], quarter)
        tiny[layer, :, zz * width : (zz + 1) * width] = jnp.where(
            lax.div(lane, group) == quarter, moved, 0.0
        )
    tiny[layer, :, DI:] = conv_ref[:, width:]
    tiny[layer, 6:7, :D] = jnp.zeros((1, D), jnp.float32) if norm_grad is None else norm_grad
    per = H // 16
    given, head = iota((LANES, LANES), 0), iota((LANES, LANES), 1)
    taken = (lax.rem(lax.div(head, per), 4) == quarter) & (head < H)
    taken = taken & (given == lax.div(head, 4 * per) * per + lax.rem(head, per))
    heads = exact(head_ref[...], jnp.where(taken, 1.0, 0.0))
    for row in range(3):
        tiny[layer, 6:7, D + row * LANES : D + (row + 1) * LANES] = heads[row : row + 1]


def own_totals(z, whole, refs):
    norm_ref, taps_ref, bias_ref, *head_refs, gain_ref = refs
    piece = CONV // 4
    taps = turn_by(whole[...], piece, [(4 - k) % 4 for k in range(4)], z)
    taps_ref[...] = taps[0:KW, :piece]
    bias_ref[...] = taps[KW : KW + 1, :piece]
    width = DI // 4
    gain_ref[...] = whole[:, pl.ds(pl.multiple_of(z * width, LANES), width)][5:6]
    norm_ref[...] = whole[:, pl.ds(pl.multiple_of(z * LANE_PART, LANES), LANE_PART)][6:7]
    per = H // 4
    for row, ref in enumerate(head_refs):
        heads = whole[:, D + row * LANES : D + (row + 1) * LANES]
        heads = turn_by(heads, 1, [(LANES - k * per) % LANES for k in range(4)], z)
        ref[...] = heads[6:7, :per]


def layer_sums(layer, gate, grad, out_grad, theirs, mine, entering, incoming, gain, extra, *more):
    dma = pltpu.SemaphoreType.DMA
    inside = pl.BlockSpec(memory_space=pltpu.VMEM)
    span = (HALF, LANE_PART)
    out = (OUT_PART, D)
    steps = len(STEPS)
    two = (CORES, steps)
    rows = entering.shape
    half, whole = jnp.bfloat16, jnp.float32
    last = layer == 0
    out_shape = [
        jax.ShapeDtypeStruct((GROUP, LOCAL, LANE_PART) if last else (CORES,) + span, half),
        jax.ShapeDtypeStruct((DI // GROUP, D) if last else (CORES,) + out, half),
        jax.ShapeDtypeStruct((MICRO,) + rows if last else rows, half),
    ]
    scratch = [
        pltpu.VMEM(theirs.shape, half),
        pltpu.VMEM(rows, half),
        pltpu.VMEM(rows, half),
        pltpu.VMEM(rows, half),
        pltpu.VMEM((4,) + span, half),
        pltpu.VMEM((5,) + span, half),
        pltpu.VMEM((4,) + span, half),
        pltpu.VMEM(out, half),
        pltpu.VMEM(out, half),
        dma((4, steps)), dma((4, steps)), dma((4, steps)), dma((5, steps)), dma((2,)),
        dma((steps + 1,)), dma((steps + 1,)),
        dma(two), dma(two), dma(two), dma(two), dma(two), dma(two),
        dma((CORES,)), dma((CORES,)), dma((4,)),
    ]
    if layer == 0:
        small = (8, CONV)
        piece = CONV // 4
        shapes = ((1, LANE_PART), (KW, piece), (1, piece)) + ((1, H // 4),) * 3 + ((1, DI // 4),)
        out_shape += [jax.ShapeDtypeStruct(shape, whole) for shape in shapes]
        scratch += [
            pltpu.VMEM((CORES,) + small, whole),
            pltpu.VMEM(small, whole),
            pltpu.VMEM(small, whole),
            pltpu.VMEM((3,) + small, whole),
            pltpu.VMEM(small, whole),
            pltpu.VMEM((3,) + small, whole),
            pltpu.VMEM((8, D), whole),
            pltpu.VMEM((7, 8, D), whole),
            pltpu.VMEM((8, D), whole),
            pltpu.VMEM((8, D), whole),
            dma((7,)), dma((7,)), dma((1,)), dma((MICRO,)), dma((7,)), dma((7,)),
        ]
    else:
        out_shape += [
            jax.ShapeDtypeStruct(rows, half),
            jax.ShapeDtypeStruct((GROUP * rows[0], D), half),
            jax.ShapeDtypeStruct((GROUP, 8, LANES), whole),
            jax.ShapeDtypeStruct((1, D), whole),
        ]
        out_shape += [jax.ShapeDtypeStruct((8, LANES), whole)] * 3
        scratch += [
            pltpu.VMEM(theirs.shape, half),
            pltpu.VMEM(rows, half),
            pltpu.VMEM(rows, half),
            dma((3,)), dma((3,)), dma((3,)), dma((3,)), dma((4,)),
        ]
    return pl.pallas_call(
        functools.partial(sum_kernel, layer),
        in_specs=[inside] * (9 + len(more)),
        out_specs=[inside] * 10,
        out_shape=out_shape,
        scratch_shapes=scratch,
        compiler_params=pltpu.CompilerParams(
            collective_id=2 + layer, has_side_effects=True, vmem_limit_bytes=VMEM_BYTES
        ),
        name="layer_sums",
    )(gate, grad, out_grad, theirs, mine, entering, incoming, gain, extra, *more)


def assemble_kernel(part_ref, shared_ref, out_ref, total_ref, out_total_ref):
    turn = pl.program_id(0)
    step = DI // 16

    @pl.when(turn == 8)
    def _():
        shared = [shared_ref[i, :SHARED].astype(jnp.float32) for i in range(GROUP)]
        total_ref[:SHARED] = (shared[0] + shared[1]) + (shared[2] + shared[3])

    @pl.when(turn < 8)
    def _():
        for i in range(GROUP):
            total_ref[i * step : (i + 1) * step] = part_ref[i].astype(jnp.float32)
        out_total_ref[0] = out_ref[...].astype(jnp.float32)


def assemble_rows(parts, out):
    lanes = parts.shape[-1]
    step = DI // 16
    some = out.shape[0] // 8

    def near(i):
        return jnp.minimum(i, 7)

    return pl.pallas_call(
        assemble_kernel,
        grid=(9,),
        in_specs=[
            pl.BlockSpec((GROUP, step, lanes), lambda i: (0, near(i), 0)),
            pl.BlockSpec((GROUP, 2 * step, lanes), lambda i: (0, 4, 0)),
            pl.BlockSpec((some, out.shape[1]), lambda i: (near(i), 0)),
        ],
        out_specs=[
            pl.BlockSpec((GROUP * step, lanes), lambda i: (i, 0)),
            pl.BlockSpec((1, some, out.shape[1]), lambda i: (0, near(i), 0)),
        ],
        out_shape=[
            jax.ShapeDtypeStruct((DI + CONV + H, lanes), jnp.float32),
            jax.ShapeDtypeStruct((1,) + out.shape, jnp.float32),
        ],
        compiler_params=pltpu.CompilerParams(vmem_limit_bytes=VMEM_BYTES),
        name="assemble_rows",
    )(parts, parts, out)


def per_device_split(
    boundary_in,
    lengths,
    seq_order,
    norm_gain,
    in_weight,
    conv_weight,
    conv_bias,
    dt_bias,
    a_log,
    d_skip,
    out_gain,
    out_weight,
):
    c = lax.axis_index("section")
    z = lax.axis_index("shard")
    r = lax.axis_index("rep")
    y, x = r // 2, r % 2
    block = boundary_in.shape[3]
    rows = GROUP * block
    width = DI // GROUP
    heads = H // GROUP
    span = width + 2 * N
    quarter = 2 * x + c

    def spot(cc, zz, rr):
        return (cc * 4 + zz) * 4 + rr

    def home(m, zz, rr):
        return spot(zz % 2, 2 * m + rr % 2, (rr // 2) * 2 + zz // 2)

    axes = ("section", "shard", "rep")

    params = (norm_gain, conv_weight, conv_bias, dt_bias, a_log, d_skip, out_gain)
    lanes = -(-conv_bias.shape[1] // LANES) * LANES
    given = (conv_weight[0], conv_bias, out_gain, norm_gain, dt_bias, a_log, d_skip)
    flat = [jnp.pad(p, ((0, 0), (0, lanes - p.shape[1]))) for p in given]
    flat = jnp.concatenate(flat + [jnp.zeros((6, lanes), jnp.bfloat16)], axis=0)
    in_rows = jnp.swapaxes(in_weight[0], 0, 1)
    w_in0, w_out0, source, normed0, small, norms = enter_first(
        in_rows, out_weight[0], boundary_in, flat
    )
    late_in = after(boundary_in, source)[0, :, 0]
    arrivals = [
        lax.ppermute(
            late_in[m], axes, [(spot(1, zz, rr), home(m, zz, rr)) for zz in range(4) for rr in range(4)]
        )
        for m in range(MICRO)
    ]
    cotangent = jnp.where(z < 2, *arrivals)

    order = jnp.stack([lengths[:, 0], seq_order[:, 0]])
    order = jnp.where(x == z % 2, order, swap_x(order))
    order = lax.dynamic_index_in_dim(order, z // 2, 1, False)
    chosen = (order[1][:, None] == jnp.arange(NSEQ, dtype=jnp.int32)[None, :]).astype(jnp.int32)
    finish = jnp.cumsum(jnp.sum(chosen * order[0][None, :], axis=1), dtype=jnp.int32)

    def segment_of(positions):
        found = jnp.sum((positions[:, None] >= finish[None, :]).astype(jnp.int32), axis=1)
        return jnp.where(positions < 0, -1, found)

    token = jnp.arange(rows, dtype=jnp.int32)
    segment = segment_of(token)
    opening = token // Q * Q
    columns = [segment_of(token - lag) == segment for lag in range(1, KW)]
    columns.append(segment_of(opening - 1) == segment)
    columns.append(segment_of(opening + (Q - 1)) == segment)
    columns = [column.astype(jnp.float32) for column in columns] + [segment.astype(jnp.float32)]
    marks = jnp.stack(columns + [jnp.zeros((rows,), jnp.float32)] * 2, axis=1)
    seg_row = segment.astype(jnp.float32)[None]

    def own(v):
        return lax.dynamic_slice_in_dim(v, (2 * x + c) * block, block, 0)

    def row_sums(v):
        v = v + swap_core(v)
        return v + swap_x(v)

    def forward(layer, normed, w_in):
        projected = projection(normed, w_in)
        gg, squares, mixer, starts = mixer_forward(layer, projected, marks, seg_row, small)
        return gg, squares.reshape((rows // LANES, LANES)), (normed, projected, mixer, starts)

    def inverse(sums):
        return lax.rsqrt(sums / DI + EPSILON)

    def out_sum(gg, out_inv, g):
        outgoing = low(gg.astype(jnp.float32) * out_inv)
        grad = low(mm(outgoing, g, 0, 0)).reshape((4, OUT_PART, D))
        return lax.psum_scatter(grad, "shard", scatter_dimension=0, tiled=False)

    def backward(layer, kept, og, per_row, ready=(), sent_on=()):
        normed, projected, out, starts = kept
        gate_grad, out_grad, gains = gate_backward(
            layer, projected, small, out, og, per_row, DI
        )
        gate = low(mm(gate_grad, normed, 0, 0)).reshape((2, GATE_HALF, D))
        sent = lax.dynamic_index_in_dim(gate, 1 - y, 0, False)
        received = swap_y(sent)
        gate = lax.dynamic_index_in_dim(gate, y, 0, False)
        pg, conv, head = mixer_backward(
            layer, projected, marks, seg_row, small, out, starts, out_grad, after(gate_grad, sent, *ready)
        )
        pg = after(pg, *sent_on)
        gate = low(gate.astype(jnp.float32) + received.astype(jnp.float32))
        rest = low(mm(pg[:, GATE:], normed, 0, 0))
        return pg, gate, rest, (conv, gains, head)

    gg0, squares0, kept0 = forward(0, normed0, w_in0)
    theirs, mine = group_parts(gg0, w_out0)
    w_in1, w_out1, added0, middle, normed1, g1, out_inv0 = enter_second(
        in_rows, out_weight[0], theirs, mine, squares0, source, norms[1, 0:1], cotangent
    )
    out_inv0 = out_inv0.reshape((rows, 1))
    og1 = mm(g1, w_out1, 1, 1)
    gg1, squares1, kept1 = forward(1, normed1, w_in1)
    dots1 = jnp.sum(gg1.astype(jnp.float32) * og1, axis=1).reshape((rows // LANES, LANES))
    sums1 = row_sums(jnp.stack([squares1, dots1]))
    out_inv1 = inverse(sums1[0]).reshape((rows, 1))
    per_row1 = jnp.concatenate([out_inv1, out_inv1 * sums1[1].reshape((rows, 1))], axis=1)
    out_theirs, out_mine = group_parts(gg1, w_out1)
    out_part1 = out_sum(gg1, out_inv1, g1)
    pg1, gate1, rest1, small_grads1 = backward(1, kept1, og1, per_row1)
    theirs, mine = group_parts(pg1, w_in1)
    in_own, out_own, result, middle_grad, g0, dots0, norm_grad1, *_ = layer_sums(
        1, gate1, rest1, out_part1, theirs, mine, middle, cotangent, norms[1, 0:1], added0,
        out_theirs, out_mine, own(out_inv1),
    )
    dots0 = dots0[:, : block // LANES].reshape((rows, 1))

    def on_second(v, flip):
        return lax.ppermute(v, ("section", "rep"), [(4 + i, 4 + (i ^ flip)) for i in range(4)])

    in_near, in_across = on_second(in_own, 1), on_second(in_own, 2)
    out_near = on_second(out_own, 1)
    in_far = on_second(in_across, 1)
    results = [
        lax.ppermute(
            result, axes, [(home(m, zz, rr), spot(1, zz, rr)) for zz in range(4) for rr in range(4)]
        )
        for m in range(MICRO)
    ]

    og0 = mm(g0, w_out0, 1, 1)
    out_part0 = out_sum(gg0, out_inv0, after(g0, *results))
    per_row0 = jnp.concatenate([out_inv0, dots0], axis=1)
    pg0, gate0, rest0, small_grads0 = backward(
        0, kept0, og0, per_row0, (in_own, out_own), (in_near, in_across, out_near)
    )
    theirs, mine = group_parts(pg0, w_in0)
    in_all, out_all, entry_grads, *totals = layer_sums(
        0, gate0, rest0, out_part0, theirs, mine, source, middle_grad, norms[0, 0:1], norm_grad1,
        *small_grads0, *small_grads1, in_own, in_near, in_across, in_far, out_own, out_near,
    )
    in_total, out_total = assemble_rows(in_all, out_all)
    in_total = jnp.swapaxes(in_total, 0, 1)[None]

    boundary = jnp.stack(
        [jnp.where(c == 0, entry_grads[m], results[m]) for m in range(MICRO)]
    ).astype(jnp.float32)[None, :, None]

    norm_total, conv_total, bias_total, dt_total, log_total, skip_total, gain_total = totals
    return (
        boundary,
        norm_total,
        in_total,
        conv_total[None],
        bias_total,
        dt_total,
        log_total,
        skip_total,
        gain_total,
        out_total,
    )


def solution(mesh):
    fits = mesh.shape["shard"] == GROUP and mesh.shape["rep"] == 4
    return jax.shard_map(
        per_device_split if fits else per_device,
        mesh=mesh,
        in_specs=(
            P("section", None, "rep", "shard", None),
            P(None, "rep", None),
            P(None, "rep", None),
            P("section", "shard"),
            P("section", "shard", None),
            P("section", None, "shard"),
            P("section", "shard"),
            P("section", "shard"),
            P("section", "shard"),
            P("section", "shard"),
            P("section", "shard"),
            P("section", "shard", None),
        ),
        out_specs=(
            P("section", None, "rep", "shard", None),
            P("section", "shard"),
            P("section", "shard", None),
            P("section", None, "shard"),
            P("section", "shard"),
            P("section", "shard"),
            P("section", "shard"),
            P("section", "shard"),
            P("section", "shard"),
            P("section", "shard", None),
        ),
        check_vma=False,
    )
```

```python
import functools

import jax
import jax.numpy as jnp
from jax import lax
from jax.experimental import pallas as pl
from jax.experimental.pallas import tpu as pltpu
from jax.sharding import PartitionSpec as P

D = 1536
P_SIZE = 64
N = 128
KW = 4
BLOCK = 256
MICRO = 2
NSEQ = 4
DI = 3072
H = 48
CONV = 3328


EPSILON = 1e-05
PRECISE = lax.Precision.HIGHEST


def from_behind(shard, axis, by):
    devices = lax.axis_size(axis)
    pairs = [(i, i + by) for i in range(devices) if 0 <= i + by < devices]
    return lax.ppermute(shard, axis, pairs)


def entering(value, axis, join, neutral):
    count, mine = (lax.axis_size(axis), lax.axis_index(axis))
    pieces = jax.tree.map(lambda part: lax.all_gather(part, axis), value)
    subtotal = jax.tree.map(
        lambda part, zero: jnp.full_like(part, 0) + jnp.asarray(zero, part.dtype), value, neutral
    )

    def turn(position, subtotal):
        longer = join(subtotal, jax.tree.map(lambda part: part[position], pieces))
        return jax.tree.map(lambda new, old: jnp.where(position < mine, new, old), longer, subtotal)

    return lax.fori_loop(0, count - 1, turn, subtotal)


def entering_2(shard, axis, join, neutral):
    count = lax.axis_size(axis)
    place = lax.axis_index(axis)
    ahead = count - 1 - place
    gathered = jax.tree.map(
        lambda a, kind: lax.all_gather(a.astype(kind), axis),
        shard,
        jax.tree.map(lambda a: jnp.bfloat16 if a.dtype == jnp.float32 else a.dtype, shard),
    )
    state = jax.tree.map(lambda a, e: jnp.zeros_like(a) + jnp.asarray(e, a.dtype), shard, neutral)

    def one(turn, state):
        source = count - 1 - turn
        return join(
            state,
            jax.tree.map(
                lambda a, own: lax.dynamic_index_in_dim(a, source, 0, False).astype(own.dtype),
                gathered,
                shard,
            ),
        )

    return lax.fori_loop(0, ahead, one, state)


def contract(left, right, left_dim, right_dim):
    return lax.dot_general(
        left, right, (((left_dim,), (right_dim,)), ((), ())), preferred_element_type=jnp.float32
    )


def input_norm(source, gain):
    inv_rms = lax.rsqrt(jnp.mean(source * source, axis=-1, keepdims=True) + EPSILON)
    return source * inv_rms * gain


def block_step(carry_state, pieces):
    x_heads, b_rows, c_rows, log_decay, step_size, segment, before = pieces
    running = jnp.cumsum(log_decay, axis=0)
    places = jnp.arange(x_heads.shape[0])
    linked = (places[:, None] >= places[None, :]) & (segment[:, None] == segment[None, :])
    linked3 = linked[:, :, None]
    gap_sums = jnp.where(linked3, running[:, None, :] - running[None, :, :], 0.0)
    decays = jnp.where(linked3, jnp.exp(gap_sums), 0.0)
    scores = jnp.dot(c_rows, b_rows.T, precision=PRECISE)
    mixing = scores[:, :, None] * decays * step_size[None, :, :]
    inside_part = jnp.einsum("tsh,shp->thp", mixing, x_heads, precision=PRECISE)
    carried = (segment == before).astype(jnp.float32)
    reach = jnp.exp(running) * carried[:, None]
    carried_part = (
        jnp.einsum("tn,hpn->thp", c_rows, carry_state, precision=PRECISE) * reach[:, :, None]
    )
    closing = segment[-1]
    tail_weight = (
        jnp.exp(running[-1][None, :] - running)
        * step_size
        * (segment == closing).astype(jnp.float32)[:, None]
    )
    fresh_state = jnp.einsum("sh,shp,sn->hpn", tail_weight, x_heads, b_rows, precision=PRECISE)
    retained = jnp.exp(running[-1]) * (closing == before).astype(jnp.float32)
    return (retained[:, None, None] * carry_state + fresh_state, inside_part + carried_part)


def conv_inputs(wide_rows, raw_step, conv_weight, conv_bias, dt_bias, a_log, lag_masks):
    rows_here = raw_step.shape[0]
    conv_sum = conv_bias + conv_weight[KW - 1] * wide_rows[KW - 1 :]
    for lag in range(1, KW):
        conv_sum = (
            conv_sum
            + conv_weight[KW - 1 - lag]
            * wide_rows[KW - 1 - lag : KW - 1 - lag + rows_here]
            * lag_masks[lag - 1][:, None]
        )
    active = jax.nn.silu(conv_sum)
    x_heads = active[:, :DI].reshape(rows_here, H, P_SIZE)
    b_rows = active[:, DI : DI + N]
    c_rows = active[:, DI + N :]
    step_size = jax.nn.softplus(raw_step + dt_bias)
    log_decay = -step_size * jnp.exp(a_log)
    return (x_heads, b_rows, c_rows, log_decay, step_size)


def local_scan(x_heads, b_rows, c_rows, log_decay, step_size, segment, befores, seg_before):
    rows_here = x_heads.shape[0]

    def blocks(member):
        return member.reshape((rows_here // BLOCK, BLOCK) + member.shape[1:])

    start_state = jnp.zeros((H, P_SIZE, N), jnp.float32)
    pieces = (
        blocks(x_heads),
        blocks(b_rows),
        blocks(c_rows),
        blocks(log_decay),
        blocks(step_size),
        blocks(segment),
        befores,
    )
    end_state, mixer_out = lax.scan(jax.checkpoint(block_step), start_state, pieces)
    retained = jnp.exp(jnp.sum(log_decay, axis=0)) * (segment[-1] == seg_before).astype(jnp.float32)
    return (mixer_out.reshape(rows_here, H, P_SIZE), end_state, retained)


def state_entry(c_rows, log_decay, state_in, carried):
    reach = jnp.exp(jnp.cumsum(log_decay, axis=0)) * carried[:, None]
    return jnp.einsum("tn,hpn->thp", c_rows, state_in, precision=PRECISE) * reach[:, :, None]


def gate_norm(mixer_out, x_heads, d_skip, gate_part, out_gain):
    rows_here = x_heads.shape[0]
    total_out = mixer_out + d_skip[:, None] * x_heads
    gated = total_out.reshape(rows_here, DI) * jax.nn.silu(gate_part)
    inv_gated = lax.rsqrt(jnp.mean(gated * gated, axis=-1, keepdims=True) + EPSILON)
    return gated * inv_gated * out_gain


def carry_forward(earlier, later):
    return (earlier[0] * later[0], later[0][:, None, None] * earlier[1] + later[1])


def carry_backward(earlier, later):
    return (later[0] * earlier[0], later[1] + later[0][:, None, None] * earlier[1])


def segment_marks(lengths, seq_order, micro_slot, row_start, rows_here):
    micro_slot = jnp.clip(micro_slot, 0, MICRO - 1)
    seq_lengths = lax.dynamic_index_in_dim(lengths[:, 0], micro_slot, 0, keepdims=False)
    row_order = lax.dynamic_index_in_dim(seq_order[:, 0], micro_slot, 0, keepdims=False)
    picks = (row_order[:, None] == jnp.arange(NSEQ, dtype=jnp.int32)[None, :]).astype(jnp.int32)
    placed = jnp.sum(picks * seq_lengths[None, :], axis=1)
    finish = jnp.cumsum(placed, dtype=jnp.int32)
    positions = row_start + jnp.arange(-(KW - 1), rows_here, dtype=jnp.int32)
    extended = jnp.sum((positions[:, None] >= finish[None, :]).astype(jnp.int32), axis=1)
    extended = jnp.where(positions < 0, -1, extended)
    segment = extended[KW - 1 :]
    seg_before = extended[KW - 2]
    lag_masks = jnp.stack(
        [
            (extended[KW - 1 - lag : KW - 1 - lag + rows_here] == segment).astype(jnp.float32)
            for lag in range(1, KW)
        ]
    )
    befores = jnp.concatenate([seg_before[None], segment[:-1]])[::BLOCK]
    carried = (segment == seg_before).astype(jnp.float32)
    return (segment, lag_masks, befores, seg_before, carried)


def mixer_pass(projected, weights, marks):
    norm_gain, in_weight, conv_weight, conv_bias, dt_bias, a_log, d_skip, out_gain, out_weight = (
        weights
    )
    segment, lag_masks, befores, seg_before, carried = marks
    rows_here = projected.shape[0]
    gate_part = projected[:, :DI].astype(jnp.float32)
    mixed_part = projected[:, DI : DI + CONV]
    raw_step = projected[:, DI + CONV :].astype(jnp.float32)
    rim_rows = from_behind(mixed_part[rows_here - (KW - 1) :], "shard", 1)
    wide_rows = jnp.concatenate([rim_rows, mixed_part], axis=0).astype(jnp.float32)

    def conv_section(wide_rows, raw_step, conv_weight, conv_bias, dt_bias, a_log):
        return conv_inputs(wide_rows, raw_step, conv_weight, conv_bias, dt_bias, a_log, lag_masks)

    conv_outs, conv_pull = jax.vjp(
        conv_section, wide_rows, raw_step, conv_weight, conv_bias, dt_bias, a_log
    )
    x_heads, b_rows, c_rows, log_decay, step_size = conv_outs

    def scan_section(x_heads, b_rows, c_rows, log_decay, step_size):
        return local_scan(
            x_heads, b_rows, c_rows, log_decay, step_size, segment, befores, seg_before
        )

    scan_outs, scan_pull = jax.vjp(scan_section, x_heads, b_rows, c_rows, log_decay, step_size)
    local_out, end_state, retained = scan_outs
    identity = (jnp.ones((H,), jnp.float32), jnp.zeros((H, P_SIZE, N), jnp.float32))
    prefix = entering((retained, end_state), "shard", carry_forward, identity)
    state_in = prefix[1]

    def entry_section(c_rows, log_decay, state_in):
        return state_entry(c_rows, log_decay, state_in, carried)

    entered, entry_pull = jax.vjp(entry_section, c_rows, log_decay, state_in)
    mixer_out = local_out + entered
    outgoing, norm_pull = jax.vjp(gate_norm, mixer_out, x_heads, d_skip, gate_part, out_gain)
    return (
        outgoing.astype(jnp.bfloat16),
        (conv_pull, scan_pull, entry_pull, norm_pull, retained, state_in),
    )


def mamba_forward(source, weights, marks):
    normed = input_norm(source, weights[0]).astype(jnp.bfloat16)
    projected = jnp.dot(normed, weights[1], preferred_element_type=jnp.float32).astype(jnp.bfloat16)
    outgoing, unused_pulls = mixer_pass(projected, weights, marks)
    return source + jnp.dot(outgoing, weights[8], preferred_element_type=jnp.float32)


def mamba_backward(source, incoming, weights, marks):
    norm_gain, in_weight, conv_weight, conv_bias, dt_bias, a_log, d_skip, out_gain, out_weight = (
        weights
    )
    rows_here = source.shape[0]
    normed, front_pull = jax.vjp(input_norm, source, norm_gain)
    normed_low = normed.astype(jnp.bfloat16)
    projected = jnp.dot(normed_low, in_weight, preferred_element_type=jnp.float32).astype(
        jnp.bfloat16
    )
    outgoing, pulls = mixer_pass(projected, weights, marks)
    conv_pull, scan_pull, entry_pull, norm_pull, retained, state_in = pulls
    incoming_low = incoming.astype(jnp.bfloat16)
    out_weight_grad = contract(outgoing, incoming_low, 0, 0)
    outgoing_grad = contract(incoming_low, out_weight, 1, 1)
    mixer_grad, x_grad_a, d_skip_grad, gate_grad, out_gain_grad = norm_pull(outgoing_grad)
    c_grad_a, decay_grad_a, direct = entry_pull(mixer_grad)
    identity = (jnp.ones((H,), jnp.float32), jnp.zeros((H, P_SIZE, N), jnp.float32))
    suffix = entering_2((retained, direct), "shard", carry_backward, identity)
    later_grad = suffix[1]
    retained_grad = jnp.sum(later_grad * state_in, axis=(1, 2))
    x_grad_b, b_grad, c_grad_b, decay_grad_b, step_grad = scan_pull(
        (mixer_grad, later_grad, retained_grad)
    )
    conv_grads = conv_pull(
        (x_grad_a + x_grad_b, b_grad, c_grad_a + c_grad_b, decay_grad_a + decay_grad_b, step_grad)
    )
    wide_grad, raw_grad, conv_weight_grad, conv_bias_grad, dt_bias_grad, a_log_grad = conv_grads
    back_rows = from_behind(wide_grad[: KW - 1].astype(jnp.bfloat16), "shard", -1).astype(
        jnp.float32
    )
    filler = jnp.zeros((rows_here - (KW - 1), CONV), jnp.float32)
    mixed_grad = wide_grad[KW - 1 :] + jnp.concatenate([filler, back_rows], axis=0)
    projected_grad = jnp.concatenate([gate_grad, mixed_grad, raw_grad], axis=1).astype(jnp.bfloat16)
    in_weight_grad = contract(normed_low, projected_grad, 0, 0)
    normed_grad = contract(projected_grad, in_weight, 1, 1)
    source_grad, norm_gain_grad = front_pull(normed_grad)
    weight_grads = (
        norm_gain_grad,
        in_weight_grad,
        conv_weight_grad,
        conv_bias_grad,
        dt_bias_grad,
        a_log_grad,
        d_skip_grad,
        out_gain_grad,
        out_weight_grad,
    )
    return (incoming + source_grad, weight_grads)


def per_device(
    boundary_in,
    lengths,
    seq_order,
    norm_gain,
    in_weight,
    conv_weight,
    conv_bias,
    dt_bias,
    a_log,
    d_skip,
    out_gain,
    out_weight,
):
    section_index = lax.axis_index("section")
    is_first = section_index == 0
    rows_here = boundary_in.shape[3]
    row_start = lax.axis_index("shard") * rows_here

    def current():
        whole = (
            lax.all_gather(norm_gain, "shard", axis=1, tiled=True),
            lax.all_gather(in_weight, "shard", axis=1, tiled=True),
            lax.all_gather(conv_weight, "shard", axis=2, tiled=True),
            lax.all_gather(conv_bias, "shard", axis=1, tiled=True),
            lax.all_gather(dt_bias, "shard", axis=1, tiled=True),
            lax.all_gather(a_log, "shard", axis=1, tiled=True),
            lax.all_gather(d_skip, "shard", axis=1, tiled=True),
            lax.all_gather(out_gain, "shard", axis=1, tiled=True),
            lax.all_gather(out_weight, "shard", axis=1, tiled=True),
        )
        return tuple(
            (
                member[0] if slot_index in (1, 8) else member[0].astype(jnp.float32)
                for slot_index, member in enumerate(whole)
            )
        )

    source_rows = boundary_in[0, :, 0]
    arrived = jnp.zeros((rows_here, D), jnp.bfloat16)
    inputs = []
    results = []
    for step_index in range(MICRO + 1):
        own_rows = source_rows[min(step_index, MICRO - 1)]
        layer_in = jnp.where(is_first, own_rows, arrived)
        inputs.append(layer_in)
        marks = segment_marks(lengths, seq_order, step_index - section_index, row_start, rows_here)
        layer_out = mamba_forward(layer_in.astype(jnp.float32), current(), marks)
        results.append(layer_out)
        if step_index < MICRO:
            arrived = from_behind(layer_out.astype(jnp.bfloat16), "section", 1)
    returned = jnp.zeros((rows_here, D), jnp.bfloat16)
    totals = None
    source_grads = []
    for step_index in range(MICRO + 1):
        micro_slot = step_index - 1 + section_index
        is_valid = (micro_slot >= 0) & (micro_slot < MICRO)
        own_rows = source_rows[min(step_index, MICRO - 1)]
        incoming = jnp.where(is_first, returned, own_rows).astype(jnp.float32)
        incoming = jnp.where(is_valid, incoming, 0.0)
        layer_in = jnp.where(
            is_first, inputs[max(step_index - 1, 0)], inputs[min(step_index + 1, MICRO)]
        )
        marks = segment_marks(lengths, seq_order, micro_slot, row_start, rows_here)
        source_grad, weight_grads = mamba_backward(
            layer_in.astype(jnp.float32), incoming, current(), marks
        )
        if totals is None:
            totals = tuple(weight_grads)
        else:
            totals = tuple((earlier + added for earlier, added in zip(totals, weight_grads)))
        source_grads.append(source_grad)
        if step_index < MICRO:
            returned = from_behind(source_grad.astype(jnp.bfloat16), "section", -1)
    boundary = jnp.stack(
        [
            jnp.where(is_first, source_grads[micro_pos + 1], results[micro_pos + 1])
            for micro_pos in range(MICRO)
        ]
    )[None, :, None]
    shares = (
        lax.psum_scatter(
            totals[0][None].astype(jnp.bfloat16), "shard", scatter_dimension=1, tiled=True
        ).astype(jnp.float32),
        lax.psum_scatter(
            totals[1][None].astype(jnp.bfloat16), "shard", scatter_dimension=1, tiled=True
        ).astype(jnp.float32),
        lax.psum_scatter(
            totals[2][None].astype(jnp.bfloat16), "shard", scatter_dimension=2, tiled=True
        ).astype(jnp.float32),
        lax.psum_scatter(
            totals[3][None].astype(jnp.bfloat16), "shard", scatter_dimension=1, tiled=True
        ).astype(jnp.float32),
        lax.psum_scatter(
            totals[4][None].astype(jnp.bfloat16), "shard", scatter_dimension=1, tiled=True
        ).astype(jnp.float32),
        lax.psum_scatter(
            totals[5][None].astype(jnp.bfloat16), "shard", scatter_dimension=1, tiled=True
        ).astype(jnp.float32),
        lax.psum_scatter(
            totals[6][None].astype(jnp.bfloat16), "shard", scatter_dimension=1, tiled=True
        ).astype(jnp.float32),
        lax.psum_scatter(
            totals[7][None].astype(jnp.bfloat16), "shard", scatter_dimension=1, tiled=True
        ).astype(jnp.float32),
        lax.psum_scatter(
            totals[8][None].astype(jnp.bfloat16), "shard", scatter_dimension=1, tiled=True
        ).astype(jnp.float32),
    )
    reduced = (
        lax.psum(shares[0].astype(jnp.bfloat16), "rep").astype(jnp.float32),
        lax.psum(shares[1].astype(jnp.bfloat16), "rep").astype(jnp.float32),
        lax.psum(shares[2].astype(jnp.bfloat16), "rep").astype(jnp.float32),
        lax.psum(shares[3].astype(jnp.bfloat16), "rep").astype(jnp.float32),
        lax.psum(shares[4].astype(jnp.bfloat16), "rep").astype(jnp.float32),
        lax.psum(shares[5].astype(jnp.bfloat16), "rep").astype(jnp.float32),
        lax.psum(shares[6].astype(jnp.bfloat16), "rep").astype(jnp.float32),
        lax.psum(shares[7].astype(jnp.bfloat16), "rep").astype(jnp.float32),
        lax.psum(shares[8].astype(jnp.bfloat16), "rep").astype(jnp.float32),
    )
    return (boundary,) + tuple(reduced)


Q = 128
LANES = 128
VMEM_BYTES = 56 * 1024 * 1024
EXACT = lax.Precision.HIGHEST


def mm(a, b, da=1, db=0):
    return lax.dot_general(
        a, b, (((da,), (db,)), ((), ())), preferred_element_type=jnp.float32
    )


def exact(a, b):
    return jnp.dot(a, b, precision=EXACT, preferred_element_type=jnp.float32)


def low(v):
    return v.astype(jnp.bfloat16)


def split(v, parts):
    found = []
    for _ in range(parts):
        found.append(low(v))
        v = v - found[-1].astype(jnp.float32)
    return found


def pick_sums(v, ones, parts=2):
    return sum(mm(part, ones) for part in split(v, parts))


def sums_of(ones, v, parts=3):
    return sum(mm(ones, part) for part in split(v, parts))


def iota(shape, dim):
    return lax.broadcasted_iota(jnp.int32, shape, dim)


def pair_cols(v, p):
    rows = v.shape[0]
    left = jnp.broadcast_to(v[:, 2 * p : 2 * p + 1], (rows, LANES))
    right = jnp.broadcast_to(v[:, 2 * p + 1 : 2 * p + 2], (rows, LANES))
    return jnp.where(iota((rows, LANES), 1) < LANES // 2, left, right)


def widen(v, pairs):
    return jnp.concatenate([pair_cols(v, p) for p in range(pairs)], axis=1)


def stack_pair(v, p):
    block = v[:, p * LANES : (p + 1) * LANES]
    left = iota(block.shape, 1) < LANES // 2
    zero = jnp.zeros_like(block)
    return jnp.concatenate([jnp.where(left, block, zero), jnp.where(left, zero, block)], axis=0)


def softplus(v):
    small = jnp.exp(-jnp.abs(v))
    series = small * (1 + small * (-1 / 2 + small * (1 / 3 + small * (-1 / 4 + small / 5))))
    return jnp.maximum(v, 0.0) + jnp.where(small < 0.01, series, jnp.log(1 + small))


def sigmoid(v):
    return 1.0 / (1.0 + jnp.exp(-v))


def gate_of(v):
    return 0.5 * jnp.tanh(0.5 * v) + 0.5


def head_picks():
    quarter = 2 * lax.rem(lax.axis_index("rep"), 2) + lax.axis_index("section")
    given, local = iota((64, LANES), 0), iota((64, LANES), 1)
    per = H // 16
    taken = (lax.rem(lax.div(given, per), 4) == quarter) & (given < H)
    taken = taken & (local == lax.div(given, 4 * per) * per + lax.rem(given, per))
    return jnp.where(taken, 1.0, 0.0).astype(jnp.bfloat16)


def chunk_parts(width, proj, before8, marks, seg_row, small_ref, pick):
    conv_w = small_ref[0, 0:KW]
    conv_b = small_ref[0, KW : KW + 1]
    dt_bias = small_ref[0, 7:8, :LANES]
    rate = small_ref[0, 8:9, :LANES]
    span = width + 2 * LANES
    gate = proj[:, :width].astype(jnp.float32)
    mixed = proj[:, width : width + span].astype(jnp.float32)
    raw = mm(proj[:, width + span :], pick)
    shifts = [mixed]
    top = iota((8, span), 0)
    for lag in range(1, KW):
        rolled = pltpu.roll(mixed, lag, 0)
        head = jnp.where(top < lag, pltpu.roll(before8, lag, 0), rolled[:8])
        moved = jnp.concatenate([head, rolled[8:]], axis=0)
        shifts.append(moved * marks[:, lag - 1 : lag])
    conv = conv_b
    for lag in range(KW):
        conv = conv + conv_w[KW - 1 - lag : KW - lag] * shifts[lag]
    sig = gate_of(conv)
    active = conv * sig
    stepped = raw + dt_bias
    step = softplus(stepped)
    decay = -step * rate
    lower = iota((Q, Q), 0) >= iota((Q, Q), 1)
    total = sums_of(jnp.where(lower, 1.0, 0.0).astype(jnp.bfloat16), decay)
    linked = lower & (marks[:, 5:6] == seg_row)
    shut = jnp.where(linked, 0.0, -1e30)
    reach = jnp.exp(total) * marks[:, 3:4]
    tail = jnp.exp(total[Q - 1 : Q] - total) * marks[:, 4:5]
    return gate, mixed, shifts, conv, sig, active, stepped, step, decay, total, shut, reach, tail


def forward_kernel(
    width, proj_ref, marks_ref, seg_ref, small_ref, gg_ref, squares_ref, mixer_ref, starts_ref, state, before,
):
    pairs = width // LANES

    @pl.when(pl.program_id(0) == 0)
    def _():
        state[...] = jnp.zeros_like(state)
        before[...] = jnp.zeros_like(before)

    gate, mixed, _, _, _, active, _, step, _, total, shut, reach, tail = chunk_parts(
        width, proj_ref[...], before[...], marks_ref[...], seg_ref[...], small_ref, head_picks()
    )
    skip, gain = small_ref[0, 6:7, :width], small_ref[0, 5:6, :width]
    before[...] = mixed[Q - 8 :]
    heads = active[:, :width]
    b_low = low(active[:, width : width + LANES])
    c_low = low(active[:, width + LANES :])
    entry = state[...]
    starts_ref[0] = entry
    scores = mm(c_low, b_low, 1, 1)
    total_t = total.T
    scaled = heads * widen(step, pairs)
    scaled_low = low(scaled)
    inside = []
    for p in range(pairs):
        both = []
        for h in (2 * p, 2 * p + 1):
            both.append(low(jnp.exp(total[:, h : h + 1] - total_t[h : h + 1] + shut) * scores))
        inside.append(mm(jnp.concatenate(both, axis=1), stack_pair(scaled_low, p)))
    mixer = jnp.concatenate(inside, axis=1) + widen(reach, pairs) * mm(c_low, low(entry))
    b_turned = low(active[:, width : width + LANES].T)
    state[...] = entry * widen(reach[Q - 1 : Q], pairs) + mm(
        b_turned, low(scaled * widen(tail, pairs))
    )
    out = mixer + skip * heads
    mixer_ref[...] = out
    gated = out * (gate * gate_of(gate))
    squares = jnp.sum(gated * gated, axis=1, keepdims=True)
    squares_ref[0] = jnp.broadcast_to(squares, (Q, LANES)).T[:1]
    gg_ref[...] = low(gated * gain)


def gate_kernel(width, whole_width, proj_ref, small_ref, out_ref, og_ref, rows_ref, gate_grad_ref, out_grad_ref, sums_ref):
    @pl.when(pl.program_id(0) == 0)
    def _():
        sums_ref[...] = jnp.zeros_like(sums_ref)

    gate = proj_ref[...].astype(jnp.float32)
    inv = rows_ref[:, 0:1]
    dots = rows_ref[:, 1:2]
    og = og_ref[...]
    out = out_ref[...]
    gate_sig = gate_of(gate)
    gate_on = gate * gate_sig
    hat = out * gate_on * inv
    gated_grad = inv * (small_ref[0, 5:6, :width] * og - hat * (dots * (1.0 / whole_width)))
    out_grad_ref[...] = low(gated_grad * gate_on)
    gate_grad_ref[...] = low(gated_grad * out * (gate_sig * (1.0 + gate * (1.0 - gate_sig))))
    sums_ref[0:1] += jnp.sum(hat * og, axis=0, keepdims=True)


def gate_backward(layer, projected, small, out, og, per_row, whole_width):
    rows, width = out.shape
    step = 2 * Q

    def by_row(count):
        return pl.BlockSpec((step, count), lambda i: (i, 0))

    half = jax.ShapeDtypeStruct((rows, width), jnp.bfloat16)
    return pl.pallas_call(
        functools.partial(gate_kernel, width, whole_width),
        grid=(rows // step,),
        in_specs=[by_row(width), small_spec(layer), by_row(width), by_row(width), by_row(2)],
        out_specs=[by_row(width), by_row(width), full_spec((8, width))],
        out_shape=[half, half, jax.ShapeDtypeStruct((8, width), jnp.float32)],
        compiler_params=pltpu.CompilerParams(vmem_limit_bytes=VMEM_BYTES),
        cost_estimate=cost(6),
        name="gate_backward",
    )(projected, small, out, og, per_row)


def backward_kernel(
    width, proj_ref, rim_ref, marks_ref, seg_ref, small_ref, out_ref, starts_ref, out_grad_ref,
    gate_grad_ref, pg_ref, conv_ref, head_ref, later, after, skips,
):
    pairs = width // LANES
    turn = pl.program_id(0)
    chunk = pl.num_programs(0) - 1 - turn

    @pl.when(turn == 0)
    def _():
        later[...] = jnp.zeros_like(later)
        after[...] = jnp.zeros_like(after)
        skips[...] = jnp.zeros_like(skips)
        conv_ref[...] = jnp.zeros_like(conv_ref)
        head_ref[...] = jnp.zeros_like(head_ref)

    span = width + 2 * LANES
    marks = marks_ref[...]
    rim = rim_ref[...][8:, width : width + span].astype(jnp.float32)
    rim = jnp.where(chunk > 0, rim, 0.0)
    pick = head_picks()
    skip, rate = small_ref[0, 6:7, :width], small_ref[0, 8:9, :LANES]
    _, mixed, shifts, conv, sig, active, stepped, step, decay, total, shut, reach, tail = (
        chunk_parts(
            width, proj_ref[...], rim, marks, seg_ref[...], small_ref, pick
        )
    )
    heads = active[:, :width]
    b_low = low(active[:, width : width + LANES])
    c_low = low(active[:, width + LANES :])

    grad_low = out_grad_ref[...]
    out_grad = grad_low.astype(jnp.float32)
    mixer = out_ref[...] - skip * heads

    entry = starts_ref[0]
    entry_low = low(entry)
    late = later[...]
    late_low = low(late)
    scores = mm(c_low, b_low, 1, 1)
    total_t = total.T
    step_wide = widen(step, pairs)
    scaled = heads * step_wide
    scaled_low = low(scaled)
    from_late = widen(tail, pairs) * mm(b_low, late_low)
    inside = []
    score_grad = jnp.zeros((Q, Q), jnp.float32)
    for p in range(pairs):
        gains = []
        both = []
        for h in (2 * p, 2 * p + 1):
            gain = jnp.exp(total[:, h : h + 1] - total_t[h : h + 1] + shut)
            gains.append(gain)
            both.append(low(gain * scores))
        stacked = stack_pair(grad_low, p)
        inside.append(mm(jnp.concatenate(both, axis=0), stacked, 0, 0))
        mix_grad = mm(stacked, scaled_low[:, p * LANES : (p + 1) * LANES], 1, 1)
        score_grad = score_grad + gains[0] * mix_grad[:Q] + gains[1] * mix_grad[Q:]
    scaled_grad = jnp.concatenate(inside, axis=1) + from_late
    reached = low(widen(reach, pairs) * out_grad)
    score_low = low(score_grad)
    c_grad = mm(score_low, b_low) + mm(reached, entry_low, 1, 1)
    b_grad = mm(score_low, c_low, 0, 0) + mm(low(scaled * widen(tail, pairs)), late_low, 1, 1)
    kept = widen(reach[Q - 1 : Q], pairs)
    later[...] = late * kept + mm(c_low, reached, 0, 0)

    scaled_seen = scaled_low.astype(jnp.float32)
    balance = out_grad * mixer - scaled_seen * scaled_grad
    closing = jnp.sum(scaled_seen * from_late, axis=0, keepdims=True) + kept * jnp.sum(
        late * entry, axis=0, keepdims=True
    )
    picks = iota((width, LANES), 0) // (LANES // 2) == iota((width, LANES), 1)
    picks = jnp.where(picks, 1.0, 0.0).astype(jnp.bfloat16)
    sums = pick_sums(
        jnp.concatenate([balance, heads * scaled_grad, jnp.broadcast_to(closing, (8, width))], 0),
        picks,
    )
    upper = jnp.where(iota((Q, Q), 0) <= iota((Q, Q), 1), 1.0, 0.0).astype(jnp.bfloat16)
    decay_grad = sums_of(upper, sums[:Q]) + sums[2 * Q : 2 * Q + 1]
    step_grad = sums[Q : 2 * Q] - decay_grad * rate
    raw_grad = step_grad * sigmoid(stepped)

    head_grad = step_wide * scaled_grad + skip * out_grad
    conv_grad = jnp.concatenate([head_grad, b_grad, c_grad], axis=1) * (
        sig * (1.0 + conv * (1.0 - sig))
    )
    mixed_grad = small_ref[0, KW - 1 : KW] * conv_grad
    bottom = iota((8, span), 0)
    for lag in range(1, KW):
        sent = conv_grad * marks[:, lag - 1 : lag]
        rolled = pltpu.roll(sent, Q - lag, 0)
        ending = jnp.where(
            bottom >= 8 - lag, pltpu.roll(after[lag - 1], 8 - lag, 0), rolled[Q - 8 :]
        )
        mixed_grad = mixed_grad + small_ref[0, KW - 1 - lag : KW - lag] * jnp.concatenate(
            [rolled[: Q - 8], ending], axis=0
        )
        after[lag - 1] = sent[:8]
    pg_ref[:, :width] = gate_grad_ref[...]
    pg_ref[:, width:] = low(
        jnp.concatenate([mixed_grad, mm(low(raw_grad), pick, 1, 1)], axis=1)
    )

    skips[0:1] += jnp.sum(out_grad * heads, axis=0, keepdims=True)
    for lag in range(KW):
        conv_ref[KW - 1 - lag : KW - lag] += jnp.sum(
            conv_grad * shifts[lag], axis=0, keepdims=True
        )
    conv_ref[KW : KW + 1] += jnp.sum(conv_grad, axis=0, keepdims=True)
    head_ref[0:1] += jnp.sum(raw_grad, axis=0, keepdims=True)
    head_ref[1:2] += jnp.sum(decay_grad * decay, axis=0, keepdims=True)

    @pl.when(chunk == 0)
    def _():
        head_ref[2:3] = pick_sums(skips[...], picks, 3)[0:1]


def cost(micros):
    return pl.CostEstimate(flops=micros * 1_100_000_000, bytes_accessed=0, transcendentals=0)


def small_spec(layer):
    return pl.BlockSpec((1, 16, 2 * D // 3), lambda i: (layer, 0, 0))


def full_spec(shape):
    return pl.BlockSpec(shape, lambda i: (0,) * len(shape))


def product_kernel(left_ref, weight_ref, theirs_ref, mine_ref, ordered_ref):
    c = lax.axis_index("section")
    block = left_ref.shape[0] // 4

    @pl.when(pl.program_id(0) == 0)
    def _():
        for i in range(4):
            at = 2 * (i % 2) + (1 - c if i < 2 else c)
            rows = pl.ds(pl.multiple_of(at * block, block), block)
            ordered_ref[i * block : (i + 1) * block] = left_ref[rows]

    found = mm(ordered_ref[...], weight_ref[...])
    theirs_ref[...] = low(found[: 2 * block])
    mine_ref[...] = found[2 * block :]


def group_parts(left, weight):
    rows, depth = left.shape
    columns = weight.shape[1]
    step = columns // 3
    half = rows // 2
    return pl.pallas_call(
        product_kernel,
        grid=(3,),
        in_specs=[
            pl.BlockSpec((rows, depth), lambda i: (0, 0)),
            pl.BlockSpec((depth, step), lambda i: (0, i)),
        ],
        out_specs=[pl.BlockSpec((half, step), lambda i: (0, i))] * 2,
        out_shape=[
            jax.ShapeDtypeStruct((half, columns), jnp.bfloat16),
            jax.ShapeDtypeStruct((half, columns), jnp.float32),
        ],
        scratch_shapes=[pltpu.VMEM((rows, depth), jnp.bfloat16)],
        compiler_params=pltpu.CompilerParams(vmem_limit_bytes=VMEM_BYTES),
        cost_estimate=cost(6),
        name="group_parts",
    )(left, weight)


def projection_kernel(left_ref, weight_ref, out_ref):
    out_ref[...] = low(mm(left_ref[...], weight_ref[...], 1, 1))


def projection(left, weight):
    rows, depth = left.shape
    columns = weight.shape[0]
    step = 640
    return pl.pallas_call(
        projection_kernel,
        grid=(pl.cdiv(columns, step),),
        in_specs=[
            pl.BlockSpec((rows, depth), lambda i: (0, 0)),
            pl.BlockSpec((step, depth), lambda i: (i, 0)),
        ],
        out_specs=pl.BlockSpec((rows, step), lambda i: (0, i)),
        out_shape=jax.ShapeDtypeStruct((rows, columns), jnp.bfloat16),
        compiler_params=pltpu.CompilerParams(vmem_limit_bytes=VMEM_BYTES),
        cost_estimate=cost(6),
        name="projection",
    )(left, weight)


def mixer_forward(layer, projected, marks, seg_row, small):
    rows, columns = projected.shape
    width = DI // 4
    chunks = rows // Q
    span = width + 2 * LANES

    def by_row(count):
        return pl.BlockSpec((Q, count), lambda i: (i, 0))

    return pl.pallas_call(
        functools.partial(forward_kernel, width),
        grid=(chunks,),
        in_specs=[
            by_row(columns), by_row(8), pl.BlockSpec((1, Q), lambda i: (0, i)), small_spec(layer),
        ],
        out_specs=[
            by_row(width),
            pl.BlockSpec((1, 1, Q), lambda i: (i, 0, 0)),
            by_row(width),
            pl.BlockSpec((1, LANES, width), lambda i: (i, 0, 0)),
        ],
        out_shape=[
            jax.ShapeDtypeStruct((rows, width), jnp.bfloat16),
            jax.ShapeDtypeStruct((chunks, 1, Q), jnp.float32),
            jax.ShapeDtypeStruct((rows, width), jnp.float32),
            jax.ShapeDtypeStruct((chunks, LANES, width), jnp.float32),
        ],
        scratch_shapes=[
            pltpu.VMEM((LANES, width), jnp.float32),
            pltpu.VMEM((8, span), jnp.float32),
        ],
        compiler_params=pltpu.CompilerParams(vmem_limit_bytes=VMEM_BYTES),
        cost_estimate=cost(16),
        name="mixer_forward",
    )(projected, marks, seg_row, small)


def mixer_backward(layer, projected, marks, seg_row, small, out, starts, out_grad, gate_grad):
    rows, columns = projected.shape
    width = out.shape[1]
    chunks = rows // Q
    span = width + 2 * LANES

    def by_row(count):
        return pl.BlockSpec((Q, count), lambda i: (chunks - 1 - i, 0))

    rim = pl.BlockSpec(
        (16, columns), lambda i: (jnp.maximum((chunks - 1 - i) * (Q // 16) - 1, 0), 0)
    )
    return pl.pallas_call(
        functools.partial(backward_kernel, width),
        grid=(chunks,),
        in_specs=[
            by_row(columns),
            rim,
            by_row(8),
            pl.BlockSpec((1, Q), lambda i: (0, chunks - 1 - i)),
            small_spec(layer),
            by_row(width),
            pl.BlockSpec((1, LANES, width), lambda i: (chunks - 1 - i, 0, 0)),
            by_row(width),
            by_row(width),
        ],
        out_specs=[
            by_row(columns),
            full_spec((8, span)),
            full_spec((8, LANES)),
        ],
        out_shape=[
            jax.ShapeDtypeStruct((rows, columns), jnp.bfloat16),
            jax.ShapeDtypeStruct((8, span), jnp.float32),
            jax.ShapeDtypeStruct((8, LANES), jnp.float32),
        ],
        scratch_shapes=[
            pltpu.VMEM((LANES, width), jnp.float32),
            pltpu.VMEM((KW - 1, 8, span), jnp.float32),
            pltpu.VMEM((8, width), jnp.float32),
        ],
        compiler_params=pltpu.CompilerParams(vmem_limit_bytes=VMEM_BYTES),
        cost_estimate=cost(33),
        name="mixer_backward",
    )(projected, projected, marks, seg_row, small, out, starts, out_grad, gate_grad)


CORES = 2
GROUP = 4
SHARED = CONV - DI + H
LOCAL = 2 * DI // GROUP + SHARED + 16
HALF = LOCAL // 2
CHUNKS = 2
LANE_PART = D // 4
OUT_PART = DI // 16
UNITS = CHUNKS + 1
GATE = DI // GROUP
GATE_HALF = GATE // 2
REST_HALF = HALF - GATE_HALF
STEPS = ((0, 192), (192, 192), (0, 272), (272, 272))


def place():
    c, z, r = (lax.axis_index(name) for name in ("section", "shard", "rep"))
    return c, z, lax.div(r, 2), lax.rem(r, 2)


def weight_pieces(quarter):
    part = DI // 16
    found = []
    for side in range(2):
        for zz in range(4):
            found.append(
                (side * 4 * part + zz * part, side * DI + zz * 4 * part + quarter * part, part)
            )
    found.append((8 * part, 2 * DI, SHARED))
    return found


def mesh_copy(source, target, send, recv, device):
    return pltpu.make_async_remote_copy(
        src_ref=source, dst_ref=target, send_sem=send, recv_sem=recv,
        device_id=device, device_id_type=pl.DeviceIdType.MESH,
    )


def greet(barrier, device):
    pl.semaphore_signal(barrier, inc=1, device_id=device, device_id_type=pl.DeviceIdType.MESH)


def rows_at(start, count):
    return pl.ds(pl.multiple_of(start, 16), count)


class WeightGather:
    def __init__(self, layer, in_ref, out_ref, w_ref, wo_ref, sems):
        self.layer, self.in_ref, self.out_ref = layer, in_ref, out_ref
        self.w_ref, self.wo_ref = w_ref, wo_ref
        (
            self.local_sem, self.core_send, self.core_recv, self.right_send, self.left_send,
            self.z_recv, self.y_send, self.y_recv,
        ) = sems
        self.c, self.z, self.y, self.x = place()
        self.core = {"section": 1 - self.c}
        self.y_other = {"rep": (1 - self.y) * 2 + self.x}

    def own_pieces(self, quarter):
        lanes = pl.ds(pl.multiple_of(self.z * LANE_PART, LANES), LANE_PART)
        found = []
        for at, start, count in weight_pieces(quarter):
            found.append((self.in_ref.at[rows_at(start, count)], self.w_ref.at[pl.ds(at, count), lanes]))
        found.append(
            (
                self.out_ref.at[rows_at(quarter * OUT_PART, OUT_PART)],
                self.wo_ref.at[rows_at(self.z * OUT_PART, OUT_PART)],
            )
        )
        return found

    def local_copies(self):
        return [
            pltpu.make_async_copy(source, target, self.local_sem.at[i])
            for i, (source, target) in enumerate(self.own_pieces(2 * self.x + self.c))
        ]

    def core_copies(self):
        return [
            mesh_copy(source, target, self.core_send.at[i], self.core_recv.at[i], self.core)
            for i, (source, target) in enumerate(self.own_pieces(2 * self.x + 1 - self.c))
        ]

    def begin(self):
        lanes = pl.ds(pl.multiple_of(self.z * LANE_PART, LANES), LANE_PART)
        self.w_ref[LOCAL - 16 :, lanes] = jnp.zeros((16, LANE_PART), self.w_ref.dtype)

        @pl.when(self.c == self.layer)
        def _():
            for copy in self.core_copies():
                copy.start()
            for copy in self.local_copies():
                copy.start()
            for copy in self.local_copies():
                copy.wait()

        @pl.when(self.c != self.layer)
        def _():
            for copy in self.core_copies():
                copy.wait_recv()

    def slab(self, unit, shard, side):
        if unit == CHUNKS:
            return self.wo_ref.at[rows_at(shard * OUT_PART + side * (OUT_PART // 2), OUT_PART // 2)]
        return self.w_ref.at[
            rows_at(side * HALF + unit * (HALF // CHUNKS), HALF // CHUNKS),
            pl.ds(pl.multiple_of(shard * LANE_PART, LANES), LANE_PART),
        ]

    def z_copy(self, unit, shard, step, k):
        piece = self.slab(unit, shard, self.y)
        send = (self.right_send if step > 0 else self.left_send).at[unit, k]
        return mesh_copy(piece, piece, send, self.z_recv.at[unit, shard], {"shard": self.z + step})

    def y_copy(self, unit, shard, side):
        piece = self.slab(unit, shard, side)
        return mesh_copy(
            piece, piece, self.y_send.at[unit, shard], self.y_recv.at[unit, shard], self.y_other
        )

    def cases(self, step, k):
        shard = self.z - k * step
        there = (shard >= 0) if step > 0 else (shard <= 3)
        more = (self.z < 3) if step > 0 else (self.z > 0)
        return shard, there, more

    def first(self, unit):
        for step in (1, -1):
            _, _, more = self.cases(step, 0)

            @pl.when(more)
            def _():
                self.z_copy(unit, self.z, step, 0).start()

    def arrive(self, unit, k):
        for step in (1, -1):
            shard, there, more = self.cases(step, k)

            @pl.when(there)
            def _():
                self.z_copy(unit, shard, step, 0).wait_recv()

                @pl.when(more)
                def _():
                    self.z_copy(unit, shard, step, k).start()

                self.y_copy(unit, shard, self.y).start()

    def end(self):
        for unit in range(UNITS):
            for away in (1, 2, 3):
                shard = lax.rem(self.z + away, 4)
                self.y_copy(unit, shard, 1 - self.y).wait_recv()
                self.y_copy(unit, shard, self.y).wait_send()
            for step in (1, -1):
                for k in range(3):
                    shard, there, more = self.cases(step, k)

                    @pl.when(there & more)
                    def _():
                        self.z_copy(unit, shard, step, k).wait_send()

        @pl.when(self.c == self.layer)
        def _():
            for copy in self.core_copies():
                copy.wait_send()


def weight_scratch():
    dma = pltpu.SemaphoreType.DMA
    return [
        dma((10,)), dma((10,)), dma((10,)),
        dma((UNITS, 3)), dma((UNITS, 3)), dma((UNITS, 4)), dma((UNITS, 4)), dma((UNITS, 4)),
    ]


class RowGather:
    def __init__(self, whole, count, sems):
        self.whole, self.count = whole, count
        self.send, self.recv = sems
        self.c, self.z, self.y, self.x = place()

    def copy(self, i, xx, cc, device):
        if self.count is None:
            piece = self.whole.at[2 * xx + cc]
        else:
            piece = self.whole.at[rows_at((2 * xx + cc) * self.count, self.count)]
        return mesh_copy(piece, piece, self.send.at[i], self.recv.at[i], device)

    def near(self):
        return self.copy(0, self.x, self.c, {"rep": 2 * self.y + 1 - self.x})

    def other(self):
        return self.copy(1, self.x, self.c, {"section": 1 - self.c})

    def far(self):
        return self.copy(2, 1 - self.x, self.c, {"section": 1 - self.c})

    def begin(self, value):
        if self.count is None:
            self.whole[2 * self.x + self.c] = value
        else:
            self.whole[rows_at((2 * self.x + self.c) * self.count, self.count)] = value
        self.near().start()
        self.other().start()

    def middle(self):
        self.near().wait_recv()
        self.far().start()

    def end(self):
        self.near().wait_send()
        self.other().wait()
        self.far().wait()


def normal_rows(rows, gain):
    inv = lax.rsqrt(jnp.mean(rows * rows, axis=-1, keepdims=True) + EPSILON)
    return low(rows * inv * gain)


def turn_by(value, step, counts, which):
    found = pltpu.roll(value, step * counts[0], 1) if counts[0] else value
    for k in range(1, len(counts)):
        other = pltpu.roll(value, step * counts[k], 1) if counts[k] else value
        found = jnp.where(which == k, other, found)
    return found


def small_parts(layer, quarter, params_ref, small_ref):
    width, group = DI // GROUP, DI // 16
    piece = CONV // 4
    lane = iota((16, width), 1)
    pieces = [params_ref[4 * layer + zz].astype(jnp.float32) for zz in range(4)]
    gap = jnp.zeros((16, CONV - pieces[0].shape[1]), jnp.float32)
    conv = jnp.zeros((16, CONV), jnp.float32)
    for zz in range(4):
        own = jnp.where(iota(pieces[zz].shape, 1) < piece, pieces[zz], 0.0)
        conv = conv + pltpu.roll(jnp.concatenate([own, gap], axis=1), zz * piece, 1)

    def turned(part, zz):
        moved = turn_by(part, group, [(zz - k) % GROUP for k in range(GROUP)], quarter)
        return jnp.where(lax.div(lane, group) == zz, moved, 0.0)

    taps = sum(turned(conv[:, zz * width : (zz + 1) * width], zz) for zz in range(4))
    gain = sum(turned(pieces[zz][:, :width], zz) for zz in range(4))
    per = H // 16
    head, given = iota((LANES, LANES), 1), iota((LANES, LANES), 0)
    heads = jnp.zeros((16, LANES), jnp.float32)
    for zz in range(4):
        taken = (lax.div(head, per) == zz) & (given == per * quarter + lax.rem(head, per))
        heads = heads + mm(low(pieces[zz][:, :LANES]), jnp.where(taken, 1.0, 0.0).astype(jnp.bfloat16))
    wide_head = iota((LANES, width), 1)
    wide = jnp.where(lax.div(wide_head, P_SIZE) == iota((LANES, width), 0), 1.0, 0.0)
    skip = mm(low(heads), wide.astype(jnp.bfloat16))
    small_ref[layer] = jnp.zeros(small_ref.shape[1:], jnp.float32)
    small_ref[layer, 0:5, :width] = taps[0:5]
    small_ref[layer, 0:5, width:] = conv[0:5, DI:]
    small_ref[layer, 5:6, :width] = gain[5:6]
    small_ref[layer, 6:7, :width] = skip[9:10]
    small_ref[layer, 7:8, :LANES] = heads[7:8]
    rate = jnp.exp(heads[8:9])
    small_ref[layer, 8:9, :LANES] = jnp.where(iota((1, LANES), 1) < H // GROUP, rate, 0.0)


def enter_first_kernel(
    in_ref, out_ref, blocks_ref, flat_ref, w_ref, wo_ref, rows_ref, normed_ref, small_ref, norms_ref,
    params_ref, row_send, row_recv, home_send, home_recv, p_send, p_recv, *sems,
):
    c, z, y, x = place()
    weights = WeightGather(0, in_ref, out_ref, w_ref, wo_ref, sems)
    gather = RowGather(normed_ref, rows_ref.shape[0], (row_send, row_recv))
    source = {"section": 0, "shard": 2 * x + c, "rep": 2 * y + lax.rem(z, 2)}
    from_self = (c == 0) & (z == 2 * x) & (x == lax.rem(z, 2))
    targets = tuple(
        {"section": lax.rem(z, 2), "shard": 2 * m + x, "rep": 2 * y + lax.div(z, 2)}
        for m in range(MICRO)
    )
    to_self = tuple(
        (lax.rem(z, 2) == 0) & (z == 2 * m + x) & (x == lax.div(z, 2)) for m in range(MICRO)
    )
    others = [{"section": 1 - c}]
    for away in (1, 2, 3):
        others.append({"shard": lax.rem(z + away, 4)})
        others.append({"section": 1 - c, "shard": lax.rem(z + away, 4)})

    barrier = pltpu.get_barrier_semaphore()
    for device in others + [{"rep": 2 * y + 1 - x}, {"rep": 2 * (1 - y) + x}]:
        greet(barrier, device)

    @pl.when(jnp.logical_not(from_self))
    def _():
        greet(barrier, source)

    guests = sum(jnp.logical_not(own).astype(jnp.int32) for own in to_self)
    pl.semaphore_wait(barrier, 9 + jnp.where(c == 0, guests, 0))

    def home_copy(m):
        return mesh_copy(
            blocks_ref.at[0, m, 0], rows_ref, home_send.at[m], home_recv.at[0], targets[m]
        )

    def own_copy(m):
        return pltpu.make_async_copy(blocks_ref.at[0, m, 0], rows_ref, home_send.at[m])

    def param_copy(i):
        return mesh_copy(
            flat_ref, params_ref.at[4 * c + z], p_send.at[i], p_recv.at[i], others[i]
        )

    def param_from(i):
        cc = c if i % 2 == 1 else 1 - c
        zz = z if i == 0 else lax.rem(z + 4 - (i + 1) // 2, 4)
        return mesh_copy(
            flat_ref, params_ref.at[4 * cc + zz], p_send.at[i], p_recv.at[i], others[i]
        )

    for m in range(MICRO):

        @pl.when((c == 0) & jnp.logical_not(to_self[m]))
        def _():
            home_copy(m).start()

        @pl.when((c == 0) & to_self[m])
        def _():
            own_copy(m).start()

    for i in range(7):
        param_copy(i).start()
    params_ref[4 * c + z] = flat_ref[...]
    weights.begin()
    for i in range(7):
        param_from(i).wait_recv()

    @pl.when(jnp.logical_not(from_self))
    def _():
        home_copy(0).wait_recv()

    for m in range(MICRO):

        @pl.when((c == 0) & to_self[m])
        def _():
            own_copy(m).wait()

    for layer in range(2):
        for zz in range(4):
            part = params_ref[4 * layer + zz].astype(jnp.float32)[6:7, :LANE_PART]
            norms_ref[layer, :, zz * LANE_PART : (zz + 1) * LANE_PART] = jnp.broadcast_to(
                part, (8, LANE_PART)
            )
    gain = norms_ref[0, 0:1]
    for unit in range(CHUNKS):
        weights.first(unit)
    gather.begin(normal_rows(rows_ref[...].astype(jnp.float32), gain))
    for k in (1, 2):
        for unit in range(CHUNKS):
            weights.arrive(unit, k)
    weights.first(CHUNKS)
    gather.middle()
    for layer in range(2):
        small_parts(layer, 2 * x + c, params_ref, small_ref)
    for unit in range(CHUNKS):
        weights.arrive(unit, 3)
    for k in (1, 2, 3):
        weights.arrive(CHUNKS, k)
    weights.end()
    gather.end()
    for i in range(7):
        param_copy(i).wait_send()
    for m in range(MICRO):

        @pl.when((c == 0) & jnp.logical_not(to_self[m]))
        def _():
            home_copy(m).wait_send()


def weight_shapes():
    return [
        jax.ShapeDtypeStruct((LOCAL, D), jnp.bfloat16),
        jax.ShapeDtypeStruct((DI // GROUP, D), jnp.bfloat16),
    ]


def enter_first(in_rows, out_rows, blocks, flat):
    dma = pltpu.SemaphoreType.DMA
    block = blocks.shape[-2]
    anywhere, inside = pl.BlockSpec(memory_space=pl.ANY), pl.BlockSpec(memory_space=pltpu.VMEM)
    return pl.pallas_call(
        enter_first_kernel,
        in_specs=[anywhere] * 3 + [inside],
        out_specs=[inside] * 6,
        out_shape=weight_shapes()
        + [
            jax.ShapeDtypeStruct((block, D), jnp.bfloat16),
            jax.ShapeDtypeStruct((GROUP * block, D), jnp.bfloat16),
            jax.ShapeDtypeStruct((CORES, 16, DI // GROUP + 2 * N), jnp.float32),
            jax.ShapeDtypeStruct((CORES, 8, D), jnp.float32),
        ],
        scratch_shapes=[pltpu.VMEM((2 * 4,) + flat.shape, jnp.bfloat16), dma((3,)), dma((3,)), dma((MICRO,)), dma((1,)), dma((7,)), dma((7,))]
        + weight_scratch(),
        compiler_params=pltpu.CompilerParams(
            collective_id=0, has_side_effects=True, vmem_limit_bytes=VMEM_BYTES
        ),
        name="enter_first",
    )(in_rows, out_rows, blocks, flat)


def enter_second_kernel(
    in_ref, out_ref, theirs_ref, mine_ref, squares_ref, entering_ref, gain_ref, g_ref,
    w_ref, wo_ref, added_ref, middle_ref, normed_ref, g_all_ref, inv_ref,
    n_core, n_send, n_across, s_core, s_mine, s_across,
    row_send, row_recv, g_send, g_recv, n_sem, s_sem, *sems,
):
    c, z, y, x = place()
    weights = WeightGather(1, in_ref, out_ref, w_ref, wo_ref, sems)
    block = entering_ref.shape[0]
    gather = RowGather(normed_ref, block, (row_send, row_recv))
    g_gather = RowGather(g_all_ref, block, (g_send, g_recv))
    core, x_other = {"section": 1 - c}, {"rep": 2 * y + 1 - x}
    barrier = pltpu.get_barrier_semaphore()
    for device in (core, x_other, {"rep": 2 * (1 - y) + x}):
        greet(barrier, device)

    @pl.when(z < 3)
    def _():
        greet(barrier, {"shard": z + 1})

    @pl.when(z > 0)
    def _():
        greet(barrier, {"shard": z - 1})

    ends = jnp.where(z == 0, 1, 0) + jnp.where(z == 3, 1, 0)
    pl.semaphore_wait(barrier, 5 - ends)

    n_core_copy = mesh_copy(theirs_ref, n_core, n_sem.at[0], n_sem.at[1], core)
    n_x_copy = mesh_copy(n_send, n_across, n_sem.at[2], n_sem.at[3], x_other)
    s_core_copy = mesh_copy(squares_ref, s_core, s_sem.at[0], s_sem.at[1], core)
    s_x_copy = mesh_copy(s_mine, s_across, s_sem.at[2], s_sem.at[3], x_other)

    n_core_copy.start()
    s_core_copy.start()
    weights.begin()
    for unit in range(CHUNKS):
        weights.first(unit)

    def summed(which):
        rows = rows_at(which * block, block)
        return mine_ref[rows] + n_core[rows].astype(jnp.float32)

    s_core_copy.wait_recv()
    s_mine[...] = squares_ref[...] + s_core[...]
    s_x_copy.start()
    n_core_copy.wait_recv()
    n_send[...] = low(summed(1 - x))
    n_x_copy.start()
    for unit in range(CHUNKS):
        weights.arrive(unit, 1)

    s_x_copy.wait_recv()
    inv_ref[...] = lax.rsqrt((s_mine[...] + s_across[...]) * (1.0 / DI) + EPSILON)
    n_x_copy.wait_recv()
    product = summed(x) + n_across[...].astype(jnp.float32)
    per = block // LANES
    here = (2 * x + c) * per
    own_inv = jnp.concatenate(
        [
            jnp.broadcast_to(inv_ref[pl.ds(here + i, 1)], (LANES, LANES)).T[:, :1]
            for i in range(per)
        ],
        axis=0,
    )
    added = own_inv * product
    added_ref[...] = added
    middle = low(entering_ref[...].astype(jnp.float32) + added)
    middle_ref[...] = middle
    gather.begin(normal_rows(middle.astype(jnp.float32), gain_ref[...]))
    g_gather.begin(g_ref[...])
    for unit in range(CHUNKS):
        weights.arrive(unit, 2)
    weights.first(CHUNKS)
    for unit in range(CHUNKS):
        weights.arrive(unit, 3)
    gather.middle()
    for k in (1, 2, 3):
        weights.arrive(CHUNKS, k)
    g_gather.middle()
    weights.end()
    gather.end()
    g_gather.end()
    n_core_copy.wait_send()
    n_x_copy.wait_send()
    s_core_copy.wait_send()
    s_x_copy.wait_send()


def enter_second(in_rows, out_rows, theirs, mine, squares, entering, gain, g):
    dma = pltpu.SemaphoreType.DMA
    block = entering.shape[0]
    anywhere, inside = pl.BlockSpec(memory_space=pl.ANY), pl.BlockSpec(memory_space=pltpu.VMEM)
    whole = jax.ShapeDtypeStruct((GROUP * block, D), jnp.bfloat16)
    return pl.pallas_call(
        enter_second_kernel,
        in_specs=[anywhere] * 2 + [inside] * 6,
        out_specs=[inside] * 7,
        out_shape=weight_shapes()
        + [
            jax.ShapeDtypeStruct((block, D), jnp.float32),
            jax.ShapeDtypeStruct((block, D), jnp.bfloat16),
            whole,
            whole,
            jax.ShapeDtypeStruct(squares.shape, jnp.float32),
        ],
        scratch_shapes=[
            pltpu.VMEM(theirs.shape, jnp.bfloat16),
            pltpu.VMEM(entering.shape, jnp.bfloat16),
            pltpu.VMEM(entering.shape, jnp.bfloat16),
            pltpu.VMEM(squares.shape, jnp.float32),
            pltpu.VMEM(squares.shape, jnp.float32),
            pltpu.VMEM(squares.shape, jnp.float32),
            dma((3,)), dma((3,)), dma((3,)), dma((3,)), dma((4,)), dma((4,)),
        ]
        + weight_scratch(),
        compiler_params=pltpu.CompilerParams(
            collective_id=1, has_side_effects=True, vmem_limit_bytes=VMEM_BYTES
        ),
        name="enter_second",
    )(in_rows, out_rows, theirs, mine, squares, entering, gain, g)


def swap_core(v):
    return lax.ppermute(v, "section", [(0, 1), (1, 0)])


def swap_x(v):
    return lax.ppermute(v, "rep", [(i, i ^ 1) for i in range(4)])


def swap_y(v):
    return lax.ppermute(v, "rep", [(i, i ^ 2) for i in range(4)])


def swap_z(v, bit):
    return lax.ppermute(v, "shard", [(i, i ^ bit) for i in range(4)])


def ordered(first, mine, other, axis=0):
    return jnp.where(first, jnp.stack([mine, other], axis), jnp.stack([other, mine], axis))


def joined(first, mine, other, axis=0):
    return jnp.where(
        first, jnp.concatenate([mine, other], axis), jnp.concatenate([other, mine], axis)
    )


def after(value, *earlier):
    return lax.optimization_barrier((value,) + earlier)[0]


def sum_kernel(layer, *refs):
    last = layer == 0
    (
        gate_ref, grad_ref, out_grad_ref, left_ref, weight_ref, entering_ref, incoming_ref, gain_ref,
        extra_ref,
    ) = refs[:9]
    if last:
        small_refs = (refs[9:12], refs[12:15])
        late_refs, late_out_refs = refs[15:19], refs[19:21]
        refs = refs[:9] + refs[21:]
    else:
        r_theirs_ref, r_mine_ref, r_inv_ref = refs[9:12]
        refs = refs[:9] + refs[12:]
    all_ref, out_all_ref, bound_ref = refs[9:12]
    (
        theirs_ref, mine_ref, n_core, n_send, n_across, n_done, y_buf, z_buf, s_buf, yo_buf, yo_mine,
        y_send, y_recv, z_send, z_recv, yo_sem, core_send, core_recv,
        x_send, x_recv, ya_send, ya_recv, relay_send, relay_recv, xo_send, xo_recv, n_sem,
    ) = refs[19:46]
    if last:
        total_refs = refs[12:19]
        tiny_mine, t1_buf, t1_sum, t2_buf, t2_sum, t3_buf, g_mine, g_buf, g_sum, g_all = refs[46:56]
        t_send, t_recv, home_send, home_recv, g_send, g_recv, late_sem = refs[56:]
    else:
        g_ref, g_all_ref, dots_ref, norm_ref = refs[12:16]
        r_core, r_send, r_across = refs[46:49]
        row_send, row_recv, dot_send, dot_recv, r_sem = refs[49:]
    c, z, y, x = place()
    quarter = 2 * x + c
    core, x_other, y_other = {"section": 1 - c}, {"rep": 2 * y + 1 - x}, {"rep": 2 * (1 - y) + x}
    chunks = range(len(STEPS))
    block = n_done.shape[0]
    copy = mesh_copy

    home = {"section": layer, "shard": quarter, "rep": 2 * y + lax.rem(z, 2)}
    at_home = (c == layer) & (z == quarter) & (x == lax.rem(z, 2))
    guests = tuple(
        {"section": lax.rem(z, 2), "shard": 2 * m + x, "rep": 2 * y + lax.div(z, 2)}
        for m in range(MICRO)
    )
    guest_self = tuple(
        (c == layer) & (lax.rem(z, 2) == layer) & (z == 2 * m + x) & (x == lax.div(z, 2))
        for m in range(MICRO)
    )
    reps = (x_other, y_other, {"rep": 2 * (1 - y) + 1 - x})
    shards = tuple({"shard": lax.rem(z + away, 4)} for away in (1, 2, 3))
    barrier = pltpu.get_barrier_semaphore()
    for device in (core,) + reps + shards:
        greet(barrier, device)
    if last:
        for m in range(MICRO):

            @pl.when((c == layer) & jnp.logical_not(guest_self[m]))
            def _():
                greet(barrier, guests[m])

        pl.semaphore_wait(barrier, 8 - at_home.astype(jnp.int32))
    else:
        pl.semaphore_wait(barrier, 7)

    orders = ((3, 2, 1, 0), (3, 0, 2, 1), (0, 3, 1, 2), (0, 1, 2, 3))

    def shard_at(i):
        found = jnp.int32(orders[3][i])
        for zz in range(3):
            found = jnp.where(z == zz, orders[zz][i], found)
        return found

    def grad_part(shard, side, ch):
        lanes = pl.ds(pl.multiple_of(shard * LANE_PART, LANES), LANE_PART)
        if ch < 2:
            return gate_ref.at[pl.ds(*STEPS[ch]), lanes]
        return grad_ref.at[rows_at(side * REST_HALF + STEPS[ch][0], STEPS[ch][1]), lanes]

    def span_of(ch):
        return pl.ds(STEPS[ch][0] + (0 if ch < 2 else GATE_HALF), STEPS[ch][1])

    def y_copy(shard, ch):
        return copy(
            grad_part(shard, 1 - y, ch), y_buf.at[shard, span_of(ch)],
            y_send.at[shard, ch], y_recv.at[shard, ch], y_other,
        )

    def z_target(shard):
        right = shard > z
        there = {"shard": jnp.clip(z + jnp.where(right, 1, -1), 0, 3)}
        slot = jnp.where(right, shard, jnp.where(shard == z - 1, 4, shard))
        return there, slot

    def z_copy(shard, ch):
        there, slot = z_target(shard)
        return copy(
            s_buf.at[shard, span_of(ch)], z_buf.at[slot, span_of(ch)],
            z_send.at[shard, ch], z_recv.at[slot, ch], there,
        )

    def z_wait(slot, ch):
        there, _ = z_target(shard_at(0))
        copy(
            s_buf.at[0, span_of(ch)], z_buf.at[slot, span_of(ch)],
            z_send.at[0, ch], z_recv.at[slot, ch], there,
        ).wait_recv()

    def all_part(which, side, ch):
        start = side * GATE_HALF if ch < 2 else GATE + side * REST_HALF
        return all_ref.at[which, rows_at(start + STEPS[ch][0], STEPS[ch][1])]

    def out_part(which):
        return out_all_ref.at[rows_at(which * OUT_PART, OUT_PART)]

    def x_copy(who, ch):
        piece = all_part(2 * x + who, y, ch)
        return copy(piece, piece, x_send.at[who, ch], x_recv.at[who, ch], x_other)

    def ya_copy(who, ch):
        piece = all_part(2 * x + who, y, ch)
        return copy(piece, piece, ya_send.at[who, ch], ya_recv.at[who, ch], y_other)

    def relay_copy(who, ch):
        if who == 0:
            piece = all_part(2 * x, 1 - y, ch)
            return copy(piece, piece, relay_send.at[0, ch], relay_recv.at[0, ch], x_other)
        piece = all_part(2 * (1 - x) + 1, y, ch)
        return copy(piece, piece, relay_send.at[1, ch], relay_recv.at[1, ch], y_other)

    def xo_copy(who):
        piece = out_part(2 * x + who)
        return copy(piece, piece, xo_send.at[who], xo_recv.at[who], x_other)

    def spread(who, ch):
        x_copy(who, ch).start()
        ya_copy(who, ch).start()

    def owner_copy(ch):
        span = span_of(ch)
        piece = all_part(quarter, y, ch) if last else all_ref.at[1 - layer, span]
        return copy(s_buf.at[z, span], piece, core_send.at[ch], core_recv.at[ch], core)

    def owner_out_copy():
        piece = out_part(quarter) if last else out_all_ref.at[1 - layer]
        return copy(
            yo_mine, piece, core_send.at[len(STEPS)], core_recv.at[len(STEPS)], core
        )

    def yo_copy():
        return copy(out_grad_ref, yo_buf, yo_sem.at[0], yo_sem.at[1], y_other)

    def n_core_copy():
        return copy(theirs_ref, n_core, n_sem.at[0], n_sem.at[1], core)

    def n_x_copy():
        return copy(n_send, n_across, n_sem.at[2], n_sem.at[3], x_other)

    def home_copy(m):
        return copy(n_done, bound_ref.at[m], home_send.at[0], home_recv.at[m], home)

    def go_home():
        for m in range(MICRO):
            there = lax.div(z, 2) == m

            @pl.when(there & jnp.logical_not(at_home))
            def _():
                home_copy(m).start()

            @pl.when(there & at_home)
            def _():
                bound_ref[m] = n_done[...]

    if last:

        def t1_copy():
            return copy(tiny_mine.at[1 - c], t1_buf, t_send.at[0], t_recv.at[0], core)

        def t2_copy(away):
            return copy(
                t1_sum, t2_buf.at[away - 1], t_send.at[away], t_recv.at[away], shards[away - 1]
            )

        def t3_copy(i):
            return copy(t2_sum, t3_buf.at[i], t_send.at[4 + i], t_recv.at[4 + i], reps[i])

        def g1_copy():
            return copy(g_mine, g_buf.at[0], g_send.at[0], g_recv.at[0], core)

        def g2_copy(away):
            return copy(g_sum, g_buf.at[away], g_send.at[away], g_recv.at[away], shards[away - 1])

        def g3_copy(i):
            return copy(g_all, g_buf.at[4 + i], g_send.at[4 + i], g_recv.at[4 + i], reps[i])

    else:

        def r_core_copy():
            return copy(r_theirs_ref, r_core, r_sem.at[0], r_sem.at[1], core)

        def r_x_copy():
            return copy(r_send, r_across, r_sem.at[2], r_sem.at[3], x_other)

        def r_summed(which):
            rows = rows_at(which * block, block)
            return r_mine_ref[rows] + r_core[rows].astype(jnp.float32)

        g_gather = RowGather(g_all_ref, block, (row_send, row_recv))
        dot_gather = RowGather(dots_ref, None, (dot_send, dot_recv))

    if not last:
        r_core_copy().start()
    for ch in chunks[2:]:
        for i in range(4):
            y_copy(shard_at(i), ch).start()
        if ch == 2:
            yo_copy().start()

    def more(shard):
        return ((shard > z) & (z > 0)) | ((shard < z) & (z < 3))

    def y_sum(shard, ch):
        own = grad_part(shard, y, ch)[...].astype(jnp.float32)
        if ch < 2:
            return own
        y_copy(shard, ch).wait_recv()
        return own + y_buf[shard, span_of(ch)].astype(jnp.float32)

    def send_in(i, ch):
        shard = shard_at(i)
        span = span_of(ch)
        both = y_sum(shard, ch)

        @pl.when(more(shard))
        def _():
            z_wait(shard, ch)
            s_buf[shard, span] = low(both + z_buf[shard, span].astype(jnp.float32))

        @pl.when(jnp.logical_not(more(shard)))
        def _():
            s_buf[shard, span] = low(both)

        z_copy(shard, ch).start()

    def finish(ch):
        span = span_of(ch)
        s_buf[z, span] = low(y_sum(z, ch))

        @pl.when(z > 0)
        def _():
            z_wait(z, ch)
            s_buf[z, span] = low(
                s_buf[z, span].astype(jnp.float32) + z_buf[z, span].astype(jnp.float32)
            )

        @pl.when(z < 3)
        def _():
            z_wait(4, ch)
            s_buf[z, span] = low(
                s_buf[z, span].astype(jnp.float32) + z_buf[4, span].astype(jnp.float32)
            )

        @pl.when(c != layer)
        def _():
            owner_copy(ch).start()

        @pl.when(c == layer)
        def _():
            if last:
                all_part(quarter, y, ch)[...] = s_buf[z, span]
                spread(layer, ch)
            else:
                all_ref[layer, span] = s_buf[z, span]

    def pass_on(ch):
        if not last:
            return

        @pl.when(c == layer)
        def _():
            owner_copy(ch).wait_recv()
            spread(1 - layer, ch)

    def relay(ch):
        if not last:
            return

        @pl.when(c == layer)
        def _():
            ya_copy(0, ch).wait_recv()
            relay_copy(0, ch).start()
            x_copy(1, ch).wait_recv()
            relay_copy(1, ch).start()

    def summed(which):
        rows = rows_at(which * block, block)
        return mine_ref[rows] + n_core[rows].astype(jnp.float32)

    def late_copies():
        pairs = []
        for i, (xx, yy) in enumerate(((x, y), (1 - x, y), (x, 1 - y), (1 - x, 1 - y))):
            for who in range(CORES):
                found, whole = late_refs[i].at[who], all_ref.at[2 * xx + who]
                pairs.append(
                    (found.at[pl.ds(0, GATE_HALF)], whole.at[rows_at(yy * GATE_HALF, GATE_HALF)])
                )
                pairs.append(
                    (
                        found.at[pl.ds(GATE_HALF, REST_HALF)],
                        whole.at[rows_at(GATE + yy * REST_HALF, REST_HALF)],
                    )
                )
        for i, xx in enumerate((x, 1 - x)):
            for who in range(CORES):
                pairs.append((late_out_refs[i].at[who], out_part(2 * xx + who)))
        return [
            pltpu.make_async_copy(source, target, late_sem.at[n])
            for n, (source, target) in enumerate(pairs)
        ]

    def start_across():
        n_core_copy().wait_recv()
        n_send[...] = low(summed(1 - x))
        n_x_copy().start()

    def norm_step():
        n_x_copy().wait_recv()
        if not last:
            r_core_copy().wait_recv()
            r_send[...] = low(r_summed(1 - x))
            r_x_copy().start()
        normed_grad = summed(x) + n_across[...].astype(jnp.float32)
        entering = entering_ref[...].astype(jnp.float32)
        inv = lax.rsqrt(jnp.mean(entering * entering, axis=-1, keepdims=True) + EPSILON)
        hat = entering * inv
        hat_grad = normed_grad * gain_ref[...]
        mean = jnp.mean(hat_grad * hat, axis=-1, keepdims=True)
        source_grad = low(incoming_ref[...].astype(jnp.float32) + inv * (hat_grad - hat * mean))
        norm_grad = jnp.sum(normed_grad * hat, axis=0, keepdims=True)
        if last:
            n_done[...] = source_grad
            g_mine[...] = jnp.broadcast_to(norm_grad, g_mine.shape)

            @pl.when(c != layer)
            def _():
                g1_copy().start()

            return
        g_ref[...] = source_grad
        g_gather.begin(source_grad)
        norm_ref[...] = norm_grad
        dots = jnp.sum(source_grad.astype(jnp.float32) * extra_ref[...], axis=1, keepdims=True)
        flat = [
            jnp.broadcast_to(dots[i * LANES : (i + 1) * LANES], (LANES, LANES)).T[:1]
            for i in range(block // LANES)
        ]
        flat.append(jnp.zeros((8 - len(flat), LANES), jnp.float32))
        dot_gather.begin(jnp.concatenate(flat, axis=0))

    def result_step():
        r_x_copy().wait_recv()
        product = r_summed(x) + r_across[...].astype(jnp.float32)
        bound_ref[...] = low(entering_ref[...].astype(jnp.float32) + r_inv_ref[...] * product)

    def out_step():
        yo_copy().wait()
        total = low(out_grad_ref[...].astype(jnp.float32) + yo_buf[...].astype(jnp.float32))
        yo_mine[...] = total

        @pl.when(c != layer)
        def _():
            owner_out_copy().start()

        @pl.when(c == layer)
        def _():
            if last:
                out_part(quarter)[...] = yo_mine[...]
            else:
                out_all_ref[layer] = yo_mine[...]

    def out_across():
        @pl.when(c == layer)
        def _():
            owner_out_copy().wait_recv()
            for who in range(CORES):
                xo_copy(who).start()

    def early_small():
        if last:
            small_totals(0, quarter, small_refs[0], None, tiny_mine)
            small_totals(1, quarter, small_refs[1], extra_ref[...], tiny_mine)
            t1_copy().start()

    def small_along_z():
        if last:
            t1_copy().wait_recv()
            t1_sum[...] = tiny_mine[c] + t1_buf[...]
            for away in (1, 2, 3):
                t2_copy(away).start()

    def small_across():
        if last:
            for away in (1, 2, 3):
                t2_copy(away).wait_recv()
            t2_sum[...] = (t1_sum[...] + t2_buf[0]) + (t2_buf[1] + t2_buf[2])
            for i in range(3):
                t3_copy(i).start()

    def gain_along_z():
        @pl.when(c == layer)
        def _():
            g1_copy().wait_recv()
            g_sum[...] = g_mine[...] + g_buf[0]
            for away in (1, 2, 3):
                g2_copy(away).start()

    def gain_across():
        @pl.when(c == layer)
        def _():
            for away in (1, 2, 3):
                g2_copy(away).wait_recv()
            g_all[...] = (g_sum[...] + g_buf[1]) + (g_buf[2] + g_buf[3])
            for i in range(3):
                g3_copy(i).start()

    def product(core_of, target):
        rows = [
            left_ref[rows_at((2 * i + core_of) * block, block)] for i in range(2)
        ]
        rows = jnp.concatenate(rows, axis=0)
        step = D // 3
        for i in range(3):
            lanes = slice(i * step, (i + 1) * step)
            target[:, lanes] = mm(rows, weight_ref[:, lanes]).astype(target.dtype)

    send_in(0, 0)
    send_in(0, 1)
    if last:

        @pl.when(c != layer)
        def _():
            for late in late_copies():
                late.start()

    product(1 - c, theirs_ref)
    n_core_copy().start()
    product(c, mine_ref)
    start_across()
    early_small()
    send_in(1, 0)
    send_in(0, 2)
    send_in(1, 1)
    small_along_z()
    send_in(2, 0)
    send_in(1, 2)
    send_in(2, 1)
    finish(0)
    small_across()
    norm_step()
    out_step()
    send_in(2, 2)
    finish(1)
    if last:
        out_across()
    pass_on(0)
    send_in(0, 3)
    pass_on(1)
    finish(2)
    if last:
        gain_along_z()
        send_in(1, 3)
        pass_on(2)
        relay(0)
        send_in(2, 3)
        go_home()
        relay(1)
        gain_across()
        finish(3)
        pass_on(3)
        relay(2)
        relay(3)
    else:
        send_in(1, 3)
        result_step()
        send_in(2, 3)
        g_gather.middle()
        dot_gather.middle()
        finish(3)

    if last:

        @pl.when(c == layer)
        def _():
            for ch in chunks:
                x_copy(0, ch).wait_recv()
                ya_copy(1, ch).wait_recv()
                for who in range(CORES):
                    x_copy(who, ch).wait_send()
                    ya_copy(who, ch).wait_send()
                    relay_copy(who, ch).wait()
            for who in range(CORES):
                xo_copy(who).wait()

        @pl.when(c != layer)
        def _():
            for late in late_copies():
                late.wait()

    if last:
        for i in range(3):
            t3_copy(i).wait_recv()
        t1_buf[...] = (t2_sum[...] + t3_buf[0]) + (t3_buf[1] + t3_buf[2])

        @pl.when(c == layer)
        def _():
            for i in range(3):
                g3_copy(i).wait_recv()
            total = (g_all[...] + g_buf[4]) + (g_buf[5] + g_buf[6])
            t1_buf[6:7, :D] = total[0:1]
            for away in (1, 2, 3):
                g2_copy(away).wait_send()
            for i in range(3):
                g3_copy(i).wait_send()

        @pl.when(c != layer)
        def _():
            g1_copy().wait_send()

        own_totals(z, t1_buf, total_refs)

        t1_copy().wait_send()
        for away in (1, 2, 3):
            t2_copy(away).wait_send()
        for i in range(3):
            t3_copy(i).wait_send()
    else:
        g_gather.end()
        dot_gather.end()
        r_core_copy().wait_send()
        r_x_copy().wait_send()

    if last:

        @pl.when(jnp.logical_not(at_home))
        def _():
            home_copy(0).wait_send()

        for m in range(MICRO):

            @pl.when((c == layer) & jnp.logical_not(guest_self[m]))
            def _():
                home_copy(m).wait_recv()

    n_core_copy().wait_send()
    n_x_copy().wait_send()
    for i in range(3):
        for ch in chunks:
            z_copy(shard_at(i), ch).wait_send()
    for i in range(4):
        for ch in chunks[2:]:
            y_copy(shard_at(i), ch).wait_send()


    @pl.when(c != layer)
    def _():
        for ch in chunks:
            owner_copy(ch).wait_send()
        owner_out_copy().wait_send()

    if not last:

        @pl.when(c == layer)
        def _():
            for ch in chunks:
                owner_copy(ch).wait_recv()
            owner_out_copy().wait_recv()


def small_totals(layer, quarter, refs, norm_grad, tiny):
    conv_ref, gain_ref, head_ref = refs
    width, group = DI // GROUP, DI // 16
    lane = iota((8, width), 1)
    wide = jnp.where(iota((8, width), 0) == 5, jnp.broadcast_to(gain_ref[0:1], (8, width)), conv_ref[:, :width])
    for zz in range(4):
        moved = turn_by(wide, group, [(k - zz) % GROUP for k in range(GROUP)], quarter)
        tiny[layer, :, zz * width : (zz + 1) * width] = jnp.where(
            lax.div(lane, group) == quarter, moved, 0.0
        )
    tiny[layer, :, DI:] = conv_ref[:, width:]
    tiny[layer, 6:7, :D] = jnp.zeros((1, D), jnp.float32) if norm_grad is None else norm_grad
    per = H // 16
    given, head = iota((LANES, LANES), 0), iota((LANES, LANES), 1)
    taken = (lax.rem(lax.div(head, per), 4) == quarter) & (head < H)
    taken = taken & (given == lax.div(head, 4 * per) * per + lax.rem(head, per))
    heads = exact(head_ref[...], jnp.where(taken, 1.0, 0.0))
    for row in range(3):
        tiny[layer, 6:7, D + row * LANES : D + (row + 1) * LANES] = heads[row : row + 1]


def own_totals(z, whole, refs):
    norm_ref, taps_ref, bias_ref, *head_refs, gain_ref = refs
    piece = CONV // 4
    taps = turn_by(whole[...], piece, [(4 - k) % 4 for k in range(4)], z)
    taps_ref[...] = taps[0:KW, :piece]
    bias_ref[...] = taps[KW : KW + 1, :piece]
    width = DI // 4
    gain_ref[...] = whole[:, pl.ds(pl.multiple_of(z * width, LANES), width)][5:6]
    norm_ref[...] = whole[:, pl.ds(pl.multiple_of(z * LANE_PART, LANES), LANE_PART)][6:7]
    per = H // 4
    for row, ref in enumerate(head_refs):
        heads = whole[:, D + row * LANES : D + (row + 1) * LANES]
        heads = turn_by(heads, 1, [(LANES - k * per) % LANES for k in range(4)], z)
        ref[...] = heads[6:7, :per]


def layer_sums(layer, gate, grad, out_grad, left, weight, entering, incoming, gain, extra, *more):
    dma = pltpu.SemaphoreType.DMA
    inside = pl.BlockSpec(memory_space=pltpu.VMEM)
    span = (HALF, LANE_PART)
    out = (OUT_PART, D)
    steps = len(STEPS)
    two = (CORES, steps)
    rows = entering.shape
    two_blocks = (2 * rows[0], rows[1])
    half, whole = jnp.bfloat16, jnp.float32
    last = layer == 0
    out_shape = [
        jax.ShapeDtypeStruct((GROUP, LOCAL, LANE_PART) if last else (CORES,) + span, half),
        jax.ShapeDtypeStruct((DI // GROUP, D) if last else (CORES,) + out, half),
        jax.ShapeDtypeStruct((MICRO,) + rows if last else rows, half),
    ]
    scratch = [
        pltpu.VMEM(two_blocks, half),
        pltpu.VMEM(two_blocks, whole),
        pltpu.VMEM(two_blocks, half),
        pltpu.VMEM(rows, half),
        pltpu.VMEM(rows, half),
        pltpu.VMEM(rows, half),
        pltpu.VMEM((4,) + span, half),
        pltpu.VMEM((5,) + span, half),
        pltpu.VMEM((4,) + span, half),
        pltpu.VMEM(out, half),
        pltpu.VMEM(out, half),
        dma((4, steps)), dma((4, steps)), dma((4, steps)), dma((5, steps)), dma((2,)),
        dma((steps + 1,)), dma((steps + 1,)),
        dma(two), dma(two), dma(two), dma(two), dma(two), dma(two),
        dma((CORES,)), dma((CORES,)), dma((4,)),
    ]
    if layer == 0:
        small = (8, CONV)
        piece = CONV // 4
        shapes = ((1, LANE_PART), (KW, piece), (1, piece)) + ((1, H // 4),) * 3 + ((1, DI // 4),)
        out_shape += [jax.ShapeDtypeStruct(shape, whole) for shape in shapes]
        scratch += [
            pltpu.VMEM((CORES,) + small, whole),
            pltpu.VMEM(small, whole),
            pltpu.VMEM(small, whole),
            pltpu.VMEM((3,) + small, whole),
            pltpu.VMEM(small, whole),
            pltpu.VMEM((3,) + small, whole),
            pltpu.VMEM((8, D), whole),
            pltpu.VMEM((7, 8, D), whole),
            pltpu.VMEM((8, D), whole),
            pltpu.VMEM((8, D), whole),
            dma((7,)), dma((7,)), dma((1,)), dma((MICRO,)), dma((7,)), dma((7,)),
            dma((20,)),
        ]
    else:
        out_shape += [
            jax.ShapeDtypeStruct(rows, half),
            jax.ShapeDtypeStruct((GROUP * rows[0], D), half),
            jax.ShapeDtypeStruct((GROUP, 8, LANES), whole),
            jax.ShapeDtypeStruct((1, D), whole),
        ]
        out_shape += [jax.ShapeDtypeStruct((8, LANES), whole)] * 3
        scratch += [
            pltpu.VMEM(two_blocks, half),
            pltpu.VMEM(rows, half),
            pltpu.VMEM(rows, half),
            dma((3,)), dma((3,)), dma((3,)), dma((3,)), dma((4,)),
        ]
    beside = 6 if last else 0
    return pl.pallas_call(
        functools.partial(sum_kernel, layer),
        in_specs=[inside] * (9 + len(more) - beside) + [pl.BlockSpec(memory_space=pl.ANY)] * beside,
        out_specs=[inside] * 10,
        out_shape=out_shape,
        scratch_shapes=scratch,
        compiler_params=pltpu.CompilerParams(
            collective_id=2 + layer, has_side_effects=True, vmem_limit_bytes=62 * 1024 * 1024
        ),
        name="layer_sums",
    )(gate, grad, out_grad, left, weight, entering, incoming, gain, extra, *more)


def assemble_kernel(part_ref, shared_ref, out_ref, total_ref, out_total_ref):
    turn = pl.program_id(0)
    step = DI // 16

    @pl.when(turn == 8)
    def _():
        shared = [shared_ref[i, :SHARED].astype(jnp.float32) for i in range(GROUP)]
        total_ref[:SHARED] = (shared[0] + shared[1]) + (shared[2] + shared[3])

    @pl.when(turn < 8)
    def _():
        for i in range(GROUP):
            total_ref[i * step : (i + 1) * step] = part_ref[i].astype(jnp.float32)
        out_total_ref[0] = out_ref[...].astype(jnp.float32)


def assemble_rows(parts, out):
    lanes = parts.shape[-1]
    step = DI // 16
    some = out.shape[0] // 8

    def near(i):
        return jnp.minimum(i, 7)

    return pl.pallas_call(
        assemble_kernel,
        grid=(9,),
        in_specs=[
            pl.BlockSpec((GROUP, step, lanes), lambda i: (0, near(i), 0)),
            pl.BlockSpec((GROUP, 2 * step, lanes), lambda i: (0, 4, 0)),
            pl.BlockSpec((some, out.shape[1]), lambda i: (near(i), 0)),
        ],
        out_specs=[
            pl.BlockSpec((GROUP * step, lanes), lambda i: (i, 0)),
            pl.BlockSpec((1, some, out.shape[1]), lambda i: (0, near(i), 0)),
        ],
        out_shape=[
            jax.ShapeDtypeStruct((DI + CONV + H, lanes), jnp.float32),
            jax.ShapeDtypeStruct((1,) + out.shape, jnp.float32),
        ],
        compiler_params=pltpu.CompilerParams(vmem_limit_bytes=VMEM_BYTES),
        name="assemble_rows",
    )(parts, parts, out)


def per_device_split(
    boundary_in,
    lengths,
    seq_order,
    norm_gain,
    in_weight,
    conv_weight,
    conv_bias,
    dt_bias,
    a_log,
    d_skip,
    out_gain,
    out_weight,
):
    c = lax.axis_index("section")
    z = lax.axis_index("shard")
    r = lax.axis_index("rep")
    y, x = r // 2, r % 2
    block = boundary_in.shape[3]
    rows = GROUP * block
    width = DI // GROUP
    heads = H // GROUP
    span = width + 2 * N
    quarter = 2 * x + c

    def spot(cc, zz, rr):
        return (cc * 4 + zz) * 4 + rr

    def home(m, zz, rr):
        return spot(zz % 2, 2 * m + rr % 2, (rr // 2) * 2 + zz // 2)

    axes = ("section", "shard", "rep")

    params = (norm_gain, conv_weight, conv_bias, dt_bias, a_log, d_skip, out_gain)
    lanes = -(-conv_bias.shape[1] // LANES) * LANES
    given = (conv_weight[0], conv_bias, out_gain, norm_gain, dt_bias, a_log, d_skip)
    flat = [jnp.pad(p, ((0, 0), (0, lanes - p.shape[1]))) for p in given]
    flat = jnp.concatenate(flat + [jnp.zeros((6, lanes), jnp.bfloat16)], axis=0)
    in_rows = jnp.swapaxes(in_weight[0], 0, 1)
    w_in0, w_out0, source, normed0, small, norms = enter_first(
        in_rows, out_weight[0], boundary_in, flat
    )
    late_in = after(boundary_in, source)[0, :, 0]
    arrivals = [
        lax.ppermute(
            late_in[m], axes, [(spot(1, zz, rr), home(m, zz, rr)) for zz in range(4) for rr in range(4)]
        )
        for m in range(MICRO)
    ]
    cotangent = jnp.where(z < 2, *arrivals)

    order = jnp.stack([lengths[:, 0], seq_order[:, 0]])
    order = jnp.where(x == z % 2, order, swap_x(order))
    order = lax.dynamic_index_in_dim(order, z // 2, 1, False)
    chosen = (order[1][:, None] == jnp.arange(NSEQ, dtype=jnp.int32)[None, :]).astype(jnp.int32)
    finish = jnp.cumsum(jnp.sum(chosen * order[0][None, :], axis=1), dtype=jnp.int32)

    def segment_of(positions):
        found = jnp.sum((positions[:, None] >= finish[None, :]).astype(jnp.int32), axis=1)
        return jnp.where(positions < 0, -1, found)

    token = jnp.arange(rows, dtype=jnp.int32)
    segment = segment_of(token)
    opening = token // Q * Q
    columns = [segment_of(token - lag) == segment for lag in range(1, KW)]
    columns.append(segment_of(opening - 1) == segment)
    columns.append(segment_of(opening + (Q - 1)) == segment)
    columns = [column.astype(jnp.float32) for column in columns] + [segment.astype(jnp.float32)]
    marks = jnp.stack(columns + [jnp.zeros((rows,), jnp.float32)] * 2, axis=1)
    seg_row = segment.astype(jnp.float32)[None]

    def own(v):
        return lax.dynamic_slice_in_dim(v, (2 * x + c) * block, block, 0)

    def row_sums(v):
        v = v + swap_core(v)
        return v + swap_x(v)

    def forward(layer, normed, w_in):
        projected = projection(normed, w_in)
        gg, squares, mixer, starts = mixer_forward(layer, projected, marks, seg_row, small)
        return gg, squares.reshape((rows // LANES, LANES)), (normed, projected, mixer, starts)

    def inverse(sums):
        return lax.rsqrt(sums / DI + EPSILON)

    def out_sum(gg, out_inv, g):
        outgoing = low(gg.astype(jnp.float32) * out_inv)
        grad = low(mm(outgoing, g, 0, 0)).reshape((4, OUT_PART, D))
        return lax.psum_scatter(grad, "shard", scatter_dimension=0, tiled=False)

    def backward(layer, kept, og, per_row, ready=(), sent_on=()):
        normed, projected, out, starts = kept
        gate_grad, out_grad, gains = gate_backward(
            layer, projected, small, out, og, per_row, DI
        )
        gate = low(mm(gate_grad, normed, 0, 0)).reshape((2, GATE_HALF, D))
        sent = lax.dynamic_index_in_dim(gate, 1 - y, 0, False)
        received = swap_y(sent)
        gate = lax.dynamic_index_in_dim(gate, y, 0, False)
        pg, conv, head = mixer_backward(
            layer, projected, marks, seg_row, small, out, starts, out_grad, after(gate_grad, sent, *ready)
        )
        pg = after(pg, *sent_on)
        gate = low(gate.astype(jnp.float32) + received.astype(jnp.float32))
        rest = low(mm(pg[:, GATE:], normed, 0, 0))
        return pg, gate, rest, (conv, gains, head)

    gg0, squares0, kept0 = forward(0, normed0, w_in0)
    theirs, mine = group_parts(gg0, w_out0)
    w_in1, w_out1, added0, middle, normed1, g1, out_inv0 = enter_second(
        in_rows, out_weight[0], theirs, mine, squares0, source, norms[1, 0:1], cotangent
    )
    out_inv0 = out_inv0.reshape((rows, 1))
    og1 = mm(g1, w_out1, 1, 1)
    gg1, squares1, kept1 = forward(1, normed1, w_in1)
    dots1 = jnp.sum(gg1.astype(jnp.float32) * og1, axis=1).reshape((rows // LANES, LANES))
    sums1 = row_sums(jnp.stack([squares1, dots1]))
    out_inv1 = inverse(sums1[0]).reshape((rows, 1))
    per_row1 = jnp.concatenate([out_inv1, out_inv1 * sums1[1].reshape((rows, 1))], axis=1)
    out_theirs, out_mine = group_parts(gg1, w_out1)
    out_part1 = out_sum(gg1, out_inv1, g1)
    pg1, gate1, rest1, small_grads1 = backward(1, kept1, og1, per_row1)
    in_own, out_own, result, middle_grad, g0, dots0, norm_grad1, *_ = layer_sums(
        1, gate1, rest1, out_part1, pg1, w_in1, middle, cotangent, norms[1, 0:1], added0,
        out_theirs, out_mine, own(out_inv1),
    )
    dots0 = dots0[:, : block // LANES].reshape((rows, 1))

    def on_second(v, flip):
        return lax.ppermute(v, ("section", "rep"), [(4 + i, 4 + (i ^ flip)) for i in range(4)])

    in_near, in_across = on_second(in_own, 1), on_second(in_own, 2)
    out_near = on_second(out_own, 1)
    in_far = on_second(in_across, 1)
    og0 = mm(g0, w_out0, 1, 1)
    out_part0 = out_sum(gg0, out_inv0, g0)
    result = after(result, out_part0)
    results = [
        lax.ppermute(
            result, axes, [(home(m, zz, rr), spot(1, zz, rr)) for zz in range(4) for rr in range(4)]
        )
        for m in range(MICRO)
    ]
    per_row0 = jnp.concatenate([out_inv0, dots0], axis=1)
    pg0, gate0, rest0, small_grads0 = backward(
        0, kept0, og0, per_row0, (in_own, out_own), (in_near, in_across, out_near, result)
    )
    in_all, out_all, entry_grads, *totals = layer_sums(
        0, gate0, rest0, out_part0, pg0, w_in0, source, middle_grad, norms[0, 0:1], norm_grad1,
        *small_grads0, *small_grads1, in_own, in_near, in_across, in_far, out_own, out_near,
    )
    in_total, out_total = assemble_rows(in_all, out_all)
    in_total = jnp.swapaxes(in_total, 0, 1)[None]

    boundary = jnp.stack(
        [jnp.where(c == 0, entry_grads[m], results[m]) for m in range(MICRO)]
    ).astype(jnp.float32)[None, :, None]

    norm_total, conv_total, bias_total, dt_total, log_total, skip_total, gain_total = totals
    return (
        boundary,
        norm_total,
        in_total,
        conv_total[None],
        bias_total,
        dt_total,
        log_total,
        skip_total,
        gain_total,
        out_total,
    )


def solution(mesh):
    fits = mesh.shape["shard"] == GROUP and mesh.shape["rep"] == 4
    return jax.shard_map(
        per_device_split if fits else per_device,
        mesh=mesh,
        in_specs=(
            P("section", None, "rep", "shard", None),
            P(None, "rep", None),
            P(None, "rep", None),
            P("section", "shard"),
            P("section", "shard", None),
            P("section", None, "shard"),
            P("section", "shard"),
            P("section", "shard"),
            P("section", "shard"),
            P("section", "shard"),
            P("section", "shard"),
            P("section", "shard", None),
        ),
        out_specs=(
            P("section", None, "rep", "shard", None),
            P("section", "shard"),
            P("section", "shard", None),
            P("section", None, "shard"),
            P("section", "shard"),
            P("section", "shard"),
            P("section", "shard"),
            P("section", "shard"),
            P("section", "shard"),
            P("section", "shard", None),
        ),
        check_vma=False,
    )
```
